32 devices in a mesh: wide: 16 (over z, x, core), narrow: 2 (over y).
Axes of the slice: x: 2, y: 2, z: 4, core: 2. Of those that a mesh axis runs over, the one named last changes fastest.
Arguments:
- tokens: bfloat16 [16384, 768], P(('wide', 'narrow')), may hold values from -6 to 6
- cotangent: bfloat16 [16384, 768], P(('wide', 'narrow')), may hold values from -6 to 6
- clip_lengths: int32 [32, 3], P(('wide', 'narrow')), may hold values from 0 to 512, as said below
- ln1_gain: bfloat16 [768], P(('wide', 'narrow')), may hold values from 0.099609375 to 1.8984375
- ln1_bias: bfloat16 [768], P(('wide', 'narrow')), may hold values from -3 to 3
- qkv_weight: bfloat16 [768, 2304], P(('wide', 'narrow')), may hold values from -0.21875 to 0.21875
- qv_bias: bfloat16 [1536], P(('wide', 'narrow')), may hold values from -3 to 3
- out_weight: bfloat16 [768, 768], P(('wide', 'narrow')), may hold values from -0.875 to 0.875
- out_bias: bfloat16 [768], P(('wide', 'narrow')), may hold values from -3 to 3
- ln2_gain: bfloat16 [768], P(('wide', 'narrow')), may hold values from 0.099609375 to 1.8984375
- ln2_bias: bfloat16 [768], P(('wide', 'narrow')), may hold values from -3 to 3
- up_weight: bfloat16 [768, 3072], P(('wide', 'narrow')), may hold values from -0.21875 to 0.21875
- up_bias: bfloat16 [3072], P(('wide', 'narrow')), may hold values from -3 to 3
- down_weight: bfloat16 [3072, 768], P(('wide', 'narrow')), may hold values from -0.109375 to 0.109375
- down_bias: bfloat16 [768], P(('wide', 'narrow')), may hold values from -3 to 3
Outputs:
- block_out: bfloat16 [16384, 768], P(('wide', 'narrow'))
- tokens_grad: float32 [16384, 768], P(('wide', 'narrow'))
- ln1_gain_grad: float32 [768], P(('wide', 'narrow'))
- ln1_bias_grad: float32 [768], P(('wide', 'narrow'))
- qkv_weight_grad: float32 [768, 2304], P(('wide', 'narrow'))
- qv_bias_grad: float32 [1536], P(('wide', 'narrow'))
- out_weight_grad: float32 [768, 768], P(('wide', 'narrow'))
- out_bias_grad: float32 [768], P(('wide', 'narrow'))
- ln2_gain_grad: float32 [768], P(('wide', 'narrow'))
- ln2_bias_grad: float32 [768], P(('wide', 'narrow'))
- up_weight_grad: float32 [768, 3072], P(('wide', 'narrow'))
- up_bias_grad: float32 [3072], P(('wide', 'narrow'))
- down_weight_grad: float32 [3072, 768], P(('wide', 'narrow'))
- down_bias_grad: float32 [768], P(('wide', 'narrow'))
The draws below stay inside these ranges and needn't reach their ends.
Inputs may be any that keep to these rules, and one draw needn't show every extreme that they name: `clip_lengths`: each row is either one clip of 512 tokens followed by empty slots (0), or 3 clips of 129 to 170 tokens each; some row is of the first kind.
All inputs are finite; a program needn't handle non-finite values.
Results may differ from the reference program's by a relative error of at most 0.012.
Values may be sent and summed in bfloat16 or wider, within the bound.
A program may use at most 192 MiB of HBM per device.

```python
import math
import jax
import jax.numpy as jnp
from jax import lax

D = 768
H = 12
FF = 3072
TOK_DEV = 512
CLIPS_DEV = 3
SHORT_MOST = 170
TOKENS = 16384
DEVICES = 32


def draw_clip_lengths(key, part):
    key = jax.random.fold_in(key, 11)
    key_kind, key_pick, key_short = jax.random.split(key, 3)
    long_device = jax.random.randint(key_kind, (DEVICES,), 0, 4) == 0
    chosen = jax.random.randint(key_pick, (), 0, DEVICES)
    long_device = jnp.logical_or(long_device, jnp.arange(DEVICES) == chosen)
    short_rows = SHORT_MOST - jax.random.randint(key_short, (DEVICES, CLIPS_DEV), 0, max(SHORT_MOST // 4, 1))
    long_rows = jnp.where(jnp.arange(CLIPS_DEV)[None, :] == 0, TOK_DEV, 0) * jnp.ones((DEVICES, 1), jnp.int32)
    return jnp.where(long_device[:, None], long_rows, short_rows).astype(jnp.int32)


def with_spikes(values, own_key, source, target, shards_of, factor):
    owner, partner = [(jnp.arange(values.shape[dim]) // (values.shape[dim] // shards_of)).reshape([-1 if axis == dim else 1 for axis in range(values.ndim)]) for dim in (source, target)]
    chosen = jax.random.permutation(own_key, shards_of)[partner]
    strong = (owner == chosen) | (owner == (partner + shards_of // 2) % shards_of)
    return jnp.where(strong, factor * values, values)


def level_of(rng, extent, cuts, least, largest):
    level, own = 1.0, jax.random.fold_in(rng, 6)
    for axis_at, blocks in cuts:
        steps = jnp.exp(jax.random.uniform(jax.random.fold_in(own, axis_at), (blocks,), jnp.float32, least / len(cuts), largest / len(cuts)))
        level = level * jnp.repeat(steps, extent[axis_at] // blocks).reshape([-1 if axis == axis_at else 1 for axis in range(len(extent))])
    return level


def normal_values(rng, shape, width, bound, cuts=(), held_as=jnp.bfloat16):
    level = level_of(rng, shape, cuts, -0.22, 0.18) if cuts else 1.0
    entries = jax.random.normal(rng, shape, jnp.float32) * width * level
    return jnp.minimum(jnp.maximum(entries, -bound), bound).astype(held_as)


def heavy_noise(key, extent, scale, reach, cuts, heavy, kind=jnp.bfloat16):
    values = scale * jax.random.normal(key, extent, jnp.float32)
    if cuts:
        values = values * level_of(key, extent, cuts, -0.22, 0.18)
    return jnp.clip(with_spikes(values, jax.random.fold_in(key, 3), *heavy), -reach, reach).astype(kind)


def setup_inputs(seed: int = 0) -> dict:
    splits = jax.random.split(jax.random.key(seed), 16)
    return {
        "tokens": heavy_noise(splits[0], (TOKENS, D), 1.0, 6.0, ((0, 32),), (0, 1, 32, 2.75)),
        "cotangent": normal_values(splits[1], (TOKENS, D), 1.0, 6.0, ((0, 32),)),
        "clip_lengths": draw_clip_lengths(jax.random.fold_in(splits[15], 71), 0),
        "ln1_gain": jnp.clip(1.0 + 0.18 * jax.random.normal(splits[3], (D,), jnp.float32), 0.099609375, 1.8984375).astype(jnp.bfloat16),
        "ln1_bias": normal_values(splits[4], (D,), 0.5, 3.0, ((0, 32),)),
        "qkv_weight": normal_values(splits[5], (D, 3 * D), D ** -0.5, 0.21875, ((0, 32),)),
        "qv_bias": normal_values(splits[6], (2 * D,), 0.5, 3.0, ((0, 32),)),
        "out_weight": normal_values(splits[7], (D, D), (D // 16) ** -0.5, 0.875, ((0, 32),)),
        "out_bias": normal_values(splits[8], (D,), 0.5, 3.0, ((0, 32),)),
        "ln2_gain": jnp.clip(1.0 + 0.18 * jax.random.normal(splits[9], (D,), jnp.float32), 0.099609375, 1.8984375).astype(jnp.bfloat16),
        "ln2_bias": normal_values(splits[10], (D,), 0.5, 3.0, ((0, 32),)),
        "up_weight": normal_values(splits[11], (D, FF), D ** -0.5, 0.21875, ((0, 32),)),
        "up_bias": normal_values(splits[12], (FF,), 0.5, 3.0, ((0, 32),)),
        "down_weight": normal_values(splits[13], (FF, D), FF ** -0.5, 0.109375, ((0, 32),)),
        "down_bias": normal_values(splits[14], (D,), 0.5, 3.0, ((0, 32),)),
    }


HIGHEST = lax.Precision.HIGHEST
MASKED_SCORE = -1000000000.0

@jax.custom_vjp
def low(v):
    return lax.optimization_barrier(v.astype(jnp.bfloat16)).astype(jnp.float32)

@jax.custom_vjp
def low_back(v):
    return v

def low_keep(v):
    return (low(v), None)

def low_pass(kept, grad):
    return (grad,)

def back_keep(v):
    return (v, None)

def back_low(kept, grad):
    return (low(grad),)
low.defvjp(low_keep, low_pass)
low_back.defvjp(back_keep, back_low)

def layer_norm(inputs, ln_gain, ln_bias):
    row_mean = lax.optimization_barrier(jnp.mean(inputs, axis=-1, keepdims=True))
    centred = inputs - row_mean
    spread = lax.optimization_barrier(jnp.mean(centred * centred, axis=-1, keepdims=True))
    return centred * lax.rsqrt(spread + 1e-06) * ln_gain + ln_bias

def gelu_exact(inputs):
    return 0.5 * inputs * (1.0 + lax.erf(inputs * 0.7071067811865476))

def clip_index(lengths, row_count):
    clip_ends = jnp.cumsum(lengths).astype(jnp.int32)
    position = jnp.arange(row_count, dtype=jnp.int32)
    return lax.optimization_barrier(jnp.sum((position[:, None] >= clip_ends[None, :]).astype(jnp.int32), axis=1))

def device_forward(inputs, segment, params):
    gain_one, bias_one, merged_weight, merged_bias, proj_weight, proj_bias, gain_two, bias_two, w_up, b_up, w_down, b_down = params
    row_count, model_width = inputs.shape
    head_size = model_width // H
    score_scale = 1.0 / math.sqrt(head_size)
    live_rows = (segment < CLIPS_DEV).astype(jnp.float32)[:, None]
    normed_one = low(layer_norm(inputs, gain_one, bias_one))
    full_bias = jnp.concatenate([merged_bias[:model_width], jnp.zeros((model_width,), jnp.float32), merged_bias[model_width:]])
    merged_rows = low(low_back(jnp.dot(normed_one, merged_weight, precision=HIGHEST) + full_bias))
    queries = merged_rows[:, :model_width].reshape(row_count, H, head_size)
    key_rows = merged_rows[:, model_width:2 * model_width].reshape(row_count, H, head_size)
    value_rows = merged_rows[:, 2 * model_width:].reshape(row_count, H, head_size)
    scores = low_back(jnp.einsum('qhd,khd->hqk', queries, key_rows, precision=HIGHEST) * score_scale)
    allowed = segment[:, None] == segment[None, :]
    scores = jnp.where(allowed[None], scores, MASKED_SCORE)
    highest = lax.optimization_barrier(jnp.max(scores, axis=-1, keepdims=True))
    raised = jnp.exp(scores - highest)
    softmax = raised / lax.optimization_barrier(jnp.sum(raised, axis=-1, keepdims=True))
    attended = jnp.einsum('hqk,khd->qhd', low(softmax), value_rows, precision=HIGHEST).reshape(row_count, model_width)
    attended = low(low_back(attended))
    branch_one = low_back(jnp.dot(attended, proj_weight, precision=HIGHEST) + proj_bias)
    middle = inputs + live_rows * branch_one
    normed_two = low(layer_norm(middle, gain_two, bias_two))
    hidden_pre = low_back(jnp.dot(normed_two, w_up, precision=HIGHEST) + b_up)
    activated = low(gelu_exact(hidden_pre))
    branch_two = low_back(jnp.dot(activated, w_down, precision=HIGHEST) + b_down)
    return middle + live_rows * branch_two

def reference(tokens, cotangent, clip_lengths, ln1_gain, ln1_bias, qkv_weight, qv_bias, out_weight, out_bias, ln2_gain, ln2_bias, up_weight, up_bias, down_weight, down_bias):
    params = tuple((member.astype(jnp.float32) for member in (ln1_gain, ln1_bias, qkv_weight, qv_bias, out_weight, out_bias, ln2_gain, ln2_bias, up_weight, up_bias, down_weight, down_bias)))
    device_count = clip_lengths.shape[0]
    model_width = tokens.shape[1]
    inputs = tokens.astype(jnp.float32).reshape(device_count, -1, model_width)
    upstream = cotangent.astype(jnp.float32).reshape(device_count, -1, model_width)
    row_count = inputs.shape[1]
    segments = jax.vmap(lambda lengths: clip_index(lengths, row_count))(clip_lengths)
    checked = jax.checkpoint(device_forward)

    def total_pass(all_inputs, all_params):

        def advance(carried, element):
            return (carried, checked(element[0], element[1], all_params))
        _, outputs = lax.scan(advance, jnp.zeros((), jnp.float32), (all_inputs, segments))
        return outputs
    outputs, pull_back = jax.vjp(total_pass, inputs, params)
    grad_inputs, grad_params = pull_back(upstream)
    return (outputs.reshape(-1, model_width).astype(jnp.bfloat16), grad_inputs.reshape(-1, model_width), grad_params[0], grad_params[1], grad_params[2], grad_params[3], grad_params[4], grad_params[5], grad_params[6], grad_params[7], grad_params[8], grad_params[9], grad_params[10], grad_params[11])
```

```python
import functools
import math

import jax
import jax.numpy as jnp
from jax import lax
from jax.experimental import pallas as pl
from jax.experimental.pallas import tpu as pltpu
from jax.sharding import PartitionSpec as P

H = 12
MASKED_SCORE = -1000000000.0
MESH = pl.DeviceIdType.MESH
F32 = jnp.float32
BF16 = jnp.bfloat16
ALL = slice(None)
CHUNK = 64


def layer_norm(inputs, ln_gain, ln_bias):
    row_mean = jnp.mean(inputs, axis=-1, keepdims=True)
    centred = inputs - row_mean
    spread = jnp.mean(centred * centred, axis=-1, keepdims=True)
    return centred * lax.rsqrt(spread + 1e-06) * ln_gain + ln_bias


def gelu_exact(inputs):
    return 0.5 * inputs * (1.0 + lax.erf(inputs * 0.7071067811865476))


def clip_index(lengths, row_count):
    clip_ends = jnp.cumsum(lengths)
    position = jnp.arange(row_count, dtype=jnp.int32)
    return jnp.sum((position[:, None] >= clip_ends[None, :]).astype(jnp.int32), axis=1)


def split_heads(matrix, head_count):
    row_count = matrix.shape[0]
    return matrix.reshape(row_count, head_count, -1).transpose(1, 0, 2)


def join_heads(stacked):
    head_count, row_count, head_size = stacked.shape
    return stacked.transpose(1, 0, 2).reshape(row_count, head_count * head_size)


def attend_forward(queries, key_rows, value_rows, segment, block_rows, score_scale):
    scores = (
        lax.dot_general(
            queries, key_rows, (((1,), (1,)), ((), ())), preferred_element_type=jnp.float32
        )
        * score_scale
    )
    allowed = segment[0:block_rows, None] == segment[None, :]
    scores = jnp.where(allowed, scores, MASKED_SCORE)
    highest = jnp.max(scores, axis=1, keepdims=True)
    raised = jnp.exp(scores - highest)
    denominator = jnp.sum(raised, axis=1, keepdims=True)
    softmax = (raised / denominator).astype(jnp.bfloat16)
    outputs = [jnp.dot(softmax, value_rows, preferred_element_type=jnp.float32)]
    totals = [highest + jnp.log(denominator)]
    return (jnp.concatenate(outputs, 0), jnp.concatenate(totals, 0))


def attend_backward(
    queries, key_rows, value_rows, segment, grad_out, lse_rows, block_rows, score_scale
):
    grad_keys = jnp.zeros(key_rows.shape, jnp.float32)
    grad_values = jnp.zeros(value_rows.shape, jnp.float32)
    g_rows = grad_out[0:block_rows]
    scores = (
        lax.dot_general(
            queries, key_rows, (((1,), (1,)), ((), ())), preferred_element_type=jnp.float32
        )
        * score_scale
    )
    allowed = segment[0:block_rows, None] == segment[None, :]
    softmax = jnp.where(allowed, jnp.exp(scores - lse_rows[0:block_rows]), 0.0)
    grad_values = grad_values + lax.dot_general(
        softmax.astype(jnp.bfloat16),
        g_rows,
        (((0,), (0,)), ((), ())),
        preferred_element_type=jnp.float32,
    )
    grad_probs = lax.dot_general(
        g_rows, value_rows, (((1,), (1,)), ((), ())), preferred_element_type=jnp.float32
    )
    grad_scores = (
        softmax * (grad_probs - jnp.sum(softmax * grad_probs, axis=1, keepdims=True))
    ).astype(jnp.bfloat16)
    grad_queries = [
        jnp.dot(grad_scores, key_rows, preferred_element_type=jnp.float32) * score_scale
    ]
    grad_keys = (
        grad_keys
        + lax.dot_general(
            grad_scores, queries, (((0,), (0,)), ((), ())), preferred_element_type=jnp.float32
        )
        * score_scale
    )
    return (jnp.concatenate(grad_queries, 0), grad_keys, grad_values)


def by_collectives(
    tokens,
    cotangent,
    clip_lengths,
    ln1_gain,
    ln1_bias,
    qkv_weight,
    qv_bias,
    out_weight,
    out_bias,
    ln2_gain,
    ln2_bias,
    up_weight,
    up_bias,
    down_weight,
    down_bias,
):
    gathered = (
        lax.all_gather(ln1_gain, ("wide", "narrow"), axis=0, tiled=True),
        lax.all_gather(ln1_bias, ("wide", "narrow"), axis=0, tiled=True),
        lax.all_gather(qkv_weight, ("wide", "narrow"), axis=0, tiled=True),
        lax.all_gather(qv_bias, ("wide", "narrow"), axis=0, tiled=True),
        lax.all_gather(out_weight, ("wide", "narrow"), axis=0, tiled=True),
        lax.all_gather(out_bias, ("wide", "narrow"), axis=0, tiled=True),
        lax.all_gather(ln2_gain, ("wide", "narrow"), axis=0, tiled=True),
        lax.all_gather(ln2_bias, ("wide", "narrow"), axis=0, tiled=True),
        lax.all_gather(up_weight, ("wide", "narrow"), axis=0, tiled=True),
        lax.all_gather(up_bias, ("wide", "narrow"), axis=0, tiled=True),
        lax.all_gather(down_weight, ("wide", "narrow"), axis=0, tiled=True),
        lax.all_gather(down_bias, ("wide", "narrow"), axis=0, tiled=True),
    )
    (
        gain_one,
        bias_one,
        merged_weight,
        merged_bias,
        proj_weight,
        proj_bias,
        gain_two,
        bias_two,
        w_up,
        b_up,
        w_down,
        b_down,
    ) = gathered
    inputs = tokens.astype(jnp.float32)
    row_count, model_width = inputs.shape
    head_size = model_width // H
    score_scale = 1.0 / math.sqrt(head_size)
    block_rows = min(512, row_count)
    clip_count = clip_lengths.shape[1]
    segment = clip_index(clip_lengths[0], row_count)
    live_rows = (segment < clip_count).astype(jnp.float32)[:, None]
    normed_one = layer_norm(
        inputs, gain_one.astype(jnp.float32), bias_one.astype(jnp.float32)
    ).astype(jnp.bfloat16)
    bias_float = merged_bias.astype(jnp.float32)
    full_bias = jnp.concatenate(
        [bias_float[:model_width], jnp.zeros((model_width,), jnp.float32), bias_float[model_width:]]
    )
    merged_rows = (
        jnp.dot(normed_one, merged_weight, preferred_element_type=jnp.float32) + full_bias
    ).astype(jnp.bfloat16)
    q_heads = split_heads(merged_rows[:, :model_width], H)
    k_heads = split_heads(merged_rows[:, model_width : 2 * model_width], H)
    v_heads = split_heads(merged_rows[:, 2 * model_width :], H)

    def head_forward(triple):
        return attend_forward(triple[0], triple[1], triple[2], segment, block_rows, score_scale)

    att_heads, lse_heads = lax.map(head_forward, (q_heads, k_heads, v_heads))
    attended = join_heads(att_heads).astype(jnp.bfloat16)
    branch_one = jnp.dot(
        attended, proj_weight, preferred_element_type=jnp.float32
    ) + proj_bias.astype(jnp.float32)
    middle = inputs + live_rows * branch_one
    normed_two = layer_norm(
        middle, gain_two.astype(jnp.float32), bias_two.astype(jnp.float32)
    ).astype(jnp.bfloat16)
    hidden_pre = jnp.dot(normed_two, w_up, preferred_element_type=jnp.float32) + b_up.astype(
        jnp.float32
    )
    activated, gelu_pull = jax.vjp(gelu_exact, hidden_pre)
    activated = activated.astype(jnp.bfloat16)
    branch_two = jnp.dot(activated, w_down, preferred_element_type=jnp.float32) + b_down.astype(
        jnp.float32
    )
    block_out = (middle + live_rows * branch_two).astype(jnp.bfloat16)
    back_gain_one, back_merged, back_proj, back_gain_two, back_up, back_down = (
        lax.all_gather(ln1_gain, ("wide", "narrow"), axis=0, tiled=True),
        lax.all_gather(qkv_weight, ("wide", "narrow"), axis=0, tiled=True),
        lax.all_gather(out_weight, ("wide", "narrow"), axis=0, tiled=True),
        lax.all_gather(ln2_gain, ("wide", "narrow"), axis=0, tiled=True),
        lax.all_gather(up_weight, ("wide", "narrow"), axis=0, tiled=True),
        lax.all_gather(down_weight, ("wide", "narrow"), axis=0, tiled=True),
    )
    upstream = cotangent.astype(jnp.float32)
    grad_two = (live_rows * upstream).astype(jnp.bfloat16)
    grad_b_down = jnp.sum(grad_two.astype(jnp.float32), axis=0)
    grad_w_down = jnp.einsum("tf,td->fd", activated, grad_two, preferred_element_type=jnp.float32)
    grad_act = jnp.einsum("td,fd->tf", grad_two, back_down, preferred_element_type=jnp.float32)
    grad_hidden = gelu_pull(grad_act)[0].astype(jnp.bfloat16)
    grad_b_up = jnp.sum(grad_hidden.astype(jnp.float32), axis=0)
    grad_w_up = jnp.einsum("td,tf->df", normed_two, grad_hidden, preferred_element_type=jnp.float32)
    grad_normed_two = jnp.einsum(
        "tf,df->td", grad_hidden, back_up, preferred_element_type=jnp.float32
    )
    _, norm_pull_two = jax.vjp(
        layer_norm, middle, back_gain_two.astype(jnp.float32), bias_two.astype(jnp.float32)
    )
    grad_middle_norm, grad_gain_two, grad_bias_two = norm_pull_two(grad_normed_two)
    grad_middle = upstream + grad_middle_norm
    grad_one = (live_rows * grad_middle).astype(jnp.bfloat16)
    grad_b_proj = jnp.sum(grad_one.astype(jnp.float32), axis=0)
    grad_w_proj = jnp.einsum("te,td->ed", attended, grad_one, preferred_element_type=jnp.float32)
    grad_att = jnp.einsum(
        "td,ed->te", grad_one, back_proj, preferred_element_type=jnp.float32
    ).astype(jnp.bfloat16)
    grad_att_heads = split_heads(grad_att, H)

    def head_backward(members):
        return attend_backward(
            members[0],
            members[1],
            members[2],
            segment,
            members[3],
            members[4],
            block_rows,
            score_scale,
        )

    grad_q, grad_k, grad_v = lax.map(
        head_backward, (q_heads, k_heads, v_heads, grad_att_heads, lse_heads)
    )
    grad_merged = jnp.concatenate(
        [join_heads(grad_q), join_heads(grad_k), join_heads(grad_v)], 1
    ).astype(jnp.bfloat16)
    column_sums = jnp.sum(grad_merged.astype(jnp.float32), axis=0)
    grad_merged_bias = jnp.concatenate([column_sums[:model_width], column_sums[2 * model_width :]])
    grad_w_merged = jnp.einsum(
        "te,tf->ef", normed_one, grad_merged, preferred_element_type=jnp.float32
    )
    grad_normed_one = jnp.einsum(
        "tf,ef->te", grad_merged, back_merged, preferred_element_type=jnp.float32
    )
    _, norm_pull_one = jax.vjp(
        layer_norm, inputs, back_gain_one.astype(jnp.float32), bias_one.astype(jnp.float32)
    )
    grad_input_norm, grad_gain_one, grad_bias_one = norm_pull_one(grad_normed_one)
    tokens_grad = grad_middle + grad_input_norm
    shares = (
        lax.psum_scatter(grad_gain_one, ("wide", "narrow"), scatter_dimension=0, tiled=True),
        lax.psum_scatter(grad_bias_one, ("wide", "narrow"), scatter_dimension=0, tiled=True),
        lax.psum_scatter(grad_w_merged, ("wide", "narrow"), scatter_dimension=0, tiled=True),
        lax.psum_scatter(grad_merged_bias, ("wide", "narrow"), scatter_dimension=0, tiled=True),
        lax.psum_scatter(grad_w_proj, ("wide", "narrow"), scatter_dimension=0, tiled=True),
        lax.psum_scatter(grad_b_proj, ("wide", "narrow"), scatter_dimension=0, tiled=True),
        lax.psum_scatter(grad_gain_two, ("wide", "narrow"), scatter_dimension=0, tiled=True),
        lax.psum_scatter(grad_bias_two, ("wide", "narrow"), scatter_dimension=0, tiled=True),
        lax.psum_scatter(grad_w_up, ("wide", "narrow"), scatter_dimension=0, tiled=True),
        lax.psum_scatter(grad_b_up, ("wide", "narrow"), scatter_dimension=0, tiled=True),
        lax.psum_scatter(grad_w_down, ("wide", "narrow"), scatter_dimension=0, tiled=True),
        lax.psum_scatter(grad_b_down, ("wide", "narrow"), scatter_dimension=0, tiled=True),
    )
    return (
        block_out,
        tokens_grad,
        shares[0],
        shares[1],
        shares[2],
        shares[3],
        shares[4],
        shares[5],
        shares[6],
        shares[7],
        shares[8],
        shares[9],
        shares[10],
        shares[11],
    )


def nt_dot(left, right):
    return lax.dot_general(left, right, (((1,), (1,)), ((), ())), preferred_element_type=F32)


def nn_dot(left, right):
    return jnp.dot(left, right, preferred_element_type=F32)


def rows_of(step, size=CHUNK):
    return pl.ds(pl.multiple_of(step * size, size), size)


def norm_parts(values):
    centred = values - jnp.mean(values, axis=-1, keepdims=True)
    scale = lax.rsqrt(jnp.mean(centred * centred, axis=-1, keepdims=True) + 1e-06)
    return centred * scale, scale


def fold_rows(values):
    return jnp.sum(values.reshape(-1, 8, values.shape[-1]), axis=0)


def gelu_both(u):
    tail = 0.5 * (1.0 + lax.erf(u * 0.7071067811865476))
    return u * tail, tail + u * jnp.exp(-0.5 * u * u) * 0.3989422804014327


def spread_maps(width, columns):
    column = lax.broadcasted_iota(jnp.int32, (1, columns), 1).astype(F32)
    group = jnp.floor((column + 0.5) * (1.0 / width))
    place = column - group * width
    lane = lax.broadcasted_iota(jnp.int32, (128, columns), 0).astype(F32)
    picks = jnp.where(lane == place, 1.0, 0.0).astype(BF16)
    owners = columns // width
    owner = lax.broadcasted_iota(jnp.int32, (owners, 8, columns), 0).astype(F32)
    mine = owner == group.reshape(1, 1, columns)
    return picks, mine


def spread(pieces, width, columns):
    picks, mine = spread_maps(width, columns)
    wide_rows = nn_dot(pieces.reshape(-1, 128).astype(BF16), picks)
    return jnp.sum(jnp.where(mine, wide_rows.reshape(-1, 8, columns), 0.0), axis=0)


def gather_back(vectors, width):
    columns = vectors.shape[-1]
    picks, mine = spread_maps(width, columns)
    rest = jnp.where(mine, vectors[None], 0.0).reshape(-1, columns)
    total = None
    for _ in range(3):
        part = rest.astype(BF16)
        rest = rest - part.astype(F32)
        term = nt_dot(part, picks)
        total = term if total is None else total + term
    return total.reshape(-1, 8, 128)


def layer_kernel(
    clip_ref, tok_ref, cot_ref, small_ref, wqkv_ref, wout_ref, wup_ref, wdown_ref,
    out_ref, tgrad_ref, gqkv_ref, gout_ref, gup_ref, gdown_ref, gsmall_ref,
    slabs, downs, smalls, gsmalls, weights, w_up,
    row_c, row_2, row_3, row_z, down_c, down_2, down_3, down_z, sm_c, sm_2, sm_3, sm_z,
    qkv, n1t, n1, att_t, middle, n2, n2t, g2, acc_out, acc_grad, act, grad_h, pre, grad_act,
    tok, cot, bias, lse, dq_t, vec24, vec48, vec96, sums, up_sums, block_out,
    ag_send, ag_recv, rs_send, rs_recv, local,
):
    n_z, width = slabs.shape[1], slabs.shape[-1]
    count = tok.shape[0]
    pairs = width // 128
    chunks = count // CHUNK
    wide_at, y = lax.axis_index("wide"), lax.axis_index("narrow")
    core = lax.rem(wide_at, 2)
    x = lax.rem(lax.div(wide_at, 2), 2)
    z = lax.div(wide_at, 4)
    own = {"z": z, "x": x, "c": core, "y": y}

    def device(z_at, x_at, c_at, y_at):
        return ((z_at * 2 + x_at) * 2 + c_at, y_at)

    def others(axis):
        if axis == "z":
            return [(step, device(lax.rem(z + step, n_z), x, core, y)) for step in range(1, n_z)]
        if axis == "x":
            return [(n_z, device(z, 1 - x, core, y))]
        if axis == "y":
            return [(n_z + 1, device(z, x, core, 1 - y))]
        return [(n_z + 2, device(z, x, 1 - core, y))]

    def index(held, **fixed):
        return tuple(fixed.get(a, ALL if a in held else own[a]) for a in "zxcy")

    def row_view(block, columns=ALL):
        def view(at):
            if isinstance(columns, slice):
                return slabs.at[(block, *at)]
            return slabs.at[(block, *at, ALL, columns)]
        return view

    def down_view(tile):
        def view(at):
            return downs.at[(tile, *at[1:])]
        return view

    def small_view(ref):
        def view(at):
            return ref.at[at]
        return view

    def ag_copies(unit, phase):
        view, order, row = unit
        axis = order[phase]
        at = index(order[:phase])
        return [
            pltpu.make_async_remote_copy(
                src_ref=view(at), dst_ref=view(at), send_sem=ag_send.at[row, sem], recv_sem=ag_recv.at[row, sem],
                device_id=to, device_id_type=MESH,
            )
            for sem, to in others(axis)
        ]

    def ag_start(unit, phase):
        for copy in ag_copies(unit, phase):
            copy.start()

    def ag_arrived(unit, phase):
        for copy in ag_copies(unit, phase):
            copy.wait_recv()

    def ag_sent(unit):
        for phase in range(len(unit[1])):
            for copy in ag_copies(unit, phase):
                copy.wait_send()

    half = width // 2
    left, right = pl.ds(0, half), pl.ds(half, half)
    small_unit = (small_view(smalls), "zxyc", 0)
    gather_groups = [[small_unit, (row_view(0, left), "zxyc", 1), (row_view(0, right), "zyxc", 2)]]
    for block in (1, 2, 3):
        gather_groups.append(
            [(row_view(block, left), "zxyc", 2 * block + 1), (row_view(block, right), "zyxc", 2 * block + 2)]
        )
    for tile in range(n_z):
        gather_groups.append(
            [(row_view(4 + tile), "zxyc", 9 + tile), (down_view(tile), "yxc", 9 + n_z + tile)]
        )
    down_first = (lambda at: downs.at[(at[0], *at[1:])], "z", 9 + 2 * n_z)

    def ag_stage(unit, stage):
        order = unit[1]
        phase = stage - (4 - len(order))
        if phase > 0:
            ag_arrived(unit, phase - 1)
        if 0 <= phase < len(order):
            ag_start(unit, phase)
        if stage == 4:
            ag_sent(unit)

    def ag_slot(slot):
        for stage in (4, 3, 2, 1, 0):
            group = slot - stage
            if 0 <= group < len(gather_groups):
                if group == 4 and stage == 1:
                    ag_arrived(down_first, 0)
                    ag_sent(down_first)
                for unit in gather_groups[group]:
                    ag_stage(unit, stage)
                if group == 2 and stage == 0:
                    ag_start(down_first, 0)

    def rs_index(order, phase, partner):
        done = order[:phase]
        at = []
        for a in "zxcy":
            if a in done:
                at.append(own[a])
            elif a == order[phase]:
                at.append(1 - own[a] if partner else own[a])
            else:
                at.append(ALL)
        return tuple(at)

    def rs_copies(unit, phase):
        view, order, row, landing = unit
        axis = order[phase]
        if axis == "z":
            copies = []
            for sem, to in others("z"):
                at = (lax.rem(z + sem, n_z), x, core, y)
                copies.append((view(at), landing[phase].at[sem - 1], sem, to))
        else:
            sem, to = others(axis)[0]
            copies = [(view(rs_index(order, phase, True)), landing[phase], sem, to)]
        return [
            pltpu.make_async_remote_copy(
                src_ref=src, dst_ref=dst, send_sem=rs_send.at[row, sem], recv_sem=rs_recv.at[row, sem],
                device_id=to, device_id_type=MESH,
            )
            for src, dst, sem, to in copies
        ]

    def rs_start(unit, phase):
        for copy in rs_copies(unit, phase):
            copy.start()

    def rs_arrived(unit, phase):
        for copy in rs_copies(unit, phase):
            copy.wait_recv()

    def rs_sent(unit):
        for phase in range(len(unit[1])):
            for copy in rs_copies(unit, phase):
                copy.wait_send()

    def add_into(target, source):
        total = target[...].astype(F32) + source[...].astype(F32)
        target[...] = total.astype(target.dtype)

    def rs_add(unit, phase):
        view, order, _, landing = unit
        at = rs_index(order, phase, False)
        target, source = view(at), landing[phase]
        free = len(target.shape) - 2
        if free == 0:
            add_into(target, source)
            return
        inner = target.shape[1:free]

        def step(i, carry):
            places = [()]
            for extent in inner:
                places = [place + (k,) for place in places for k in range(extent)]
            for place in places:
                add_into(target.at[(i, *place)], source.at[(i, *place)])
            return carry

        lax.fori_loop(0, target.shape[0], step, 0)

    def rs_final(unit, phase, result):
        view, _, _, landing = unit
        total = view((z, x, core, y))[...].astype(F32)
        for sem in range(n_z - 1):
            total = total + landing[phase].at[sem][...].astype(F32)
        result[...] = total

    def row_unit(block, order, row):
        return (row_view(block), order, row, (row_c.at[block], row_2.at[block], row_3.at[block], row_z.at[block]))

    def down_unit(tile, order, row):
        return (down_view(tile), order, row, (down_c.at[tile], down_2.at[tile], down_3.at[tile]))

    def block_columns(block):
        return pl.ds(block * width, width)

    up_units = [row_unit(4 + t, "cyxz", t) for t in range(n_z)]
    down_units = [down_unit(t, "cxy", n_z + t) for t in range(n_z)]
    out_unit = row_unit(3, "cyxz", 2 * n_z)
    v_unit = row_unit(2, "cxyz", 2 * n_z + 1)
    k_unit = row_unit(1, "cyxz", 2 * n_z + 2)
    q_unit = row_unit(0, "cxyz", 2 * n_z + 3)
    small_grad_unit = (small_view(gsmalls), "cyxz", 2 * n_z + 4, (sm_c, sm_2, sm_3, sm_z))
    down_last = (lambda at: downs.at[at], "z", 2 * n_z + 5, (down_z,))

    def rs_stage(unit, stage):
        order = unit[1]
        if 0 < stage <= len(order) and order[stage - 1] != "z":
            rs_arrived(unit, stage - 1)
            rs_add(unit, stage - 1)
        if stage < len(order):
            rs_start(unit, stage)

    def rs_end(unit, result):
        phase = len(unit[1]) - 1
        rs_arrived(unit, phase)
        rs_final(unit, phase, result)

    def local_copies():
        pairs_of = [(tok_ref, tok), (cot_ref, cot), (small_ref, smalls.at[z, x, core, y])]
        for block in range(3):
            pairs_of.append((wqkv_ref.at[:, block_columns(block)], slabs.at[block, z, x, core, y]))
        pairs_of.append((wout_ref, slabs.at[3, z, x, core, y]))
        for tile in range(n_z):
            pairs_of.append((wup_ref.at[:, block_columns(tile)], slabs.at[4 + tile, z, x, core, y]))
        pairs_of.append((wdown_ref, downs.at[z, x, core, y]))
        return [pltpu.make_async_copy(src, dst, local.at[k]) for k, (src, dst) in enumerate(pairs_of)]

    starts = local_copies()
    for copy in starts:
        copy.start()
    barrier = pltpu.get_barrier_semaphore()
    partners = [to for axis in "zxyc" for _, to in others(axis)]
    for to in partners:
        pl.semaphore_signal(barrier, inc=1, device_id=to, device_id_type=MESH)
    for copy in starts:
        copy.wait()
    pl.semaphore_wait(barrier, len(partners))
    ag_slot(0)

    ends = []
    for k in range(clip_ref.shape[1]):
        ends.append(clip_ref[0, k] + (ends[-1] if ends else 0))

    def segment_of(position):
        total = jnp.zeros(position.shape, jnp.int32)
        for end in ends:
            total = total + jnp.where(position >= end, 1, 0)
        return total

    across = segment_of(lax.broadcasted_iota(jnp.int32, (CHUNK, count), 1))

    def live_of(step):
        position = lax.broadcasted_iota(jnp.int32, (CHUNK, 1), 0) + step * CHUNK
        return jnp.where(position < ends[-1], 1.0, 0.0)

    def mask_step(i, total):
        down = segment_of(lax.broadcasted_iota(jnp.int32, (CHUNK, count), 0) + i * CHUNK)
        bias[rows_of(i), :] = jnp.where(down == across, 0.0, -1e30)
        grad = (live_of(i) * cot[rows_of(i), :].astype(F32)).astype(BF16)
        g2[rows_of(i), :] = grad
        return total + fold_rows(grad.astype(F32))

    down_bias_sum = lax.fori_loop(0, chunks, mask_step, jnp.zeros((8, width), F32))
    sums[...] = jnp.zeros_like(sums)
    sums[0, 7:8, :] = jnp.sum(down_bias_sum, axis=0, keepdims=True)

    ag_slot(1)
    ag_slot(2)
    ag_slot(3)
    ag_slot(4)

    vec24[...] = spread(smalls[...], 24, width)
    for k in range(2):
        vec48[k] = spread(smalls[k * n_z // 2 : (k + 1) * n_z // 2], 48, width)
    for k in range(n_z):
        vec96[k] = spread(smalls[k], 96, width)

    def norm_one(i, carry):
        normed, _ = norm_parts(tok[rows_of(i), :].astype(F32))
        n1[rows_of(i), :] = (normed * vec24[0:1, :] + vec24[1:2, :]).astype(BF16)
        return carry

    lax.fori_loop(0, chunks, norm_one, 0)

    def turn(source, target):
        def step(i, carry):
            at = rows_of(i, 128)
            target[at, :] = source[:, at].T
            return carry

        lax.fori_loop(0, pairs, step, 0)

    turn(n1, n1t)

    def assemble(block, target):
        def step(z_at, carry):
            for x_at in range(2):
                for c_at in range(2):
                    two = slabs[block, z_at, x_at, c_at].astype(F32)
                    size = 2 * two.shape[1]
                    first = pl.multiple_of(((z_at * 2 + x_at) * 2 + c_at) * size, 16)
                    target[pl.ds(first, size), :] = two.reshape(size, width).astype(BF16)
            return carry

        lax.fori_loop(0, n_z, step, 0)

    def project(block, add):
        assemble(block, weights.at[block])
        total = nn_dot(n1[...], weights[block])
        qkv[block] = (total if add is None else total + add).astype(BF16)

    project(0, vec48[0, 2:3, :])
    ag_slot(5)
    project(1, None)
    ag_slot(6)
    project(2, vec48[1, 2:3, :])

    lane = lax.broadcasted_iota(jnp.int32, (count, 128), 1)

    def one_head(values, head):
        keep = lane < 64 if head == 0 else lane >= 64
        return jnp.where(keep, values, jnp.zeros_like(values))

    q_block = 256
    parts = count // q_block

    def attend(p, carry):
        for when, slot in ((0, 7), (2, 8), (4, 9)):
            @pl.when(p == when)
            def _():
                ag_slot(slot)
        at = rows_of(p, 128)
        keys = qkv[1, :, at]
        queries = qkv[0, :, at] * 0.125
        values_t = qkv[2, :, at].T
        for head in range(2):
            mine = one_head(queries, head)
            for part in range(parts):
                span = slice(part * q_block, (part + 1) * q_block)
                scores = nt_dot(keys, mine[span]) + bias[:, span]
                highest = jnp.max(scores, axis=0, keepdims=True)
                raised = jnp.exp(scores - highest)
                total = jnp.sum(raised, axis=0, keepdims=True)
                chances = (raised * (1.0 / total)).astype(BF16)
                lse[p, head : head + 1, span] = highest + jnp.log(total)
                result = nn_dot(values_t[64 * head : 64 * head + 64], chances)
                att_t[pl.ds(pl.multiple_of(p * 128 + 64 * head, 64), 64), span] = result.astype(BF16)
        return carry

    lax.fori_loop(0, pairs, attend, 0)
    att = n1
    def turn_back(p, carry):
        at = rows_of(p, 128)
        att[:, at] = att_t[at, :].T
        return carry
    lax.fori_loop(0, pairs, turn_back, 0)

    assemble(3, weights.at[3])
    pre[...] = nn_dot(att[...], weights[3])

    def norm_two(i, carry):
        at = rows_of(i)
        branch = pre[at, :] + vec24[3:4, :]
        mid = tok[at, :].astype(F32) + live_of(i) * branch
        middle[at, :] = mid
        normed, _ = norm_parts(mid)
        n2[at, :] = (normed * vec24[4:5, :] + vec24[5:6, :]).astype(BF16)
        return carry

    lax.fori_loop(0, chunks, norm_two, 0)
    turn(n2, n2t)
    acc_out[...] = jnp.zeros_like(acc_out)
    acc_grad[...] = jnp.zeros_like(acc_grad)

    def store_rows(block, lhs_t, rhs):
        deep = width // n_z
        size = slabs.shape[-2]

        def step(z_at, carry):
            total = nn_dot(lhs_t[rows_of(z_at, deep), :], rhs)
            for x_at in range(2):
                for c_at in range(2):
                    for y_at in range(2):
                        first = ((x_at * 2 + c_at) * 2 + y_at) * size
                        slabs[block, z_at, x_at, c_at, y_at] = total[first : first + size].astype(BF16)
            return carry

        lax.fori_loop(0, n_z, step, 0)

    def feed(t, carry):
        for when in range(n_z):
            @pl.when(t == when)
            def _():
                if when + 10 < len(gather_groups) + 4:
                    ag_slot(when + 10)
                if when >= 1:
                    rs_stage(up_units[when - 1], 1)
                    rs_stage(down_units[when - 1], 1)
                if when >= 2:
                    rs_stage(up_units[when - 2], 2)
                    rs_stage(down_units[when - 2], 2)
                if when >= 3:
                    rs_stage(up_units[when - 3], 3)
                    rs_stage(down_units[when - 3], 3)
        assemble(4 + t, w_up)
        pre[...] = nn_dot(n2[...], w_up[...])
        w_down = downs[t].reshape(width, width)
        grad_act[...] = nt_dot(g2[...], w_down)
        up_bias = vec96[t, 6:7, :]

        def gelu_step(i, total):
            at = rows_of(i, 32)
            active, slope = gelu_both(pre[at, :] + up_bias)
            act[at, :] = active.astype(BF16)
            grad = (grad_act[at, :] * slope).astype(BF16)
            grad_h[at, :] = grad
            return total + fold_rows(grad.astype(F32))

        total = lax.fori_loop(0, count // 32, gelu_step, jnp.zeros((8, width), F32))
        up_sums[t, 6:7, :] = jnp.sum(total, axis=0, keepdims=True)
        acc_out[...] += nn_dot(act[...], w_down)
        acc_grad[...] += nt_dot(grad_h[...], w_up[...])
        store_rows(4 + t, n2t, grad_h[...])
        for j in range(pairs):
            span = slice(j * 128, (j + 1) * 128)
            piece = nn_dot(act[:, span].T, g2[...]).astype(BF16)
            size = downs.shape[-2]
            at = j * 128
            while at < (j + 1) * 128:
                owner, inside = at // size, at % size
                length = min(size - inside, (j + 1) * 128 - at)
                downs[t, owner // 4, owner // 2 % 2, owner % 2, inside : inside + length, :] = piece[at - j * 128 : at - j * 128 + length]
                at += length
        for when in range(n_z):
            @pl.when(t == when)
            def _():
                rs_stage(up_units[when], 0)
                rs_stage(down_units[when], 0)
        return carry

    up_sums[...] = jnp.zeros_like(up_sums)
    lax.fori_loop(0, n_z, feed, 0)

    def norm_two_back(i, carry):
        gain_sum, bias_sum, one_sum = carry
        at = rows_of(i)
        alive = live_of(i)
        mid = middle[at, :]
        block_out[at, :] = (mid + alive * (acc_out[at, :] + vec24[7:8, :])).astype(BF16)
        normed, scale = norm_parts(mid)
        e = acc_grad[at, :]
        scaled = e * vec24[4:5, :]
        inner = scaled - jnp.mean(scaled, axis=-1, keepdims=True) - normed * jnp.mean(scaled * normed, axis=-1, keepdims=True)
        grad_mid = cot[at, :].astype(F32) + inner * scale
        acc_grad[at, :] = grad_mid
        one = (alive * grad_mid).astype(BF16)
        g2[at, :] = one
        return (gain_sum + fold_rows(e * normed), bias_sum + fold_rows(e), one_sum + fold_rows(one.astype(F32)))

    zero = jnp.zeros((8, width), F32)
    gain_sum, bias_sum, one_sum = lax.fori_loop(0, chunks, norm_two_back, (zero, zero, zero))
    sums[0, 4:5, :] = jnp.sum(gain_sum, axis=0, keepdims=True)
    sums[0, 5:6, :] = jnp.sum(bias_sum, axis=0, keepdims=True)
    sums[0, 3:4, :] = jnp.sum(one_sum, axis=0, keepdims=True)
    out_copy = pltpu.make_async_copy(block_out, out_ref, local.at[0])
    out_copy.start()

    def rs_points(points):
        for unit, stage in points:
            rs_stage(unit, stage)

    rs_points([(up_units[3], 1), (down_units[3], 1), (up_units[2], 2), (down_units[2], 2), (up_units[1], 3), (down_units[1], 3)])
    store_rows(3, att_t, g2[...])
    rs_stage(out_unit, 0)
    grad_att = n2
    grad_att[...] = nt_dot(g2[...], weights[3]).astype(BF16)

    back_points = {
        0: [(up_units[3], 2), (down_units[3], 2), (up_units[2], 3), (down_units[2], 3), (out_unit, 1)],
        2: [(up_units[3], 3), (down_units[3], 3), (down_last, 0), (out_unit, 2)],
        4: [(out_unit, 3)],
    }

    def attend_back(p, carry):
        for when in sorted(back_points):
            @pl.when(p == when)
            def _():
                rs_points(back_points[when])
        at = rows_of(p, 128)
        keys = qkv[1, :, at]
        values = qkv[2, :, at]
        queries = qkv[0, :, at] * 0.125
        grads = grad_att[:, at]
        keys_t = keys.T
        grad_keys = jnp.zeros((count, 128), F32)
        grad_values = jnp.zeros((count, 128), F32)
        for head in range(2):
            my_queries, my_grads = one_head(queries, head), one_head(grads, head)
            for part in range(parts):
                span = slice(part * q_block, (part + 1) * q_block)
                scores = nt_dot(keys, my_queries[span]) + bias[:, span]
                chances = jnp.exp(scores - lse[p, head : head + 1, span])
                slopes = nt_dot(values, my_grads[span])
                level = jnp.sum(chances * slopes, axis=0, keepdims=True)
                grad_scores = (chances * (slopes - level)).astype(BF16)
                grad_values += nn_dot(chances.astype(BF16), my_grads[span])
                grad_keys += nn_dot(grad_scores, my_queries[span])
                dq_t[64 * head : 64 * head + 64, span] = nn_dot(keys_t[64 * head : 64 * head + 64], grad_scores) * 0.125
        qkv[0, :, at] = dq_t[...].T.astype(BF16)
        qkv[1, :, at] = grad_keys.astype(BF16)
        qkv[2, :, at] = grad_values.astype(BF16)
        return carry

    lax.fori_loop(0, pairs, attend_back, 0)

    store_rows(2, n1t, qkv[2])
    rs_stage(v_unit, 0)
    store_rows(1, n1t, qkv[1])
    rs_points([(k_unit, 0), (v_unit, 1)])
    store_rows(0, n1t, qkv[0])
    rs_points([(q_unit, 0), (k_unit, 1), (v_unit, 2)])
    pre[...] = nt_dot(qkv[2], weights[2])
    rs_points([(q_unit, 1), (k_unit, 2), (v_unit, 3)])
    pre[...] += nt_dot(qkv[1], weights[1])
    rs_points([(q_unit, 2), (k_unit, 3)])
    pre[...] += nt_dot(qkv[0], weights[0])

    def norm_one_back(i, carry):
        gain_sum, bias_sum, q_sum, v_sum = carry
        at = rows_of(i)
        normed, scale = norm_parts(tok[at, :].astype(F32))
        e = pre[at, :]
        scaled = e * vec24[0:1, :]
        inner = scaled - jnp.mean(scaled, axis=-1, keepdims=True) - normed * jnp.mean(scaled * normed, axis=-1, keepdims=True)
        acc_grad[at, :] = acc_grad[at, :] + inner * scale
        return (
            gain_sum + fold_rows(e * normed), bias_sum + fold_rows(e),
            q_sum + fold_rows(qkv[0, at, :].astype(F32)), v_sum + fold_rows(qkv[2, at, :].astype(F32)),
        )

    gain_sum, bias_sum, q_sum, v_sum = lax.fori_loop(0, chunks, norm_one_back, (zero, zero, zero, zero))
    tgrad_copy = pltpu.make_async_copy(acc_grad, tgrad_ref, local.at[1])
    tgrad_copy.start()
    sums[0, 0:1, :] = jnp.sum(gain_sum, axis=0, keepdims=True)
    sums[0, 1:2, :] = jnp.sum(bias_sum, axis=0, keepdims=True)
    sums[1, 2:3, :] = jnp.sum(q_sum, axis=0, keepdims=True)
    sums[2, 2:3, :] = jnp.sum(v_sum, axis=0, keepdims=True)
    gsmalls[...] = gather_back(sums[0], 24).reshape(gsmalls.shape)
    for k in range(2):
        part = gather_back(sums[1 + k], 48)
        span = slice(k * n_z // 2, (k + 1) * n_z // 2)
        gsmalls[span] = gsmalls[span] + part.reshape(n_z // 2, 2, 2, 2, 8, 128)
    for k in range(n_z):
        gsmalls[k] = gsmalls[k] + gather_back(up_sums[k], 96).reshape(2, 2, 2, 8, 128)
    rs_points([(small_grad_unit, 0), (q_unit, 3)])

    for t in range(n_z):
        rs_end(up_units[t], gup_ref.at[:, block_columns(t)])
    rs_end(down_last, gdown_ref)
    rs_points([(small_grad_unit, 1)])
    rs_end(out_unit, gout_ref)
    rs_points([(small_grad_unit, 2)])
    rs_end(v_unit, gqkv_ref.at[:, block_columns(2)])
    rs_points([(small_grad_unit, 3)])
    rs_end(k_unit, gqkv_ref.at[:, block_columns(1)])
    rs_end(q_unit, gqkv_ref.at[:, block_columns(0)])
    rs_end(small_grad_unit, gsmall_ref)
    for unit in [*up_units, *down_units, out_unit, v_unit, k_unit, q_unit, small_grad_unit, down_last]:
        rs_sent(unit)
    out_copy.wait()
    tgrad_copy.wait()


def by_kernel(
    n_z, tokens, cotangent, clip_lengths, ln1_gain, ln1_bias, qkv_weight, qv_bias, out_weight, out_bias,
    ln2_gain, ln2_bias, up_weight, up_bias, down_weight, down_bias,
):
    count, width = tokens.shape
    size, deep = qkv_weight.shape[0], down_weight.shape[0]
    blocks = 4 + n_z
    vectors = (ln1_gain, ln1_bias, qv_bias, out_bias, ln2_gain, ln2_bias, up_bias, down_bias)
    packed = jnp.stack([jnp.pad(v.astype(F32), (0, 128 - v.shape[0])) for v in vectors])
    vmem, dma = pltpu.VMEM, pltpu.SemaphoreType.DMA
    held = [
        vmem((blocks, n_z, 2, 2, 2, size, width), BF16),
        vmem((n_z, 2, 2, 2, deep, width), BF16),
        vmem((n_z, 2, 2, 2, 8, 128), F32),
        vmem((n_z, 2, 2, 2, 8, 128), F32),
        vmem((4, width, width), BF16),
        vmem((width, width), BF16),
        vmem((blocks, n_z, 2, 2, size, width), BF16),
        vmem((blocks, n_z, 2, size, width), BF16),
        vmem((blocks, n_z, size, width), BF16),
        vmem((blocks, n_z - 1, size, width), BF16),
        vmem((n_z, 2, 2, deep, width), BF16),
        vmem((n_z, 2, deep, width), BF16),
        vmem((n_z, deep, width), BF16),
        vmem((n_z - 1, deep, width), BF16),
        vmem((n_z, 2, 2, 8, 128), F32),
        vmem((n_z, 2, 8, 128), F32),
        vmem((n_z, 8, 128), F32),
        vmem((n_z - 1, 8, 128), F32),
        vmem((3, count, width), BF16),
        vmem((width, count), BF16),
        vmem((count, width), BF16),
        vmem((width, count), BF16),
        vmem((count, width), F32),
        vmem((count, width), BF16),
        vmem((width, count), BF16),
        vmem((count, width), BF16),
        vmem((count, width), F32),
        vmem((count, width), F32),
        vmem((count, width), BF16),
        vmem((count, width), BF16),
        vmem((count, width), F32),
        vmem((count, width), F32),
        vmem((count, width), BF16),
        vmem((count, width), BF16),
        vmem((count, count), F32),
        vmem((width // 128, 2, count), F32),
        vmem((128, count), F32),
        vmem((8, width), F32),
        vmem((2, 8, width), F32),
        vmem((n_z, 8, width), F32),
        vmem((3, 8, width), F32),
        vmem((n_z, 8, width), F32),
        vmem((count, width), BF16),
        dma((10 + 2 * n_z, n_z + 3)),
        dma((10 + 2 * n_z, n_z + 3)),
        dma((6 + 2 * n_z, n_z + 3)),
        dma((6 + 2 * n_z, n_z + 3)),
        dma((8 + n_z,)),
    ]
    anywhere, whole = pl.BlockSpec(memory_space=pl.ANY), pl.BlockSpec(memory_space=pltpu.VMEM)
    shape = jax.ShapeDtypeStruct
    out, grad, g_qkv, g_out, g_up, g_down, g_small = pl.pallas_call(
        layer_kernel,
        out_shape=(
            shape((count, width), BF16),
            shape((count, width), F32),
            shape(qkv_weight.shape, F32),
            shape(out_weight.shape, F32),
            shape(up_weight.shape, F32),
            shape(down_weight.shape, F32),
            shape((8, 128), F32),
        ),
        in_specs=[pl.BlockSpec(memory_space=pltpu.SMEM)] + [anywhere] * 7,
        out_specs=(anywhere, anywhere, whole, whole, whole, whole, whole),
        scratch_shapes=held,
        compiler_params=pltpu.CompilerParams(collective_id=0, has_side_effects=True, vmem_limit_bytes=VMEM_BYTES),
    )(clip_lengths, tokens, cotangent, packed, qkv_weight, out_weight, up_weight, down_weight)
    parts = [g_small[k, : v.shape[0]] for k, v in enumerate(vectors)]
    return (out, grad, parts[0], parts[1], g_qkv, parts[2], g_out, parts[3], parts[4], parts[5], g_up, parts[6], g_down, parts[7])


VMEM_BYTES = 63 * 1024 * 1024


def kernel_fits(n_wide, n_narrow, tokens, qkv_weight, up_weight, down_weight):
    width, hidden = qkv_weight.shape[0], up_weight.shape[1]
    n_z = n_wide // 4
    devices = n_wide * n_narrow
    return (
        n_narrow == 2
        and n_wide == 4 * n_z
        and n_z % 2 == 0
        and hidden == n_z * width
        and width % (8 * devices) == 0
        and hidden % (16 * devices) == 0
        and 2 * width // devices <= 128
        and hidden // devices <= 128
        and width // devices == 24
        and (tokens.shape[0] // devices) % 256 == 0
    )


def solution(mesh):
    n_wide, n_narrow = mesh.shape["wide"], mesh.shape["narrow"]
    both = ("wide", "narrow")
    matrix, vector = P(both, None), P(both)
    in_specs = (
        matrix, matrix, matrix, vector, vector, matrix, vector, matrix, vector, vector, vector, matrix, vector, matrix, vector,
    )
    out_specs = (
        matrix, matrix, vector, vector, matrix, vector, matrix, vector, vector, vector, matrix, vector, matrix, vector,
    )

    def run(*arrays):
        fits = kernel_fits(n_wide, n_narrow, arrays[0], arrays[5], arrays[11], arrays[13])
        body = functools.partial(by_kernel, n_wide // 4) if fits else by_collectives
        return jax.shard_map(body, mesh=mesh, in_specs=in_specs, out_specs=out_specs, check_vma=False)(*arrays)

    return run
```

```python
import functools
import math

import jax
import jax.numpy as jnp
from jax import lax
from jax.experimental import pallas as pl
from jax.experimental.pallas import tpu as pltpu
from jax.sharding import PartitionSpec as P

H = 12
MASKED_SCORE = -1000000000.0
MESH = pl.DeviceIdType.MESH
F32 = jnp.float32
BF16 = jnp.bfloat16
ALL = slice(None)
CHUNK = 64


def layer_norm(inputs, ln_gain, ln_bias):
    row_mean = jnp.mean(inputs, axis=-1, keepdims=True)
    centred = inputs - row_mean
    spread = jnp.mean(centred * centred, axis=-1, keepdims=True)
    return centred * lax.rsqrt(spread + 1e-06) * ln_gain + ln_bias


def gelu_exact(inputs):
    return 0.5 * inputs * (1.0 + lax.erf(inputs * 0.7071067811865476))


def clip_index(lengths, row_count):
    clip_ends = jnp.cumsum(lengths)
    position = jnp.arange(row_count, dtype=jnp.int32)
    return jnp.sum((position[:, None] >= clip_ends[None, :]).astype(jnp.int32), axis=1)


def split_heads(matrix, head_count):
    row_count = matrix.shape[0]
    return matrix.reshape(row_count, head_count, -1).transpose(1, 0, 2)


def join_heads(stacked):
    head_count, row_count, head_size = stacked.shape
    return stacked.transpose(1, 0, 2).reshape(row_count, head_count * head_size)


def attend_forward(queries, key_rows, value_rows, segment, block_rows, score_scale):
    scores = (
        lax.dot_general(
            queries, key_rows, (((1,), (1,)), ((), ())), preferred_element_type=jnp.float32
        )
        * score_scale
    )
    allowed = segment[0:block_rows, None] == segment[None, :]
    scores = jnp.where(allowed, scores, MASKED_SCORE)
    highest = jnp.max(scores, axis=1, keepdims=True)
    raised = jnp.exp(scores - highest)
    denominator = jnp.sum(raised, axis=1, keepdims=True)
    softmax = (raised / denominator).astype(jnp.bfloat16)
    outputs = [jnp.dot(softmax, value_rows, preferred_element_type=jnp.float32)]
    totals = [highest + jnp.log(denominator)]
    return (jnp.concatenate(outputs, 0), jnp.concatenate(totals, 0))


def attend_backward(
    queries, key_rows, value_rows, segment, grad_out, lse_rows, block_rows, score_scale
):
    grad_keys = jnp.zeros(key_rows.shape, jnp.float32)
    grad_values = jnp.zeros(value_rows.shape, jnp.float32)
    g_rows = grad_out[0:block_rows]
    scores = (
        lax.dot_general(
            queries, key_rows, (((1,), (1,)), ((), ())), preferred_element_type=jnp.float32
        )
        * score_scale
    )
    allowed = segment[0:block_rows, None] == segment[None, :]
    softmax = jnp.where(allowed, jnp.exp(scores - lse_rows[0:block_rows]), 0.0)
    grad_values = grad_values + lax.dot_general(
        softmax.astype(jnp.bfloat16),
        g_rows,
        (((0,), (0,)), ((), ())),
        preferred_element_type=jnp.float32,
    )
    grad_probs = lax.dot_general(
        g_rows, value_rows, (((1,), (1,)), ((), ())), preferred_element_type=jnp.float32
    )
    grad_scores = (
        softmax * (grad_probs - jnp.sum(softmax * grad_probs, axis=1, keepdims=True))
    ).astype(jnp.bfloat16)
    grad_queries = [
        jnp.dot(grad_scores, key_rows, preferred_element_type=jnp.float32) * score_scale
    ]
    grad_keys = (
        grad_keys
        + lax.dot_general(
            grad_scores, queries, (((0,), (0,)), ((), ())), preferred_element_type=jnp.float32
        )
        * score_scale
    )
    return (jnp.concatenate(grad_queries, 0), grad_keys, grad_values)


def by_collectives(
    tokens,
    cotangent,
    clip_lengths,
    ln1_gain,
    ln1_bias,
    qkv_weight,
    qv_bias,
    out_weight,
    out_bias,
    ln2_gain,
    ln2_bias,
    up_weight,
    up_bias,
    down_weight,
    down_bias,
):
    gathered = (
        lax.all_gather(ln1_gain, ("wide", "narrow"), axis=0, tiled=True),
        lax.all_gather(ln1_bias, ("wide", "narrow"), axis=0, tiled=True),
        lax.all_gather(qkv_weight, ("wide", "narrow"), axis=0, tiled=True),
        lax.all_gather(qv_bias, ("wide", "narrow"), axis=0, tiled=True),
        lax.all_gather(out_weight, ("wide", "narrow"), axis=0, tiled=True),
        lax.all_gather(out_bias, ("wide", "narrow"), axis=0, tiled=True),
        lax.all_gather(ln2_gain, ("wide", "narrow"), axis=0, tiled=True),
        lax.all_gather(ln2_bias, ("wide", "narrow"), axis=0, tiled=True),
        lax.all_gather(up_weight, ("wide", "narrow"), axis=0, tiled=True),
        lax.all_gather(up_bias, ("wide", "narrow"), axis=0, tiled=True),
        lax.all_gather(down_weight, ("wide", "narrow"), axis=0, tiled=True),
        lax.all_gather(down_bias, ("wide", "narrow"), axis=0, tiled=True),
    )
    (
        gain_one,
        bias_one,
        merged_weight,
        merged_bias,
        proj_weight,
        proj_bias,
        gain_two,
        bias_two,
        w_up,
        b_up,
        w_down,
        b_down,
    ) = gathered
    inputs = tokens.astype(jnp.float32)
    row_count, model_width = inputs.shape
    head_size = model_width // H
    score_scale = 1.0 / math.sqrt(head_size)
    block_rows = min(512, row_count)
    clip_count = clip_lengths.shape[1]
    segment = clip_index(clip_lengths[0], row_count)
    live_rows = (segment < clip_count).astype(jnp.float32)[:, None]
    normed_one = layer_norm(
        inputs, gain_one.astype(jnp.float32), bias_one.astype(jnp.float32)
    ).astype(jnp.bfloat16)
    bias_float = merged_bias.astype(jnp.float32)
    full_bias = jnp.concatenate(
        [bias_float[:model_width], jnp.zeros((model_width,), jnp.float32), bias_float[model_width:]]
    )
    merged_rows = (
        jnp.dot(normed_one, merged_weight, preferred_element_type=jnp.float32) + full_bias
    ).astype(jnp.bfloat16)
    q_heads = split_heads(merged_rows[:, :model_width], H)
    k_heads = split_heads(merged_rows[:, model_width : 2 * model_width], H)
    v_heads = split_heads(merged_rows[:, 2 * model_width :], H)

    def head_forward(triple):
        return attend_forward(triple[0], triple[1], triple[2], segment, block_rows, score_scale)

    att_heads, lse_heads = lax.map(head_forward, (q_heads, k_heads, v_heads))
    attended = join_heads(att_heads).astype(jnp.bfloat16)
    branch_one = jnp.dot(
        attended, proj_weight, preferred_element_type=jnp.float32
    ) + proj_bias.astype(jnp.float32)
    middle = inputs + live_rows * branch_one
    normed_two = layer_norm(
        middle, gain_two.astype(jnp.float32), bias_two.astype(jnp.float32)
    ).astype(jnp.bfloat16)
    hidden_pre = jnp.dot(normed_two, w_up, preferred_element_type=jnp.float32) + b_up.astype(
        jnp.float32
    )
    activated, gelu_pull = jax.vjp(gelu_exact, hidden_pre)
    activated = activated.astype(jnp.bfloat16)
    branch_two = jnp.dot(activated, w_down, preferred_element_type=jnp.float32) + b_down.astype(
        jnp.float32
    )
    block_out = (middle + live_rows * branch_two).astype(jnp.bfloat16)
    back_gain_one, back_merged, back_proj, back_gain_two, back_up, back_down = (
        lax.all_gather(ln1_gain, ("wide", "narrow"), axis=0, tiled=True),
        lax.all_gather(qkv_weight, ("wide", "narrow"), axis=0, tiled=True),
        lax.all_gather(out_weight, ("wide", "narrow"), axis=0, tiled=True),
        lax.all_gather(ln2_gain, ("wide", "narrow"), axis=0, tiled=True),
        lax.all_gather(up_weight, ("wide", "narrow"), axis=0, tiled=True),
        lax.all_gather(down_weight, ("wide", "narrow"), axis=0, tiled=True),
    )
    upstream = cotangent.astype(jnp.float32)
    grad_two = (live_rows * upstream).astype(jnp.bfloat16)
    grad_b_down = jnp.sum(grad_two.astype(jnp.float32), axis=0)
    grad_w_down = jnp.einsum("tf,td->fd", activated, grad_two, preferred_element_type=jnp.float32)
    grad_act = jnp.einsum("td,fd->tf", grad_two, back_down, preferred_element_type=jnp.float32)
    grad_hidden = gelu_pull(grad_act)[0].astype(jnp.bfloat16)
    grad_b_up = jnp.sum(grad_hidden.astype(jnp.float32), axis=0)
    grad_w_up = jnp.einsum("td,tf->df", normed_two, grad_hidden, preferred_element_type=jnp.float32)
    grad_normed_two = jnp.einsum(
        "tf,df->td", grad_hidden, back_up, preferred_element_type=jnp.float32
    )
    _, norm_pull_two = jax.vjp(
        layer_norm, middle, back_gain_two.astype(jnp.float32), bias_two.astype(jnp.float32)
    )
    grad_middle_norm, grad_gain_two, grad_bias_two = norm_pull_two(grad_normed_two)
    grad_middle = upstream + grad_middle_norm
    grad_one = (live_rows * grad_middle).astype(jnp.bfloat16)
    grad_b_proj = jnp.sum(grad_one.astype(jnp.float32), axis=0)
    grad_w_proj = jnp.einsum("te,td->ed", attended, grad_one, preferred_element_type=jnp.float32)
    grad_att = jnp.einsum(
        "td,ed->te", grad_one, back_proj, preferred_element_type=jnp.float32
    ).astype(jnp.bfloat16)
    grad_att_heads = split_heads(grad_att, H)

    def head_backward(members):
        return attend_backward(
            members[0],
            members[1],
            members[2],
            segment,
            members[3],
            members[4],
            block_rows,
            score_scale,
        )

    grad_q, grad_k, grad_v = lax.map(
        head_backward, (q_heads, k_heads, v_heads, grad_att_heads, lse_heads)
    )
    grad_merged = jnp.concatenate(
        [join_heads(grad_q), join_heads(grad_k), join_heads(grad_v)], 1
    ).astype(jnp.bfloat16)
    column_sums = jnp.sum(grad_merged.astype(jnp.float32), axis=0)
    grad_merged_bias = jnp.concatenate([column_sums[:model_width], column_sums[2 * model_width :]])
    grad_w_merged = jnp.einsum(
        "te,tf->ef", normed_one, grad_merged, preferred_element_type=jnp.float32
    )
    grad_normed_one = jnp.einsum(
        "tf,ef->te", grad_merged, back_merged, preferred_element_type=jnp.float32
    )
    _, norm_pull_one = jax.vjp(
        layer_norm, inputs, back_gain_one.astype(jnp.float32), bias_one.astype(jnp.float32)
    )
    grad_input_norm, grad_gain_one, grad_bias_one = norm_pull_one(grad_normed_one)
    tokens_grad = grad_middle + grad_input_norm
    shares = (
        lax.psum_scatter(grad_gain_one, ("wide", "narrow"), scatter_dimension=0, tiled=True),
        lax.psum_scatter(grad_bias_one, ("wide", "narrow"), scatter_dimension=0, tiled=True),
        lax.psum_scatter(grad_w_merged, ("wide", "narrow"), scatter_dimension=0, tiled=True),
        lax.psum_scatter(grad_merged_bias, ("wide", "narrow"), scatter_dimension=0, tiled=True),
        lax.psum_scatter(grad_w_proj, ("wide", "narrow"), scatter_dimension=0, tiled=True),
        lax.psum_scatter(grad_b_proj, ("wide", "narrow"), scatter_dimension=0, tiled=True),
        lax.psum_scatter(grad_gain_two, ("wide", "narrow"), scatter_dimension=0, tiled=True),
        lax.psum_scatter(grad_bias_two, ("wide", "narrow"), scatter_dimension=0, tiled=True),
        lax.psum_scatter(grad_w_up, ("wide", "narrow"), scatter_dimension=0, tiled=True),
        lax.psum_scatter(grad_b_up, ("wide", "narrow"), scatter_dimension=0, tiled=True),
        lax.psum_scatter(grad_w_down, ("wide", "narrow"), scatter_dimension=0, tiled=True),
        lax.psum_scatter(grad_b_down, ("wide", "narrow"), scatter_dimension=0, tiled=True),
    )
    return (
        block_out,
        tokens_grad,
        shares[0],
        shares[1],
        shares[2],
        shares[3],
        shares[4],
        shares[5],
        shares[6],
        shares[7],
        shares[8],
        shares[9],
        shares[10],
        shares[11],
    )


def nt_dot(left, right):
    return lax.dot_general(left, right, (((1,), (1,)), ((), ())), preferred_element_type=F32)


def nn_dot(left, right):
    return jnp.dot(left, right, preferred_element_type=F32)


def rows_of(step, size=CHUNK):
    return pl.ds(pl.multiple_of(step * size, size), size)


def norm_parts(values):
    centred = values - jnp.mean(values, axis=-1, keepdims=True)
    scale = lax.rsqrt(jnp.mean(centred * centred, axis=-1, keepdims=True) + 1e-06)
    return centred * scale, scale


def fold_rows(values):
    return jnp.sum(values.reshape(-1, 8, values.shape[-1]), axis=0)


def gelu_both(u):
    tail = 0.5 * (1.0 + lax.erf(u * 0.7071067811865476))
    return u * tail, tail + u * jnp.exp(-0.5 * u * u) * 0.3989422804014327


def spread_maps(width, columns):
    column = lax.broadcasted_iota(jnp.int32, (1, columns), 1).astype(F32)
    group = jnp.floor((column + 0.5) * (1.0 / width))
    place = column - group * width
    lane = lax.broadcasted_iota(jnp.int32, (128, columns), 0).astype(F32)
    picks = jnp.where(lane == place, 1.0, 0.0).astype(BF16)
    owners = columns // width
    owner = lax.broadcasted_iota(jnp.int32, (owners, 8, columns), 0).astype(F32)
    mine = owner == group.reshape(1, 1, columns)
    return picks, mine


def spread(pieces, width, columns):
    picks, mine = spread_maps(width, columns)
    wide_rows = nn_dot(pieces.reshape(-1, 128).astype(BF16), picks)
    return jnp.sum(jnp.where(mine, wide_rows.reshape(-1, 8, columns), 0.0), axis=0)


def gather_back(vectors, width):
    columns = vectors.shape[-1]
    picks, mine = spread_maps(width, columns)
    rest = jnp.where(mine, vectors[None], 0.0).reshape(-1, columns)
    total = None
    for _ in range(3):
        part = rest.astype(BF16)
        rest = rest - part.astype(F32)
        term = nt_dot(part, picks)
        total = term if total is None else total + term
    return total.reshape(-1, 8, 128)


def layer_kernel(
    clip_ref, tok_ref, cot_ref, v0, v1, v2, v3, v4, v5, v6, v7, wqkv_ref, wout_ref, wup_ref, wdown_ref,
    out_ref, tgrad_ref, gqkv_ref, gout_ref, gup_ref, gdown_ref, gsmall_ref,
    slabs, downs, smalls, gsmalls, weights, w_up,
    row_c, row_d, row_n, row_z, late_d, late_n, late_z, down_c, down_d, down_n, down_z, sm_c, sm_d, sm_n, sm_z,
    qkv, n1t, n1, att_t, middle, n2, n2t, g2, acc_out, acc_grad, act, grad_h, pre, grad_act,
    tok, cot, bias, lse, dq_t, vec24, vec48, vec96, sums, up_sums, block_out,
    ag_send, ag_recv, rs_send, rs_recv, local,
):
    n_z, width = slabs.shape[1], slabs.shape[-1]
    count = tok.shape[0]
    pairs = width // 128
    chunks = count // CHUNK
    wide_at, y = lax.axis_index("wide"), lax.axis_index("narrow")
    core = lax.rem(wide_at, 2)
    x = lax.rem(lax.div(wide_at, 2), 2)
    z = lax.div(wide_at, 4)

    def device(z_at, x_at, c_at, y_at):
        return ((z_at * 2 + x_at) * 2 + c_at, y_at)

    def row_view(block):
        def view(at):
            return slabs.at[(block, *at)]
        return view

    def down_view(tile):
        def view(at):
            return downs.at[(tile, *at[1:])]
        return view

    def small_view(ref):
        def view(at):
            return ref.at[at]
        return view

    def half_of(ref, side):
        if ref.shape[-1] < 2 * 128:
            return ref
        cut = ref.shape[-1] // 2
        return ref.at[(*([ALL] * (len(ref.shape) - 1)), pl.ds(side * cut, cut))]

    to_x, to_y, to_c = device(z, 1 - x, core, y), device(z, x, core, 1 - y), device(z, x, 1 - core, y)
    near_z, far_z, last_z = z + 1 - 2 * lax.rem(z, 2), lax.rem(z + 2, n_z), n_z - 1 - z
    inner = lax.rem(z + 1, n_z) >= 2
    to_near, to_far, to_last = device(near_z, x, core, y), device(far_z, x, core, y), device(last_z, x, core, y)
    Z1, Z2, Z3, ZR, X0, Y0, DX, DY, C0 = range(9)

    def remote(src, dst, sems, row, sem, to, recv_sem=None):
        send, recv = sems
        return pltpu.make_async_remote_copy(
            src_ref=src, dst_ref=dst, send_sem=send.at[row, sem], recv_sem=recv.at[row, sem if recv_sem is None else recv_sem],
            device_id=to, device_id_type=MESH,
        )

    def do_all(copies, what):
        for copy in copies:
            getattr(copy, what)()

    def ag_copies(unit, phase):
        view, row, phases, along = unit
        sems = (ag_send, ag_recv)
        late = phases.index("z") > phases.index("near") if "z" in phases and "near" in phases else False
        held = z if late else ALL
        own = view((z, *along))
        if phase == "z":
            return [remote(own, own, sems, row, Z1, to_near), remote(own, own, sems, row, Z2, to_far)]
        if phase == "z near":
            return [remote(own, own, sems, row, Z1, to_near)]
        if phase == "z far":
            return [remote(own, own, sems, row, Z2, to_far)]
        if phase == "z inner":
            return [remote(own, own, sems, row, Z3, to_last)]
        if phase == "relay":
            passed = view((far_z, *along))
            return [remote(passed, passed, sems, row, ZR, to_near, Z3)]
        if phase == "near":
            mine = view((held, x, core, y))
            return [remote(mine, mine, sems, row, X0, to_x), remote(mine, mine, sems, row, Y0, to_y)]
        if phase == "across":
            from_x, from_y = view((held, 1 - x, core, y)), view((held, x, core, 1 - y))
            first = half_of(from_x, 0)
            copies = [remote(first, first, sems, row, DY, to_y)]
            if from_x.shape[-1] >= 2 * 128:
                second = half_of(from_y, 1)
                copies.append(remote(second, second, sems, row, DX, to_x))
            return copies
        plane = view((ALL, ALL, core, ALL))
        return [remote(plane, plane, sems, row, C0, to_c)]

    def ag_arrived(unit, phase):
        if phase == "z":
            @pl.when(jnp.logical_not(inner))
            def _():
                do_all(ag_copies(unit, "z far"), "wait_recv")
            do_all(ag_copies(unit, "z near") + ag_copies(unit, "z inner"), "wait_recv")
        else:
            do_all(ag_copies(unit, phase), "wait_recv")

    def ag_stage(unit, stage):
        phases = unit[2]
        waits = [p for p in phases[:stage] if p != "relay"][-1:]
        phase = phases[stage] if stage < len(phases) else None
        if phase == "relay":
            @pl.when(inner)
            def _():
                do_all(ag_copies(unit, "z far"), "wait_recv")
                do_all(ag_copies(unit, "relay"), "start")
            return
        if waits:
            ag_arrived(unit, waits[0])
        if phase:
            do_all(ag_copies(unit, phase), "start")
            if phase == "z":
                @pl.when(inner)
                def _():
                    do_all(ag_copies(unit, "z inner"), "start")
        else:
            for sent in phases:
                if sent != "relay":
                    do_all(ag_copies(unit, sent), "wait_send")
            if "z" in phases:
                @pl.when(inner)
                def _():
                    do_all(ag_copies(unit, "z inner") + ag_copies(unit, "relay"), "wait_send")

    first_z = ("z", "relay", "near", "across", "core")
    last_z_order = ("near", "across", "z", "relay", "core")
    one, plane_of = (x, core, y), (ALL, core, ALL)
    small_unit = (small_view(smalls), 0, first_z, one)

    def gather_unit(block, late=False):
        return (row_view(block), 1 + block, last_z_order if late else first_z, plane_of if late else one)

    down_first = (lambda at: downs.at[at], 5 + 2 * n_z, ("z", "relay"), one)

    def gather_down(tile):
        return (down_view(tile), 5 + n_z + tile, ("near", "across", "core"), one)

    A_TICKS, F_TICKS, D_TICKS = (-4, -2, -1, 0, 1, 2), (-7, -6, -5, -3, 0, 1), (-1, 0, 1, 2)
    gathers = [(0, small_unit, A_TICKS)] + [(b, gather_unit(b), A_TICKS) for b in range(4)]
    for tile in range(n_z):
        late = tile in LATE_GATHERS
        gathers.append((4 + 2 * tile, gather_unit(4 + tile, late), F_TICKS if late else A_TICKS))
        gathers.append((5 + 2 * tile, gather_down(tile), D_TICKS))
    gathers.append((5, down_first, (-4, -2, -1)))
    FIRST_TICK = min(place + ticks[0] for place, _, ticks in gathers)
    rank = {"z": 0, "relay": 1, "near": 2, "core": 3, None: 4, "across": 5}

    def ag_tick(tick):
        todo = []
        for place, unit, ticks in gathers:
            for stage, at in enumerate(ticks):
                if place + at == tick:
                    phase = unit[2][stage] if stage < len(unit[2]) else None
                    todo.append((rank[phase] - (10 if unit is down_first else 0), place, stage, unit))
        for _, _, stage, unit in sorted(todo, key=lambda entry: entry[:3]):
            ag_stage(unit, stage)

    def rs_copies(unit, phase):
        view, row, phases, landing, along = unit
        sems = (rs_send, rs_recv)
        late = "near" in phases and "z" in phases and phases.index("z") < phases.index("near")
        held = z if late else ALL
        if phase == "core":
            return [remote(view((ALL, ALL, 1 - core, ALL)), landing["core"], sems, row, C0, to_c)]
        if phase == "across":
            away = view((held, 1 - x, core, 1 - y))
            copies = [remote(half_of(away, 0), landing["dx"], sems, row, DX, to_x)]
            if away.shape[-1] >= 2 * 128:
                copies.append(remote(half_of(away, 1), landing["dy"], sems, row, DY, to_y))
            return copies
        if phase == "near":
            return [
                remote(view((held, 1 - x, core, y)), landing["x"], sems, row, X0, to_x),
                remote(view((held, x, core, 1 - y)), landing["y"], sems, row, Y0, to_y),
            ]
        if phase == "z":
            return [remote(view((near_z, *along)), landing["z1"], sems, row, Z1, to_near)]
        if phase == "z inner":
            return [remote(view((last_z, *along)), landing["z3"], sems, row, Z3, to_last)]
        if phase == "z outer":
            return [remote(view((last_z, *along)), landing["zr"], sems, row, ZR, to_near)]
        return [remote(view((far_z, *along)), landing["z2"], sems, row, Z2, to_far)]

    def add_into(target, *sources):
        total = target[...].astype(F32)
        for source in sources:
            total = total + source[...].astype(F32)
        target[...] = total.astype(target.dtype)

    def add_all(target, *sources):
        free = len(target.shape) - 2
        if free == 0:
            add_into(target, *sources)
            return
        places = [()]
        for extent in target.shape[1:free]:
            places = [place + (k,) for place in places for k in range(extent)]

        def step(i, carry):
            for place in places:
                add_into(target.at[(i, *place)], *[source.at[(i, *place)] for source in sources])
            return carry

        lax.fori_loop(0, target.shape[0], step, 0)

    def rs_take(unit, phase):
        view, _, phases, landing, along = unit
        late = "near" in phases and "z" in phases and phases.index("z") < phases.index("near")
        held = z if late else ALL
        if phase == "z":
            do_all(rs_copies(unit, "z") + rs_copies(unit, "z far"), "wait_recv")
            add_all(view((z, *along)), landing["z1"], landing["z2"])

            @pl.when(inner)
            def _():
                do_all(rs_copies(unit, "z inner"), "wait_recv")
                add_all(view((z, *along)), landing["z3"])
            return
        do_all(rs_copies(unit, phase), "wait_recv")
        if phase == "core":
            add_all(view((ALL, ALL, core, ALL)), landing["core"])
        elif phase == "across":
            on_y = view((held, x, core, 1 - y))
            add_all(half_of(on_y, 0), landing["dx"])
            if on_y.shape[-1] >= 2 * 128:
                add_all(half_of(view((held, 1 - x, core, y)), 1), landing["dy"])
        else:
            add_all(view((held, x, core, y)), landing["x"], landing["y"])

    def rs_stage(unit, stage):
        view, _, phases, landing, along = unit
        if stage == len(phases):
            rs_take(unit, phases[-1])
            return
        phase = phases[stage]
        if phase == "z far":
            @pl.when(inner)
            def _():
                do_all(rs_copies(unit, "z outer"), "wait_recv")
                add_all(view((far_z, *along)), landing["zr"])
            do_all(rs_copies(unit, phase), "start")
            return
        if stage > 0:
            rs_take(unit, "z" if phases[stage - 1] == "z far" else phases[stage - 1])
        do_all(rs_copies(unit, phase), "start")
        if phase == "z":
            @pl.when(inner)
            def _():
                do_all(rs_copies(unit, "z inner"), "start")

            @pl.when(jnp.logical_not(inner))
            def _():
                do_all(rs_copies(unit, "z outer"), "start")

    def rs_end(unit, *results):
        view, _, phases, landing, along = unit
        own = view((z, x, core, y))
        if phases[-1] == "near":
            do_all(rs_copies(unit, "near"), "wait_recv")
            total = own[...].astype(F32) + landing["x"][...].astype(F32) + landing["y"][...].astype(F32)
        else:
            do_all(rs_copies(unit, "z") + rs_copies(unit, "z far"), "wait_recv")
            total = own[...].astype(F32) + landing["z1"][...].astype(F32) + landing["z2"][...].astype(F32)
        size = total.shape[-1] // len(results)
        for k, result in enumerate(results):
            result[...] = total[:, k * size : (k + 1) * size]
        if phases[-1] != "near":
            @pl.when(inner)
            def _():
                do_all(rs_copies(unit, "z inner"), "wait_recv")
                for k, result in enumerate(results):
                    result[...] += landing["z3"][:, k * size : (k + 1) * size].astype(F32)

    def rs_sent(unit):
        for phase in unit[2]:
            do_all(rs_copies(unit, phase), "wait_send")
        if "z" in unit[2]:
            @pl.when(inner)
            def _():
                do_all(rs_copies(unit, "z inner"), "wait_send")

            @pl.when(jnp.logical_not(inner))
            def _():
                do_all(rs_copies(unit, "z outer"), "wait_send")

    back_last, back_first = ("core", "across", "near", "z", "z far"), ("core", "z", "z far", "across", "near")

    def z_landing(ref):
        return {"z1": ref.at[0], "z2": ref.at[1], "z3": ref.at[2], "zr": ref.at[3]}

    def row_unit(block, row, late=None):
        if late is not None:
            landing = {"core": row_c.at[block], "dx": late_d.at[late, 0], "dy": late_d.at[late, 1], "x": late_n.at[late, 0], "y": late_n.at[late, 1], **z_landing(late_z.at[late])}
            return (row_view(block), row, back_first, landing, plane_of)
        landing = {"core": row_c.at[block], "dx": row_d.at[block, 0], "dy": row_d.at[block, 1], "x": row_n.at[block, 0], "y": row_n.at[block, 1], **z_landing(row_z.at[block])}
        return (row_view(block), row, back_last, landing, one)

    def down_unit(tile, row):
        landing = {"core": down_c.at[tile], "dx": down_d.at[tile, 0], "dy": down_d.at[tile, 1], "x": down_n.at[tile, 0], "y": down_n.at[tile, 1]}
        return (down_view(tile), row, back_last[:3], landing, one)

    def block_columns(block):
        return pl.ds(block * width, width)

    up_units = [row_unit(4 + t, t, LATE_SUMS.index(t) if t in LATE_SUMS else None) for t in range(n_z)]
    down_units = [down_unit(t, n_z + t) for t in range(n_z)]
    head_units = [row_unit(g, 2 * n_z + g) for g in range(3)]
    out_unit = row_unit(3, 2 * n_z + 3)
    small_landing = {"core": sm_c, "dx": sm_d, "x": sm_n.at[0], "y": sm_n.at[1], **z_landing(sm_z)}
    small_grad_unit = (small_view(gsmalls), 2 * n_z + 4, back_last, small_landing, one)
    down_last = (lambda at: downs.at[at], 2 * n_z + 5, ("z", "z far"), z_landing(down_z), one)

    POINTS = ["f0m", "f0e", "f1m", "f1e", "f2m", "f2e", "f3m", "f3e", "n2", "og", "a0", "a1", "h0", "a2", "a3", "h1", "a4", "a5", "h2", "g2", "g1", "g0", "nb", "gb", "e0", "e1", "e2", "e3"]
    A_POINTS, F_POINTS = (0, 1, 2, 3, 4), (0, 1, 2, 5, 6)
    plan = {name: [] for name in POINTS}

    def plan_unit(unit, first, offsets):
        for stage in range(len(unit[2]) + (unit[2][-1] == "near" and "z" not in unit[2])):
            plan[POINTS[POINTS.index(first) + offsets[stage]]].append((unit, stage))

    for t in range(n_z):
        plan_unit(up_units[t], f"f{t}e", F_POINTS if t in LATE_SUMS else A_POINTS)
        plan_unit(down_units[t], f"f{t}e", A_POINTS)
    plan_unit(down_last, "a1", (0, 3))
    plan_unit(out_unit, "og", (0, 2, 4, 6, 8))
    plan_unit(head_units[0], "h0", (0, 2, 4, 5, 7))
    plan_unit(head_units[1], "h1", (0, 2, 4, 5, 6))
    plan_unit(head_units[2], "h2", (0, 1, 2, 3, 4))
    plan_unit(small_grad_unit, "gb", (0, 1, 2, 3, 4))

    def point(name):
        for unit, stage in plan[name]:
            rs_stage(unit, stage)

    def local_copies():
        pairs_of = [(tok_ref, tok), (cot_ref, cot)]
        for block in range(3):
            pairs_of.append((wqkv_ref.at[:, block_columns(block)], slabs.at[block, z, x, core, y]))
        pairs_of.append((wout_ref, slabs.at[3, z, x, core, y]))
        for tile in range(n_z):
            pairs_of.append((wup_ref.at[:, block_columns(tile)], slabs.at[4 + tile, z, x, core, y]))
        pairs_of.append((wdown_ref, downs.at[z, x, core, y]))
        return [pltpu.make_async_copy(src, dst, local.at[k]) for k, (src, dst) in enumerate(pairs_of)]

    starts = local_copies()
    for copy in starts:
        copy.start()
    smalls[z, x, core, y] = jnp.zeros((8, 128), F32)
    for k, vector in enumerate((v0, v1, v2, v3, v4, v5, v6, v7)):
        smalls[z, x, core, y, k, 0 : vector.shape[0]] = vector[...].astype(F32)
    barrier = pltpu.get_barrier_semaphore()
    partners = [to_near, to_far, to_last, to_x, to_y, to_c]
    for to in partners:
        pl.semaphore_signal(barrier, inc=1, device_id=to, device_id_type=MESH)
    for copy in starts:
        copy.wait()
    pl.semaphore_wait(barrier, len(partners))
    for tick in range(FIRST_TICK, 0):
        ag_tick(tick)

    ends = []
    for k in range(clip_ref.shape[1]):
        ends.append(clip_ref[0, k] + (ends[-1] if ends else 0))

    def segment_of(position):
        total = jnp.zeros(position.shape, jnp.int32)
        for end in ends:
            total = total + jnp.where(position >= end, 1, 0)
        return total

    across = segment_of(lax.broadcasted_iota(jnp.int32, (CHUNK, count), 1))

    def live_of(step):
        position = lax.broadcasted_iota(jnp.int32, (CHUNK, 1), 0) + step * CHUNK
        return jnp.where(position < ends[-1], 1.0, 0.0)

    def mask_step(i, total):
        down = segment_of(lax.broadcasted_iota(jnp.int32, (CHUNK, count), 0) + i * CHUNK)
        bias[rows_of(i), :] = jnp.where(down == across, 0.0, -1e30)
        grad = (live_of(i) * cot[rows_of(i), :].astype(F32)).astype(BF16)
        g2[rows_of(i), :] = grad
        return total + fold_rows(grad.astype(F32))

    down_bias_sum = lax.fori_loop(0, chunks, mask_step, jnp.zeros((8, width), F32))
    sums[...] = jnp.zeros_like(sums)
    sums[0, 7:8, :] = jnp.sum(down_bias_sum, axis=0, keepdims=True)

    for tick in range(3):
        ag_tick(tick)

    vec24[...] = spread(smalls[...], 24, width)
    for k in range(2):
        vec48[k] = spread(smalls[k * n_z // 2 : (k + 1) * n_z // 2], 48, width)
    for k in range(n_z):
        vec96[k] = spread(smalls[k], 96, width)

    def norm_one(i, carry):
        normed, _ = norm_parts(tok[rows_of(i), :].astype(F32))
        n1[rows_of(i), :] = (normed * vec24[0:1, :] + vec24[1:2, :]).astype(BF16)
        return carry

    lax.fori_loop(0, chunks, norm_one, 0)

    def turn(source, target):
        def step(i, carry):
            at = rows_of(i, 128)
            target[at, :] = source[:, at].T
            return carry

        lax.fori_loop(0, pairs, step, 0)

    turn(n1, n1t)

    def assemble(block, target):
        def step(z_at, carry):
            for x_at in range(2):
                for c_at in range(2):
                    two = slabs[block, z_at, x_at, c_at].astype(F32)
                    size = 2 * two.shape[1]
                    first = pl.multiple_of(((z_at * 2 + x_at) * 2 + c_at) * size, 16)
                    target[pl.ds(first, size), :] = two.reshape(size, width).astype(BF16)
            return carry

        lax.fori_loop(0, n_z, step, 0)

    def project(block, add):
        assemble(block, weights.at[block])
        total = nn_dot(n1[...], weights[block])
        qkv[block] = (total if add is None else total + add).astype(BF16)

    project(0, vec48[0, 2:3, :])
    ag_tick(3)
    project(1, None)
    ag_tick(4)
    project(2, vec48[1, 2:3, :])

    lane = lax.broadcasted_iota(jnp.int32, (count, 128), 1)

    def one_head(values, head):
        keep = lane < 64 if head == 0 else lane >= 64
        return jnp.where(keep, values, jnp.zeros_like(values))

    q_block = 256
    parts = count // q_block

    def attend(p, carry):
        for when, tick in ((1, 5), (3, 6), (5, 7)):
            @pl.when(p == when)
            def _():
                ag_tick(tick)
        at = rows_of(p, 128)
        keys = qkv[1, :, at]
        queries = qkv[0, :, at] * 0.125
        values_t = qkv[2, :, at].T
        for head in range(2):
            mine = one_head(queries, head)
            for part in range(parts):
                span = slice(part * q_block, (part + 1) * q_block)
                scores = nt_dot(keys, mine[span]) + bias[:, span]
                highest = jnp.max(scores, axis=0, keepdims=True)
                raised = jnp.exp(scores - highest)
                total = jnp.sum(raised, axis=0, keepdims=True)
                chances = (raised * (1.0 / total)).astype(BF16)
                lse[p, head : head + 1, span] = highest + jnp.log(total)
                result = nn_dot(values_t[64 * head : 64 * head + 64], chances)
                att_t[pl.ds(pl.multiple_of(p * 128 + 64 * head, 64), 64), span] = result.astype(BF16)
        return carry

    lax.fori_loop(0, pairs, attend, 0)
    att = n1
    def turn_back(p, carry):
        at = rows_of(p, 128)
        att[:, at] = att_t[at, :].T
        return carry
    lax.fori_loop(0, pairs, turn_back, 0)

    assemble(3, weights.at[3])
    pre[...] = nn_dot(att[...], weights[3])

    def norm_two(i, carry):
        at = rows_of(i)
        branch = pre[at, :] + vec24[3:4, :]
        mid = tok[at, :].astype(F32) + live_of(i) * branch
        middle[at, :] = mid
        normed, _ = norm_parts(mid)
        n2[at, :] = (normed * vec24[4:5, :] + vec24[5:6, :]).astype(BF16)
        return carry

    lax.fori_loop(0, chunks, norm_two, 0)
    turn(n2, n2t)
    ag_tick(8)
    acc_out[...] = jnp.zeros_like(acc_out)
    acc_grad[...] = jnp.zeros_like(acc_grad)

    def store_rows(block, lhs_t, rhs):
        deep = width // n_z
        size = slabs.shape[-2]

        def step(z_at, carry):
            total = nn_dot(lhs_t[rows_of(z_at, deep), :], rhs)
            for x_at in range(2):
                for c_at in range(2):
                    for y_at in range(2):
                        first = ((x_at * 2 + c_at) * 2 + y_at) * size
                        slabs[block, z_at, x_at, c_at, y_at] = total[first : first + size].astype(BF16)
            return carry

        lax.fori_loop(0, n_z, step, 0)

    def feed(t, carry):
        assemble(4 + t, w_up)
        pre[...] = nn_dot(n2[...], w_up[...])
        w_down = downs[t].reshape(width, width)
        grad_act[...] = nt_dot(g2[...], w_down)
        up_bias = vec96[t, 6:7, :]

        def gelu_step(i, total):
            at = rows_of(i, 32)
            active, slope = gelu_both(pre[at, :] + up_bias)
            act[at, :] = active.astype(BF16)
            grad = (grad_act[at, :] * slope).astype(BF16)
            grad_h[at, :] = grad
            return total + fold_rows(grad.astype(F32))

        total = lax.fori_loop(0, count // 32, gelu_step, jnp.zeros((8, width), F32))
        up_sums[t, 6:7, :] = jnp.sum(total, axis=0, keepdims=True)
        for when in range(n_z):
            @pl.when(t == when)
            def _():
                if when < 3:
                    ag_tick(9 + 2 * when)
                point(f"f{when}m")
        acc_out[...] += nn_dot(act[...], w_down)
        acc_grad[...] += nt_dot(grad_h[...], w_up[...])
        store_rows(4 + t, n2t, grad_h[...])
        for j in range(pairs):
            span = slice(j * 128, (j + 1) * 128)
            piece = nn_dot(act[:, span].T, g2[...]).astype(BF16)
            size = downs.shape[-2]
            at = j * 128
            while at < (j + 1) * 128:
                owner, inside = at // size, at % size
                length = min(size - inside, (j + 1) * 128 - at)
                downs[t, owner // 4, owner // 2 % 2, owner % 2, inside : inside + length, :] = piece[at - j * 128 : at - j * 128 + length]
                at += length
        for when in range(n_z):
            @pl.when(t == when)
            def _():
                if when < 2:
                    ag_tick(10 + 2 * when)
                point(f"f{when}e")
        return carry

    up_sums[...] = jnp.zeros_like(up_sums)
    lax.fori_loop(0, n_z, feed, 0)

    def norm_two_back(i, carry):
        gain_sum, bias_sum, one_sum = carry
        at = rows_of(i)
        alive = live_of(i)
        mid = middle[at, :]
        block_out[at, :] = (mid + alive * (acc_out[at, :] + vec24[7:8, :])).astype(BF16)
        normed, scale = norm_parts(mid)
        e = acc_grad[at, :]
        scaled = e * vec24[4:5, :]
        inner = scaled - jnp.mean(scaled, axis=-1, keepdims=True) - normed * jnp.mean(scaled * normed, axis=-1, keepdims=True)
        grad_mid = cot[at, :].astype(F32) + inner * scale
        acc_grad[at, :] = grad_mid
        one = (alive * grad_mid).astype(BF16)
        g2[at, :] = one
        return (gain_sum + fold_rows(e * normed), bias_sum + fold_rows(e), one_sum + fold_rows(one.astype(F32)))

    zero = jnp.zeros((8, width), F32)
    gain_sum, bias_sum, one_sum = lax.fori_loop(0, chunks, norm_two_back, (zero, zero, zero))
    sums[0, 4:5, :] = jnp.sum(gain_sum, axis=0, keepdims=True)
    sums[0, 5:6, :] = jnp.sum(bias_sum, axis=0, keepdims=True)
    sums[0, 3:4, :] = jnp.sum(one_sum, axis=0, keepdims=True)
    out_copy = pltpu.make_async_copy(block_out, out_ref, local.at[0])
    out_copy.start()

    point("n2")
    store_rows(3, att_t, g2[...])
    point("og")
    grad_att = n2
    grad_att[...] = nt_dot(g2[...], weights[3]).astype(BF16)

    def head_rows(group):
        deep = width // n_z
        size = slabs.shape[-2]
        third = width // 3
        columns = pl.ds(pl.multiple_of(group * third, third), third)

        def step(z_at, carry):
            for j in range(3):
                total = nn_dot(n1t[rows_of(z_at, deep), :], qkv[j, :, columns])
                for k in range(8):
                    slabs[group, z_at, k // 4, k // 2 % 2, k % 2, :, j * third : (j + 1) * third] = total[k * size : (k + 1) * size].astype(BF16)
            return carry

        lax.fori_loop(0, n_z, step, 0)

    per_group = pairs // 3

    def attend_back(p, carry):
        for when in range(pairs):
            @pl.when(p == when)
            def _():
                point(f"a{when}")
        at = rows_of(p, 128)
        keys = qkv[1, :, at]
        values = qkv[2, :, at]
        queries = qkv[0, :, at] * 0.125
        grads = grad_att[:, at]
        keys_t = keys.T
        grad_keys = jnp.zeros((count, 128), F32)
        grad_values = jnp.zeros((count, 128), F32)
        for head in range(2):
            my_queries, my_grads = one_head(queries, head), one_head(grads, head)
            for part in range(parts):
                span = slice(part * q_block, (part + 1) * q_block)
                scores = nt_dot(keys, my_queries[span]) + bias[:, span]
                chances = jnp.exp(scores - lse[p, head : head + 1, span])
                slopes = nt_dot(values, my_grads[span])
                level = jnp.sum(chances * slopes, axis=0, keepdims=True)
                grad_scores = (chances * (slopes - level)).astype(BF16)
                grad_values += nn_dot(chances.astype(BF16), my_grads[span])
                grad_keys += nn_dot(grad_scores, my_queries[span])
                dq_t[64 * head : 64 * head + 64, span] = nn_dot(keys_t[64 * head : 64 * head + 64], grad_scores) * 0.125
        qkv[0, :, at] = dq_t[...].T.astype(BF16)
        qkv[1, :, at] = grad_keys.astype(BF16)
        qkv[2, :, at] = grad_values.astype(BF16)

        @pl.when(lax.rem(p, per_group) == per_group - 1)
        def _():
            head_rows(lax.div(p, per_group))
        for group in range(3):
            @pl.when(p == group * per_group + per_group - 1)
            def _():
                point(f"h{group}")
        return carry

    lax.fori_loop(0, pairs, attend_back, 0)

    pre[...] = nt_dot(qkv[2], weights[2])
    point("g2")
    pre[...] += nt_dot(qkv[1], weights[1])
    point("g1")
    pre[...] += nt_dot(qkv[0], weights[0])
    point("g0")

    def norm_one_back(i, carry):
        gain_sum, bias_sum, q_sum, v_sum = carry
        at = rows_of(i)
        normed, scale = norm_parts(tok[at, :].astype(F32))
        e = pre[at, :]
        scaled = e * vec24[0:1, :]
        inner = scaled - jnp.mean(scaled, axis=-1, keepdims=True) - normed * jnp.mean(scaled * normed, axis=-1, keepdims=True)
        acc_grad[at, :] = acc_grad[at, :] + inner * scale
        return (
            gain_sum + fold_rows(e * normed), bias_sum + fold_rows(e),
            q_sum + fold_rows(qkv[0, at, :].astype(F32)), v_sum + fold_rows(qkv[2, at, :].astype(F32)),
        )

    gain_sum, bias_sum, q_sum, v_sum = lax.fori_loop(0, chunks, norm_one_back, (zero, zero, zero, zero))
    tgrad_copy = pltpu.make_async_copy(acc_grad, tgrad_ref, local.at[1])
    tgrad_copy.start()
    sums[0, 0:1, :] = jnp.sum(gain_sum, axis=0, keepdims=True)
    sums[0, 1:2, :] = jnp.sum(bias_sum, axis=0, keepdims=True)
    sums[1, 2:3, :] = jnp.sum(q_sum, axis=0, keepdims=True)
    sums[2, 2:3, :] = jnp.sum(v_sum, axis=0, keepdims=True)
    point("nb")
    gsmalls[...] = gather_back(sums[0], 24).reshape(gsmalls.shape)
    for k in range(2):
        part = gather_back(sums[1 + k], 48)
        span = slice(k * n_z // 2, (k + 1) * n_z // 2)
        gsmalls[span] = gsmalls[span] + part.reshape(n_z // 2, 2, 2, 2, 8, 128)
    for k in range(n_z):
        gsmalls[k] = gsmalls[k] + gather_back(up_sums[k], 96).reshape(2, 2, 2, 8, 128)
    point("gb")

    rs_end(up_units[0], gup_ref.at[:, block_columns(0)])
    rs_end(up_units[1], gup_ref.at[:, block_columns(1)])
    point("e0")
    rs_end(up_units[2], gup_ref.at[:, block_columns(2)])
    rs_end(up_units[3], gup_ref.at[:, block_columns(3)])
    point("e1")
    rs_end(down_last, gdown_ref)
    rs_end(out_unit, gout_ref)
    point("e2")
    third = width // 3
    for group in range(3):
        rs_end(head_units[group], *[gqkv_ref.at[:, pl.ds(j * width + group * third, third)] for j in range(3)])
        if group == 1:
            point("e3")
    rs_end(small_grad_unit, gsmall_ref)
    for unit in [*up_units, *down_units, *head_units, out_unit, small_grad_unit, down_last]:
        rs_sent(unit)
    out_copy.wait()
    tgrad_copy.wait()


def by_kernel(
    n_z, tokens, cotangent, clip_lengths, ln1_gain, ln1_bias, qkv_weight, qv_bias, out_weight, out_bias,
    ln2_gain, ln2_bias, up_weight, up_bias, down_weight, down_bias,
):
    count, width = tokens.shape
    size, deep = qkv_weight.shape[0], down_weight.shape[0]
    blocks = 4 + n_z
    vectors = (ln1_gain, ln1_bias, qv_bias, out_bias, ln2_gain, ln2_bias, up_bias, down_bias)
    vmem, dma = pltpu.VMEM, pltpu.SemaphoreType.DMA
    held = [
        vmem((blocks, n_z, 2, 2, 2, size, width), BF16),
        vmem((n_z, 2, 2, 2, deep, width), BF16),
        vmem((n_z, 2, 2, 2, 8, 128), F32),
        vmem((n_z, 2, 2, 2, 8, 128), F32),
        vmem((4, width, width), BF16),
        vmem((width, width), BF16),
        vmem((blocks, n_z, 2, 2, size, width), BF16),
        vmem((blocks, 2, n_z, size, width // 2), BF16),
        vmem((blocks, 2, n_z, size, width), BF16),
        vmem((blocks, n_z, size, width), BF16),
        vmem((max(len(LATE_SUMS), 1), 2, size, width // 2), BF16),
        vmem((max(len(LATE_SUMS), 1), 2, size, width), BF16),
        vmem((max(len(LATE_SUMS), 1), n_z, 2, 2, size, width), BF16),
        vmem((n_z, 2, 2, deep, width), BF16),
        vmem((n_z, 2, deep, width // 2), BF16),
        vmem((n_z, 2, deep, width), BF16),
        vmem((n_z, deep, width), BF16),
        vmem((n_z, 2, 2, 8, 128), F32),
        vmem((n_z, 8, 128), F32),
        vmem((2, n_z, 8, 128), F32),
        vmem((n_z, 8, 128), F32),
        vmem((3, count, width), BF16),
        vmem((width, count), BF16),
        vmem((count, width), BF16),
        vmem((width, count), BF16),
        vmem((count, width), F32),
        vmem((count, width), BF16),
        vmem((width, count), BF16),
        vmem((count, width), BF16),
        vmem((count, width), F32),
        vmem((count, width), F32),
        vmem((count, width), BF16),
        vmem((count, width), BF16),
        vmem((count, width), F32),
        vmem((count, width), F32),
        vmem((count, width), BF16),
        vmem((count, width), BF16),
        vmem((count, count), F32),
        vmem((width // 128, 2, count), F32),
        vmem((128, count), F32),
        vmem((8, width), F32),
        vmem((2, 8, width), F32),
        vmem((n_z, 8, width), F32),
        vmem((3, 8, width), F32),
        vmem((n_z, 8, width), F32),
        vmem((count, width), BF16),
        dma((6 + 2 * n_z, 9)),
        dma((6 + 2 * n_z, 9)),
        dma((6 + 2 * n_z, 9)),
        dma((6 + 2 * n_z, 9)),
        dma((8 + n_z,)),
    ]
    anywhere, whole = pl.BlockSpec(memory_space=pl.ANY), pl.BlockSpec(memory_space=pltpu.VMEM)
    shape = jax.ShapeDtypeStruct
    out, grad, g_qkv, g_out, g_up, g_down, g_small = pl.pallas_call(
        layer_kernel,
        out_shape=(
            shape((count, width), BF16),
            shape((count, width), F32),
            shape(qkv_weight.shape, F32),
            shape(out_weight.shape, F32),
            shape(up_weight.shape, F32),
            shape(down_weight.shape, F32),
            shape((8, 128), F32),
        ),
        in_specs=[pl.BlockSpec(memory_space=pltpu.SMEM)] + [anywhere] * 2 + [whole] * 8 + [anywhere] * 4,
        out_specs=(anywhere, anywhere, whole, whole, whole, whole, whole),
        scratch_shapes=held,
        compiler_params=pltpu.CompilerParams(collective_id=0, has_side_effects=True, vmem_limit_bytes=VMEM_BYTES),
    )(clip_lengths, tokens, cotangent, *vectors, qkv_weight, out_weight, up_weight, down_weight)
    large = (out, grad, g_qkv, g_out, g_up, g_down)
    done = pl.pallas_call(
        hand_over,
        out_shape=tuple(shape(a.shape, a.dtype) for a in large) + tuple(shape(v.shape, F32) for v in vectors),
        in_specs=[whole] + [anywhere] * len(large),
        out_specs=(anywhere,) * len(large) + (whole,) * len(vectors),
        scratch_shapes=[vmem(a.shape, a.dtype) for a in large] + [dma((2, len(large)))],
    )(g_small, *large)
    out, grad, g_qkv, g_out, g_up, g_down = done[:6]
    parts = done[6:]
    return (out, grad, parts[0], parts[1], g_qkv, parts[2], g_out, parts[3], parts[4], parts[5], g_up, parts[6], g_down, parts[7])


def hand_over(small_ref, *refs):
    sources, targets, vectors, held, sems = refs[:6], refs[6:12], refs[12:20], refs[20:26], refs[26]
    inward = [pltpu.make_async_copy(src, dst, sems.at[0, k]) for k, (src, dst) in enumerate(zip(sources, held))]
    outward = [pltpu.make_async_copy(src, dst, sems.at[1, k]) for k, (src, dst) in enumerate(zip(held, targets))]
    for copy in inward:
        copy.start()
    for k, vector in enumerate(vectors):
        vector[...] = small_ref[k, 0 : vector.shape[0]]
    for arrived, onward in zip(inward, outward):
        arrived.wait()
        onward.start()
    for copy in outward:
        copy.wait()


LATE_GATHERS = (1, 3)
LATE_SUMS = (0, 2)
VMEM_BYTES = 63 * 1024 * 1024


def kernel_fits(n_wide, n_narrow, tokens, qkv_weight, up_weight, down_weight):
    width, hidden = qkv_weight.shape[0], up_weight.shape[1]
    n_z = n_wide // 4
    devices = n_wide * n_narrow
    return (
        n_narrow == 2
        and n_wide == 4 * n_z
        and n_z == 4
        and hidden == n_z * width
        and width % (8 * devices) == 0
        and hidden % (16 * devices) == 0
        and 2 * width // devices <= 128
        and hidden // devices <= 128
        and width // devices == 24
        and (tokens.shape[0] // devices) % 256 == 0
    )


def solution(mesh):
    n_wide, n_narrow = mesh.shape["wide"], mesh.shape["narrow"]
    both = ("wide", "narrow")
    matrix, vector = P(both, None), P(both)
    in_specs = (
        matrix, matrix, matrix, vector, vector, matrix, vector, matrix, vector, vector, vector, matrix, vector, matrix, vector,
    )
    out_specs = (
        matrix, matrix, vector, vector, matrix, vector, matrix, vector, vector, vector, matrix, vector, matrix, vector,
    )

    def run(*arrays):
        fits = kernel_fits(n_wide, n_narrow, arrays[0], arrays[5], arrays[11], arrays[13])
        body = functools.partial(by_kernel, n_wide // 4) if fits else by_collectives
        return jax.shard_map(body, mesh=mesh, in_specs=in_specs, out_specs=out_specs, check_vma=False)(*arrays)

    return run
```

```python
import functools
import math

import jax
import jax.numpy as jnp
from jax import lax
from jax.experimental import pallas as pl
from jax.experimental.pallas import tpu as pltpu
from jax.sharding import PartitionSpec as P

H = 12
MASKED_SCORE = -1000000000.0
MESH = pl.DeviceIdType.MESH
F32 = jnp.float32
BF16 = jnp.bfloat16
ALL = slice(None)
CHUNK = 64


def layer_norm(inputs, ln_gain, ln_bias):
    row_mean = jnp.mean(inputs, axis=-1, keepdims=True)
    centred = inputs - row_mean
    spread = jnp.mean(centred * centred, axis=-1, keepdims=True)
    return centred * lax.rsqrt(spread + 1e-06) * ln_gain + ln_bias


def gelu_exact(inputs):
    return 0.5 * inputs * (1.0 + lax.erf(inputs * 0.7071067811865476))


def clip_index(lengths, row_count):
    clip_ends = jnp.cumsum(lengths)
    position = jnp.arange(row_count, dtype=jnp.int32)
    return jnp.sum((position[:, None] >= clip_ends[None, :]).astype(jnp.int32), axis=1)


def split_heads(matrix, head_count):
    row_count = matrix.shape[0]
    return matrix.reshape(row_count, head_count, -1).transpose(1, 0, 2)


def join_heads(stacked):
    head_count, row_count, head_size = stacked.shape
    return stacked.transpose(1, 0, 2).reshape(row_count, head_count * head_size)


def attend_forward(queries, key_rows, value_rows, segment, block_rows, score_scale):
    scores = (
        lax.dot_general(
            queries, key_rows, (((1,), (1,)), ((), ())), preferred_element_type=jnp.float32
        )
        * score_scale
    )
    allowed = segment[0:block_rows, None] == segment[None, :]
    scores = jnp.where(allowed, scores, MASKED_SCORE)
    highest = jnp.max(scores, axis=1, keepdims=True)
    raised = jnp.exp(scores - highest)
    denominator = jnp.sum(raised, axis=1, keepdims=True)
    softmax = (raised / denominator).astype(jnp.bfloat16)
    outputs = [jnp.dot(softmax, value_rows, preferred_element_type=jnp.float32)]
    totals = [highest + jnp.log(denominator)]
    return (jnp.concatenate(outputs, 0), jnp.concatenate(totals, 0))


def attend_backward(
    queries, key_rows, value_rows, segment, grad_out, lse_rows, block_rows, score_scale
):
    grad_keys = jnp.zeros(key_rows.shape, jnp.float32)
    grad_values = jnp.zeros(value_rows.shape, jnp.float32)
    g_rows = grad_out[0:block_rows]
    scores = (
        lax.dot_general(
            queries, key_rows, (((1,), (1,)), ((), ())), preferred_element_type=jnp.float32
        )
        * score_scale
    )
    allowed = segment[0:block_rows, None] == segment[None, :]
    softmax = jnp.where(allowed, jnp.exp(scores - lse_rows[0:block_rows]), 0.0)
    grad_values = grad_values + lax.dot_general(
        softmax.astype(jnp.bfloat16),
        g_rows,
        (((0,), (0,)), ((), ())),
        preferred_element_type=jnp.float32,
    )
    grad_probs = lax.dot_general(
        g_rows, value_rows, (((1,), (1,)), ((), ())), preferred_element_type=jnp.float32
    )
    grad_scores = (
        softmax * (grad_probs - jnp.sum(softmax * grad_probs, axis=1, keepdims=True))
    ).astype(jnp.bfloat16)
    grad_queries = [
        jnp.dot(grad_scores, key_rows, preferred_element_type=jnp.float32) * score_scale
    ]
    grad_keys = (
        grad_keys
        + lax.dot_general(
            grad_scores, queries, (((0,), (0,)), ((), ())), preferred_element_type=jnp.float32
        )
        * score_scale
    )
    return (jnp.concatenate(grad_queries, 0), grad_keys, grad_values)


def by_collectives(
    tokens,
    cotangent,
    clip_lengths,
    ln1_gain,
    ln1_bias,
    qkv_weight,
    qv_bias,
    out_weight,
    out_bias,
    ln2_gain,
    ln2_bias,
    up_weight,
    up_bias,
    down_weight,
    down_bias,
):
    gathered = (
        lax.all_gather(ln1_gain, ("wide", "narrow"), axis=0, tiled=True),
        lax.all_gather(ln1_bias, ("wide", "narrow"), axis=0, tiled=True),
        lax.all_gather(qkv_weight, ("wide", "narrow"), axis=0, tiled=True),
        lax.all_gather(qv_bias, ("wide", "narrow"), axis=0, tiled=True),
        lax.all_gather(out_weight, ("wide", "narrow"), axis=0, tiled=True),
        lax.all_gather(out_bias, ("wide", "narrow"), axis=0, tiled=True),
        lax.all_gather(ln2_gain, ("wide", "narrow"), axis=0, tiled=True),
        lax.all_gather(ln2_bias, ("wide", "narrow"), axis=0, tiled=True),
        lax.all_gather(up_weight, ("wide", "narrow"), axis=0, tiled=True),
        lax.all_gather(up_bias, ("wide", "narrow"), axis=0, tiled=True),
        lax.all_gather(down_weight, ("wide", "narrow"), axis=0, tiled=True),
        lax.all_gather(down_bias, ("wide", "narrow"), axis=0, tiled=True),
    )
    (
        gain_one,
        bias_one,
        merged_weight,
        merged_bias,
        proj_weight,
        proj_bias,
        gain_two,
        bias_two,
        w_up,
        b_up,
        w_down,
        b_down,
    ) = gathered
    inputs = tokens.astype(jnp.float32)
    row_count, model_width = inputs.shape
    head_size = model_width // H
    score_scale = 1.0 / math.sqrt(head_size)
    block_rows = min(512, row_count)
    clip_count = clip_lengths.shape[1]
    segment = clip_index(clip_lengths[0], row_count)
    live_rows = (segment < clip_count).astype(jnp.float32)[:, None]
    normed_one = layer_norm(
        inputs, gain_one.astype(jnp.float32), bias_one.astype(jnp.float32)
    ).astype(jnp.bfloat16)
    bias_float = merged_bias.astype(jnp.float32)
    full_bias = jnp.concatenate(
        [bias_float[:model_width], jnp.zeros((model_width,), jnp.float32), bias_float[model_width:]]
    )
    merged_rows = (
        jnp.dot(normed_one, merged_weight, preferred_element_type=jnp.float32) + full_bias
    ).astype(jnp.bfloat16)
    q_heads = split_heads(merged_rows[:, :model_width], H)
    k_heads = split_heads(merged_rows[:, model_width : 2 * model_width], H)
    v_heads = split_heads(merged_rows[:, 2 * model_width :], H)

    def head_forward(triple):
        return attend_forward(triple[0], triple[1], triple[2], segment, block_rows, score_scale)

    att_heads, lse_heads = lax.map(head_forward, (q_heads, k_heads, v_heads))
    attended = join_heads(att_heads).astype(jnp.bfloat16)
    branch_one = jnp.dot(
        attended, proj_weight, preferred_element_type=jnp.float32
    ) + proj_bias.astype(jnp.float32)
    middle = inputs + live_rows * branch_one
    normed_two = layer_norm(
        middle, gain_two.astype(jnp.float32), bias_two.astype(jnp.float32)
    ).astype(jnp.bfloat16)
    hidden_pre = jnp.dot(normed_two, w_up, preferred_element_type=jnp.float32) + b_up.astype(
        jnp.float32
    )
    activated, gelu_pull = jax.vjp(gelu_exact, hidden_pre)
    activated = activated.astype(jnp.bfloat16)
    branch_two = jnp.dot(activated, w_down, preferred_element_type=jnp.float32) + b_down.astype(
        jnp.float32
    )
    block_out = (middle + live_rows * branch_two).astype(jnp.bfloat16)
    back_gain_one, back_merged, back_proj, back_gain_two, back_up, back_down = (
        lax.all_gather(ln1_gain, ("wide", "narrow"), axis=0, tiled=True),
        lax.all_gather(qkv_weight, ("wide", "narrow"), axis=0, tiled=True),
        lax.all_gather(out_weight, ("wide", "narrow"), axis=0, tiled=True),
        lax.all_gather(ln2_gain, ("wide", "narrow"), axis=0, tiled=True),
        lax.all_gather(up_weight, ("wide", "narrow"), axis=0, tiled=True),
        lax.all_gather(down_weight, ("wide", "narrow"), axis=0, tiled=True),
    )
    upstream = cotangent.astype(jnp.float32)
    grad_two = (live_rows * upstream).astype(jnp.bfloat16)
    grad_b_down = jnp.sum(grad_two.astype(jnp.float32), axis=0)
    grad_w_down = jnp.einsum("tf,td->fd", activated, grad_two, preferred_element_type=jnp.float32)
    grad_act = jnp.einsum("td,fd->tf", grad_two, back_down, preferred_element_type=jnp.float32)
    grad_hidden = gelu_pull(grad_act)[0].astype(jnp.bfloat16)
    grad_b_up = jnp.sum(grad_hidden.astype(jnp.float32), axis=0)
    grad_w_up = jnp.einsum("td,tf->df", normed_two, grad_hidden, preferred_element_type=jnp.float32)
    grad_normed_two = jnp.einsum(
        "tf,df->td", grad_hidden, back_up, preferred_element_type=jnp.float32
    )
    _, norm_pull_two = jax.vjp(
        layer_norm, middle, back_gain_two.astype(jnp.float32), bias_two.astype(jnp.float32)
    )
    grad_middle_norm, grad_gain_two, grad_bias_two = norm_pull_two(grad_normed_two)
    grad_middle = upstream + grad_middle_norm
    grad_one = (live_rows * grad_middle).astype(jnp.bfloat16)
    grad_b_proj = jnp.sum(grad_one.astype(jnp.float32), axis=0)
    grad_w_proj = jnp.einsum("te,td->ed", attended, grad_one, preferred_element_type=jnp.float32)
    grad_att = jnp.einsum(
        "td,ed->te", grad_one, back_proj, preferred_element_type=jnp.float32
    ).astype(jnp.bfloat16)
    grad_att_heads = split_heads(grad_att, H)

    def head_backward(members):
        return attend_backward(
            members[0],
            members[1],
            members[2],
            segment,
            members[3],
            members[4],
            block_rows,
            score_scale,
        )

    grad_q, grad_k, grad_v = lax.map(
        head_backward, (q_heads, k_heads, v_heads, grad_att_heads, lse_heads)
    )
    grad_merged = jnp.concatenate(
        [join_heads(grad_q), join_heads(grad_k), join_heads(grad_v)], 1
    ).astype(jnp.bfloat16)
    column_sums = jnp.sum(grad_merged.astype(jnp.float32), axis=0)
    grad_merged_bias = jnp.concatenate([column_sums[:model_width], column_sums[2 * model_width :]])
    grad_w_merged = jnp.einsum(
        "te,tf->ef", normed_one, grad_merged, preferred_element_type=jnp.float32
    )
    grad_normed_one = jnp.einsum(
        "tf,ef->te", grad_merged, back_merged, preferred_element_type=jnp.float32
    )
    _, norm_pull_one = jax.vjp(
        layer_norm, inputs, back_gain_one.astype(jnp.float32), bias_one.astype(jnp.float32)
    )
    grad_input_norm, grad_gain_one, grad_bias_one = norm_pull_one(grad_normed_one)
    tokens_grad = grad_middle + grad_input_norm
    shares = (
        lax.psum_scatter(grad_gain_one, ("wide", "narrow"), scatter_dimension=0, tiled=True),
        lax.psum_scatter(grad_bias_one, ("wide", "narrow"), scatter_dimension=0, tiled=True),
        lax.psum_scatter(grad_w_merged, ("wide", "narrow"), scatter_dimension=0, tiled=True),
        lax.psum_scatter(grad_merged_bias, ("wide", "narrow"), scatter_dimension=0, tiled=True),
        lax.psum_scatter(grad_w_proj, ("wide", "narrow"), scatter_dimension=0, tiled=True),
        lax.psum_scatter(grad_b_proj, ("wide", "narrow"), scatter_dimension=0, tiled=True),
        lax.psum_scatter(grad_gain_two, ("wide", "narrow"), scatter_dimension=0, tiled=True),
        lax.psum_scatter(grad_bias_two, ("wide", "narrow"), scatter_dimension=0, tiled=True),
        lax.psum_scatter(grad_w_up, ("wide", "narrow"), scatter_dimension=0, tiled=True),
        lax.psum_scatter(grad_b_up, ("wide", "narrow"), scatter_dimension=0, tiled=True),
        lax.psum_scatter(grad_w_down, ("wide", "narrow"), scatter_dimension=0, tiled=True),
        lax.psum_scatter(grad_b_down, ("wide", "narrow"), scatter_dimension=0, tiled=True),
    )
    return (
        block_out,
        tokens_grad,
        shares[0],
        shares[1],
        shares[2],
        shares[3],
        shares[4],
        shares[5],
        shares[6],
        shares[7],
        shares[8],
        shares[9],
        shares[10],
        shares[11],
    )


def nt_dot(left, right):
    return lax.dot_general(left, right, (((1,), (1,)), ((), ())), preferred_element_type=F32)


def nn_dot(left, right):
    return jnp.dot(left, right, preferred_element_type=F32)


def rows_of(step, size=CHUNK):
    return pl.ds(pl.multiple_of(step * size, size), size)


def norm_parts(values):
    centred = values - jnp.mean(values, axis=-1, keepdims=True)
    scale = lax.rsqrt(jnp.mean(centred * centred, axis=-1, keepdims=True) + 1e-06)
    return centred * scale, scale


def fold_rows(values):
    return jnp.sum(values.reshape(-1, 8, values.shape[-1]), axis=0)


def gelu_both(u):
    tail = 0.5 * (1.0 + lax.erf(u * 0.7071067811865476))
    return u * tail, tail + u * jnp.exp(-0.5 * u * u) * 0.3989422804014327


def spread_maps(width, columns):
    column = lax.broadcasted_iota(jnp.int32, (1, columns), 1).astype(F32)
    group = jnp.floor((column + 0.5) * (1.0 / width))
    place = column - group * width
    lane = lax.broadcasted_iota(jnp.int32, (128, columns), 0).astype(F32)
    picks = jnp.where(lane == place, 1.0, 0.0).astype(BF16)
    owners = columns // width
    owner = lax.broadcasted_iota(jnp.int32, (owners, 8, columns), 0).astype(F32)
    mine = owner == group.reshape(1, 1, columns)
    return picks, mine


def spread(pieces, width, columns):
    picks, mine = spread_maps(width, columns)
    wide_rows = nn_dot(pieces.reshape(-1, 128).astype(BF16), picks)
    return jnp.sum(jnp.where(mine, wide_rows.reshape(-1, 8, columns), 0.0), axis=0)


def gather_back(vectors, width):
    columns = vectors.shape[-1]
    picks, mine = spread_maps(width, columns)
    rest = jnp.where(mine, vectors[None], 0.0).reshape(-1, columns)
    total = None
    for _ in range(3):
        part = rest.astype(BF16)
        rest = rest - part.astype(F32)
        term = nt_dot(part, picks)
        total = term if total is None else total + term
    return total.reshape(-1, 8, 128)


def layer_kernel(
    clip_ref, tok_ref, cot_ref, v0, v1, v2, v3, v4, v5, v6, v7, wqkv_ref, wout_ref, wup_ref, wdown_ref,
    out_ref, tgrad_ref, gqkv_ref, gout_ref, gup_ref, gdown_ref, gsmall_ref,
    slabs, downs, smalls, gsmalls, weights, w_up,
    row_c, row_d, row_n, row_z, late_d, late_n, late_z, down_c, down_d, down_n, down_z, sm_c, sm_d, sm_n, sm_z,
    qkv, n1t, n1, att_t, middle, n2, n2t, g2, acc_out, acc_grad, act, grad_h, pre, grad_act,
    tok, cot, bias, lse, dq_t, vec24, vec48, vec96, merged_bias, group_sums, sums, up_sums, block_out,
    ag_send, ag_recv, rs_send, rs_recv, local,
):
    n_z, width = slabs.shape[1], slabs.shape[-1]
    count = tok.shape[0]
    pairs = width // 128
    chunks = count // CHUNK
    wide_at, y = lax.axis_index("wide"), lax.axis_index("narrow")
    core = lax.rem(wide_at, 2)
    x = lax.rem(lax.div(wide_at, 2), 2)
    z = lax.div(wide_at, 4)

    def device(z_at, x_at, c_at, y_at):
        return ((z_at * 2 + x_at) * 2 + c_at, y_at)

    def row_view(block):
        def view(at):
            return slabs.at[(block, *at)]
        return view

    def down_view(tile):
        def view(at):
            return downs.at[(tile, *at[1:])]
        return view

    def small_view(ref):
        def view(at):
            return ref.at[at]
        return view

    def half_of(ref, side):
        if ref.shape[-1] < 2 * 128:
            return ref
        cut = ref.shape[-1] // 2
        return ref.at[(*([ALL] * (len(ref.shape) - 1)), pl.ds(side * cut, cut))]

    to_x, to_y, to_c = device(z, 1 - x, core, y), device(z, x, core, 1 - y), device(z, x, 1 - core, y)
    near_z, far_z, last_z = z + 1 - 2 * lax.rem(z, 2), lax.rem(z + 2, n_z), n_z - 1 - z
    inner = lax.rem(z + 1, n_z) >= 2
    to_near, to_far, to_last = device(near_z, x, core, y), device(far_z, x, core, y), device(last_z, x, core, y)
    Z1, Z2, Z3, ZR, X0, Y0, DX, DY, C0 = range(9)

    def remote(src, dst, sems, row, sem, to, recv_sem=None):
        send, recv = sems
        return pltpu.make_async_remote_copy(
            src_ref=src, dst_ref=dst, send_sem=send.at[row, sem], recv_sem=recv.at[row, sem if recv_sem is None else recv_sem],
            device_id=to, device_id_type=MESH,
        )

    def do_all(copies, what):
        for copy in copies:
            getattr(copy, what)()

    def ag_copies(unit, phase):
        view, row, phases, along = unit
        sems = (ag_send, ag_recv)
        late = phases.index("z") > phases.index("near") if "z" in phases and "near" in phases else False
        held = z if late else ALL
        own = view((z, *along))
        if phase == "z":
            return [remote(own, own, sems, row, Z1, to_near), remote(own, own, sems, row, Z2, to_far)]
        if phase == "z near":
            return [remote(own, own, sems, row, Z1, to_near)]
        if phase == "z far":
            return [remote(own, own, sems, row, Z2, to_far)]
        if phase == "z inner":
            return [remote(own, own, sems, row, Z3, to_last)]
        if phase == "relay":
            passed = view((far_z, *along))
            return [remote(passed, passed, sems, row, ZR, to_near, Z3)]
        if phase == "near":
            mine = view((held, x, core, y))
            return [remote(mine, mine, sems, row, X0, to_x), remote(mine, mine, sems, row, Y0, to_y)]
        if phase == "across":
            from_x, from_y = view((held, 1 - x, core, y)), view((held, x, core, 1 - y))
            first = half_of(from_x, 0)
            copies = [remote(first, first, sems, row, DY, to_y)]
            if from_x.shape[-1] >= 2 * 128:
                second = half_of(from_y, 1)
                copies.append(remote(second, second, sems, row, DX, to_x))
            return copies
        plane = view((ALL, ALL, core, ALL))
        return [remote(plane, plane, sems, row, C0, to_c)]

    def ag_arrived(unit, phase):
        if phase == "z":
            @pl.when(jnp.logical_not(inner))
            def _():
                do_all(ag_copies(unit, "z far"), "wait_recv")
            do_all(ag_copies(unit, "z near") + ag_copies(unit, "z inner"), "wait_recv")
        else:
            do_all(ag_copies(unit, phase), "wait_recv")

    def ag_stage(unit, stage):
        phases = unit[2]
        waits = [p for p in phases[:stage] if p != "relay"][-1:]
        phase = phases[stage] if stage < len(phases) else None
        if phase == "relay":
            @pl.when(inner)
            def _():
                do_all(ag_copies(unit, "z far"), "wait_recv")
                do_all(ag_copies(unit, "relay"), "start")
            return
        if waits:
            ag_arrived(unit, waits[0])
        if phase:
            do_all(ag_copies(unit, phase), "start")
            if phase == "z":
                @pl.when(inner)
                def _():
                    do_all(ag_copies(unit, "z inner"), "start")
        else:
            for sent in phases:
                if sent != "relay":
                    do_all(ag_copies(unit, sent), "wait_send")
            if "z" in phases:
                @pl.when(inner)
                def _():
                    do_all(ag_copies(unit, "z inner") + ag_copies(unit, "relay"), "wait_send")

    first_z = ("z", "relay", "near", "across", "core")
    last_z_order = ("near", "across", "z", "relay", "core")
    one, plane_of = (x, core, y), (ALL, core, ALL)
    small_unit = (small_view(smalls), 0, first_z, one)

    def gather_unit(block, late=False):
        return (row_view(block), 1 + block, last_z_order if late else first_z, plane_of if late else one)

    down_first = (lambda at: downs.at[at], 5 + 2 * n_z, ("z", "relay"), one)

    def gather_down(tile):
        return (down_view(tile), 5 + n_z + tile, ("near", "across", "core"), one)

    units = {"aS": small_unit, "adp": down_first}
    for block in range(4):
        units[f"ab{block}"] = gather_unit(block)
    for tile in range(n_z):
        units[f"au{tile}"] = gather_unit(4 + tile, tile in LATE_GATHERS)
        units[f"ad{tile}"] = gather_down(tile)

    def rs_copies(unit, phase):
        view, row, phases, landing, along = unit
        sems = (rs_send, rs_recv)
        late = "near" in phases and "z" in phases and phases.index("z") < phases.index("near")
        held = z if late else ALL
        if phase == "core":
            return [remote(view((ALL, ALL, 1 - core, ALL)), landing["core"], sems, row, C0, to_c)]
        if phase == "across":
            away = view((held, 1 - x, core, 1 - y))
            copies = [remote(half_of(away, 0), landing["dx"], sems, row, DX, to_x)]
            if away.shape[-1] >= 2 * 128:
                copies.append(remote(half_of(away, 1), landing["dy"], sems, row, DY, to_y))
            return copies
        if phase == "near":
            return [
                remote(view((held, 1 - x, core, y)), landing["x"], sems, row, X0, to_x),
                remote(view((held, x, core, 1 - y)), landing["y"], sems, row, Y0, to_y),
            ]
        if phase == "z":
            return [remote(view((near_z, *along)), landing["z1"], sems, row, Z1, to_near)]
        if phase == "z inner":
            return [remote(view((last_z, *along)), landing["z3"], sems, row, Z3, to_last)]
        if phase == "z outer":
            return [remote(view((last_z, *along)), landing["zr"], sems, row, ZR, to_near)]
        return [remote(view((far_z, *along)), landing["z2"], sems, row, Z2, to_far)]

    def add_into(target, *sources):
        total = target[...].astype(F32)
        for source in sources:
            total = total + source[...].astype(F32)
        target[...] = total.astype(target.dtype)

    def add_all(target, *sources):
        free = len(target.shape) - 2
        if free == 0:
            add_into(target, *sources)
            return
        places = [()]
        for extent in target.shape[1:free]:
            places = [place + (k,) for place in places for k in range(extent)]

        def step(i, carry):
            for place in places:
                add_into(target.at[(i, *place)], *[source.at[(i, *place)] for source in sources])
            return carry

        lax.fori_loop(0, target.shape[0], step, 0)

    def rs_take(unit, phase):
        view, _, phases, landing, along = unit
        late = "near" in phases and "z" in phases and phases.index("z") < phases.index("near")
        held = z if late else ALL
        if phase == "z":
            do_all(rs_copies(unit, "z") + rs_copies(unit, "z far"), "wait_recv")
            add_all(view((z, *along)), landing["z1"], landing["z2"])

            @pl.when(inner)
            def _():
                do_all(rs_copies(unit, "z inner"), "wait_recv")
                add_all(view((z, *along)), landing["z3"])
            return
        do_all(rs_copies(unit, phase), "wait_recv")
        if phase == "core":
            add_all(view((ALL, ALL, core, ALL)), landing["core"])
        elif phase == "across":
            on_y = view((held, x, core, 1 - y))
            add_all(half_of(on_y, 0), landing["dx"])
            if on_y.shape[-1] >= 2 * 128:
                add_all(half_of(view((held, 1 - x, core, y)), 1), landing["dy"])
        else:
            add_all(view((held, x, core, y)), landing["x"], landing["y"])

    def rs_stage(unit, stage):
        view, _, phases, landing, along = unit
        if stage == len(phases):
            rs_take(unit, phases[-1])
            return
        phase = phases[stage]
        if phase == "z far":
            @pl.when(inner)
            def _():
                do_all(rs_copies(unit, "z outer"), "wait_recv")
                add_all(view((far_z, *along)), landing["zr"])
            do_all(rs_copies(unit, phase), "start")
            return
        if stage > 0:
            rs_take(unit, "z" if phases[stage - 1] == "z far" else phases[stage - 1])
        do_all(rs_copies(unit, phase), "start")
        if phase == "z":
            @pl.when(inner)
            def _():
                do_all(rs_copies(unit, "z inner"), "start")

            @pl.when(jnp.logical_not(inner))
            def _():
                do_all(rs_copies(unit, "z outer"), "start")

    def rs_end(unit, *results):
        view, _, phases, landing, along = unit
        own = view((z, x, core, y))
        if phases[-1] == "near":
            do_all(rs_copies(unit, "near"), "wait_recv")
            total = own[...].astype(F32) + landing["x"][...].astype(F32) + landing["y"][...].astype(F32)
        else:
            do_all(rs_copies(unit, "z") + rs_copies(unit, "z far"), "wait_recv")
            total = own[...].astype(F32) + landing["z1"][...].astype(F32) + landing["z2"][...].astype(F32)
        size = total.shape[-1] // len(results)
        for k, result in enumerate(results):
            result[...] = total[:, k * size : (k + 1) * size]
        if phases[-1] != "near":
            @pl.when(inner)
            def _():
                do_all(rs_copies(unit, "z inner"), "wait_recv")
                for k, result in enumerate(results):
                    result[...] += landing["z3"][:, k * size : (k + 1) * size].astype(F32)

    def rs_sent(unit):
        for phase in unit[2]:
            do_all(rs_copies(unit, phase), "wait_send")
        if "z" in unit[2]:
            @pl.when(inner)
            def _():
                do_all(rs_copies(unit, "z inner"), "wait_send")

            @pl.when(jnp.logical_not(inner))
            def _():
                do_all(rs_copies(unit, "z outer"), "wait_send")

    back_last, back_first = ("core", "across", "near", "z", "z far"), ("core", "z", "z far", "across", "near")

    def z_landing(ref):
        return {"z1": ref.at[0], "z2": ref.at[1], "z3": ref.at[2], "zr": ref.at[3]}

    def row_unit(block, row, late=None):
        if late is not None:
            landing = {"core": row_c.at[block], "dx": late_d.at[late, 0], "dy": late_d.at[late, 1], "x": late_n.at[late, 0], "y": late_n.at[late, 1], **z_landing(late_z.at[late])}
            return (row_view(block), row, back_first, landing, plane_of)
        landing = {"core": row_c.at[block], "dx": row_d.at[block, 0], "dy": row_d.at[block, 1], "x": row_n.at[block, 0], "y": row_n.at[block, 1], **z_landing(row_z.at[block])}
        return (row_view(block), row, back_last, landing, one)

    def down_unit(tile, row):
        landing = {"core": down_c.at[tile], "dx": down_d.at[tile, 0], "dy": down_d.at[tile, 1], "x": down_n.at[tile, 0], "y": down_n.at[tile, 1]}
        return (down_view(tile), row, back_last[:3], landing, one)

    def block_columns(block):
        return pl.ds(block * width, width)

    third = width // 3
    results = {"rdl": [gdown_ref], "ro": [gout_ref], "rS": [gsmall_ref]}
    for t in range(n_z):
        units[f"ru{t}"] = row_unit(4 + t, t, LATE_SUMS.index(t) if t in LATE_SUMS else None)
        units[f"rd{t}"] = down_unit(t, n_z + t)
        results[f"ru{t}"] = [gup_ref.at[:, block_columns(t)]]
    for g in range(3):
        units[f"rh{g}"] = row_unit(g, 2 * n_z + g)
        results[f"rh{g}"] = [gqkv_ref.at[:, pl.ds(j * width + g * third, third)] for j in range(3)]
    units["ro"] = row_unit(3, 2 * n_z + 3)
    small_landing = {"core": sm_c, "dx": sm_d, "x": sm_n.at[0], "y": sm_n.at[1], **z_landing(sm_z)}
    units["rS"] = (small_view(gsmalls), 2 * n_z + 4, back_last, small_landing, one)
    units["rdl"] = (lambda at: downs.at[at], 2 * n_z + 5, ("z", "z far"), z_landing(down_z), one)

    def point(name):
        for unit_name, stage in TABLE.get(name, ()):
            unit = units[unit_name]
            if unit_name[0] == "a":
                ag_stage(unit, stage)
            elif unit_name in results and stage == len(unit[2]):
                rs_end(unit, *results[unit_name])
            else:
                rs_stage(unit, stage)

    def points_at(index, names):
        for k, name in enumerate(names):
            if TABLE.get(name):
                pl.when(index == k)(functools.partial(point, name))

    barrier = pltpu.get_barrier_semaphore()
    partners = [to_near, to_far, to_last, to_x, to_y, to_c]
    for to in partners:
        pl.semaphore_signal(barrier, inc=1, device_id=to, device_id_type=MESH)
    shards = []
    for g in range(3):
        for j in range(3):
            shards.append((wqkv_ref.at[:, pl.ds(j * width + g * third, third)], slabs.at[g, z, x, core, y, :, pl.ds(j * third, third)]))
    shards.append((wout_ref, slabs.at[3, z, x, core, y]))
    for tile in range(n_z):
        shards.append((wup_ref.at[:, block_columns(tile)], slabs.at[4 + tile, z, x, core, y]))
    shards.append((wdown_ref, downs.at[z, x, core, y]))
    shard_copies = [pltpu.make_async_copy(src, dst, local.at[k]) for k, (src, dst) in enumerate(shards)]
    row_copies = [pltpu.make_async_copy(tok_ref, tok, local.at[len(shards)]), pltpu.make_async_copy(cot_ref, cot, local.at[len(shards) + 1])]
    do_all(shard_copies + row_copies, "start")
    smalls[z, x, core, y] = jnp.zeros((8, 128), F32)
    for k, vector in enumerate((v0, v1, v2, v3, v4, v5, v6, v7)):
        smalls[z, x, core, y, k, 0 : vector.shape[0]] = vector[...].astype(F32)
    do_all(shard_copies, "wait")
    pl.semaphore_wait(barrier, len(partners))
    point("mask")
    do_all(row_copies, "wait")

    ends = []
    for k in range(clip_ref.shape[1]):
        ends.append(clip_ref[0, k] + (ends[-1] if ends else 0))

    def segment_of(position):
        total = jnp.zeros(position.shape, jnp.int32)
        for end in ends:
            total = total + jnp.where(position >= end, 1, 0)
        return total

    across = segment_of(lax.broadcasted_iota(jnp.int32, (CHUNK, count), 1))

    def live_of(step):
        position = lax.broadcasted_iota(jnp.int32, (CHUNK, 1), 0) + step * CHUNK
        return jnp.where(position < ends[-1], 1.0, 0.0)

    ones = jnp.ones((8, count), BF16)

    def column_sums(values):
        return nn_dot(ones, values)

    def mask_step(i, carry):
        down = segment_of(lax.broadcasted_iota(jnp.int32, (CHUNK, count), 0) + i * CHUNK)
        bias[rows_of(i), :] = jnp.where(down == across, 0.0, -1e30)
        g2[rows_of(i), :] = (live_of(i) * cot[rows_of(i), :].astype(F32)).astype(BF16)
        return carry

    lax.fori_loop(0, chunks, mask_step, 0)
    sums[...] = jnp.zeros_like(sums)
    up_sums[...] = jnp.zeros_like(up_sums)
    sums[0, 7:8, :] = column_sums(g2[...])[0:1]

    point("vec")
    vec24[...] = spread(smalls[...], 24, width)
    for k in range(2):
        vec48[k] = spread(smalls[k * n_z // 2 : (k + 1) * n_z // 2], 48, width)
    for k in range(n_z):
        vec96[k] = spread(smalls[k], 96, width)
    for g in range(3):
        span = slice(g * third, (g + 1) * third)
        merged_bias[g, 0:1, :] = jnp.concatenate(
            [vec48[0, 2:3, span], jnp.zeros((1, width - 2 * third), F32), vec48[1, 2:3, span]], axis=1
        )

    def norm_one(i, carry):
        normed, _ = norm_parts(tok[rows_of(i), :].astype(F32))
        n1[rows_of(i), :] = (normed * vec24[0:1, :] + vec24[1:2, :]).astype(BF16)
        return carry

    lax.fori_loop(0, chunks, norm_one, 0)

    def turn(source, target):
        def step(i, carry):
            at = rows_of(i, 128)
            target[at, :] = source[:, at].T
            return carry

        lax.fori_loop(0, pairs, step, 0)

    point("turn")
    turn(n1, n1t)

    def assemble(block, target):
        def step(z_at, carry):
            for x_at in range(2):
                for c_at in range(2):
                    two = slabs[block, z_at, x_at, c_at].astype(F32)
                    size = 2 * two.shape[1]
                    first = pl.multiple_of(((z_at * 2 + x_at) * 2 + c_at) * size, 16)
                    target[pl.ds(first, size), :] = two.reshape(size, width).astype(BF16)
            return carry

        lax.fori_loop(0, n_z, step, 0)

    lane = lax.broadcasted_iota(jnp.int32, (count, 128), 1)

    def one_head(values, head):
        keep = lane < 64 if head == 0 else lane >= 64
        return jnp.where(keep, values, jnp.zeros_like(values))

    q_block = 256
    parts = count // q_block
    per_group = pairs // 3

    def places(p):
        first = lax.rem(p, per_group) * 128
        return lax.div(p, per_group), [pl.ds(pl.multiple_of(first + j * third, 128), 128) for j in range(3)]

    def attend(p, carry):
        group, (at_q, at_k, at_v) = places(p)
        points_at(p, [f"q{k // per_group}" if k % per_group == 0 else "" for k in range(pairs)])

        @pl.when(lax.rem(p, per_group) == 0)
        def _():
            assemble(group, weights.at[group])
            qkv[group] = (nn_dot(n1[...], weights[group]) + merged_bias[group, 0:1, :]).astype(BF16)

        points_at(p, [f"t{k}" for k in range(pairs)])
        keys = qkv[group, :, at_k]
        queries = qkv[group, :, at_q] * 0.125
        values_t = qkv[group, :, at_v].T
        for head in range(2):
            if head:
                points_at(p, [f"T{k}" for k in range(pairs)])
            mine = one_head(queries, head)
            for part in range(parts):
                span = slice(part * q_block, (part + 1) * q_block)
                scores = nt_dot(keys, mine[span]) + bias[:, span]
                highest = jnp.max(scores, axis=0, keepdims=True)
                raised = jnp.exp(scores - highest)
                total = jnp.sum(raised, axis=0, keepdims=True)
                chances = (raised * (1.0 / total)).astype(BF16)
                lse[p, head : head + 1, span] = highest + jnp.log(total)
                result = nn_dot(values_t[64 * head : 64 * head + 64], chances)
                att_t[pl.ds(pl.multiple_of(p * 128 + 64 * head, 64), 64), span] = result.astype(BF16)
        return carry

    lax.fori_loop(0, pairs, attend, 0)
    point("tb")
    att = n1

    def turn_back(p, carry):
        at = rows_of(p, 128)
        att[:, at] = att_t[at, :].T
        return carry

    lax.fori_loop(0, pairs, turn_back, 0)
    point("out")
    assemble(3, weights.at[3])
    pre[...] = nn_dot(att[...], weights[3])

    def norm_two(i, carry):
        at = rows_of(i)
        branch = pre[at, :] + vec24[3:4, :]
        mid = tok[at, :].astype(F32) + live_of(i) * branch
        middle[at, :] = mid
        normed, _ = norm_parts(mid)
        n2[at, :] = (normed * vec24[4:5, :] + vec24[5:6, :]).astype(BF16)
        return carry

    point("n2a")
    lax.fori_loop(0, chunks // 2, norm_two, 0)
    point("n2b")
    lax.fori_loop(chunks // 2, chunks, norm_two, 0)
    point("n2t")
    turn(n2, n2t)
    acc_out[...] = jnp.zeros_like(acc_out)
    acc_grad[...] = jnp.zeros_like(acc_grad)

    def store_rows(block, lhs_t, rhs):
        deep = width // n_z
        size = slabs.shape[-2]

        def step(z_at, carry):
            total = nn_dot(lhs_t[rows_of(z_at, deep), :], rhs)
            for k in range(8):
                slabs[block, z_at, k // 4, k // 2 % 2, k % 2] = total[k * size : (k + 1) * size].astype(BF16)
            return carry

        lax.fori_loop(0, n_z, step, 0)

    def feed(t, carry):
        def step_point(name):
            points_at(t, [f"{name}{k}" for k in range(n_z)])

        step_point("fa")
        assemble(4 + t, w_up)
        step_point("fb")
        pre[...] = nn_dot(n2[...], w_up[...])
        step_point("fc")
        w_down = downs[t].reshape(width, width)
        grad_act[...] = nt_dot(g2[...], w_down)
        up_bias = vec96[t, 6:7, :]

        def gelu_step(i, carry):
            at = rows_of(i, 32)
            active, slope = gelu_both(pre[at, :] + up_bias)
            act[at, :] = active.astype(BF16)
            grad_h[at, :] = (grad_act[at, :] * slope).astype(BF16)
            return carry

        step_point("fd")
        lax.fori_loop(0, count // 64, gelu_step, 0)
        step_point("fe")
        lax.fori_loop(count // 64, count // 32, gelu_step, 0)
        up_sums[t, 6:7, :] = column_sums(grad_h[...])[0:1]
        step_point("ff")
        acc_out[...] += nn_dot(act[...], w_down)
        step_point("fg")
        acc_grad[...] += nt_dot(grad_h[...], w_up[...])
        step_point("fh")
        store_rows(4 + t, n2t, grad_h[...])
        step_point("fi")
        for j in range(pairs):
            span = slice(j * 128, (j + 1) * 128)
            piece = nn_dot(act[:, span].T, g2[...]).astype(BF16)
            size = downs.shape[-2]
            at = j * 128
            while at < (j + 1) * 128:
                owner, inside = at // size, at % size
                length = min(size - inside, (j + 1) * 128 - at)
                downs[t, owner // 4, owner // 2 % 2, owner % 2, inside : inside + length, :] = piece[at - j * 128 : at - j * 128 + length]
                at += length
        return carry

    lax.fori_loop(0, n_z, feed, 0)

    def norm_two_back(i, carry):
        gain_sum, bias_sum = carry
        at = rows_of(i)
        alive = live_of(i)
        mid = middle[at, :]
        block_out[at, :] = (mid + alive * (acc_out[at, :] + vec24[7:8, :])).astype(BF16)
        normed, scale = norm_parts(mid)
        e = acc_grad[at, :]
        scaled = e * vec24[4:5, :]
        inner_part = scaled - jnp.mean(scaled, axis=-1, keepdims=True) - normed * jnp.mean(scaled * normed, axis=-1, keepdims=True)
        grad_mid = cot[at, :].astype(F32) + inner_part * scale
        acc_grad[at, :] = grad_mid
        g2[at, :] = (alive * grad_mid).astype(BF16)
        return (gain_sum + fold_rows(e * normed), bias_sum + fold_rows(e))

    zero = jnp.zeros((8, width), F32)
    point("ba")
    carry = lax.fori_loop(0, chunks // 2, norm_two_back, (zero, zero))
    point("bb")
    gain_sum, bias_sum = lax.fori_loop(chunks // 2, chunks, norm_two_back, carry)
    sums[0, 4:5, :] = jnp.sum(gain_sum, axis=0, keepdims=True)
    sums[0, 5:6, :] = jnp.sum(bias_sum, axis=0, keepdims=True)
    sums[0, 3:4, :] = column_sums(g2[...])[0:1]
    out_copy = pltpu.make_async_copy(block_out, out_ref, local.at[0])
    out_copy.start()

    point("og")
    store_rows(3, att_t, g2[...])
    point("ga")
    grad_att = n2
    grad_att[...] = nt_dot(g2[...], weights[3]).astype(BF16)

    def attend_back(p, carry):
        group, (at_q, at_k, at_v) = places(p)
        points_at(p, [f"a{k}" for k in range(pairs)])
        keys = qkv[group, :, at_k]
        values = qkv[group, :, at_v]
        queries = qkv[group, :, at_q] * 0.125
        grads = grad_att[:, rows_of(p, 128)]
        keys_t = keys.T
        grad_keys = jnp.zeros((count, 128), F32)
        grad_values = jnp.zeros((count, 128), F32)
        for head in range(2):
            if head:
                points_at(p, [f"A{k}" for k in range(pairs)])
            my_queries, my_grads = one_head(queries, head), one_head(grads, head)
            for part in range(parts):
                span = slice(part * q_block, (part + 1) * q_block)
                scores = nt_dot(keys, my_queries[span]) + bias[:, span]
                chances = jnp.exp(scores - lse[p, head : head + 1, span])
                slopes = nt_dot(values, my_grads[span])
                level = jnp.sum(chances * slopes, axis=0, keepdims=True)
                grad_scores = (chances * (slopes - level)).astype(BF16)
                grad_values += nn_dot(chances.astype(BF16), my_grads[span])
                grad_keys += nn_dot(grad_scores, my_queries[span])
                dq_t[64 * head : 64 * head + 64, span] = nn_dot(keys_t[64 * head : 64 * head + 64], grad_scores) * 0.125
        qkv[group, :, at_q] = dq_t[...].T.astype(BF16)
        qkv[group, :, at_k] = grad_keys.astype(BF16)
        qkv[group, :, at_v] = grad_values.astype(BF16)
        points_at(p, [f"H{k // per_group}" if k % per_group == per_group - 1 else "" for k in range(pairs)])

        @pl.when(lax.rem(p, per_group) == per_group - 1)
        def _():
            store_rows(group, n1t, qkv[group])
            group_sums[group] = column_sums(qkv[group])

        return carry

    lax.fori_loop(0, pairs, attend_back, 0)

    point("g2")
    pre[...] = nt_dot(qkv[2], weights[2])
    point("g1")
    pre[...] += nt_dot(qkv[1], weights[1])
    point("g0")
    pre[...] += nt_dot(qkv[0], weights[0])

    def norm_one_back(i, carry):
        gain_sum, bias_sum = carry
        at = rows_of(i)
        normed, scale = norm_parts(tok[at, :].astype(F32))
        e = pre[at, :]
        scaled = e * vec24[0:1, :]
        inner_part = scaled - jnp.mean(scaled, axis=-1, keepdims=True) - normed * jnp.mean(scaled * normed, axis=-1, keepdims=True)
        acc_grad[at, :] = acc_grad[at, :] + inner_part * scale
        return (gain_sum + fold_rows(e * normed), bias_sum + fold_rows(e))

    point("na")
    carry = lax.fori_loop(0, chunks // 2, norm_one_back, (zero, zero))
    point("nb")
    gain_sum, bias_sum = lax.fori_loop(chunks // 2, chunks, norm_one_back, carry)
    tgrad_copy = pltpu.make_async_copy(acc_grad, tgrad_ref, local.at[1])
    tgrad_copy.start()
    sums[0, 0:1, :] = jnp.sum(gain_sum, axis=0, keepdims=True)
    sums[0, 1:2, :] = jnp.sum(bias_sum, axis=0, keepdims=True)
    for g in range(3):
        span = slice(g * third, (g + 1) * third)
        sums[1, 2:3, span] = group_sums[g, 0:1, :third]
        sums[2, 2:3, span] = group_sums[g, 0:1, 2 * third :]
    point("gb")
    gsmalls[...] = gather_back(sums[0], 24).reshape(gsmalls.shape)
    for k in range(2):
        part = gather_back(sums[1 + k], 48)
        span = slice(k * n_z // 2, (k + 1) * n_z // 2)
        gsmalls[span] = gsmalls[span] + part.reshape(n_z // 2, 2, 2, 2, 8, 128)
    for k in range(n_z):
        gsmalls[k] = gsmalls[k] + gather_back(up_sums[k], 96).reshape(2, 2, 2, 8, 128)

    point("end")
    for name, unit in units.items():
        if name[0] == "r":
            rs_sent(unit)
    out_copy.wait()
    tgrad_copy.wait()


def by_kernel(
    n_z, tokens, cotangent, clip_lengths, ln1_gain, ln1_bias, qkv_weight, qv_bias, out_weight, out_bias,
    ln2_gain, ln2_bias, up_weight, up_bias, down_weight, down_bias,
):
    count, width = tokens.shape
    size, deep = qkv_weight.shape[0], down_weight.shape[0]
    blocks = 4 + n_z
    vectors = (ln1_gain, ln1_bias, qv_bias, out_bias, ln2_gain, ln2_bias, up_bias, down_bias)
    vmem, dma = pltpu.VMEM, pltpu.SemaphoreType.DMA
    held = [
        vmem((blocks, n_z, 2, 2, 2, size, width), BF16),
        vmem((n_z, 2, 2, 2, deep, width), BF16),
        vmem((n_z, 2, 2, 2, 8, 128), F32),
        vmem((n_z, 2, 2, 2, 8, 128), F32),
        vmem((4, width, width), BF16),
        vmem((width, width), BF16),
        vmem((blocks, n_z, 2, 2, size, width), BF16),
        vmem((blocks, 2, n_z, size, width // 2), BF16),
        vmem((blocks, 2, n_z, size, width), BF16),
        vmem((blocks, n_z, size, width), BF16),
        vmem((max(len(LATE_SUMS), 1), 2, size, width // 2), BF16),
        vmem((max(len(LATE_SUMS), 1), 2, size, width), BF16),
        vmem((max(len(LATE_SUMS), 1), n_z, 2, 2, size, width), BF16),
        vmem((n_z, 2, 2, deep, width), BF16),
        vmem((n_z, 2, deep, width // 2), BF16),
        vmem((n_z, 2, deep, width), BF16),
        vmem((n_z, deep, width), BF16),
        vmem((n_z, 2, 2, 8, 128), F32),
        vmem((n_z, 8, 128), F32),
        vmem((2, n_z, 8, 128), F32),
        vmem((n_z, 8, 128), F32),
        vmem((3, count, width), BF16),
        vmem((width, count), BF16),
        vmem((count, width), BF16),
        vmem((width, count), BF16),
        vmem((count, width), F32),
        vmem((count, width), BF16),
        vmem((width, count), BF16),
        vmem((count, width), BF16),
        vmem((count, width), F32),
        vmem((count, width), F32),
        vmem((count, width), BF16),
        vmem((count, width), BF16),
        vmem((count, width), F32),
        vmem((count, width), F32),
        vmem((count, width), BF16),
        vmem((count, width), BF16),
        vmem((count, count), F32),
        vmem((width // 128, 2, count), F32),
        vmem((128, count), F32),
        vmem((8, width), F32),
        vmem((2, 8, width), F32),
        vmem((n_z, 8, width), F32),
        vmem((3, 8, width), F32),
        vmem((3, 8, width), F32),
        vmem((3, 8, width), F32),
        vmem((n_z, 8, width), F32),
        vmem((count, width), BF16),
        dma((6 + 2 * n_z, 9)),
        dma((6 + 2 * n_z, 9)),
        dma((6 + 2 * n_z, 9)),
        dma((6 + 2 * n_z, 9)),
        dma((13 + n_z,)),
    ]
    anywhere, whole = pl.BlockSpec(memory_space=pl.ANY), pl.BlockSpec(memory_space=pltpu.VMEM)
    shape = jax.ShapeDtypeStruct
    out, grad, g_qkv, g_out, g_up, g_down, g_small = pl.pallas_call(
        layer_kernel,
        out_shape=(
            shape((count, width), BF16),
            shape((count, width), F32),
            shape(qkv_weight.shape, F32),
            shape(out_weight.shape, F32),
            shape(up_weight.shape, F32),
            shape(down_weight.shape, F32),
            shape((8, 128), F32),
        ),
        in_specs=[pl.BlockSpec(memory_space=pltpu.SMEM)] + [anywhere] * 2 + [whole] * 8 + [anywhere] * 4,
        out_specs=(anywhere, anywhere, whole, whole, whole, whole, whole),
        scratch_shapes=held,
        compiler_params=pltpu.CompilerParams(collective_id=0, has_side_effects=True, vmem_limit_bytes=VMEM_BYTES),
    )(clip_lengths, tokens, cotangent, *vectors, qkv_weight, out_weight, up_weight, down_weight)
    large = (out, grad, g_qkv, g_out, g_up, g_down)
    done = pl.pallas_call(
        hand_over,
        out_shape=tuple(shape(a.shape, a.dtype) for a in large) + tuple(shape(v.shape, F32) for v in vectors),
        in_specs=[whole] + [anywhere] * len(large),
        out_specs=(anywhere,) * len(large) + (whole,) * len(vectors),
        scratch_shapes=[vmem(a.shape, a.dtype) for a in large] + [dma((2, len(large)))],
    )(g_small, *large)
    out, grad, g_qkv, g_out, g_up, g_down = done[:6]
    parts = done[6:]
    return (out, grad, parts[0], parts[1], g_qkv, parts[2], g_out, parts[3], parts[4], parts[5], g_up, parts[6], g_down, parts[7])


def hand_over(small_ref, *refs):
    sources, targets, vectors, held, sems = refs[:6], refs[6:12], refs[12:20], refs[20:26], refs[26]
    inward = [pltpu.make_async_copy(src, dst, sems.at[0, k]) for k, (src, dst) in enumerate(zip(sources, held))]
    outward = [pltpu.make_async_copy(src, dst, sems.at[1, k]) for k, (src, dst) in enumerate(zip(held, targets))]
    for copy in inward:
        copy.start()
    for k, vector in enumerate(vectors):
        vector[...] = small_ref[k, 0 : vector.shape[0]]
    for arrived, onward in zip(inward, outward):
        arrived.wait()
        onward.start()
    for copy in outward:
        copy.wait()


LATE_GATHERS = ()
LATE_SUMS = ()
TABLE = {
    "mask": (("aS", 0), ("ab0", 0),),
    "vec": (("ab1", 0), ("aS", 1), ("ab0", 1), ("ab2", 0), ("ab1", 1), ("aS", 2), ("ab3", 0), ("ab0", 2), ("ab2", 1), ("aS", 3), ("adp", 0), ("ab1", 2), ("ab3", 1), ("ab2", 2), ("aS", 4), ("aS", 5),),
    "turn": (("ab0", 3),),
    "q0": (("ab1", 3), ("adp", 1), ("ab2", 3), ("ab0", 4), ("au0", 0), ("ab3", 2), ("ab0", 5), ("ab1", 4),),
    "t0": (("au1", 0),),
    "T0": (("ab1", 5), ("ab2", 4), ("adp", 2), ("ad0", 0),),
    "t1": (("au0", 1), ("ad1", 0), ("ab2", 5), ("au2", 0),),
    "q1": (("au1", 1), ("au3", 0),),
    "t2": (("ab3", 3),),
    "T2": (("au0", 2), ("au2", 1),),
    "T3": (("au3", 1),),
    "q2": (("ad0", 1),),
    "T4": (("ab3", 4), ("au1", 2),),
    "T5": (("ab3", 5),),
    "tb": (("au0", 3),),
    "n2a": (("ad0", 2), ("ad1", 1),),
    "n2b": (("au2", 2), ("ad0", 3),),
    "fa0": (("au0", 4), ("au1", 3), ("au0", 5), ("ad1", 2), ("ad2", 0),),
    "fd0": (("ad1", 3),),
    "fe0": (("au2", 3),),
    "ff0": (("au1", 4), ("au3", 2),),
    "fh0": (("au1", 5),),
    "fi0": (("ru0", 0),),
    "fa1": (("ad2", 1), ("rd0", 0),),
    "fd1": (("au2", 4), ("ad3", 0),),
    "fe1": (("au2", 5),),
    "ff1": (("au3", 3),),
    "fi1": (("ad2", 2), ("ru0", 1), ("ru1", 0),),
    "fa2": (("ad2", 3), ("rd0", 1), ("rd1", 0),),
    "fb2": (("ad3", 1),),
    "fd2": (("au3", 4), ("ru1", 1),),
    "fe2": (("au3", 5), ("ru0", 2),),
    "fh2": (("ad3", 2), ("rd0", 2),),
    "fi2": (("ru2", 0),),
    "fa3": (("ad3", 3), ("rd2", 0),),
    "fd3": (("ru1", 2),),
    "fe3": (("ru0", 3),),
    "ff3": (("rd1", 1),),
    "fg3": (("ru0", 4), ("rd0", 3), ("ru2", 1),),
    "fh3": (("rd2", 1),),
    "fi3": (("ru3", 0),),
    "ba": (("ru1", 3), ("rd3", 0),),
    "bb": (("rd1", 2),),
    "og": (("ru1", 4), ("ru2", 2),),
    "ga": (("ro", 0),),
    "a0": (("rd2", 2),),
    "A0": (("rd1", 3),),
    "a1": (("ru3", 1),),
    "A1": (("ru2", 3), ("rd3", 1),),
    "H0": (("ro", 1),),
    "a2": (("ru2", 4), ("rd2", 3), ("rh0", 0),),
    "A2": (("ru3", 2),),
    "a3": (("rd3", 2),),
    "H1": (("ro", 2),),
    "a4": (("ru3", 3), ("rh1", 0),),
    "A4": (("rh0", 1),),
    "a5": (("ru3", 4), ("rd3", 3), ("rh1", 1), ("rdl", 0),),
    "g2": (("rh0", 2), ("rh2", 0),),
    "g1": (("ro", 3), ("rh1", 2),),
    "g0": (("rdl", 1),),
    "na": (("rh2", 1),),
    "end": (("ru0", 5), ("ru1", 5), ("ru2", 5), ("ru3", 5), ("ro", 4), ("rS", 0), ("rh2", 2), ("rh0", 3), ("rS", 1), ("rh1", 3), ("rdl", 2), ("rh0", 4), ("ro", 5), ("rh1", 4), ("rh2", 3), ("rS", 2), ("rh0", 5), ("rS", 3), ("rh2", 4), ("rh1", 5), ("rS", 4), ("rh2", 5), ("rS", 5),),
}

VMEM_BYTES = 63 * 1024 * 1024


def kernel_fits(n_wide, n_narrow, tokens, qkv_weight, up_weight, down_weight):
    width, hidden = qkv_weight.shape[0], up_weight.shape[1]
    n_z = n_wide // 4
    devices = n_wide * n_narrow
    return (
        n_narrow == 2
        and n_wide == 4 * n_z
        and n_z == 4
        and hidden == n_z * width
        and width % (8 * devices) == 0
        and hidden % (16 * devices) == 0
        and 2 * width // devices <= 128
        and hidden // devices <= 128
        and width // devices == 24
        and (tokens.shape[0] // devices) % 256 == 0
    )


def solution(mesh):
    n_wide, n_narrow = mesh.shape["wide"], mesh.shape["narrow"]
    both = ("wide", "narrow")
    matrix, vector = P(both, None), P(both)
    in_specs = (
        matrix, matrix, matrix, vector, vector, matrix, vector, matrix, vector, vector, vector, matrix, vector, matrix, vector,
    )
    out_specs = (
        matrix, matrix, vector, vector, matrix, vector, matrix, vector, vector, vector, matrix, vector, matrix, vector,
    )

    def run(*arrays):
        fits = kernel_fits(n_wide, n_narrow, arrays[0], arrays[5], arrays[11], arrays[13])
        body = functools.partial(by_kernel, n_wide // 4) if fits else by_collectives
        return jax.shard_map(body, mesh=mesh, in_specs=in_specs, out_specs=out_specs, check_vma=False)(*arrays)

    return run
```

```python
import functools
import math

import jax
import jax.numpy as jnp
from jax import lax
from jax.experimental import pallas as pl
from jax.experimental.pallas import tpu as pltpu
from jax.sharding import PartitionSpec as P

H = 12
MASKED_SCORE = -1000000000.0
MESH = pl.DeviceIdType.MESH
F32 = jnp.float32
BF16 = jnp.bfloat16
ALL = slice(None)
CHUNK = 256


def layer_norm(inputs, ln_gain, ln_bias):
    row_mean = jnp.mean(inputs, axis=-1, keepdims=True)
    centred = inputs - row_mean
    spread = jnp.mean(centred * centred, axis=-1, keepdims=True)
    return centred * lax.rsqrt(spread + 1e-06) * ln_gain + ln_bias


def gelu_exact(inputs):
    return 0.5 * inputs * (1.0 + lax.erf(inputs * 0.7071067811865476))


def clip_index(lengths, row_count):
    clip_ends = jnp.cumsum(lengths)
    position = jnp.arange(row_count, dtype=jnp.int32)
    return jnp.sum((position[:, None] >= clip_ends[None, :]).astype(jnp.int32), axis=1)


def split_heads(matrix, head_count):
    row_count = matrix.shape[0]
    return matrix.reshape(row_count, head_count, -1).transpose(1, 0, 2)


def join_heads(stacked):
    head_count, row_count, head_size = stacked.shape
    return stacked.transpose(1, 0, 2).reshape(row_count, head_count * head_size)


def attend_forward(queries, key_rows, value_rows, segment, block_rows, score_scale):
    scores = (
        lax.dot_general(
            queries, key_rows, (((1,), (1,)), ((), ())), preferred_element_type=jnp.float32
        )
        * score_scale
    )
    allowed = segment[0:block_rows, None] == segment[None, :]
    scores = jnp.where(allowed, scores, MASKED_SCORE)
    highest = jnp.max(scores, axis=1, keepdims=True)
    raised = jnp.exp(scores - highest)
    denominator = jnp.sum(raised, axis=1, keepdims=True)
    softmax = (raised / denominator).astype(jnp.bfloat16)
    outputs = [jnp.dot(softmax, value_rows, preferred_element_type=jnp.float32)]
    totals = [highest + jnp.log(denominator)]
    return (jnp.concatenate(outputs, 0), jnp.concatenate(totals, 0))


def attend_backward(
    queries, key_rows, value_rows, segment, grad_out, lse_rows, block_rows, score_scale
):
    grad_keys = jnp.zeros(key_rows.shape, jnp.float32)
    grad_values = jnp.zeros(value_rows.shape, jnp.float32)
    g_rows = grad_out[0:block_rows]
    scores = (
        lax.dot_general(
            queries, key_rows, (((1,), (1,)), ((), ())), preferred_element_type=jnp.float32
        )
        * score_scale
    )
    allowed = segment[0:block_rows, None] == segment[None, :]
    softmax = jnp.where(allowed, jnp.exp(scores - lse_rows[0:block_rows]), 0.0)
    grad_values = grad_values + lax.dot_general(
        softmax.astype(jnp.bfloat16),
        g_rows,
        (((0,), (0,)), ((), ())),
        preferred_element_type=jnp.float32,
    )
    grad_probs = lax.dot_general(
        g_rows, value_rows, (((1,), (1,)), ((), ())), preferred_element_type=jnp.float32
    )
    grad_scores = (
        softmax * (grad_probs - jnp.sum(softmax * grad_probs, axis=1, keepdims=True))
    ).astype(jnp.bfloat16)
    grad_queries = [
        jnp.dot(grad_scores, key_rows, preferred_element_type=jnp.float32) * score_scale
    ]
    grad_keys = (
        grad_keys
        + lax.dot_general(
            grad_scores, queries, (((0,), (0,)), ((), ())), preferred_element_type=jnp.float32
        )
        * score_scale
    )
    return (jnp.concatenate(grad_queries, 0), grad_keys, grad_values)


def by_collectives(
    tokens,
    cotangent,
    clip_lengths,
    ln1_gain,
    ln1_bias,
    qkv_weight,
    qv_bias,
    out_weight,
    out_bias,
    ln2_gain,
    ln2_bias,
    up_weight,
    up_bias,
    down_weight,
    down_bias,
):
    gathered = (
        lax.all_gather(ln1_gain, ("wide", "narrow"), axis=0, tiled=True),
        lax.all_gather(ln1_bias, ("wide", "narrow"), axis=0, tiled=True),
        lax.all_gather(qkv_weight, ("wide", "narrow"), axis=0, tiled=True),
        lax.all_gather(qv_bias, ("wide", "narrow"), axis=0, tiled=True),
        lax.all_gather(out_weight, ("wide", "narrow"), axis=0, tiled=True),
        lax.all_gather(out_bias, ("wide", "narrow"), axis=0, tiled=True),
        lax.all_gather(ln2_gain, ("wide", "narrow"), axis=0, tiled=True),
        lax.all_gather(ln2_bias, ("wide", "narrow"), axis=0, tiled=True),
        lax.all_gather(up_weight, ("wide", "narrow"), axis=0, tiled=True),
        lax.all_gather(up_bias, ("wide", "narrow"), axis=0, tiled=True),
        lax.all_gather(down_weight, ("wide", "narrow"), axis=0, tiled=True),
        lax.all_gather(down_bias, ("wide", "narrow"), axis=0, tiled=True),
    )
    (
        gain_one,
        bias_one,
        merged_weight,
        merged_bias,
        proj_weight,
        proj_bias,
        gain_two,
        bias_two,
        w_up,
        b_up,
        w_down,
        b_down,
    ) = gathered
    inputs = tokens.astype(jnp.float32)
    row_count, model_width = inputs.shape
    head_size = model_width // H
    score_scale = 1.0 / math.sqrt(head_size)
    block_rows = min(512, row_count)
    clip_count = clip_lengths.shape[1]
    segment = clip_index(clip_lengths[0], row_count)
    live_rows = (segment < clip_count).astype(jnp.float32)[:, None]
    normed_one = layer_norm(
        inputs, gain_one.astype(jnp.float32), bias_one.astype(jnp.float32)
    ).astype(jnp.bfloat16)
    bias_float = merged_bias.astype(jnp.float32)
    full_bias = jnp.concatenate(
        [bias_float[:model_width], jnp.zeros((model_width,), jnp.float32), bias_float[model_width:]]
    )
    merged_rows = (
        jnp.dot(normed_one, merged_weight, preferred_element_type=jnp.float32) + full_bias
    ).astype(jnp.bfloat16)
    q_heads = split_heads(merged_rows[:, :model_width], H)
    k_heads = split_heads(merged_rows[:, model_width : 2 * model_width], H)
    v_heads = split_heads(merged_rows[:, 2 * model_width :], H)

    def head_forward(triple):
        return attend_forward(triple[0], triple[1], triple[2], segment, block_rows, score_scale)

    att_heads, lse_heads = lax.map(head_forward, (q_heads, k_heads, v_heads))
    attended = join_heads(att_heads).astype(jnp.bfloat16)
    branch_one = jnp.dot(
        attended, proj_weight, preferred_element_type=jnp.float32
    ) + proj_bias.astype(jnp.float32)
    middle = inputs + live_rows * branch_one
    normed_two = layer_norm(
        middle, gain_two.astype(jnp.float32), bias_two.astype(jnp.float32)
    ).astype(jnp.bfloat16)
    hidden_pre = jnp.dot(normed_two, w_up, preferred_element_type=jnp.float32) + b_up.astype(
        jnp.float32
    )
    activated, gelu_pull = jax.vjp(gelu_exact, hidden_pre)
    activated = activated.astype(jnp.bfloat16)
    branch_two = jnp.dot(activated, w_down, preferred_element_type=jnp.float32) + b_down.astype(
        jnp.float32
    )
    block_out = (middle + live_rows * branch_two).astype(jnp.bfloat16)
    back_gain_one, back_merged, back_proj, back_gain_two, back_up, back_down = (
        lax.all_gather(ln1_gain, ("wide", "narrow"), axis=0, tiled=True),
        lax.all_gather(qkv_weight, ("wide", "narrow"), axis=0, tiled=True),
        lax.all_gather(out_weight, ("wide", "narrow"), axis=0, tiled=True),
        lax.all_gather(ln2_gain, ("wide", "narrow"), axis=0, tiled=True),
        lax.all_gather(up_weight, ("wide", "narrow"), axis=0, tiled=True),
        lax.all_gather(down_weight, ("wide", "narrow"), axis=0, tiled=True),
    )
    upstream = cotangent.astype(jnp.float32)
    grad_two = (live_rows * upstream).astype(jnp.bfloat16)
    grad_b_down = jnp.sum(grad_two.astype(jnp.float32), axis=0)
    grad_w_down = jnp.einsum("tf,td->fd", activated, grad_two, preferred_element_type=jnp.float32)
    grad_act = jnp.einsum("td,fd->tf", grad_two, back_down, preferred_element_type=jnp.float32)
    grad_hidden = gelu_pull(grad_act)[0].astype(jnp.bfloat16)
    grad_b_up = jnp.sum(grad_hidden.astype(jnp.float32), axis=0)
    grad_w_up = jnp.einsum("td,tf->df", normed_two, grad_hidden, preferred_element_type=jnp.float32)
    grad_normed_two = jnp.einsum(
        "tf,df->td", grad_hidden, back_up, preferred_element_type=jnp.float32
    )
    _, norm_pull_two = jax.vjp(
        layer_norm, middle, back_gain_two.astype(jnp.float32), bias_two.astype(jnp.float32)
    )
    grad_middle_norm, grad_gain_two, grad_bias_two = norm_pull_two(grad_normed_two)
    grad_middle = upstream + grad_middle_norm
    grad_one = (live_rows * grad_middle).astype(jnp.bfloat16)
    grad_b_proj = jnp.sum(grad_one.astype(jnp.float32), axis=0)
    grad_w_proj = jnp.einsum("te,td->ed", attended, grad_one, preferred_element_type=jnp.float32)
    grad_att = jnp.einsum(
        "td,ed->te", grad_one, back_proj, preferred_element_type=jnp.float32
    ).astype(jnp.bfloat16)
    grad_att_heads = split_heads(grad_att, H)

    def head_backward(members):
        return attend_backward(
            members[0],
            members[1],
            members[2],
            segment,
            members[3],
            members[4],
            block_rows,
            score_scale,
        )

    grad_q, grad_k, grad_v = lax.map(
        head_backward, (q_heads, k_heads, v_heads, grad_att_heads, lse_heads)
    )
    grad_merged = jnp.concatenate(
        [join_heads(grad_q), join_heads(grad_k), join_heads(grad_v)], 1
    ).astype(jnp.bfloat16)
    column_sums = jnp.sum(grad_merged.astype(jnp.float32), axis=0)
    grad_merged_bias = jnp.concatenate([column_sums[:model_width], column_sums[2 * model_width :]])
    grad_w_merged = jnp.einsum(
        "te,tf->ef", normed_one, grad_merged, preferred_element_type=jnp.float32
    )
    grad_normed_one = jnp.einsum(
        "tf,ef->te", grad_merged, back_merged, preferred_element_type=jnp.float32
    )
    _, norm_pull_one = jax.vjp(
        layer_norm, inputs, back_gain_one.astype(jnp.float32), bias_one.astype(jnp.float32)
    )
    grad_input_norm, grad_gain_one, grad_bias_one = norm_pull_one(grad_normed_one)
    tokens_grad = grad_middle + grad_input_norm
    shares = (
        lax.psum_scatter(grad_gain_one, ("wide", "narrow"), scatter_dimension=0, tiled=True),
        lax.psum_scatter(grad_bias_one, ("wide", "narrow"), scatter_dimension=0, tiled=True),
        lax.psum_scatter(grad_w_merged, ("wide", "narrow"), scatter_dimension=0, tiled=True),
        lax.psum_scatter(grad_merged_bias, ("wide", "narrow"), scatter_dimension=0, tiled=True),
        lax.psum_scatter(grad_w_proj, ("wide", "narrow"), scatter_dimension=0, tiled=True),
        lax.psum_scatter(grad_b_proj, ("wide", "narrow"), scatter_dimension=0, tiled=True),
        lax.psum_scatter(grad_gain_two, ("wide", "narrow"), scatter_dimension=0, tiled=True),
        lax.psum_scatter(grad_bias_two, ("wide", "narrow"), scatter_dimension=0, tiled=True),
        lax.psum_scatter(grad_w_up, ("wide", "narrow"), scatter_dimension=0, tiled=True),
        lax.psum_scatter(grad_b_up, ("wide", "narrow"), scatter_dimension=0, tiled=True),
        lax.psum_scatter(grad_w_down, ("wide", "narrow"), scatter_dimension=0, tiled=True),
        lax.psum_scatter(grad_b_down, ("wide", "narrow"), scatter_dimension=0, tiled=True),
    )
    return (
        block_out,
        tokens_grad,
        shares[0],
        shares[1],
        shares[2],
        shares[3],
        shares[4],
        shares[5],
        shares[6],
        shares[7],
        shares[8],
        shares[9],
        shares[10],
        shares[11],
    )


def nt_dot(left, right):
    return lax.dot_general(left, right, (((1,), (1,)), ((), ())), preferred_element_type=F32)


def nn_dot(left, right):
    return jnp.dot(left, right, preferred_element_type=F32)


def rows_of(step, size=CHUNK):
    return pl.ds(pl.multiple_of(step * size, size), size)


def norm_parts(values):
    centred = values - jnp.mean(values, axis=-1, keepdims=True)
    scale = lax.rsqrt(jnp.mean(centred * centred, axis=-1, keepdims=True) + 1e-06)
    return centred * scale, scale


def fold_rows(values):
    return jnp.sum(values.reshape(-1, 8, values.shape[-1]), axis=0)


def gelu_both(u):
    tail = 0.5 * (1.0 + lax.erf(u * 0.7071067811865476))
    return u * tail, tail + u * jnp.exp(-0.5 * u * u) * 0.3989422804014327


def spread_maps(width, columns):
    column = lax.broadcasted_iota(jnp.int32, (1, columns), 1).astype(F32)
    group = jnp.floor((column + 0.5) * (1.0 / width))
    place = column - group * width
    lane = lax.broadcasted_iota(jnp.int32, (128, columns), 0).astype(F32)
    picks = jnp.where(lane == place, 1.0, 0.0).astype(BF16)
    owners = columns // width
    owner = lax.broadcasted_iota(jnp.int32, (owners, 8, columns), 0).astype(F32)
    mine = owner == group.reshape(1, 1, columns)
    return picks, mine


def spread(pieces, width, columns):
    picks, mine = spread_maps(width, columns)
    wide_rows = nn_dot(pieces.reshape(-1, 128).astype(BF16), picks)
    return jnp.sum(jnp.where(mine, wide_rows.reshape(-1, 8, columns), 0.0), axis=0)


def gather_back(vectors, width):
    columns = vectors.shape[-1]
    picks, mine = spread_maps(width, columns)
    rest = jnp.where(mine, vectors[None], 0.0).reshape(-1, columns)
    total = None
    for _ in range(3):
        part = rest.astype(BF16)
        rest = rest - part.astype(F32)
        term = nt_dot(part, picks)
        total = term if total is None else total + term
    return total.reshape(-1, 8, 128)


def layer_kernel(
    clip_ref, tok_ref, cot_ref, v0, v1, v2, v3, v4, v5, v6, v7, wqkv_ref, wout_ref, wup_ref, wdown_ref,
    out_ref, tgrad_ref, gqkv_ref, gout_ref, gup_ref, gdown_ref, gsmall_ref,
    slabs, downs, smalls, gsmalls, weights, w_up,
    row_c, row_d, row_n, row_z, late_d, late_n, late_z, down_c, down_d, down_n, down_z, sm_c, sm_d, sm_n, sm_z,
    qkv, n1t, n1, att_t, middle, n2, n2t, g2, acc_out, acc_grad, act, grad_h, pre, grad_act,
    tok, cot, bias, lse, dq_t, vec24, vec48, vec96, merged_bias, group_sums, sums, up_sums,
    ag_send, ag_recv, rs_send, rs_recv, local,
):
    n_z, width = slabs.shape[1], slabs.shape[-1]
    count = tok.shape[0]
    pairs = width // 128
    chunks = count // CHUNK
    wide_at, y = lax.axis_index("wide"), lax.axis_index("narrow")
    core = lax.rem(wide_at, 2)
    x = lax.rem(lax.div(wide_at, 2), 2)
    z = lax.div(wide_at, 4)

    def device(z_at, x_at, c_at, y_at):
        return ((z_at * 2 + x_at) * 2 + c_at, y_at)

    def row_view(block):
        def view(at):
            return slabs.at[(block, *at)]
        return view

    def down_view(tile):
        def view(at):
            return downs.at[(tile, *at[1:])]
        return view

    def small_view(ref):
        def view(at):
            return ref.at[at]
        return view

    def half_of(ref, side):
        if ref.shape[-1] < 2 * 128:
            return ref
        cut = ref.shape[-1] // 2
        return ref.at[(*([ALL] * (len(ref.shape) - 1)), pl.ds(side * cut, cut))]

    to_x, to_y, to_c = device(z, 1 - x, core, y), device(z, x, core, 1 - y), device(z, x, 1 - core, y)
    z_places = (z + 1 - 2 * lax.rem(z, 2), lax.rem(z + 2, n_z), n_z - 1 - z)
    along_z = [device(at, x, core, y) for at in z_places]
    other_pair = pl.ds(2 * (1 - lax.div(z, 2)), 2)
    inner = lax.rem(z + 1, n_z) >= 2
    Z0, Z1, Z2, ZR, X0, Y0, X1, Y1, X2, Y2, DX, DY, C0 = range(13)

    def remote(src, dst, sems, row, sem, to, recv_sem=None):
        send, recv = sems
        return pltpu.make_async_remote_copy(
            src_ref=src, dst_ref=dst, send_sem=send.at[row, sem], recv_sem=recv.at[row, sem if recv_sem is None else recv_sem],
            device_id=to, device_id_type=MESH,
        )

    def do_all(copies, what):
        for copy in copies:
            getattr(copy, what)()

    one, plane = (x, core, y), (ALL, core, ALL)

    def ag_copies(unit, phase):
        view, row, phases, along = unit
        sems = (ag_send, ag_recv)
        held = z if along is plane else ALL

        def both(at, sem):
            mine = view((at, x, core, y))
            return [remote(mine, mine, sems, row, sem, to_x), remote(mine, mine, sems, row, sem + 1, to_y)]

        def own_to(*which):
            own = view((z, *along))
            return [remote(own, own, sems, row, k, along_z[k]) for k in which]

        if phase == "z":
            return own_to(Z0, Z1)
        if phase == "zd":
            return own_to(Z0, Z1, Z2)
        if phase in ("z near", "z far", "z last"):
            return own_to(("z near", "z far", "z last").index(phase))
        if phase == "relay":
            passed = view((z_places[1], *along))
            return [remote(passed, passed, sems, row, ZR, along_z[0], Z2)]
        if phase == "own":
            return both(z, X1)
        if phase == "pair":
            return both(z_places[0], X2)
        if phase == "rest":
            return both(other_pair, X0)
        if phase == "near":
            return both(held, X0)
        if phase == "across":
            from_x, from_y = view((held, 1 - x, core, y)), view((held, x, core, 1 - y))
            first = half_of(from_x, 0)
            copies = [remote(first, first, sems, row, DY, to_y)]
            if from_x.shape[-1] >= 2 * 128:
                second = half_of(from_y, 1)
                copies.append(remote(second, second, sems, row, DX, to_x))
            return copies
        whole_plane = view((ALL, ALL, core, ALL))
        return [remote(whole_plane, whole_plane, sems, row, C0, to_c)]

    def ag_wait(unit, *phases):
        for phase in phases:
            do_all(ag_copies(unit, phase), "wait_recv")

    def ag_stage(unit, stage):
        phases = unit[2]
        phase = phases[stage] if stage < len(phases) else None
        if phase == "relay":
            @pl.when(inner)
            def _():
                ag_wait(unit, "z far")
                do_all(ag_copies(unit, "relay"), "start")
            return
        if phase == "pair":
            ag_wait(unit, "z near")
        elif phase == "rest":
            ag_wait(unit, "z far", "z last")
        elif phase == "across" and "own" in phases:
            ag_wait(unit, "own", "pair", "rest")
        elif stage > 0 and phases[stage - 1] == "relay":
            @pl.when(jnp.logical_not(inner))
            def _():
                ag_wait(unit, "z far")
            ag_wait(unit, "z near", "z last")
        elif stage > 0 and phases[stage - 1] != "own":
            ag_wait(unit, phases[stage - 1])
        if phase:
            do_all(ag_copies(unit, phase), "start")
            if phase == "z":
                @pl.when(inner)
                def _():
                    do_all(ag_copies(unit, "z last"), "start")
        else:
            for sent in phases:
                if sent != "relay":
                    do_all(ag_copies(unit, sent), "wait_send")
            if "relay" in phases:
                @pl.when(inner)
                def _():
                    do_all(ag_copies(unit, "z last") + ag_copies(unit, "relay"), "wait_send")

    ORDERS = {
        "plain": ("z", "relay", "near", "across", "core"), "direct": ("zd", "near", "across", "core"),
        "boot": ("own", "zd", "pair", "rest", "across", "core"),
        "late": ("near", "across", "z", "relay", "core"), "late direct": ("near", "across", "zd", "core"),
    }

    def gather_unit(block, kind):
        return (row_view(block), 1 + block, ORDERS[kind], plane if kind[:4] == "late" else one)

    units = {"aS": (small_view(smalls), 0, ORDERS["direct"], one)}
    units["adp"] = (lambda at: downs.at[at], 5 + 2 * n_z, ("z", "relay") if KINDS.get("adp", "plain") == "plain" else ("zd",), one)
    for block in range(4):
        units[f"ab{block}"] = gather_unit(block, KINDS.get(f"ab{block}", "plain"))
    for tile in range(n_z):
        units[f"au{tile}"] = gather_unit(4 + tile, KINDS.get(f"au{tile}", "plain"))
        units[f"ad{tile}"] = (down_view(tile), 5 + n_z + tile, ("near", "across", "core"), one)

    def rs_copies(unit, phase):
        view, row, phases, landing, along = unit
        sems = (rs_send, rs_recv)
        held = z if along is plane else ALL
        if phase == "core":
            return [remote(view((ALL, ALL, 1 - core, ALL)), landing["core"], sems, row, C0, to_c)]
        if phase == "across":
            away = view((held, 1 - x, core, 1 - y))
            copies = [remote(half_of(away, 0), landing["dx"], sems, row, DX, to_x)]
            if away.shape[-1] >= 2 * 128:
                copies.append(remote(half_of(away, 1), landing["dy"], sems, row, DY, to_y))
            return copies
        if phase == "near":
            return [
                remote(view((held, 1 - x, core, y)), landing["x"], sems, row, X0, to_x),
                remote(view((held, x, core, 1 - y)), landing["y"], sems, row, Y0, to_y),
            ]
        if phase == "z outer":
            return [remote(view((z_places[2], *along)), landing["z"].at[ZR], sems, row, ZR, along_z[0])]
        which = {"z": (Z0,), "z far": (Z1,), "z last": (Z2,), "zd": (Z0, Z1, Z2)}[phase]
        return [remote(view((z_places[k], *along)), landing["z"].at[k], sems, row, k, along_z[k]) for k in which]

    def add_into(target, *sources):
        total = target[...].astype(F32)
        for source in sources:
            total = total + source[...].astype(F32)
        target[...] = total.astype(target.dtype)

    def add_all(target, *sources):
        free = len(target.shape) - 2
        if free == 0:
            add_into(target, *sources)
            return
        places = [()]
        for extent in target.shape[1:free]:
            places = [place + (k,) for place in places for k in range(extent)]

        def step(i, carry):
            for place in places:
                add_into(target.at[(i, *place)], *[source.at[(i, *place)] for source in sources])
            return carry

        lax.fori_loop(0, target.shape[0], step, 0)

    def rs_stage(unit, stage):
        view, _, phases, landing, along = unit
        held = z if along is plane else ALL
        before = phases[stage - 1] if stage > 0 else None
        phase = phases[stage] if stage < len(phases) else None
        if phase == "z far":
            @pl.when(inner)
            def _():
                do_all(rs_copies(unit, "z outer"), "wait_recv")
                add_all(view((z_places[1], *along)), landing["z"].at[ZR])
        elif before == "z far":
            rs_wait(unit, "z", "z far")
            add_all(view((z, *along)), landing["z"].at[Z0], landing["z"].at[Z1])

            @pl.when(inner)
            def _():
                rs_wait(unit, "z last")
                add_all(view((z, *along)), landing["z"].at[Z2])
        elif before:
            rs_wait(unit, before)
        if before == "core":
            add_all(view((ALL, ALL, core, ALL)), landing["core"])
        elif before == "across":
            on_y = view((held, x, core, 1 - y))
            add_all(half_of(on_y, 0), landing["dx"])
            if on_y.shape[-1] >= 2 * 128:
                add_all(half_of(view((held, 1 - x, core, y)), 1), landing["dy"])
        elif before == "near":
            add_all(view((held, x, core, y)), landing["x"], landing["y"])
        elif before == "zd":
            add_all(view((z, *along)), *[landing["z"].at[k] for k in (Z0, Z1, Z2)])
        if phase:
            do_all(rs_copies(unit, phase), "start")
        if phase == "z":
            @pl.when(inner)
            def _():
                do_all(rs_copies(unit, "z last"), "start")

            @pl.when(jnp.logical_not(inner))
            def _():
                do_all(rs_copies(unit, "z outer"), "start")

    def rs_wait(unit, *phases):
        for phase in phases:
            do_all(rs_copies(unit, phase), "wait_recv")

    def rs_end(unit, *results):
        view, _, phases, landing, along = unit
        last = phases[-1]
        if last == "near":
            sources = [landing["x"], landing["y"]]
        else:
            sources = [landing["z"].at[k] for k in ((Z0, Z1) if last == "z far" else (Z0, Z1, Z2))]
        rs_wait(unit, *(("z", "z far") if last == "z far" else (last,)))
        total = view((z, x, core, y))[...].astype(F32)
        for part in sources:
            total = total + part[...].astype(F32)
        size = total.shape[-1] // len(results)
        for k, result in enumerate(results):
            result[...] = total[:, k * size : (k + 1) * size]
        if last == "z far":
            @pl.when(inner)
            def _():
                rs_wait(unit, "z last")
                for k, result in enumerate(results):
                    result[...] += landing["z"][Z2, :, k * size : (k + 1) * size].astype(F32)

    def rs_sent(unit):
        for phase in unit[2]:
            do_all(rs_copies(unit, phase), "wait_send")
        if "z far" in unit[2]:
            @pl.when(inner)
            def _():
                do_all(rs_copies(unit, "z last"), "wait_send")

            @pl.when(jnp.logical_not(inner))
            def _():
                do_all(rs_copies(unit, "z outer"), "wait_send")

    BACK = {
        "plain": ("core", "across", "near", "z", "z far"), "direct": ("core", "across", "near", "zd"),
        "late": ("core", "z", "z far", "across", "near"), "late direct": ("core", "zd", "across", "near"),
    }

    def row_unit(block, row, name):
        if name in LATE_SUMS:
            late = LATE_SUMS.index(name)
            landing = {"core": row_c.at[block], "dx": late_d.at[late, 0], "dy": late_d.at[late, 1], "x": late_n.at[late, 0], "y": late_n.at[late, 1], "z": late_z.at[late]}
            return (row_view(block), row, BACK[KINDS[name]], landing, plane)
        at = block - sum(earlier in LATE_SUMS for earlier in ROW_SUMS[:block])
        landing = {"core": row_c.at[block], "dx": row_d.at[at, 0], "dy": row_d.at[at, 1], "x": row_n.at[at, 0], "y": row_n.at[at, 1], "z": row_z.at[at]}
        return (row_view(block), row, BACK[KINDS.get(name, "plain")], landing, one)

    def down_unit(tile, row):
        landing = {"core": down_c.at[tile], "dx": down_d.at[tile, 0], "dy": down_d.at[tile, 1], "x": down_n.at[tile, 0], "y": down_n.at[tile, 1]}
        return (down_view(tile), row, BACK["plain"][:3], landing, one)

    def block_columns(block):
        return pl.ds(block * width, width)

    third = width // 3
    results = {"rdl": [gdown_ref], "ro": [gout_ref], "rS": [gsmall_ref]}
    for t in range(n_z):
        units[f"ru{t}"] = row_unit(4 + t, t, f"ru{t}")
        units[f"rd{t}"] = down_unit(t, n_z + t)
        results[f"ru{t}"] = [gup_ref.at[:, block_columns(t)]]
    for g in range(3):
        units[f"rh{g}"] = row_unit(g, 2 * n_z + g, f"rh{g}")
        results[f"rh{g}"] = [gqkv_ref.at[:, pl.ds(j * width + g * third, third)] for j in range(3)]
    units["ro"] = row_unit(3, 2 * n_z + 3, "ro")
    small_landing = {"core": sm_c, "dx": sm_d, "x": sm_n.at[0], "y": sm_n.at[1], "z": sm_z}
    units["rS"] = (small_view(gsmalls), 2 * n_z + 4, BACK["direct"], small_landing, one)
    units["rdl"] = (lambda at: downs.at[at], 2 * n_z + 5, ("z", "z far") if KINDS.get("rdl", "plain") == "plain" else ("zd",), {"z": down_z}, one)

    def point(name):
        for unit_name, stage in TABLE.get(name, ()):
            unit = units[unit_name]
            if unit_name[0] == "a":
                ag_stage(unit, stage)
            elif unit_name in results and stage == len(unit[2]):
                rs_end(unit, *results[unit_name])
            else:
                rs_stage(unit, stage)

    def points_at(index, names):
        for k, name in enumerate(names):
            if TABLE.get(name):
                pl.when(index == k)(functools.partial(point, name))

    barrier = pltpu.get_barrier_semaphore()
    partners = [*along_z, to_x, to_y, to_c]
    for to in partners:
        pl.semaphore_signal(barrier, inc=1, device_id=to, device_id_type=MESH)
    shards = []
    for g in range(3):
        for j in range(3):
            shards.append((wqkv_ref.at[:, pl.ds(j * width + g * third, third)], slabs.at[g, z, x, core, y, :, pl.ds(j * third, third)]))
    shards.append((wout_ref, slabs.at[3, z, x, core, y]))
    for tile in range(n_z):
        shards.append((wup_ref.at[:, block_columns(tile)], slabs.at[4 + tile, z, x, core, y]))
    shards.append((wdown_ref, downs.at[z, x, core, y]))
    shard_copies = [pltpu.make_async_copy(src, dst, local.at[k]) for k, (src, dst) in enumerate(shards)]
    row_copies = [pltpu.make_async_copy(tok_ref, tok, local.at[len(shards)]), pltpu.make_async_copy(cot_ref, cot, local.at[len(shards) + 1])]
    do_all(shard_copies + row_copies, "start")
    smalls[z, x, core, y] = jnp.zeros((8, 128), F32)
    for k, vector in enumerate((v0, v1, v2, v3, v4, v5, v6, v7)):
        smalls[z, x, core, y, k, 0 : vector.shape[0]] = vector[...].astype(F32)
    do_all(shard_copies, "wait")
    pl.semaphore_wait(barrier, len(partners))
    point("mask")
    do_all(row_copies, "wait")

    ends = []
    for k in range(clip_ref.shape[1]):
        ends.append(clip_ref[0, k] + (ends[-1] if ends else 0))

    def segment_of(position):
        total = jnp.zeros(position.shape, jnp.int32)
        for end in ends:
            total = total + jnp.where(position >= end, 1, 0)
        return total

    across = segment_of(lax.broadcasted_iota(jnp.int32, (CHUNK, count), 1))

    def live_of(step):
        position = lax.broadcasted_iota(jnp.int32, (CHUNK, 1), 0) + step * CHUNK
        return jnp.where(position < ends[-1], 1.0, 0.0)

    ones = jnp.ones((8, count), BF16)

    def column_sums(values):
        return nn_dot(ones, values)

    def mask_step(i, carry):
        down = segment_of(lax.broadcasted_iota(jnp.int32, (CHUNK, count), 0) + i * CHUNK)
        bias[rows_of(i), :] = jnp.where(down == across, 0.0, -1e30)
        g2[rows_of(i), :] = (live_of(i) * cot[rows_of(i), :].astype(F32)).astype(BF16)
        return carry

    lax.fori_loop(0, chunks, mask_step, 0)
    sums[...] = jnp.zeros_like(sums)
    up_sums[...] = jnp.zeros_like(up_sums)
    sums[0, 7:8, :] = column_sums(g2[...])[0:1]

    point("vec")
    vec24[...] = spread(smalls[...], 24, width)
    for k in range(2):
        vec48[k] = spread(smalls[k * n_z // 2 : (k + 1) * n_z // 2], 48, width)
    for k in range(n_z):
        vec96[k] = spread(smalls[k], 96, width)
    for g in range(3):
        span = slice(g * third, (g + 1) * third)
        merged_bias[g, 0:1, :] = jnp.concatenate(
            [vec48[0, 2:3, span], jnp.zeros((1, width - 2 * third), F32), vec48[1, 2:3, span]], axis=1
        )

    def norm_one(i, carry):
        normed, _ = norm_parts(tok[rows_of(i), :].astype(F32))
        n1[rows_of(i), :] = (normed * vec24[0:1, :] + vec24[1:2, :]).astype(BF16)
        return carry

    lax.fori_loop(0, chunks, norm_one, 0)

    def turn(source, target):
        def step(i, carry):
            at = rows_of(i, 128)
            target[at, :] = source[:, at].T
            return carry

        lax.fori_loop(0, pairs, step, 0)

    point("turn")
    turn(n1, n1t)

    def assemble(block, target):
        def step(z_at, carry):
            for x_at in range(2):
                for c_at in range(2):
                    two = slabs[block, z_at, x_at, c_at].astype(F32)
                    size = 2 * two.shape[1]
                    first = pl.multiple_of(((z_at * 2 + x_at) * 2 + c_at) * size, 16)
                    target[pl.ds(first, size), :] = two.reshape(size, width).astype(BF16)
            return carry

        lax.fori_loop(0, n_z, step, 0)

    lane = lax.broadcasted_iota(jnp.int32, (count, 128), 1)

    def one_head(values, head):
        keep = lane < 64 if head == 0 else lane >= 64
        return jnp.where(keep, values, jnp.zeros_like(values))

    q_block = 512
    parts = count // q_block
    per_group = pairs // 3

    def places(p):
        first = lax.rem(p, per_group) * 128
        return lax.div(p, per_group), [pl.ds(pl.multiple_of(first + j * third, 128), 128) for j in range(3)]

    def attend(p, carry):
        group, (at_q, at_k, at_v) = places(p)
        points_at(p, [f"q{k // per_group}" if k % per_group == 0 else "" for k in range(pairs)])

        @pl.when(lax.rem(p, per_group) == 0)
        def _():
            assemble(group, weights.at[group])
            qkv[group] = (nn_dot(n1[...], weights[group]) + merged_bias[group, 0:1, :]).astype(BF16)

        points_at(p, [f"t{k}" for k in range(pairs)])
        keys = qkv[group, :, at_k]
        queries = qkv[group, :, at_q] * 0.125
        values_t = qkv[group, :, at_v].T
        for head in range(2):
            mine = one_head(queries, head)
            for part in range(parts):
                span = slice(part * q_block, (part + 1) * q_block)
                scores = nt_dot(keys, mine[span]) + bias[:, span]
                highest = jnp.max(scores, axis=0, keepdims=True)
                raised = jnp.exp(scores - highest)
                total = jnp.sum(raised, axis=0, keepdims=True)
                chances = (raised * (1.0 / total)).astype(BF16)
                lse[p, head : head + 1, span] = highest + jnp.log(total)
                result = nn_dot(values_t[64 * head : 64 * head + 64], chances)
                att_t[pl.ds(pl.multiple_of(p * 128 + 64 * head, 64), 64), span] = result.astype(BF16)
        return carry

    lax.fori_loop(0, pairs, attend, 0)
    point("tb")
    att = n1

    def turn_back(p, carry):
        at = rows_of(p, 128)
        att[:, at] = att_t[at, :].T
        return carry

    lax.fori_loop(0, pairs, turn_back, 0)
    point("out")
    assemble(3, weights.at[3])
    pre[...] = nn_dot(att[...], weights[3])

    def norm_two(i, carry):
        at = rows_of(i)
        branch = pre[at, :] + vec24[3:4, :]
        mid = tok[at, :].astype(F32) + live_of(i) * branch
        middle[at, :] = mid
        normed, _ = norm_parts(mid)
        n2[at, :] = (normed * vec24[4:5, :] + vec24[5:6, :]).astype(BF16)
        return carry

    point("n2a")
    lax.fori_loop(0, chunks // 2, norm_two, 0)
    point("n2b")
    lax.fori_loop(chunks // 2, chunks, norm_two, 0)
    point("n2t")
    turn(n2, n2t)
    acc_out[...] = jnp.zeros_like(acc_out)
    acc_grad[...] = jnp.zeros_like(acc_grad)

    def store_rows(block, lhs_t, rhs):
        size = slabs.shape[-2]
        for first in range(0, width, 192):
            total = nn_dot(lhs_t[first : first + 192, :], rhs)
            for k in range(192 // size // 2):
                at = first // size + 2 * k
                two = total[2 * k * size : 2 * (k + 1) * size].reshape(2, size, width).astype(BF16)
                slabs[block, at // 8, at // 4 % 2, at // 2 % 2] = two

    def feed(t, carry):
        def step_point(name):
            points_at(t, [f"{name}{k}" for k in range(n_z)])

        step_point("fa")
        assemble(4 + t, w_up)
        up_bias = vec96[t, 6:7, :]
        half = count // 2

        def into_hidden(rows):
            pre[rows] = nn_dot(n2[rows], w_up[...])

        def into_grads(rows):
            grad_act[rows] = nt_dot(g2[rows], downs[t].reshape(width, width))

        def gelu_rows(first):
            for at in range(first, first + half, 32):
                rows = slice(at, at + 32)
                active, slope = gelu_both(pre[rows] + up_bias)
                act[rows] = active.astype(BF16)
                grad_h[rows] = (grad_act[rows] * slope).astype(BF16)

        def out_of(rows):
            acc_out[rows] += nn_dot(act[rows], downs[t].reshape(width, width))
            acc_grad[rows] += nt_dot(grad_h[rows], w_up[...])

        upper, lower = slice(0, half), slice(half, count)
        step_point("fb")
        into_hidden(upper)
        step_point("fc")
        into_grads(upper)
        step_point("fd")
        into_hidden(lower)
        into_grads(lower)
        gelu_rows(0)
        step_point("fe")
        out_of(upper)
        gelu_rows(half)
        step_point("ff")
        out_of(lower)
        step_point("fg")
        up_sums[t, 6:7, :] = column_sums(grad_h[...])[0:1]
        step_point("fh")
        store_rows(4 + t, n2t, grad_h[...])
        step_point("fi")
        for j in range(pairs):
            span = slice(j * 128, (j + 1) * 128)
            piece = nn_dot(act[:, span].T, g2[...]).astype(BF16)
            size = downs.shape[-2]
            at = j * 128
            while at < (j + 1) * 128:
                owner, inside = at // size, at % size
                length = min(size - inside, (j + 1) * 128 - at)
                downs[t, owner // 4, owner // 2 % 2, owner % 2, inside : inside + length, :] = piece[at - j * 128 : at - j * 128 + length]
                at += length
        return carry

    lax.fori_loop(0, n_z, feed, 0)

    def norm_two_back(i, carry):
        gain_sum, bias_sum = carry
        at = rows_of(i)
        alive = live_of(i)
        mid = middle[at, :]
        block_out[at, :] = (mid + alive * (acc_out[at, :] + vec24[7:8, :])).astype(BF16)
        normed, scale = norm_parts(mid)
        e = acc_grad[at, :]
        scaled = e * vec24[4:5, :]
        inner_part = scaled - jnp.mean(scaled, axis=-1, keepdims=True) - normed * jnp.mean(scaled * normed, axis=-1, keepdims=True)
        grad_mid = cot[at, :].astype(F32) + inner_part * scale
        acc_grad[at, :] = grad_mid
        g2[at, :] = (alive * grad_mid).astype(BF16)
        return (gain_sum + fold_rows(e * normed), bias_sum + fold_rows(e))

    zero = jnp.zeros((8, width), F32)
    block_out = act
    point("ba")
    carry = lax.fori_loop(0, chunks // 2, norm_two_back, (zero, zero))
    point("bb")
    gain_sum, bias_sum = lax.fori_loop(chunks // 2, chunks, norm_two_back, carry)
    sums[0, 4:5, :] = jnp.sum(gain_sum, axis=0, keepdims=True)
    sums[0, 5:6, :] = jnp.sum(bias_sum, axis=0, keepdims=True)
    sums[0, 3:4, :] = column_sums(g2[...])[0:1]
    out_copy = pltpu.make_async_copy(block_out, out_ref, local.at[0])
    out_copy.start()

    point("og")
    store_rows(3, att_t, g2[...])
    point("ga")
    grad_att = n2
    grad_att[...] = nt_dot(g2[...], weights[3]).astype(BF16)

    def attend_back(p, carry):
        group, (at_q, at_k, at_v) = places(p)
        points_at(p, [f"a{k}" for k in range(pairs)])
        keys = qkv[group, :, at_k]
        values = qkv[group, :, at_v]
        queries = qkv[group, :, at_q] * 0.125
        grads = grad_att[:, rows_of(p, 128)]
        keys_t = keys.T
        grad_keys = jnp.zeros((count, 128), F32)
        grad_values = jnp.zeros((count, 128), F32)
        for head in range(2):
            my_queries, my_grads = one_head(queries, head), one_head(grads, head)
            for part in range(parts):
                span = slice(part * q_block, (part + 1) * q_block)
                scores = nt_dot(keys, my_queries[span]) + bias[:, span]
                chances = jnp.exp(scores - lse[p, head : head + 1, span])
                slopes = nt_dot(values, my_grads[span])
                level = jnp.sum(chances * slopes, axis=0, keepdims=True)
                grad_scores = (chances * (slopes - level)).astype(BF16)
                grad_values += nn_dot(chances.astype(BF16), my_grads[span])
                grad_keys += nn_dot(grad_scores, my_queries[span])
                dq_t[64 * head : 64 * head + 64, span] = nn_dot(keys_t[64 * head : 64 * head + 64], grad_scores) * 0.125
        qkv[group, :, at_q] = dq_t[...].T.astype(BF16)
        qkv[group, :, at_k] = grad_keys.astype(BF16)
        qkv[group, :, at_v] = grad_values.astype(BF16)
        points_at(p, [f"H{k // per_group}" if k % per_group == per_group - 1 else "" for k in range(pairs)])

        @pl.when(lax.rem(p, per_group) == per_group - 1)
        def _():
            store_rows(group, n1t, qkv[group])
            group_sums[group] = column_sums(qkv[group])

        return carry

    lax.fori_loop(0, pairs, attend_back, 0)

    point("g2")
    pre[...] = nt_dot(qkv[2], weights[2])
    point("g1")
    pre[...] += nt_dot(qkv[1], weights[1])
    point("g0")
    pre[...] += nt_dot(qkv[0], weights[0])

    def norm_one_back(i, carry):
        gain_sum, bias_sum = carry
        at = rows_of(i)
        normed, scale = norm_parts(tok[at, :].astype(F32))
        e = pre[at, :]
        scaled = e * vec24[0:1, :]
        inner_part = scaled - jnp.mean(scaled, axis=-1, keepdims=True) - normed * jnp.mean(scaled * normed, axis=-1, keepdims=True)
        acc_grad[at, :] = acc_grad[at, :] + inner_part * scale
        return (gain_sum + fold_rows(e * normed), bias_sum + fold_rows(e))

    point("na")
    carry = lax.fori_loop(0, chunks // 2, norm_one_back, (zero, zero))
    point("nb")
    gain_sum, bias_sum = lax.fori_loop(chunks // 2, chunks, norm_one_back, carry)
    tgrad_copy = pltpu.make_async_copy(acc_grad, tgrad_ref, local.at[1])
    tgrad_copy.start()
    sums[0, 0:1, :] = jnp.sum(gain_sum, axis=0, keepdims=True)
    sums[0, 1:2, :] = jnp.sum(bias_sum, axis=0, keepdims=True)
    for g in range(3):
        span = slice(g * third, (g + 1) * third)
        sums[1, 2:3, span] = group_sums[g, 0:1, :third]
        sums[2, 2:3, span] = group_sums[g, 0:1, 2 * third :]
    point("gb")
    gsmalls[...] = gather_back(sums[0], 24).reshape(gsmalls.shape)
    for k in range(2):
        part = gather_back(sums[1 + k], 48)
        span = slice(k * n_z // 2, (k + 1) * n_z // 2)
        gsmalls[span] = gsmalls[span] + part.reshape(n_z // 2, 2, 2, 2, 8, 128)
    for k in range(n_z):
        gsmalls[k] = gsmalls[k] + gather_back(up_sums[k], 96).reshape(2, 2, 2, 8, 128)

    point("end")
    for name, unit in units.items():
        if name[0] == "r":
            rs_sent(unit)
    out_copy.wait()
    tgrad_copy.wait()


def by_kernel(
    n_z, tokens, cotangent, clip_lengths, ln1_gain, ln1_bias, qkv_weight, qv_bias, out_weight, out_bias,
    ln2_gain, ln2_bias, up_weight, up_bias, down_weight, down_bias,
):
    count, width = tokens.shape
    size, deep = qkv_weight.shape[0], down_weight.shape[0]
    blocks = 4 + n_z
    vectors = (ln1_gain, ln1_bias, qv_bias, out_bias, ln2_gain, ln2_bias, up_bias, down_bias)
    vmem, dma = pltpu.VMEM, pltpu.SemaphoreType.DMA
    held = [
        vmem((blocks, n_z, 2, 2, 2, size, width), BF16),
        vmem((n_z, 2, 2, 2, deep, width), BF16),
        vmem((n_z, 2, 2, 2, 8, 128), F32),
        vmem((n_z, 2, 2, 2, 8, 128), F32),
        vmem((4, width, width), BF16),
        vmem((width, width), BF16),
        vmem((blocks, n_z, 2, 2, size, width), BF16),
        vmem((blocks - len(LATE_SUMS), 2, n_z, size, width // 2), BF16),
        vmem((blocks - len(LATE_SUMS), 2, n_z, size, width), BF16),
        vmem((blocks - len(LATE_SUMS), n_z, size, width), BF16),
        vmem((max(len(LATE_SUMS), 1), 2, size, width // 2), BF16),
        vmem((max(len(LATE_SUMS), 1), 2, size, width), BF16),
        vmem((max(len(LATE_SUMS), 1), n_z, 2, 2, size, width), BF16),
        vmem((n_z, 2, 2, deep, width), BF16),
        vmem((n_z, 2, deep, width // 2), BF16),
        vmem((n_z, 2, deep, width), BF16),
        vmem((n_z, deep, width), BF16),
        vmem((n_z, 2, 2, 8, 128), F32),
        vmem((n_z, 8, 128), F32),
        vmem((2, n_z, 8, 128), F32),
        vmem((n_z - 1, 8, 128), F32),
        vmem((3, count, width), BF16),
        vmem((width, count), BF16),
        vmem((count, width), BF16),
        vmem((width, count), BF16),
        vmem((count, width), F32),
        vmem((count, width), BF16),
        vmem((width, count), BF16),
        vmem((count, width), BF16),
        vmem((count, width), F32),
        vmem((count, width), F32),
        vmem((count, width), BF16),
        vmem((count, width), BF16),
        vmem((count, width), F32),
        vmem((count, width), F32),
        vmem((count, width), BF16),
        vmem((count, width), BF16),
        vmem((count, count), F32),
        vmem((width // 128, 2, count), F32),
        vmem((128, count), F32),
        vmem((8, width), F32),
        vmem((2, 8, width), F32),
        vmem((n_z, 8, width), F32),
        vmem((3, 8, width), F32),
        vmem((3, 8, width), F32),
        vmem((3, 8, width), F32),
        vmem((n_z, 8, width), F32),
        dma((6 + 2 * n_z, 13)),
        dma((6 + 2 * n_z, 13)),
        dma((6 + 2 * n_z, 13)),
        dma((6 + 2 * n_z, 13)),
        dma((13 + n_z,)),
    ]
    anywhere, whole = pl.BlockSpec(memory_space=pl.ANY), pl.BlockSpec(memory_space=pltpu.VMEM)
    shape = jax.ShapeDtypeStruct
    out, grad, g_qkv, g_out, g_up, g_down, g_small = pl.pallas_call(
        layer_kernel,
        out_shape=(
            shape((count, width), BF16),
            shape((count, width), F32),
            shape(qkv_weight.shape, F32),
            shape(out_weight.shape, F32),
            shape(up_weight.shape, F32),
            shape(down_weight.shape, F32),
            shape((8, 128), F32),
        ),
        in_specs=[pl.BlockSpec(memory_space=pltpu.SMEM)] + [anywhere] * 2 + [whole] * 8 + [anywhere] * 4,
        out_specs=(anywhere, anywhere, whole, whole, whole, whole, whole),
        scratch_shapes=held,
        compiler_params=pltpu.CompilerParams(collective_id=0, has_side_effects=True, vmem_limit_bytes=VMEM_BYTES),
    )(clip_lengths, tokens, cotangent, *vectors, qkv_weight, out_weight, up_weight, down_weight)
    large = (out, grad, g_qkv, g_out, g_up, g_down)
    done = pl.pallas_call(
        hand_over,
        out_shape=tuple(shape(a.shape, a.dtype) for a in large) + tuple(shape(v.shape, F32) for v in vectors),
        in_specs=[whole] + [anywhere] * len(large),
        out_specs=(anywhere,) * len(large) + (whole,) * len(vectors),
        scratch_shapes=[vmem(a.shape, a.dtype) for a in large] + [dma((2, len(large)))],
    )(g_small, *large)
    out, grad, g_qkv, g_out, g_up, g_down = done[:6]
    parts = done[6:]
    return (out, grad, parts[0], parts[1], g_qkv, parts[2], g_out, parts[3], parts[4], parts[5], g_up, parts[6], g_down, parts[7])


def hand_over(small_ref, *refs):
    sources, targets, vectors, held, sems = refs[:6], refs[6:12], refs[12:20], refs[20:26], refs[26]
    inward = [pltpu.make_async_copy(src, dst, sems.at[0, k]) for k, (src, dst) in enumerate(zip(sources, held))]
    outward = [pltpu.make_async_copy(src, dst, sems.at[1, k]) for k, (src, dst) in enumerate(zip(held, targets))]
    for copy in inward:
        copy.start()
    for k, vector in enumerate(vectors):
        vector[...] = small_ref[k, 0 : vector.shape[0]]
    for arrived, onward in zip(inward, outward):
        arrived.wait()
        onward.start()
    for copy in outward:
        copy.wait()


KINDS = {
    "ab0": "boot",
    "ab1": "boot",
    "ab2": "boot",
    "ab3": "boot",
    "au0": "late",
    "au1": "boot",
    "au2": "boot",
    "au3": "late",
    "ro": "direct",
    "ru0": "late",
    "ru1": "late",
    "ru3": "late",
}
LATE_SUMS = ("ru0", "ru1", "ru3")
TABLE = {
    "mask": (("aS", 0), ("ab0", 0), ("ab0", 1), ("au1", 0), ("ab3", 0),),
    "vec": (("au1", 1), ("ab2", 0), ("ab1", 0), ("au2", 0), ("aS", 1), ("ab0", 2), ("ab3", 1), ("au3", 0), ("ab0", 3), ("aS", 2), ("au1", 2), ("ab1", 1), ("au0", 0), ("au3", 1), ("au1", 3), ("aS", 3), ("ab0", 4), ("ab2", 1), ("aS", 4),),
    "turn": (("au0", 1), ("ab3", 2),),
    "q0": (("ab3", 3), ("adp", 0), ("au1", 4), ("ab0", 5), ("ab2", 2), ("ab0", 6), ("ab1", 2),),
    "t0": (("ab1", 3),),
    "q1": (("au1", 5), ("ab3", 4), ("ab2", 3), ("au1", 6), ("adp", 1), ("au0", 2), ("ab1", 4), ("ab3", 5), ("ab3", 6), ("ab2", 4), ("ab1", 5), ("adp", 2), ("ad0", 0), ("ab1", 6),),
    "t2": (("ab2", 5), ("ad1", 0),),
    "t3": (("au0", 3), ("ab2", 6),),
    "q2": (("ad2", 0), ("au2", 1),),
    "tb": (("ad0", 1), ("au3", 2),),
    "n2a": (("au0", 4), ("ad1", 1),),
    "fa0": (("au0", 5), ("ad2", 1),),
    "fc0": (("au2", 2), ("ad0", 2), ("au2", 3), ("ad0", 3), ("ad1", 2),),
    "ff0": (("ad2", 2), ("ad3", 0), ("ad1", 3), ("au3", 3),),
    "fi0": (("ru0", 0), ("ad2", 3), ("au2", 4),),
    "fa1": (("rd0", 0),),
    "fc1": (("ru0", 1),),
    "fe1": (("rd0", 1), ("ad3", 1),),
    "ff1": (("au3", 4),),
    "fg1": (("au2", 5),),
    "fi1": (("ru1", 0), ("au3", 5),),
    "fa2": (("rd1", 0), ("au2", 6), ("rd0", 2), ("ru0", 2),),
    "fe2": (("rd1", 1), ("ad3", 2),),
    "fg2": (("ad3", 3),),
    "fi2": (("ru2", 0), ("ru1", 1),),
    "fa3": (("rd0", 3), ("rd2", 0),),
    "fb3": (("ru2", 1),),
    "fc3": (("rd1", 2),),
    "fg3": (("rd2", 1), ("ru1", 2),),
    "fi3": (("ru2", 2), ("ru3", 0),),
    "ba": (("rd3", 0),),
    "og": (("rd1", 3),),
    "ga": (("rd3", 1), ("ro", 0), ("ru3", 1),),
    "a0": (("rd2", 2),),
    "H0": (("ru2", 3), ("ru1", 3), ("rd3", 2), ("ru3", 2),),
    "a2": (("rh0", 0),),
    "a3": (("rh0", 1), ("rd2", 3), ("ru1", 4),),
    "H1": (("ru2", 4), ("rd3", 3), ("ro", 1), ("ru0", 3),),
    "a4": (("rdl", 0), ("rh0", 2), ("rh1", 0),),
    "a5": (("rh1", 1),),
    "H2": (("ro", 2), ("rdl", 1),),
    "g2": (("rh2", 0),),
    "g0": (("rh2", 1),),
    "na": (("rh1", 2),),
    "nb": (("rh0", 3),),
    "end": (("ru2", 5), ("ru1", 5), ("rS", 0), ("rh0", 4), ("rh2", 2), ("ro", 3), ("rdl", 2), ("rS", 1), ("ru0", 4), ("rh1", 3), ("ru3", 3), ("rh0", 5), ("rh1", 4), ("rh2", 3), ("rS", 2), ("ru0", 5), ("ru3", 4), ("ro", 4), ("rS", 3), ("rh2", 4), ("rh1", 5), ("ru3", 5), ("rS", 4), ("rh2", 5),),
}

ROW_SUMS = ("rh0", "rh1", "rh2", "ro", "ru0", "ru1", "ru2", "ru3")
VMEM_BYTES = 63 * 1024 * 1024


def kernel_fits(n_wide, n_narrow, tokens, qkv_weight, up_weight, down_weight):
    width, hidden = qkv_weight.shape[0], up_weight.shape[1]
    n_z = n_wide // 4
    devices = n_wide * n_narrow
    return (
        n_narrow == 2
        and n_wide == 4 * n_z
        and n_z == 4
        and hidden == n_z * width
        and width % (8 * devices) == 0
        and hidden % (16 * devices) == 0
        and 2 * width // devices <= 128
        and hidden // devices <= 128
        and width // devices == 24
        and (tokens.shape[0] // devices) % (2 * CHUNK) == 0
    )


def solution(mesh):
    n_wide, n_narrow = mesh.shape["wide"], mesh.shape["narrow"]
    both = ("wide", "narrow")
    matrix, vector = P(both, None), P(both)
    in_specs = (
        matrix, matrix, matrix, vector, vector, matrix, vector, matrix, vector, vector, vector, matrix, vector, matrix, vector,
    )
    out_specs = (
        matrix, matrix, vector, vector, matrix, vector, matrix, vector, vector, vector, matrix, vector, matrix, vector,
    )

    def run(*arrays):
        fits = kernel_fits(n_wide, n_narrow, arrays[0], arrays[5], arrays[11], arrays[13])
        body = functools.partial(by_kernel, n_wide // 4) if fits else by_collectives
        return jax.shard_map(body, mesh=mesh, in_specs=in_specs, out_specs=out_specs, check_vma=False)(*arrays)

    return run
```

```python
import functools
import math

import jax
import jax.numpy as jnp
from jax import lax
from jax.experimental import pallas as pl
from jax.experimental.pallas import tpu as pltpu
from jax.sharding import PartitionSpec as P

H = 12
MASKED_SCORE = -1000000000.0
MESH = pl.DeviceIdType.MESH
F32 = jnp.float32
BF16 = jnp.bfloat16
ALL = slice(None)
CHUNK = 256


def layer_norm(inputs, ln_gain, ln_bias):
    row_mean = jnp.mean(inputs, axis=-1, keepdims=True)
    centred = inputs - row_mean
    spread = jnp.mean(centred * centred, axis=-1, keepdims=True)
    return centred * lax.rsqrt(spread + 1e-06) * ln_gain + ln_bias


def gelu_exact(inputs):
    return 0.5 * inputs * (1.0 + lax.erf(inputs * 0.7071067811865476))


def clip_index(lengths, row_count):
    clip_ends = jnp.cumsum(lengths)
    position = jnp.arange(row_count, dtype=jnp.int32)
    return jnp.sum((position[:, None] >= clip_ends[None, :]).astype(jnp.int32), axis=1)


def split_heads(matrix, head_count):
    row_count = matrix.shape[0]
    return matrix.reshape(row_count, head_count, -1).transpose(1, 0, 2)


def join_heads(stacked):
    head_count, row_count, head_size = stacked.shape
    return stacked.transpose(1, 0, 2).reshape(row_count, head_count * head_size)


def attend_forward(queries, key_rows, value_rows, segment, block_rows, score_scale):
    scores = (
        lax.dot_general(
            queries, key_rows, (((1,), (1,)), ((), ())), preferred_element_type=jnp.float32
        )
        * score_scale
    )
    allowed = segment[0:block_rows, None] == segment[None, :]
    scores = jnp.where(allowed, scores, MASKED_SCORE)
    highest = jnp.max(scores, axis=1, keepdims=True)
    raised = jnp.exp(scores - highest)
    denominator = jnp.sum(raised, axis=1, keepdims=True)
    softmax = (raised / denominator).astype(jnp.bfloat16)
    outputs = [jnp.dot(softmax, value_rows, preferred_element_type=jnp.float32)]
    totals = [highest + jnp.log(denominator)]
    return (jnp.concatenate(outputs, 0), jnp.concatenate(totals, 0))


def attend_backward(
    queries, key_rows, value_rows, segment, grad_out, lse_rows, block_rows, score_scale
):
    grad_keys = jnp.zeros(key_rows.shape, jnp.float32)
    grad_values = jnp.zeros(value_rows.shape, jnp.float32)
    g_rows = grad_out[0:block_rows]
    scores = (
        lax.dot_general(
            queries, key_rows, (((1,), (1,)), ((), ())), preferred_element_type=jnp.float32
        )
        * score_scale
    )
    allowed = segment[0:block_rows, None] == segment[None, :]
    softmax = jnp.where(allowed, jnp.exp(scores - lse_rows[0:block_rows]), 0.0)
    grad_values = grad_values + lax.dot_general(
        softmax.astype(jnp.bfloat16),
        g_rows,
        (((0,), (0,)), ((), ())),
        preferred_element_type=jnp.float32,
    )
    grad_probs = lax.dot_general(
        g_rows, value_rows, (((1,), (1,)), ((), ())), preferred_element_type=jnp.float32
    )
    grad_scores = (
        softmax * (grad_probs - jnp.sum(softmax * grad_probs, axis=1, keepdims=True))
    ).astype(jnp.bfloat16)
    grad_queries = [
        jnp.dot(grad_scores, key_rows, preferred_element_type=jnp.float32) * score_scale
    ]
    grad_keys = (
        grad_keys
        + lax.dot_general(
            grad_scores, queries, (((0,), (0,)), ((), ())), preferred_element_type=jnp.float32
        )
        * score_scale
    )
    return (jnp.concatenate(grad_queries, 0), grad_keys, grad_values)


def by_collectives(
    tokens,
    cotangent,
    clip_lengths,
    ln1_gain,
    ln1_bias,
    qkv_weight,
    qv_bias,
    out_weight,
    out_bias,
    ln2_gain,
    ln2_bias,
    up_weight,
    up_bias,
    down_weight,
    down_bias,
):
    gathered = (
        lax.all_gather(ln1_gain, ("wide", "narrow"), axis=0, tiled=True),
        lax.all_gather(ln1_bias, ("wide", "narrow"), axis=0, tiled=True),
        lax.all_gather(qkv_weight, ("wide", "narrow"), axis=0, tiled=True),
        lax.all_gather(qv_bias, ("wide", "narrow"), axis=0, tiled=True),
        lax.all_gather(out_weight, ("wide", "narrow"), axis=0, tiled=True),
        lax.all_gather(out_bias, ("wide", "narrow"), axis=0, tiled=True),
        lax.all_gather(ln2_gain, ("wide", "narrow"), axis=0, tiled=True),
        lax.all_gather(ln2_bias, ("wide", "narrow"), axis=0, tiled=True),
        lax.all_gather(up_weight, ("wide", "narrow"), axis=0, tiled=True),
        lax.all_gather(up_bias, ("wide", "narrow"), axis=0, tiled=True),
        lax.all_gather(down_weight, ("wide", "narrow"), axis=0, tiled=True),
        lax.all_gather(down_bias, ("wide", "narrow"), axis=0, tiled=True),
    )
    (
        gain_one,
        bias_one,
        merged_weight,
        merged_bias,
        proj_weight,
        proj_bias,
        gain_two,
        bias_two,
        w_up,
        b_up,
        w_down,
        b_down,
    ) = gathered
    inputs = tokens.astype(jnp.float32)
    row_count, model_width = inputs.shape
    head_size = model_width // H
    score_scale = 1.0 / math.sqrt(head_size)
    block_rows = min(512, row_count)
    clip_count = clip_lengths.shape[1]
    segment = clip_index(clip_lengths[0], row_count)
    live_rows = (segment < clip_count).astype(jnp.float32)[:, None]
    normed_one = layer_norm(
        inputs, gain_one.astype(jnp.float32), bias_one.astype(jnp.float32)
    ).astype(jnp.bfloat16)
    bias_float = merged_bias.astype(jnp.float32)
    full_bias = jnp.concatenate(
        [bias_float[:model_width], jnp.zeros((model_width,), jnp.float32), bias_float[model_width:]]
    )
    merged_rows = (
        jnp.dot(normed_one, merged_weight, preferred_element_type=jnp.float32) + full_bias
    ).astype(jnp.bfloat16)
    q_heads = split_heads(merged_rows[:, :model_width], H)
    k_heads = split_heads(merged_rows[:, model_width : 2 * model_width], H)
    v_heads = split_heads(merged_rows[:, 2 * model_width :], H)

    def head_forward(triple):
        return attend_forward(triple[0], triple[1], triple[2], segment, block_rows, score_scale)

    att_heads, lse_heads = lax.map(head_forward, (q_heads, k_heads, v_heads))
    attended = join_heads(att_heads).astype(jnp.bfloat16)
    branch_one = jnp.dot(
        attended, proj_weight, preferred_element_type=jnp.float32
    ) + proj_bias.astype(jnp.float32)
    middle = inputs + live_rows * branch_one
    normed_two = layer_norm(
        middle, gain_two.astype(jnp.float32), bias_two.astype(jnp.float32)
    ).astype(jnp.bfloat16)
    hidden_pre = jnp.dot(normed_two, w_up, preferred_element_type=jnp.float32) + b_up.astype(
        jnp.float32
    )
    activated, gelu_pull = jax.vjp(gelu_exact, hidden_pre)
    activated = activated.astype(jnp.bfloat16)
    branch_two = jnp.dot(activated, w_down, preferred_element_type=jnp.float32) + b_down.astype(
        jnp.float32
    )
    block_out = (middle + live_rows * branch_two).astype(jnp.bfloat16)
    back_gain_one, back_merged, back_proj, back_gain_two, back_up, back_down = (
        lax.all_gather(ln1_gain, ("wide", "narrow"), axis=0, tiled=True),
        lax.all_gather(qkv_weight, ("wide", "narrow"), axis=0, tiled=True),
        lax.all_gather(out_weight, ("wide", "narrow"), axis=0, tiled=True),
        lax.all_gather(ln2_gain, ("wide", "narrow"), axis=0, tiled=True),
        lax.all_gather(up_weight, ("wide", "narrow"), axis=0, tiled=True),
        lax.all_gather(down_weight, ("wide", "narrow"), axis=0, tiled=True),
    )
    upstream = cotangent.astype(jnp.float32)
    grad_two = (live_rows * upstream).astype(jnp.bfloat16)
    grad_b_down = jnp.sum(grad_two.astype(jnp.float32), axis=0)
    grad_w_down = jnp.einsum("tf,td->fd", activated, grad_two, preferred_element_type=jnp.float32)
    grad_act = jnp.einsum("td,fd->tf", grad_two, back_down, preferred_element_type=jnp.float32)
    grad_hidden = gelu_pull(grad_act)[0].astype(jnp.bfloat16)
    grad_b_up = jnp.sum(grad_hidden.astype(jnp.float32), axis=0)
    grad_w_up = jnp.einsum("td,tf->df", normed_two, grad_hidden, preferred_element_type=jnp.float32)
    grad_normed_two = jnp.einsum(
        "tf,df->td", grad_hidden, back_up, preferred_element_type=jnp.float32
    )
    _, norm_pull_two = jax.vjp(
        layer_norm, middle, back_gain_two.astype(jnp.float32), bias_two.astype(jnp.float32)
    )
    grad_middle_norm, grad_gain_two, grad_bias_two = norm_pull_two(grad_normed_two)
    grad_middle = upstream + grad_middle_norm
    grad_one = (live_rows * grad_middle).astype(jnp.bfloat16)
    grad_b_proj = jnp.sum(grad_one.astype(jnp.float32), axis=0)
    grad_w_proj = jnp.einsum("te,td->ed", attended, grad_one, preferred_element_type=jnp.float32)
    grad_att = jnp.einsum(
        "td,ed->te", grad_one, back_proj, preferred_element_type=jnp.float32
    ).astype(jnp.bfloat16)
    grad_att_heads = split_heads(grad_att, H)

    def head_backward(members):
        return attend_backward(
            members[0],
            members[1],
            members[2],
            segment,
            members[3],
            members[4],
            block_rows,
            score_scale,
        )

    grad_q, grad_k, grad_v = lax.map(
        head_backward, (q_heads, k_heads, v_heads, grad_att_heads, lse_heads)
    )
    grad_merged = jnp.concatenate(
        [join_heads(grad_q), join_heads(grad_k), join_heads(grad_v)], 1
    ).astype(jnp.bfloat16)
    column_sums = jnp.sum(grad_merged.astype(jnp.float32), axis=0)
    grad_merged_bias = jnp.concatenate([column_sums[:model_width], column_sums[2 * model_width :]])
    grad_w_merged = jnp.einsum(
        "te,tf->ef", normed_one, grad_merged, preferred_element_type=jnp.float32
    )
    grad_normed_one = jnp.einsum(
        "tf,ef->te", grad_merged, back_merged, preferred_element_type=jnp.float32
    )
    _, norm_pull_one = jax.vjp(
        layer_norm, inputs, back_gain_one.astype(jnp.float32), bias_one.astype(jnp.float32)
    )
    grad_input_norm, grad_gain_one, grad_bias_one = norm_pull_one(grad_normed_one)
    tokens_grad = grad_middle + grad_input_norm
    shares = (
        lax.psum_scatter(grad_gain_one, ("wide", "narrow"), scatter_dimension=0, tiled=True),
        lax.psum_scatter(grad_bias_one, ("wide", "narrow"), scatter_dimension=0, tiled=True),
        lax.psum_scatter(grad_w_merged, ("wide", "narrow"), scatter_dimension=0, tiled=True),
        lax.psum_scatter(grad_merged_bias, ("wide", "narrow"), scatter_dimension=0, tiled=True),
        lax.psum_scatter(grad_w_proj, ("wide", "narrow"), scatter_dimension=0, tiled=True),
        lax.psum_scatter(grad_b_proj, ("wide", "narrow"), scatter_dimension=0, tiled=True),
        lax.psum_scatter(grad_gain_two, ("wide", "narrow"), scatter_dimension=0, tiled=True),
        lax.psum_scatter(grad_bias_two, ("wide", "narrow"), scatter_dimension=0, tiled=True),
        lax.psum_scatter(grad_w_up, ("wide", "narrow"), scatter_dimension=0, tiled=True),
        lax.psum_scatter(grad_b_up, ("wide", "narrow"), scatter_dimension=0, tiled=True),
        lax.psum_scatter(grad_w_down, ("wide", "narrow"), scatter_dimension=0, tiled=True),
        lax.psum_scatter(grad_b_down, ("wide", "narrow"), scatter_dimension=0, tiled=True),
    )
    return (
        block_out,
        tokens_grad,
        shares[0],
        shares[1],
        shares[2],
        shares[3],
        shares[4],
        shares[5],
        shares[6],
        shares[7],
        shares[8],
        shares[9],
        shares[10],
        shares[11],
    )


def nt_dot(left, right):
    return lax.dot_general(left, right, (((1,), (1,)), ((), ())), preferred_element_type=F32)


def nn_dot(left, right):
    return jnp.dot(left, right, preferred_element_type=F32)


def rows_of(step, size=CHUNK):
    return pl.ds(pl.multiple_of(step * size, size), size)


def norm_parts(values):
    centred = values - jnp.mean(values, axis=-1, keepdims=True)
    scale = lax.rsqrt(jnp.mean(centred * centred, axis=-1, keepdims=True) + 1e-06)
    return centred * scale, scale


def fold_rows(values):
    return jnp.sum(values.reshape(-1, 8, values.shape[-1]), axis=0)


def gelu_both(u):
    tail = 0.5 * (1.0 + lax.erf(u * 0.7071067811865476))
    return u * tail, tail + u * jnp.exp(-0.5 * u * u) * 0.3989422804014327


def spread_maps(width, columns):
    column = lax.broadcasted_iota(jnp.int32, (1, columns), 1).astype(F32)
    group = jnp.floor((column + 0.5) * (1.0 / width))
    place = column - group * width
    lane = lax.broadcasted_iota(jnp.int32, (128, columns), 0).astype(F32)
    picks = jnp.where(lane == place, 1.0, 0.0).astype(BF16)
    owners = columns // width
    owner = lax.broadcasted_iota(jnp.int32, (owners, 8, columns), 0).astype(F32)
    mine = owner == group.reshape(1, 1, columns)
    return picks, mine


def spread(pieces, width, columns):
    picks, mine = spread_maps(width, columns)
    wide_rows = nn_dot(pieces.reshape(-1, 128).astype(BF16), picks)
    return jnp.sum(jnp.where(mine, wide_rows.reshape(-1, 8, columns), 0.0), axis=0)


def gather_back(vectors, width):
    columns = vectors.shape[-1]
    picks, mine = spread_maps(width, columns)
    rest = jnp.where(mine, vectors[None], 0.0).reshape(-1, columns)
    total = None
    for _ in range(3):
        part = rest.astype(BF16)
        rest = rest - part.astype(F32)
        term = nt_dot(part, picks)
        total = term if total is None else total + term
    return total.reshape(-1, 8, 128)


Z0, Z1, Z2, ZR, X0, Y0, X1, Y1, X2, Y2, DX, DY, C0 = range(13)
ORDERS = {
    "plain": ("z", "relay", "near", "across", "core"),
    "direct": ("zd", "near", "across", "core"),
    "boot": ("own", "zd", "pair", "rest", "across", "core"),
    "late": ("near", "across", "z", "relay", "core"),
    "late direct": ("near", "across", "zd", "core"),
}
BACK = {
    "plain": ("core", "across", "near", "z", "z far"),
    "direct": ("core", "across", "near", "zd"),
    "late": ("core", "z", "z far", "across", "near"),
    "late direct": ("core", "zd", "across", "near"),
}


def phases_of(name):
    kind = "direct" if name[1:] == "S" else KINDS.get(name, "plain")
    if name[:2] == "ad":
        return (("z", "relay") if kind == "plain" else ("zd",)) if name == "adp" else ("near", "across", "core")
    if name[:2] == "rd":
        return (("z", "z far") if kind == "plain" else ("zd",)) if name == "rdl" else ("core", "across", "near")
    return (ORDERS if name[0] == "a" else BACK)[kind]


def semaphore_slots():
    used = {
        "z": (Z0, Z1, Z2), "relay": (ZR,), "zd": (Z0, Z1, Z2), "own": (X1, Y1), "pair": (X2, Y2), "rest": (X0, Y0),
        "near": (X0, Y0), "across": (DX, DY), "core": (C0,), "z far": (ZR, Z1),
    }
    gathers = ["aS", "ab0", "ab1", "ab2", "ab3", "adp", "au0", "ad0", "au1", "ad1", "au2", "ad2", "au3", "ad3"]
    sums = ["ru0", "rd0", "ru1", "rd1", "ru2", "rd2", "ru3", "rd3", "ro", "rdl", "rh0", "rh1", "rh2", "rS"]
    slots = []
    for names in (gathers, sums):
        places = {}
        for name in names:
            for sem in sorted({sem for phase in phases_of(name) for sem in used[phase]}):
                places[name, sem] = len(places)
        slots.append(places)
    return slots[0], slots[1], max(len(slots[0]), len(slots[1])), len(slots[0])


def layer_kernel(
    clip_ref, tok_ref, cot_ref, v0, v1, v2, v3, v4, v5, v6, v7, wqkv_ref, wout_ref, wup_ref, wdown_ref,
    out_ref, tgrad_ref, gqkv_ref, gout_ref, gup_ref, gdown_ref, gsmall_ref,
    slabs, downs, smalls, gsmalls, weights, w_up,
    row_c, row_d, row_n, row_z, late_d, late_n, late_z, down_c, down_d, down_n, down_z, sm_c, sm_d, sm_n, sm_z,
    qkv, n1t, n1, att_t, middle, n2, n2t, g2, acc_out, acc_grad, act, grad_h, pre, grad_act,
    tok, cot, bias, lse, dq_t, vec24, vec48, vec96, merged_bias, group_sums, sums, up_sums, gqkv, gout, gup, gdown, gsmall,
    sends, ag_recv, rs_recv, local,
):
    n_z, width = slabs.shape[1], slabs.shape[-1]
    count = tok.shape[0]
    pairs = width // 128
    chunks = count // CHUNK
    wide_at, y = lax.axis_index("wide"), lax.axis_index("narrow")
    core = lax.rem(wide_at, 2)
    x = lax.rem(lax.div(wide_at, 2), 2)
    z = lax.div(wide_at, 4)

    def device(z_at, x_at, c_at, y_at):
        return ((z_at * 2 + x_at) * 2 + c_at, y_at)

    def row_view(block):
        def view(at):
            return slabs.at[(block, *at)]
        return view

    def down_view(tile):
        def view(at):
            return downs.at[(tile, *at[1:])]
        return view

    def small_view(ref):
        def view(at):
            return ref.at[at]
        return view

    def half_of(ref, side):
        if ref.shape[-1] < 2 * 128:
            return ref
        cut = ref.shape[-1] // 2
        return ref.at[(*([ALL] * (len(ref.shape) - 1)), pl.ds(side * cut, cut))]

    to_x, to_y, to_c = device(z, 1 - x, core, y), device(z, x, core, 1 - y), device(z, x, 1 - core, y)
    z_places = (z + 1 - 2 * lax.rem(z, 2), lax.rem(z + 2, n_z), n_z - 1 - z)
    along_z = [device(at, x, core, y) for at in z_places]
    other_pair = pl.ds(2 * (1 - lax.div(z, 2)), 2)
    inner = lax.rem(z + 1, n_z) >= 2

    ag_slots, rs_slots, _, _ = semaphore_slots()

    def remote(src, dst, sums, unit_name, sem, to, recv_sem=None):
        slots = rs_slots if sums else ag_slots
        recv = rs_recv if sums else ag_recv
        return pltpu.make_async_remote_copy(
            src_ref=src, dst_ref=dst, send_sem=sends.at[slots[unit_name, sem]],
            recv_sem=recv.at[slots[unit_name, sem if recv_sem is None else recv_sem]],
            device_id=to, device_id_type=MESH,
        )

    def do_all(copies, what):
        for copy in copies:
            getattr(copy, what)()

    one, plane = (x, core, y), (ALL, core, ALL)

    def ag_copies(unit, phase):
        view, row, phases, along = unit
        sems = False
        held = z if along is plane else ALL

        def both(at, sem):
            mine = view((at, x, core, y))
            return [remote(mine, mine, sems, row, sem, to_x), remote(mine, mine, sems, row, sem + 1, to_y)]

        def own_to(*which):
            own = view((z, *along))
            return [remote(own, own, sems, row, k, along_z[k]) for k in which]

        if phase == "z":
            return own_to(Z0, Z1)
        if phase == "zd":
            return own_to(Z0, Z1, Z2)
        if phase in ("z near", "z far", "z last"):
            return own_to(("z near", "z far", "z last").index(phase))
        if phase == "relay":
            passed = view((z_places[1], *along))
            return [remote(passed, passed, sems, row, ZR, along_z[0], Z2)]
        if phase == "own":
            return both(z, X1)
        if phase == "pair":
            return both(z_places[0], X2)
        if phase == "rest":
            return both(other_pair, X0)
        if phase == "near":
            return both(held, X0)
        if phase == "across":
            from_x, from_y = view((held, 1 - x, core, y)), view((held, x, core, 1 - y))
            first = half_of(from_x, 0)
            copies = [remote(first, first, sems, row, DY, to_y)]
            if from_x.shape[-1] >= 2 * 128:
                second = half_of(from_y, 1)
                copies.append(remote(second, second, sems, row, DX, to_x))
            return copies
        whole_plane = view((ALL, ALL, core, ALL))
        return [remote(whole_plane, whole_plane, sems, row, C0, to_c)]

    def ag_wait(unit, *phases):
        for phase in phases:
            do_all(ag_copies(unit, phase), "wait_recv")

    def ag_stage(unit, stage):
        phases = unit[2]
        phase = phases[stage] if stage < len(phases) else None
        if phase == "relay":
            @pl.when(inner)
            def _():
                ag_wait(unit, "z far")
                do_all(ag_copies(unit, "relay"), "start")
            return
        if phase == "pair":
            ag_wait(unit, "z near")
        elif phase == "rest":
            ag_wait(unit, "z far", "z last")
        elif phase == "across" and "own" in phases:
            ag_wait(unit, "own", "pair", "rest")
        elif stage > 0 and phases[stage - 1] == "relay":
            @pl.when(jnp.logical_not(inner))
            def _():
                ag_wait(unit, "z far")
            ag_wait(unit, "z near", "z last")
        elif stage > 0 and phases[stage - 1] != "own":
            ag_wait(unit, phases[stage - 1])
        if phase:
            do_all(ag_copies(unit, phase), "start")
            if phase == "z":
                @pl.when(inner)
                def _():
                    do_all(ag_copies(unit, "z last"), "start")
        else:
            for sent in phases:
                if sent != "relay":
                    do_all(ag_copies(unit, sent), "wait_send")
            if "relay" in phases:
                @pl.when(inner)
                def _():
                    do_all(ag_copies(unit, "z last") + ag_copies(unit, "relay"), "wait_send")

    def gather_unit(name, view):
        kind = KINDS.get(name, "plain")
        return (view, name, phases_of(name), plane if kind[:4] == "late" else one)

    units = {"aS": gather_unit("aS", small_view(smalls)), "adp": gather_unit("adp", lambda at: downs.at[at])}
    for block in range(4):
        units[f"ab{block}"] = gather_unit(f"ab{block}", row_view(block))
    for tile in range(n_z):
        units[f"au{tile}"] = gather_unit(f"au{tile}", row_view(4 + tile))
        units[f"ad{tile}"] = gather_unit(f"ad{tile}", down_view(tile))

    def rs_copies(unit, phase):
        view, row, phases, landing, along = unit
        sems = True
        held = z if along is plane else ALL
        if phase == "core":
            return [remote(view((ALL, ALL, 1 - core, ALL)), landing["core"], sems, row, C0, to_c)]
        if phase == "across":
            away = view((held, 1 - x, core, 1 - y))
            copies = [remote(half_of(away, 0), landing["dx"], sems, row, DX, to_x)]
            if away.shape[-1] >= 2 * 128:
                copies.append(remote(half_of(away, 1), landing["dy"], sems, row, DY, to_y))
            return copies
        if phase == "near":
            return [
                remote(view((held, 1 - x, core, y)), landing["x"], sems, row, X0, to_x),
                remote(view((held, x, core, 1 - y)), landing["y"], sems, row, Y0, to_y),
            ]
        if phase == "z outer":
            return [remote(view((z_places[2], *along)), landing["z"].at[ZR], sems, row, ZR, along_z[0])]
        which = {"z": (Z0,), "z far": (Z1,), "z last": (Z2,), "zd": (Z0, Z1, Z2)}[phase]
        return [remote(view((z_places[k], *along)), landing["z"].at[k], sems, row, k, along_z[k]) for k in which]

    def add_into(target, *sources):
        total = target[...].astype(F32)
        for source in sources:
            total = total + source[...].astype(F32)
        target[...] = total.astype(target.dtype)

    def add_all(target, *sources):
        free = len(target.shape) - 2
        if free == 0:
            add_into(target, *sources)
            return
        places = [()]
        for extent in target.shape[1:free]:
            places = [place + (k,) for place in places for k in range(extent)]

        def step(i, carry):
            for place in places:
                add_into(target.at[(i, *place)], *[source.at[(i, *place)] for source in sources])
            return carry

        lax.fori_loop(0, target.shape[0], step, 0)

    def rs_stage(unit, stage):
        view, _, phases, landing, along = unit
        held = z if along is plane else ALL
        before = phases[stage - 1] if stage > 0 else None
        phase = phases[stage] if stage < len(phases) else None
        if phase == "z far":
            @pl.when(inner)
            def _():
                do_all(rs_copies(unit, "z outer"), "wait_recv")
                add_all(view((z_places[1], *along)), landing["z"].at[ZR])
        elif before == "z far":
            rs_wait(unit, "z", "z far")
            add_all(view((z, *along)), landing["z"].at[Z0], landing["z"].at[Z1])

            @pl.when(inner)
            def _():
                rs_wait(unit, "z last")
                add_all(view((z, *along)), landing["z"].at[Z2])
        elif before:
            rs_wait(unit, before)
        if before == "core":
            add_all(view((ALL, ALL, core, ALL)), landing["core"])
        elif before == "across":
            on_y = view((held, x, core, 1 - y))
            add_all(half_of(on_y, 0), landing["dx"])
            if on_y.shape[-1] >= 2 * 128:
                add_all(half_of(view((held, 1 - x, core, y)), 1), landing["dy"])
        elif before == "near":
            add_all(view((held, x, core, y)), landing["x"], landing["y"])
        elif before == "zd":
            add_all(view((z, *along)), *[landing["z"].at[k] for k in (Z0, Z1, Z2)])
        if phase:
            do_all(rs_copies(unit, phase), "start")
        if phase == "z":
            @pl.when(inner)
            def _():
                do_all(rs_copies(unit, "z last"), "start")

            @pl.when(jnp.logical_not(inner))
            def _():
                do_all(rs_copies(unit, "z outer"), "start")

    def rs_wait(unit, *phases):
        for phase in phases:
            do_all(rs_copies(unit, phase), "wait_recv")

    def rs_end(unit, *results):
        view, _, phases, landing, along = unit
        last = phases[-1]
        if last == "near":
            sources = [landing["x"], landing["y"]]
        else:
            sources = [landing["z"].at[k] for k in ((Z0, Z1) if last == "z far" else (Z0, Z1, Z2))]
        rs_wait(unit, *(("z", "z far") if last == "z far" else (last,)))
        total = view((z, x, core, y))[...].astype(F32)
        for part in sources:
            total = total + part[...].astype(F32)
        size = total.shape[-1] // len(results)
        for k, result in enumerate(results):
            result[...] = total[:, k * size : (k + 1) * size]
        if last == "z far":
            @pl.when(inner)
            def _():
                rs_wait(unit, "z last")
                for k, result in enumerate(results):
                    result[...] += landing["z"][Z2, :, k * size : (k + 1) * size].astype(F32)

    def rs_sent(unit):
        for phase in unit[2]:
            do_all(rs_copies(unit, phase), "wait_send")
        if "z far" in unit[2]:
            @pl.when(inner)
            def _():
                do_all(rs_copies(unit, "z last"), "wait_send")

            @pl.when(jnp.logical_not(inner))
            def _():
                do_all(rs_copies(unit, "z outer"), "wait_send")

    def row_unit(block, name):
        if name in LATE_SUMS:
            late = LATE_SUMS.index(name)
            landing = {"core": row_c.at[block], "dx": late_d.at[late, 0], "dy": late_d.at[late, 1], "x": late_n.at[late, 0], "y": late_n.at[late, 1], "z": late_z.at[late]}
            return (row_view(block), name, phases_of(name), landing, plane)
        at = block - sum(earlier in LATE_SUMS for earlier in ROW_SUMS[:block])
        landing = {"core": row_c.at[block], "dx": row_d.at[at, 0], "dy": row_d.at[at, 1], "x": row_n.at[at, 0], "y": row_n.at[at, 1], "z": row_z.at[at]}
        return (row_view(block), name, phases_of(name), landing, one)

    def down_unit(tile, name):
        landing = {"core": down_c.at[tile], "dx": down_d.at[tile, 0], "dy": down_d.at[tile, 1], "x": down_n.at[tile, 0], "y": down_n.at[tile, 1]}
        return (down_view(tile), name, phases_of(name), landing, one)

    def block_columns(block):
        return pl.ds(block * width, width)

    third = width // 3
    results = {"rdl": [gdown], "ro": [gout], "rS": [gsmall]}
    for t in range(n_z):
        units[f"ru{t}"] = row_unit(4 + t, f"ru{t}")
        units[f"rd{t}"] = down_unit(t, f"rd{t}")
        results[f"ru{t}"] = [gup.at[:, block_columns(t)]]
    for g in range(3):
        units[f"rh{g}"] = row_unit(g, f"rh{g}")
        results[f"rh{g}"] = [gqkv.at[:, pl.ds(j * width + g * third, third)] for j in range(3)]
    units["ro"] = row_unit(3, "ro")
    small_landing = {"core": sm_c, "dx": sm_d, "x": sm_n.at[0], "y": sm_n.at[1], "z": sm_z}
    units["rS"] = (small_view(gsmalls), "rS", phases_of("rS"), small_landing, one)
    units["rdl"] = (lambda at: downs.at[at], "rdl", phases_of("rdl"), {"z": down_z}, one)
    last_copies = [
        pltpu.make_async_copy(src, dst, local.at[2 + k])
        for k, (src, dst) in enumerate(((gup, gup_ref), (gdown, gdown_ref), (gout, gout_ref), (gqkv, gqkv_ref), (gsmall, gsmall_ref)))
    ]

    def point(name):
        for unit_name, stage in TABLE.get(name, ()):
            unit = units[unit_name]
            if unit_name[0] == "a":
                ag_stage(unit, stage)
            elif unit_name in results and stage == len(unit[2]):
                rs_end(unit, *results[unit_name])
            else:
                rs_stage(unit, stage)

    def points_at(index, names):
        for k, name in enumerate(names):
            if TABLE.get(name):
                pl.when(index == k)(functools.partial(point, name))

    barrier = pltpu.get_barrier_semaphore()
    partners = [*along_z, to_x, to_y, to_c]
    for to in partners:
        pl.semaphore_signal(barrier, inc=1, device_id=to, device_id_type=MESH)
    shards = []
    for g in range(3):
        for j in range(3):
            shards.append((wqkv_ref.at[:, pl.ds(j * width + g * third, third)], slabs.at[g, z, x, core, y, :, pl.ds(j * third, third)]))
    shards.append((wout_ref, slabs.at[3, z, x, core, y]))
    for tile in range(n_z):
        shards.append((wup_ref.at[:, block_columns(tile)], slabs.at[4 + tile, z, x, core, y]))
    shards.append((wdown_ref, downs.at[z, x, core, y]))
    shard_copies = [pltpu.make_async_copy(src, dst, local.at[k]) for k, (src, dst) in enumerate(shards)]
    row_copies = [pltpu.make_async_copy(tok_ref, tok, local.at[len(shards)]), pltpu.make_async_copy(cot_ref, cot, local.at[len(shards) + 1])]
    do_all(shard_copies + row_copies, "start")
    smalls[z, x, core, y] = jnp.zeros((8, 128), F32)
    for k, vector in enumerate((v0, v1, v2, v3, v4, v5, v6, v7)):
        smalls[z, x, core, y, k, 0 : vector.shape[0]] = vector[...].astype(F32)
    do_all(shard_copies, "wait")
    pl.semaphore_wait(barrier, len(partners))
    point("mask")
    do_all(row_copies, "wait")

    ends = []
    for k in range(clip_ref.shape[1]):
        ends.append(clip_ref[0, k] + (ends[-1] if ends else 0))

    def segment_of(position):
        total = jnp.zeros(position.shape, jnp.int32)
        for end in ends:
            total = total + jnp.where(position >= end, 1, 0)
        return total

    across = segment_of(lax.broadcasted_iota(jnp.int32, (CHUNK, count), 1))

    def live_of(step):
        position = lax.broadcasted_iota(jnp.int32, (CHUNK, 1), 0) + step * CHUNK
        return jnp.where(position < ends[-1], 1.0, 0.0)

    ones = jnp.ones((8, count), BF16)

    def column_sums(values):
        return nn_dot(ones, values)

    def mask_step(i, carry):
        down = segment_of(lax.broadcasted_iota(jnp.int32, (CHUNK, count), 0) + i * CHUNK)
        bias[rows_of(i), :] = jnp.where(down == across, 0.0, -1e30)
        g2[rows_of(i), :] = (live_of(i) * cot[rows_of(i), :].astype(F32)).astype(BF16)
        return carry

    lax.fori_loop(0, chunks, mask_step, 0)
    sums[...] = jnp.zeros_like(sums)
    up_sums[...] = jnp.zeros_like(up_sums)
    sums[0, 7:8, :] = column_sums(g2[...])[0:1]

    point("vec")
    vec24[...] = spread(smalls[...], 24, width)
    for k in range(2):
        vec48[k] = spread(smalls[k * n_z // 2 : (k + 1) * n_z // 2], 48, width)
    for k in range(n_z):
        vec96[k] = spread(smalls[k], 96, width)
    for g in range(3):
        span = slice(g * third, (g + 1) * third)
        merged_bias[g, 0:1, :] = jnp.concatenate(
            [vec48[0, 2:3, span], jnp.zeros((1, width - 2 * third), F32), vec48[1, 2:3, span]], axis=1
        )

    def norm_one(i, carry):
        normed, _ = norm_parts(tok[rows_of(i), :].astype(F32))
        n1[rows_of(i), :] = (normed * vec24[0:1, :] + vec24[1:2, :]).astype(BF16)
        return carry

    lax.fori_loop(0, chunks, norm_one, 0)

    def turn(source, target):
        def step(i, carry):
            at = rows_of(i, 128)
            target[at, :] = source[:, at].T
            return carry

        lax.fori_loop(0, pairs, step, 0)

    point("turn")
    turn(n1, n1t)

    def assemble(block, target):
        def step(z_at, carry):
            for x_at in range(2):
                for c_at in range(2):
                    two = slabs[block, z_at, x_at, c_at].astype(F32)
                    size = 2 * two.shape[1]
                    first = pl.multiple_of(((z_at * 2 + x_at) * 2 + c_at) * size, 16)
                    target[pl.ds(first, size), :] = two.reshape(size, width).astype(BF16)
            return carry

        lax.fori_loop(0, n_z, step, 0)

    lane = lax.broadcasted_iota(jnp.int32, (count, 128), 1)

    def one_head(values, head):
        keep = lane < 64 if head == 0 else lane >= 64
        return jnp.where(keep, values, jnp.zeros_like(values))

    q_block = 512
    parts = count // q_block
    per_group = pairs // 3

    def places(p):
        first = lax.rem(p, per_group) * 128
        return lax.div(p, per_group), [pl.ds(pl.multiple_of(first + j * third, 128), 128) for j in range(3)]

    def attend(p, carry):
        group, (at_q, at_k, at_v) = places(p)
        points_at(p, [f"q{k // per_group}" if k % per_group == 0 else "" for k in range(pairs)])

        @pl.when(lax.rem(p, per_group) == 0)
        def _():
            assemble(group, weights.at[group])
            qkv[group] = (nn_dot(n1[...], weights[group]) + merged_bias[group, 0:1, :]).astype(BF16)

        points_at(p, [f"t{k}" for k in range(pairs)])
        keys = qkv[group, :, at_k]
        queries = qkv[group, :, at_q] * 0.125
        values_t = qkv[group, :, at_v].T
        for head in range(2):
            mine = one_head(queries, head)
            for part in range(parts):
                span = slice(part * q_block, (part + 1) * q_block)
                scores = nt_dot(keys, mine[span]) + bias[:, span]
                highest = jnp.max(scores, axis=0, keepdims=True)
                raised = jnp.exp(scores - highest)
                total = jnp.sum(raised, axis=0, keepdims=True)
                chances = (raised * (1.0 / total)).astype(BF16)
                lse[p, head : head + 1, span] = highest + jnp.log(total)
                result = nn_dot(values_t[64 * head : 64 * head + 64], chances)
                att_t[pl.ds(pl.multiple_of(p * 128 + 64 * head, 64), 64), span] = result.astype(BF16)
        return carry

    lax.fori_loop(0, pairs, attend, 0)
    point("tb")
    att = n1

    def turn_back(p, carry):
        at = rows_of(p, 128)
        att[:, at] = att_t[at, :].T
        return carry

    lax.fori_loop(0, pairs, turn_back, 0)
    point("out")
    assemble(3, weights.at[3])
    pre[...] = nn_dot(att[...], weights[3])

    def norm_two(i, carry):
        at = rows_of(i)
        branch = pre[at, :] + vec24[3:4, :]
        mid = tok[at, :].astype(F32) + live_of(i) * branch
        middle[at, :] = mid
        normed, _ = norm_parts(mid)
        n2[at, :] = (normed * vec24[4:5, :] + vec24[5:6, :]).astype(BF16)
        return carry

    point("n2a")
    lax.fori_loop(0, chunks // 2, norm_two, 0)
    point("n2b")
    lax.fori_loop(chunks // 2, chunks, norm_two, 0)
    point("n2t")
    turn(n2, n2t)
    acc_out[...] = jnp.zeros_like(acc_out)
    acc_grad[...] = jnp.zeros_like(acc_grad)

    def store_rows(block, lhs_t, rhs):
        size = slabs.shape[-2]
        for first in range(0, width, 192):
            total = nn_dot(lhs_t[first : first + 192, :], rhs)
            for k in range(192 // size // 2):
                at = first // size + 2 * k
                two = total[2 * k * size : 2 * (k + 1) * size].reshape(2, size, width).astype(BF16)
                slabs[block, at // 8, at // 4 % 2, at // 2 % 2] = two

    def feed(t, carry):
        def step_point(name):
            points_at(t, [f"{name}{k}" for k in range(n_z)])

        step_point("fa")
        assemble(4 + t, w_up)
        up_bias = vec96[t, 6:7, :]
        half = count // 2

        def into_hidden(rows):
            pre[rows] = nn_dot(n2[rows], w_up[...])

        def into_grads(rows):
            grad_act[rows] = nt_dot(g2[rows], downs[t].reshape(width, width))

        def gelu_rows(first):
            for at in range(first, first + half, 32):
                rows = slice(at, at + 32)
                active, slope = gelu_both(pre[rows] + up_bias)
                act[rows] = active.astype(BF16)
                grad_h[rows] = (grad_act[rows] * slope).astype(BF16)

        def out_of(rows):
            acc_out[rows] += nn_dot(act[rows], downs[t].reshape(width, width))
            acc_grad[rows] += nt_dot(grad_h[rows], w_up[...])

        upper, lower = slice(0, half), slice(half, count)
        step_point("fb")
        into_hidden(upper)
        step_point("fc")
        into_grads(upper)
        step_point("fd")
        into_hidden(lower)
        into_grads(lower)
        gelu_rows(0)
        step_point("fe")
        out_of(upper)
        gelu_rows(half)
        step_point("ff")
        out_of(lower)
        step_point("fg")
        up_sums[t, 6:7, :] = column_sums(grad_h[...])[0:1]
        step_point("fh")
        store_rows(4 + t, n2t, grad_h[...])
        step_point("fi")
        for j in range(pairs):
            span = slice(j * 128, (j + 1) * 128)
            piece = nn_dot(act[:, span].T, g2[...]).astype(BF16)
            size = downs.shape[-2]
            at = j * 128
            while at < (j + 1) * 128:
                owner, inside = at // size, at % size
                length = min(size - inside, (j + 1) * 128 - at)
                downs[t, owner // 4, owner // 2 % 2, owner % 2, inside : inside + length, :] = piece[at - j * 128 : at - j * 128 + length]
                at += length
        return carry

    lax.fori_loop(0, n_z, feed, 0)

    def norm_two_back(i, carry):
        gain_sum, bias_sum = carry
        at = rows_of(i)
        alive = live_of(i)
        mid = middle[at, :]
        block_out[at, :] = (mid + alive * (acc_out[at, :] + vec24[7:8, :])).astype(BF16)
        normed, scale = norm_parts(mid)
        e = acc_grad[at, :]
        scaled = e * vec24[4:5, :]
        inner_part = scaled - jnp.mean(scaled, axis=-1, keepdims=True) - normed * jnp.mean(scaled * normed, axis=-1, keepdims=True)
        grad_mid = cot[at, :].astype(F32) + inner_part * scale
        acc_grad[at, :] = grad_mid
        g2[at, :] = (alive * grad_mid).astype(BF16)
        return (gain_sum + fold_rows(e * normed), bias_sum + fold_rows(e))

    zero = jnp.zeros((8, width), F32)
    block_out = act
    point("ba")
    carry = lax.fori_loop(0, chunks // 2, norm_two_back, (zero, zero))
    point("bb")
    gain_sum, bias_sum = lax.fori_loop(chunks // 2, chunks, norm_two_back, carry)
    sums[0, 4:5, :] = jnp.sum(gain_sum, axis=0, keepdims=True)
    sums[0, 5:6, :] = jnp.sum(bias_sum, axis=0, keepdims=True)
    sums[0, 3:4, :] = column_sums(g2[...])[0:1]
    out_copy = pltpu.make_async_copy(block_out, out_ref, local.at[0])
    out_copy.start()

    point("og")
    store_rows(3, att_t, g2[...])
    point("ga")
    grad_att = n2
    grad_att[...] = nt_dot(g2[...], weights[3]).astype(BF16)

    def attend_back(p, carry):
        group, (at_q, at_k, at_v) = places(p)
        points_at(p, [f"a{k}" for k in range(pairs)])
        keys = qkv[group, :, at_k]
        values = qkv[group, :, at_v]
        queries = qkv[group, :, at_q] * 0.125
        grads = grad_att[:, rows_of(p, 128)]
        keys_t = keys.T
        grad_keys = jnp.zeros((count, 128), F32)
        grad_values = jnp.zeros((count, 128), F32)
        for head in range(2):
            my_queries, my_grads = one_head(queries, head), one_head(grads, head)
            for part in range(parts):
                span = slice(part * q_block, (part + 1) * q_block)
                scores = nt_dot(keys, my_queries[span]) + bias[:, span]
                chances = jnp.exp(scores - lse[p, head : head + 1, span])
                slopes = nt_dot(values, my_grads[span])
                level = jnp.sum(chances * slopes, axis=0, keepdims=True)
                grad_scores = (chances * (slopes - level)).astype(BF16)
                grad_values += nn_dot(chances.astype(BF16), my_grads[span])
                grad_keys += nn_dot(grad_scores, my_queries[span])
                dq_t[64 * head : 64 * head + 64, span] = nn_dot(keys_t[64 * head : 64 * head + 64], grad_scores) * 0.125
        qkv[group, :, at_q] = dq_t[...].T.astype(BF16)
        qkv[group, :, at_k] = grad_keys.astype(BF16)
        qkv[group, :, at_v] = grad_values.astype(BF16)
        points_at(p, [f"H{k // per_group}" if k % per_group == per_group - 1 else "" for k in range(pairs)])

        @pl.when(lax.rem(p, per_group) == per_group - 1)
        def _():
            store_rows(group, n1t, qkv[group])
            group_sums[group] = column_sums(qkv[group])

        return carry

    lax.fori_loop(0, pairs, attend_back, 0)

    point("g2")
    pre[...] = nt_dot(qkv[2], weights[2])
    point("g1")
    pre[...] += nt_dot(qkv[1], weights[1])
    point("g0")
    pre[...] += nt_dot(qkv[0], weights[0])

    def norm_one_back(i, carry):
        gain_sum, bias_sum = carry
        at = rows_of(i)
        normed, scale = norm_parts(tok[at, :].astype(F32))
        e = pre[at, :]
        scaled = e * vec24[0:1, :]
        inner_part = scaled - jnp.mean(scaled, axis=-1, keepdims=True) - normed * jnp.mean(scaled * normed, axis=-1, keepdims=True)
        acc_grad[at, :] = acc_grad[at, :] + inner_part * scale
        return (gain_sum + fold_rows(e * normed), bias_sum + fold_rows(e))

    point("na")
    carry = lax.fori_loop(0, chunks // 2, norm_one_back, (zero, zero))
    point("nb")
    gain_sum, bias_sum = lax.fori_loop(chunks // 2, chunks, norm_one_back, carry)
    tgrad_copy = pltpu.make_async_copy(acc_grad, tgrad_ref, local.at[1])
    tgrad_copy.start()
    sums[0, 0:1, :] = jnp.sum(gain_sum, axis=0, keepdims=True)
    sums[0, 1:2, :] = jnp.sum(bias_sum, axis=0, keepdims=True)
    for g in range(3):
        span = slice(g * third, (g + 1) * third)
        sums[1, 2:3, span] = group_sums[g, 0:1, :third]
        sums[2, 2:3, span] = group_sums[g, 0:1, 2 * third :]
    point("gb")
    gsmalls[...] = gather_back(sums[0], 24).reshape(gsmalls.shape)
    for k in range(2):
        part = gather_back(sums[1 + k], 48)
        span = slice(k * n_z // 2, (k + 1) * n_z // 2)
        gsmalls[span] = gsmalls[span] + part.reshape(n_z // 2, 2, 2, 2, 8, 128)
    for k in range(n_z):
        gsmalls[k] = gsmalls[k] + gather_back(up_sums[k], 96).reshape(2, 2, 2, 8, 128)

    point("end")
    do_all(last_copies, "start")
    for name, unit in units.items():
        if name[0] == "r":
            rs_sent(unit)
    out_copy.wait()
    tgrad_copy.wait()
    do_all(last_copies, "wait")


def by_kernel(
    n_z, tokens, cotangent, clip_lengths, ln1_gain, ln1_bias, qkv_weight, qv_bias, out_weight, out_bias,
    ln2_gain, ln2_bias, up_weight, up_bias, down_weight, down_bias,
):
    count, width = tokens.shape
    size, deep = qkv_weight.shape[0], down_weight.shape[0]
    blocks = 4 + n_z
    vectors = (ln1_gain, ln1_bias, qv_bias, out_bias, ln2_gain, ln2_bias, up_bias, down_bias)
    vmem, dma = pltpu.VMEM, pltpu.SemaphoreType.DMA
    held = [
        vmem((blocks, n_z, 2, 2, 2, size, width), BF16),
        vmem((n_z, 2, 2, 2, deep, width), BF16),
        vmem((n_z, 2, 2, 2, 8, 128), F32),
        vmem((n_z, 2, 2, 2, 8, 128), F32),
        vmem((4, width, width), BF16),
        vmem((width, width), BF16),
        vmem((blocks, n_z, 2, 2, size, width), BF16),
        vmem((blocks - len(LATE_SUMS), 2, n_z, size, width // 2), BF16),
        vmem((blocks - len(LATE_SUMS), 2, n_z, size, width), BF16),
        vmem((blocks - len(LATE_SUMS), n_z, size, width), BF16),
        vmem((max(len(LATE_SUMS), 1), 2, size, width // 2), BF16),
        vmem((max(len(LATE_SUMS), 1), 2, size, width), BF16),
        vmem((max(len(LATE_SUMS), 1), n_z, 2, 2, size, width), BF16),
        vmem((n_z, 2, 2, deep, width), BF16),
        vmem((n_z, 2, deep, width // 2), BF16),
        vmem((n_z, 2, deep, width), BF16),
        vmem((n_z, deep, width), BF16),
        vmem((n_z, 2, 2, 8, 128), F32),
        vmem((n_z, 8, 128), F32),
        vmem((2, n_z, 8, 128), F32),
        vmem((n_z - 1, 8, 128), F32),
        vmem((3, count, width), BF16),
        vmem((width, count), BF16),
        vmem((count, width), BF16),
        vmem((width, count), BF16),
        vmem((count, width), F32),
        vmem((count, width), BF16),
        vmem((width, count), BF16),
        vmem((count, width), BF16),
        vmem((count, width), F32),
        vmem((count, width), F32),
        vmem((count, width), BF16),
        vmem((count, width), BF16),
        vmem((count, width), F32),
        vmem((count, width), F32),
        vmem((count, width), BF16),
        vmem((count, width), BF16),
        vmem((count, count), F32),
        vmem((width // 128, 2, count), F32),
        vmem((128, count), F32),
        vmem((8, width), F32),
        vmem((2, 8, width), F32),
        vmem((n_z, 8, width), F32),
        vmem((3, 8, width), F32),
        vmem((3, 8, width), F32),
        vmem((3, 8, width), F32),
        vmem((n_z, 8, width), F32),
        vmem(qkv_weight.shape, F32),
        vmem(out_weight.shape, F32),
        vmem(up_weight.shape, F32),
        vmem(down_weight.shape, F32),
        vmem((8, 128), F32),
        dma((semaphore_slots()[2],)),
        dma((len(semaphore_slots()[0]),)),
        dma((len(semaphore_slots()[1]),)),
        dma((13 + n_z,)),
    ]
    anywhere, whole = pl.BlockSpec(memory_space=pl.ANY), pl.BlockSpec(memory_space=pltpu.VMEM)
    shape = jax.ShapeDtypeStruct
    out, grad, g_qkv, g_out, g_up, g_down, g_small = pl.pallas_call(
        layer_kernel,
        out_shape=(
            shape((count, width), BF16),
            shape((count, width), F32),
            shape(qkv_weight.shape, F32),
            shape(out_weight.shape, F32),
            shape(up_weight.shape, F32),
            shape(down_weight.shape, F32),
            shape((8, 128), F32),
        ),
        in_specs=[pl.BlockSpec(memory_space=pltpu.SMEM)] + [anywhere] * 2 + [whole] * 8 + [anywhere] * 4,
        out_specs=(anywhere,) * 7,
        scratch_shapes=held,
        compiler_params=pltpu.CompilerParams(collective_id=0, has_side_effects=True, vmem_limit_bytes=VMEM_BYTES),
    )(clip_lengths, tokens, cotangent, *vectors, qkv_weight, out_weight, up_weight, down_weight)
    large = (out, grad, g_qkv, g_out, g_up, g_down)
    done = pl.pallas_call(
        hand_over,
        out_shape=tuple(shape(a.shape, a.dtype) for a in large) + tuple(shape(v.shape, F32) for v in vectors),
        in_specs=[anywhere] * (1 + len(large)),
        out_specs=(anywhere,) * (len(large) + len(vectors)),
        scratch_shapes=[vmem(a.shape, a.dtype) for a in (g_small, *large)] + [vmem(v.shape, F32) for v in vectors] + [dma((2, 24))],
    )(g_small, *large)
    out, grad, g_qkv, g_out, g_up, g_down = done[:6]
    parts = done[6:]
    return (out, grad, parts[0], parts[1], g_qkv, parts[2], g_out, parts[3], parts[4], parts[5], g_up, parts[6], g_down, parts[7])


def hand_over(*refs):
    small_ref, sources, targets, vectors = refs[0], refs[1:7], refs[7:13], refs[13:21]
    small, held, cut, sems = refs[21], refs[22:28], refs[28:36], refs[36]
    small_copy = pltpu.make_async_copy(small_ref, small, sems.at[0, 23])
    small_copy.start()
    pieces = []
    for src, mid, dst in zip(sources, held, targets):
        rows = src.shape[0]
        parts = 4 if rows % 64 == 0 else 1
        for k in range(parts):
            pieces.append([ref.at[pl.ds(k * (rows // parts), rows // parts)] for ref in (src, mid, dst)])
    inward = [pltpu.make_async_copy(src, mid, sems.at[0, k]) for k, (src, mid, _) in enumerate(pieces)]
    outward = [pltpu.make_async_copy(mid, dst, sems.at[1, k]) for k, (_, mid, dst) in enumerate(pieces)]
    for copy in inward:
        copy.start()
    small_copy.wait()
    cuts = []
    for k, (part, vector) in enumerate(zip(cut, vectors)):
        part[...] = small[k, 0 : part.shape[0]]
        cuts.append(pltpu.make_async_copy(part, vector, sems.at[1, 15 + k]))
        cuts[-1].start()
    for arrived, onward in zip(inward, outward):
        arrived.wait()
        onward.start()
    for copy in outward + cuts:
        copy.wait()


KINDS = {
    "ab0": "boot",
    "ab1": "boot",
    "ab2": "boot",
    "ab3": "boot",
    "au0": "late",
    "au1": "boot",
    "au2": "boot",
    "au3": "late",
    "ro": "direct",
    "ru0": "late",
    "ru1": "late",
    "ru3": "late",
}
LATE_SUMS = ("ru0", "ru1", "ru3")
TABLE = {
    "mask": (("aS", 0), ("ab0", 0), ("ab0", 1), ("au1", 0), ("ab3", 0),),
    "vec": (("au1", 1), ("ab2", 0), ("ab1", 0), ("au2", 0), ("aS", 1), ("ab0", 2), ("ab3", 1), ("au3", 0), ("ab0", 3), ("aS", 2), ("au1", 2), ("ab1", 1), ("au0", 0), ("au3", 1), ("au1", 3), ("aS", 3), ("ab0", 4), ("ab2", 1), ("aS", 4),),
    "turn": (("au0", 1), ("ab3", 2),),
    "q0": (("ab3", 3), ("adp", 0), ("au1", 4), ("ab0", 5), ("ab2", 2), ("ab0", 6), ("ab1", 2),),
    "t0": (("ab1", 3),),
    "q1": (("au1", 5), ("ab3", 4), ("ab2", 3), ("au1", 6), ("adp", 1), ("au0", 2), ("ab1", 4), ("ab3", 5), ("ab3", 6), ("ab2", 4), ("ab1", 5), ("adp", 2), ("ad0", 0), ("ab1", 6),),
    "t2": (("ab2", 5), ("ad1", 0),),
    "t3": (("au0", 3), ("ab2", 6),),
    "q2": (("ad2", 0), ("au2", 1),),
    "tb": (("ad0", 1), ("au3", 2),),
    "n2a": (("au0", 4), ("ad1", 1),),
    "fa0": (("au0", 5), ("ad2", 1),),
    "fc0": (("au2", 2), ("ad0", 2), ("au2", 3), ("ad0", 3), ("ad1", 2),),
    "ff0": (("ad2", 2), ("ad3", 0), ("ad1", 3), ("au3", 3),),
    "fi0": (("ru0", 0), ("ad2", 3), ("au2", 4),),
    "fa1": (("rd0", 0),),
    "fc1": (("ru0", 1),),
    "fe1": (("rd0", 1), ("ad3", 1),),
    "ff1": (("au3", 4),),
    "fg1": (("au2", 5),),
    "fi1": (("ru1", 0), ("au3", 5),),
    "fa2": (("rd1", 0), ("au2", 6), ("rd0", 2), ("ru0", 2),),
    "fe2": (("rd1", 1), ("ad3", 2),),
    "fg2": (("ad3", 3),),
    "fi2": (("ru2", 0), ("ru1", 1),),
    "fa3": (("rd0", 3), ("rd2", 0),),
    "fb3": (("ru2", 1),),
    "fc3": (("rd1", 2),),
    "fg3": (("rd2", 1), ("ru1", 2),),
    "fi3": (("ru2", 2), ("ru3", 0),),
    "ba": (("rd3", 0),),
    "og": (("rd1", 3),),
    "ga": (("rd3", 1), ("ro", 0), ("ru3", 1),),
    "a0": (("rd2", 2),),
    "H0": (("ru2", 3), ("ru1", 3), ("rd3", 2), ("ru3", 2),),
    "a2": (("rh0", 0),),
    "a3": (("rh0", 1), ("rd2", 3), ("ru1", 4),),
    "H1": (("ru2", 4), ("rd3", 3), ("ro", 1), ("ru0", 3),),
    "a4": (("rdl", 0), ("rh0", 2), ("rh1", 0),),
    "a5": (("rh1", 1),),
    "H2": (("ro", 2), ("rdl", 1),),
    "g2": (("rh2", 0),),
    "g0": (("rh2", 1),),
    "na": (("rh1", 2),),
    "nb": (("rh0", 3),),
    "end": (("ru2", 5), ("ru1", 5), ("rS", 0), ("rh0", 4), ("rh2", 2), ("ro", 3), ("rdl", 2), ("rS", 1), ("ru0", 4), ("rh1", 3), ("ru3", 3), ("rh0", 5), ("rh1", 4), ("rh2", 3), ("rS", 2), ("ru0", 5), ("ru3", 4), ("ro", 4), ("rS", 3), ("rh2", 4), ("rh1", 5), ("ru3", 5), ("rS", 4), ("rh2", 5),),
}

ROW_SUMS = ("rh0", "rh1", "rh2", "ro", "ru0", "ru1", "ru2", "ru3")
VMEM_BYTES = 63 * 1024 * 1024


def kernel_fits(n_wide, n_narrow, tokens, qkv_weight, up_weight, down_weight):
    width, hidden = qkv_weight.shape[0], up_weight.shape[1]
    n_z = n_wide // 4
    devices = n_wide * n_narrow
    return (
        n_narrow == 2
        and n_wide == 4 * n_z
        and n_z == 4
        and hidden == n_z * width
        and width % (8 * devices) == 0
        and hidden % (16 * devices) == 0
        and 2 * width // devices <= 128
        and hidden // devices <= 128
        and width // devices == 24
        and (tokens.shape[0] // devices) % (2 * CHUNK) == 0
    )


def solution(mesh):
    n_wide, n_narrow = mesh.shape["wide"], mesh.shape["narrow"]
    both = ("wide", "narrow")
    matrix, vector = P(both, None), P(both)
    in_specs = (
        matrix, matrix, matrix, vector, vector, matrix, vector, matrix, vector, vector, vector, matrix, vector, matrix, vector,
    )
    out_specs = (
        matrix, matrix, vector, vector, matrix, vector, matrix, vector, vector, vector, matrix, vector, matrix, vector,
    )

    def run(*arrays):
        fits = kernel_fits(n_wide, n_narrow, arrays[0], arrays[5], arrays[11], arrays[13])
        body = functools.partial(by_kernel, n_wide // 4) if fits else by_collectives
        return jax.shard_map(body, mesh=mesh, in_specs=in_specs, out_specs=out_specs, check_vma=False)(*arrays)

    return run
```

```python
import functools
import math

import jax
import jax.numpy as jnp
from jax import lax
from jax.experimental import pallas as pl
from jax.experimental.pallas import tpu as pltpu
from jax.sharding import PartitionSpec as P

H = 12
MASKED_SCORE = -1000000000.0
MESH = pl.DeviceIdType.MESH
F32 = jnp.float32
BF16 = jnp.bfloat16
ALL = slice(None)
CHUNK = 256


def layer_norm(inputs, ln_gain, ln_bias):
    row_mean = jnp.mean(inputs, axis=-1, keepdims=True)
    centred = inputs - row_mean
    spread = jnp.mean(centred * centred, axis=-1, keepdims=True)
    return centred * lax.rsqrt(spread + 1e-06) * ln_gain + ln_bias


def gelu_exact(inputs):
    return 0.5 * inputs * (1.0 + lax.erf(inputs * 0.7071067811865476))


def clip_index(lengths, row_count):
    clip_ends = jnp.cumsum(lengths)
    position = jnp.arange(row_count, dtype=jnp.int32)
    return jnp.sum((position[:, None] >= clip_ends[None, :]).astype(jnp.int32), axis=1)


def split_heads(matrix, head_count):
    row_count = matrix.shape[0]
    return matrix.reshape(row_count, head_count, -1).transpose(1, 0, 2)


def join_heads(stacked):
    head_count, row_count, head_size = stacked.shape
    return stacked.transpose(1, 0, 2).reshape(row_count, head_count * head_size)


def attend_forward(queries, key_rows, value_rows, segment, block_rows, score_scale):
    scores = (
        lax.dot_general(
            queries, key_rows, (((1,), (1,)), ((), ())), preferred_element_type=jnp.float32
        )
        * score_scale
    )
    allowed = segment[0:block_rows, None] == segment[None, :]
    scores = jnp.where(allowed, scores, MASKED_SCORE)
    highest = jnp.max(scores, axis=1, keepdims=True)
    raised = jnp.exp(scores - highest)
    denominator = jnp.sum(raised, axis=1, keepdims=True)
    softmax = (raised / denominator).astype(jnp.bfloat16)
    outputs = [jnp.dot(softmax, value_rows, preferred_element_type=jnp.float32)]
    totals = [highest + jnp.log(denominator)]
    return (jnp.concatenate(outputs, 0), jnp.concatenate(totals, 0))


def attend_backward(
    queries, key_rows, value_rows, segment, grad_out, lse_rows, block_rows, score_scale
):
    grad_keys = jnp.zeros(key_rows.shape, jnp.float32)
    grad_values = jnp.zeros(value_rows.shape, jnp.float32)
    g_rows = grad_out[0:block_rows]
    scores = (
        lax.dot_general(
            queries, key_rows, (((1,), (1,)), ((), ())), preferred_element_type=jnp.float32
        )
        * score_scale
    )
    allowed = segment[0:block_rows, None] == segment[None, :]
    softmax = jnp.where(allowed, jnp.exp(scores - lse_rows[0:block_rows]), 0.0)
    grad_values = grad_values + lax.dot_general(
        softmax.astype(jnp.bfloat16),
        g_rows,
        (((0,), (0,)), ((), ())),
        preferred_element_type=jnp.float32,
    )
    grad_probs = lax.dot_general(
        g_rows, value_rows, (((1,), (1,)), ((), ())), preferred_element_type=jnp.float32
    )
    grad_scores = (
        softmax * (grad_probs - jnp.sum(softmax * grad_probs, axis=1, keepdims=True))
    ).astype(jnp.bfloat16)
    grad_queries = [
        jnp.dot(grad_scores, key_rows, preferred_element_type=jnp.float32) * score_scale
    ]
    grad_keys = (
        grad_keys
        + lax.dot_general(
            grad_scores, queries, (((0,), (0,)), ((), ())), preferred_element_type=jnp.float32
        )
        * score_scale
    )
    return (jnp.concatenate(grad_queries, 0), grad_keys, grad_values)


def by_collectives(
    tokens,
    cotangent,
    clip_lengths,
    ln1_gain,
    ln1_bias,
    qkv_weight,
    qv_bias,
    out_weight,
    out_bias,
    ln2_gain,
    ln2_bias,
    up_weight,
    up_bias,
    down_weight,
    down_bias,
):
    gathered = (
        lax.all_gather(ln1_gain, ("wide", "narrow"), axis=0, tiled=True),
        lax.all_gather(ln1_bias, ("wide", "narrow"), axis=0, tiled=True),
        lax.all_gather(qkv_weight, ("wide", "narrow"), axis=0, tiled=True),
        lax.all_gather(qv_bias, ("wide", "narrow"), axis=0, tiled=True),
        lax.all_gather(out_weight, ("wide", "narrow"), axis=0, tiled=True),
        lax.all_gather(out_bias, ("wide", "narrow"), axis=0, tiled=True),
        lax.all_gather(ln2_gain, ("wide", "narrow"), axis=0, tiled=True),
        lax.all_gather(ln2_bias, ("wide", "narrow"), axis=0, tiled=True),
        lax.all_gather(up_weight, ("wide", "narrow"), axis=0, tiled=True),
        lax.all_gather(up_bias, ("wide", "narrow"), axis=0, tiled=True),
        lax.all_gather(down_weight, ("wide", "narrow"), axis=0, tiled=True),
        lax.all_gather(down_bias, ("wide", "narrow"), axis=0, tiled=True),
    )
    (
        gain_one,
        bias_one,
        merged_weight,
        merged_bias,
        proj_weight,
        proj_bias,
        gain_two,
        bias_two,
        w_up,
        b_up,
        w_down,
        b_down,
    ) = gathered
    inputs = tokens.astype(jnp.float32)
    row_count, model_width = inputs.shape
    head_size = model_width // H
    score_scale = 1.0 / math.sqrt(head_size)
    block_rows = min(512, row_count)
    clip_count = clip_lengths.shape[1]
    segment = clip_index(clip_lengths[0], row_count)
    live_rows = (segment < clip_count).astype(jnp.float32)[:, None]
    normed_one = layer_norm(
        inputs, gain_one.astype(jnp.float32), bias_one.astype(jnp.float32)
    ).astype(jnp.bfloat16)
    bias_float = merged_bias.astype(jnp.float32)
    full_bias = jnp.concatenate(
        [bias_float[:model_width], jnp.zeros((model_width,), jnp.float32), bias_float[model_width:]]
    )
    merged_rows = (
        jnp.dot(normed_one, merged_weight, preferred_element_type=jnp.float32) + full_bias
    ).astype(jnp.bfloat16)
    q_heads = split_heads(merged_rows[:, :model_width], H)
    k_heads = split_heads(merged_rows[:, model_width : 2 * model_width], H)
    v_heads = split_heads(merged_rows[:, 2 * model_width :], H)

    def head_forward(triple):
        return attend_forward(triple[0], triple[1], triple[2], segment, block_rows, score_scale)

    att_heads, lse_heads = lax.map(head_forward, (q_heads, k_heads, v_heads))
    attended = join_heads(att_heads).astype(jnp.bfloat16)
    branch_one = jnp.dot(
        attended, proj_weight, preferred_element_type=jnp.float32
    ) + proj_bias.astype(jnp.float32)
    middle = inputs + live_rows * branch_one
    normed_two = layer_norm(
        middle, gain_two.astype(jnp.float32), bias_two.astype(jnp.float32)
    ).astype(jnp.bfloat16)
    hidden_pre = jnp.dot(normed_two, w_up, preferred_element_type=jnp.float32) + b_up.astype(
        jnp.float32
    )
    activated, gelu_pull = jax.vjp(gelu_exact, hidden_pre)
    activated = activated.astype(jnp.bfloat16)
    branch_two = jnp.dot(activated, w_down, preferred_element_type=jnp.float32) + b_down.astype(
        jnp.float32
    )
    block_out = (middle + live_rows * branch_two).astype(jnp.bfloat16)
    back_gain_one, back_merged, back_proj, back_gain_two, back_up, back_down = (
        lax.all_gather(ln1_gain, ("wide", "narrow"), axis=0, tiled=True),
        lax.all_gather(qkv_weight, ("wide", "narrow"), axis=0, tiled=True),
        lax.all_gather(out_weight, ("wide", "narrow"), axis=0, tiled=True),
        lax.all_gather(ln2_gain, ("wide", "narrow"), axis=0, tiled=True),
        lax.all_gather(up_weight, ("wide", "narrow"), axis=0, tiled=True),
        lax.all_gather(down_weight, ("wide", "narrow"), axis=0, tiled=True),
    )
    upstream = cotangent.astype(jnp.float32)
    grad_two = (live_rows * upstream).astype(jnp.bfloat16)
    grad_b_down = jnp.sum(grad_two.astype(jnp.float32), axis=0)
    grad_w_down = jnp.einsum("tf,td->fd", activated, grad_two, preferred_element_type=jnp.float32)
    grad_act = jnp.einsum("td,fd->tf", grad_two, back_down, preferred_element_type=jnp.float32)
    grad_hidden = gelu_pull(grad_act)[0].astype(jnp.bfloat16)
    grad_b_up = jnp.sum(grad_hidden.astype(jnp.float32), axis=0)
    grad_w_up = jnp.einsum("td,tf->df", normed_two, grad_hidden, preferred_element_type=jnp.float32)
    grad_normed_two = jnp.einsum(
        "tf,df->td", grad_hidden, back_up, preferred_element_type=jnp.float32
    )
    _, norm_pull_two = jax.vjp(
        layer_norm, middle, back_gain_two.astype(jnp.float32), bias_two.astype(jnp.float32)
    )
    grad_middle_norm, grad_gain_two, grad_bias_two = norm_pull_two(grad_normed_two)
    grad_middle = upstream + grad_middle_norm
    grad_one = (live_rows * grad_middle).astype(jnp.bfloat16)
    grad_b_proj = jnp.sum(grad_one.astype(jnp.float32), axis=0)
    grad_w_proj = jnp.einsum("te,td->ed", attended, grad_one, preferred_element_type=jnp.float32)
    grad_att = jnp.einsum(
        "td,ed->te", grad_one, back_proj, preferred_element_type=jnp.float32
    ).astype(jnp.bfloat16)
    grad_att_heads = split_heads(grad_att, H)

    def head_backward(members):
        return attend_backward(
            members[0],
            members[1],
            members[2],
            segment,
            members[3],
            members[4],
            block_rows,
            score_scale,
        )

    grad_q, grad_k, grad_v = lax.map(
        head_backward, (q_heads, k_heads, v_heads, grad_att_heads, lse_heads)
    )
    grad_merged = jnp.concatenate(
        [join_heads(grad_q), join_heads(grad_k), join_heads(grad_v)], 1
    ).astype(jnp.bfloat16)
    column_sums = jnp.sum(grad_merged.astype(jnp.float32), axis=0)
    grad_merged_bias = jnp.concatenate([column_sums[:model_width], column_sums[2 * model_width :]])
    grad_w_merged = jnp.einsum(
        "te,tf->ef", normed_one, grad_merged, preferred_element_type=jnp.float32
    )
    grad_normed_one = jnp.einsum(
        "tf,ef->te", grad_merged, back_merged, preferred_element_type=jnp.float32
    )
    _, norm_pull_one = jax.vjp(
        layer_norm, inputs, back_gain_one.astype(jnp.float32), bias_one.astype(jnp.float32)
    )
    grad_input_norm, grad_gain_one, grad_bias_one = norm_pull_one(grad_normed_one)
    tokens_grad = grad_middle + grad_input_norm
    shares = (
        lax.psum_scatter(grad_gain_one, ("wide", "narrow"), scatter_dimension=0, tiled=True),
        lax.psum_scatter(grad_bias_one, ("wide", "narrow"), scatter_dimension=0, tiled=True),
        lax.psum_scatter(grad_w_merged, ("wide", "narrow"), scatter_dimension=0, tiled=True),
        lax.psum_scatter(grad_merged_bias, ("wide", "narrow"), scatter_dimension=0, tiled=True),
        lax.psum_scatter(grad_w_proj, ("wide", "narrow"), scatter_dimension=0, tiled=True),
        lax.psum_scatter(grad_b_proj, ("wide", "narrow"), scatter_dimension=0, tiled=True),
        lax.psum_scatter(grad_gain_two, ("wide", "narrow"), scatter_dimension=0, tiled=True),
        lax.psum_scatter(grad_bias_two, ("wide", "narrow"), scatter_dimension=0, tiled=True),
        lax.psum_scatter(grad_w_up, ("wide", "narrow"), scatter_dimension=0, tiled=True),
        lax.psum_scatter(grad_b_up, ("wide", "narrow"), scatter_dimension=0, tiled=True),
        lax.psum_scatter(grad_w_down, ("wide", "narrow"), scatter_dimension=0, tiled=True),
        lax.psum_scatter(grad_b_down, ("wide", "narrow"), scatter_dimension=0, tiled=True),
    )
    return (
        block_out,
        tokens_grad,
        shares[0],
        shares[1],
        shares[2],
        shares[3],
        shares[4],
        shares[5],
        shares[6],
        shares[7],
        shares[8],
        shares[9],
        shares[10],
        shares[11],
    )


def nt_dot(left, right):
    return lax.dot_general(left, right, (((1,), (1,)), ((), ())), preferred_element_type=F32)


def nn_dot(left, right):
    return jnp.dot(left, right, preferred_element_type=F32)


def rows_of(step, size=CHUNK):
    return pl.ds(pl.multiple_of(step * size, size), size)


def norm_parts(values):
    centred = values - jnp.mean(values, axis=-1, keepdims=True)
    scale = lax.rsqrt(jnp.mean(centred * centred, axis=-1, keepdims=True) + 1e-06)
    return centred * scale, scale


def fold_rows(values):
    return jnp.sum(values.reshape(-1, 8, values.shape[-1]), axis=0)


def gelu_both(u):
    tail = 0.5 * (1.0 + lax.erf(u * 0.7071067811865476))
    return u * tail, tail + u * jnp.exp(-0.5 * u * u) * 0.3989422804014327


def spread_maps(width, columns):
    column = lax.broadcasted_iota(jnp.int32, (1, columns), 1).astype(F32)
    group = jnp.floor((column + 0.5) * (1.0 / width))
    place = column - group * width
    lane = lax.broadcasted_iota(jnp.int32, (128, columns), 0).astype(F32)
    picks = jnp.where(lane == place, 1.0, 0.0).astype(BF16)
    owners = columns // width
    owner = lax.broadcasted_iota(jnp.int32, (owners, 8, columns), 0).astype(F32)
    mine = owner == group.reshape(1, 1, columns)
    return picks, mine


def spread(pieces, width, columns):
    picks, mine = spread_maps(width, columns)
    wide_rows = nn_dot(pieces.reshape(-1, 128).astype(BF16), picks)
    return jnp.sum(jnp.where(mine, wide_rows.reshape(-1, 8, columns), 0.0), axis=0)


def gather_back(vectors, width):
    columns = vectors.shape[-1]
    picks, mine = spread_maps(width, columns)
    rest = jnp.where(mine, vectors[None], 0.0).reshape(-1, columns)
    total = None
    for _ in range(3):
        part = rest.astype(BF16)
        rest = rest - part.astype(F32)
        term = nt_dot(part, picks)
        total = term if total is None else total + term
    return total.reshape(-1, 8, 128)


Z0, Z1, Z2, ZR, X0, Y0, X1, Y1, X2, Y2, DX, DY, C0 = range(13)
ORDERS = {
    "plain": ("z", "relay", "near", "across", "core"),
    "direct": ("zd", "near", "across", "core"),
    "boot": ("own", "zd", "pair", "rest", "across", "core"),
    "late": ("near", "across", "z", "relay", "core"),
    "late direct": ("near", "across", "zd", "core"),
}
BACK = {
    "plain": ("core", "across", "near", "z", "z far"),
    "direct": ("core", "across", "near", "zd"),
    "late": ("core", "z", "z far", "across", "near"),
    "late direct": ("core", "zd", "across", "near"),
}


def phases_of(name):
    kind = "direct" if name[1:] == "S" else KINDS.get(name, "plain")
    if name[:2] == "ad":
        return (("z", "relay") if kind == "plain" else ("zd",)) if name == "adp" else ("near", "across", "core")
    if name[:2] == "rd":
        return (("z", "z far") if kind == "plain" else ("zd",)) if name == "rdl" else ("core", "across", "near")
    return (ORDERS if name[0] == "a" else BACK)[kind]


def semaphore_slots():
    used = {
        "z": (Z0, Z1, Z2), "relay": (ZR,), "zd": (Z0, Z1, Z2), "own": (X1, Y1), "pair": (X2, Y2), "rest": (X0, Y0),
        "near": (X0, Y0), "across": (DX, DY), "core": (C0,), "z far": (ZR, Z1),
    }
    gathers = ["aS", "ab0", "ab1", "ab2", "ab3", "adp", "au0", "ad0", "au1", "ad1", "au2", "ad2", "au3", "ad3"]
    sums = ["ru0", "rd0", "ru1", "rd1", "ru2", "rd2", "ru3", "rd3", "ro", "rdl", "rh0", "rh1", "rh2", "rS"]
    slots = []
    for names in (gathers, sums):
        places = {}
        for name in names:
            for sem in sorted({sem for phase in phases_of(name) for sem in used[phase]}):
                places[name, sem] = len(places)
        slots.append(places)
    return slots[0], slots[1], max(len(slots[0]), len(slots[1])), len(slots[0])


def layer_kernel(
    clip_ref, tok_ref, cot_ref, v0, v1, v2, v3, v4, v5, v6, v7, wqkv_ref, wout_ref, wup_ref, wdown_ref,
    out_ref, tgrad_ref, gqkv_ref, gout_ref, gup_ref, gdown_ref, gsmall_ref,
    slabs, downs, smalls, gsmalls, weights, w_up,
    row_c, row_d, row_n, row_z, late_d, late_n, late_z, down_c, down_d, down_n, down_z, sm_c, sm_d, sm_n, sm_z,
    qkv, n1t, n1, att_t, middle, n2, n2t, g2, acc_out, acc_grad, act, grad_h, pre, grad_act,
    tok, cot, bias, lse, dq_t, vec24, vec48, vec96, merged_bias, group_sums, sums, up_sums, gqkv, gout, gup, gdown, gsmall,
    sends, ag_recv, rs_recv, local,
):
    n_z, width = slabs.shape[1], slabs.shape[-1]
    count = tok.shape[0]
    pairs = width // 128
    chunks = count // CHUNK
    wide_at, y = lax.axis_index("wide"), lax.axis_index("narrow")
    core = lax.rem(wide_at, 2)
    x = lax.rem(lax.div(wide_at, 2), 2)
    z = lax.div(wide_at, 4)

    def device(z_at, x_at, c_at, y_at):
        return ((z_at * 2 + x_at) * 2 + c_at, y_at)

    def row_view(block):
        def view(at):
            return slabs.at[(block, *at)]
        return view

    def down_view(tile):
        def view(at):
            return downs.at[(tile, *at[1:])]
        return view

    def small_view(ref):
        def view(at):
            return ref.at[at]
        return view

    def half_of(ref, side):
        if ref.shape[-1] < 2 * 128:
            return ref
        cut = ref.shape[-1] // 2
        return ref.at[(*([ALL] * (len(ref.shape) - 1)), pl.ds(side * cut, cut))]

    to_x, to_y, to_c = device(z, 1 - x, core, y), device(z, x, core, 1 - y), device(z, x, 1 - core, y)
    z_places = (z + 1 - 2 * lax.rem(z, 2), lax.rem(z + 2, n_z), n_z - 1 - z)
    along_z = [device(at, x, core, y) for at in z_places]
    other_pair = pl.ds(2 * (1 - lax.div(z, 2)), 2)
    inner = lax.rem(z + 1, n_z) >= 2

    ag_slots, rs_slots, _, _ = semaphore_slots()

    def remote(src, dst, sums, unit_name, sem, to, recv_sem=None):
        slots = rs_slots if sums else ag_slots
        recv = rs_recv if sums else ag_recv
        return pltpu.make_async_remote_copy(
            src_ref=src, dst_ref=dst, send_sem=sends.at[slots[unit_name, sem]],
            recv_sem=recv.at[slots[unit_name, sem if recv_sem is None else recv_sem]],
            device_id=to, device_id_type=MESH,
        )

    def do_all(copies, what):
        for copy in copies:
            getattr(copy, what)()

    one, plane = (x, core, y), (ALL, core, ALL)

    def ag_copies(unit, phase):
        view, row, phases, along = unit
        sems = False
        held = z if along is plane else ALL

        def both(at, sem):
            mine = view((at, x, core, y))
            return [remote(mine, mine, sems, row, sem, to_x), remote(mine, mine, sems, row, sem + 1, to_y)]

        def own_to(*which):
            own = view((z, *along))
            return [remote(own, own, sems, row, k, along_z[k]) for k in which]

        if phase == "z":
            return own_to(Z0, Z1)
        if phase == "zd":
            return own_to(Z0, Z1, Z2)
        if phase in ("z near", "z far", "z last"):
            return own_to(("z near", "z far", "z last").index(phase))
        if phase == "relay":
            passed = view((z_places[1], *along))
            return [remote(passed, passed, sems, row, ZR, along_z[0], Z2)]
        if phase == "own":
            return both(z, X1)
        if phase == "pair":
            return both(z_places[0], X2)
        if phase == "rest":
            return both(other_pair, X0)
        if phase == "near":
            return both(held, X0)
        if phase == "across":
            from_x, from_y = view((held, 1 - x, core, y)), view((held, x, core, 1 - y))
            first = half_of(from_x, 0)
            copies = [remote(first, first, sems, row, DY, to_y)]
            if from_x.shape[-1] >= 2 * 128:
                second = half_of(from_y, 1)
                copies.append(remote(second, second, sems, row, DX, to_x))
            return copies
        whole_plane = view((ALL, ALL, core, ALL))
        return [remote(whole_plane, whole_plane, sems, row, C0, to_c)]

    def ag_wait(unit, *phases):
        for phase in phases:
            do_all(ag_copies(unit, phase), "wait_recv")

    def ag_stage(unit, stage):
        phases = unit[2]
        phase = phases[stage] if stage < len(phases) else None
        if phase == "relay":
            @pl.when(inner)
            def _():
                ag_wait(unit, "z far")
                do_all(ag_copies(unit, "relay"), "start")
            return
        if phase == "pair":
            ag_wait(unit, "z near")
        elif phase == "rest":
            ag_wait(unit, "z far", "z last")
        elif phase == "across" and "own" in phases:
            ag_wait(unit, "own", "pair", "rest")
        elif stage > 0 and phases[stage - 1] == "relay":
            @pl.when(jnp.logical_not(inner))
            def _():
                ag_wait(unit, "z far")
            ag_wait(unit, "z near", "z last")
        elif stage > 0 and phases[stage - 1] != "own":
            ag_wait(unit, phases[stage - 1])
        if phase:
            do_all(ag_copies(unit, phase), "start")
            if phase == "z":
                @pl.when(inner)
                def _():
                    do_all(ag_copies(unit, "z last"), "start")
        else:
            for sent in phases:
                if sent != "relay":
                    do_all(ag_copies(unit, sent), "wait_send")
            if "relay" in phases:
                @pl.when(inner)
                def _():
                    do_all(ag_copies(unit, "z last") + ag_copies(unit, "relay"), "wait_send")

    def gather_unit(name, view):
        kind = KINDS.get(name, "plain")
        return (view, name, phases_of(name), plane if kind[:4] == "late" else one)

    units = {"aS": gather_unit("aS", small_view(smalls)), "adp": gather_unit("adp", lambda at: downs.at[at])}
    for block in range(4):
        units[f"ab{block}"] = gather_unit(f"ab{block}", row_view(block))
    for tile in range(n_z):
        units[f"au{tile}"] = gather_unit(f"au{tile}", row_view(4 + tile))
        units[f"ad{tile}"] = gather_unit(f"ad{tile}", down_view(tile))

    def rs_copies(unit, phase):
        view, row, phases, landing, along = unit
        sems = True
        held = z if along is plane else ALL
        if phase == "core":
            return [remote(view((ALL, ALL, 1 - core, ALL)), landing["core"], sems, row, C0, to_c)]
        if phase == "across":
            away = view((held, 1 - x, core, 1 - y))
            copies = [remote(half_of(away, 0), landing["dx"], sems, row, DX, to_x)]
            if away.shape[-1] >= 2 * 128:
                copies.append(remote(half_of(away, 1), landing["dy"], sems, row, DY, to_y))
            return copies
        if phase == "near":
            return [
                remote(view((held, 1 - x, core, y)), landing["x"], sems, row, X0, to_x),
                remote(view((held, x, core, 1 - y)), landing["y"], sems, row, Y0, to_y),
            ]
        if phase == "z outer":
            return [remote(view((z_places[2], *along)), landing["z"].at[ZR], sems, row, ZR, along_z[0])]
        which = {"z": (Z0,), "z far": (Z1,), "z last": (Z2,), "zd": (Z0, Z1, Z2)}[phase]
        return [remote(view((z_places[k], *along)), landing["z"].at[k], sems, row, k, along_z[k]) for k in which]

    def add_into(target, *sources):
        total = target[...].astype(F32)
        for source in sources:
            total = total + source[...].astype(F32)
        target[...] = total.astype(target.dtype)

    def add_all(target, *sources):
        free = len(target.shape) - 2
        if free == 0:
            add_into(target, *sources)
            return
        places = [()]
        for extent in target.shape[1:free]:
            places = [place + (k,) for place in places for k in range(extent)]

        def step(i, carry):
            for place in places:
                add_into(target.at[(i, *place)], *[source.at[(i, *place)] for source in sources])
            return carry

        lax.fori_loop(0, target.shape[0], step, 0)

    def rs_stage(unit, stage):
        view, _, phases, landing, along = unit
        held = z if along is plane else ALL
        before = phases[stage - 1] if stage > 0 else None
        phase = phases[stage] if stage < len(phases) else None
        if phase == "z far":
            @pl.when(inner)
            def _():
                do_all(rs_copies(unit, "z outer"), "wait_recv")
                add_all(view((z_places[1], *along)), landing["z"].at[ZR])
        elif before == "z far":
            rs_wait(unit, "z", "z far")
            add_all(view((z, *along)), landing["z"].at[Z0], landing["z"].at[Z1])

            @pl.when(inner)
            def _():
                rs_wait(unit, "z last")
                add_all(view((z, *along)), landing["z"].at[Z2])
        elif before:
            rs_wait(unit, before)
        if before == "core":
            add_all(view((ALL, ALL, core, ALL)), landing["core"])
        elif before == "across":
            on_y = view((held, x, core, 1 - y))
            add_all(half_of(on_y, 0), landing["dx"])
            if on_y.shape[-1] >= 2 * 128:
                add_all(half_of(view((held, 1 - x, core, y)), 1), landing["dy"])
        elif before == "near":
            add_all(view((held, x, core, y)), landing["x"], landing["y"])
        elif before == "zd":
            add_all(view((z, *along)), *[landing["z"].at[k] for k in (Z0, Z1, Z2)])
        if phase:
            do_all(rs_copies(unit, phase), "start")
        if phase == "z":
            @pl.when(inner)
            def _():
                do_all(rs_copies(unit, "z last"), "start")

            @pl.when(jnp.logical_not(inner))
            def _():
                do_all(rs_copies(unit, "z outer"), "start")

    def rs_wait(unit, *phases):
        for phase in phases:
            do_all(rs_copies(unit, phase), "wait_recv")

    def rs_end(unit, *results):
        view, _, phases, landing, along = unit
        last = phases[-1]
        if last == "near":
            sources = [landing["x"], landing["y"]]
        else:
            sources = [landing["z"].at[k] for k in ((Z0, Z1) if last == "z far" else (Z0, Z1, Z2))]
        rs_wait(unit, *(("z", "z far") if last == "z far" else (last,)))
        total = view((z, x, core, y))[...].astype(F32)
        for part in sources:
            total = total + part[...].astype(F32)
        size = total.shape[-1] // len(results)
        for k, result in enumerate(results):
            result[...] = total[:, k * size : (k + 1) * size]
        if last == "z far":
            @pl.when(inner)
            def _():
                rs_wait(unit, "z last")
                for k, result in enumerate(results):
                    result[...] += landing["z"][Z2, :, k * size : (k + 1) * size].astype(F32)

    def rs_sent(unit):
        for phase in unit[2]:
            do_all(rs_copies(unit, phase), "wait_send")
        if "z far" in unit[2]:
            @pl.when(inner)
            def _():
                do_all(rs_copies(unit, "z last"), "wait_send")

            @pl.when(jnp.logical_not(inner))
            def _():
                do_all(rs_copies(unit, "z outer"), "wait_send")

    def row_unit(block, name):
        if name in LATE_SUMS:
            late = LATE_SUMS.index(name)
            landing = {"core": row_c.at[block], "dx": late_d.at[late, 0], "dy": late_d.at[late, 1], "x": late_n.at[late, 0], "y": late_n.at[late, 1], "z": late_z.at[late]}
            return (row_view(block), name, phases_of(name), landing, plane)
        at = block - sum(earlier in LATE_SUMS for earlier in ROW_SUMS[:block])
        landing = {"core": row_c.at[block], "dx": row_d.at[at, 0], "dy": row_d.at[at, 1], "x": row_n.at[at, 0], "y": row_n.at[at, 1], "z": row_z.at[at]}
        return (row_view(block), name, phases_of(name), landing, one)

    def down_unit(tile, name):
        landing = {"core": down_c.at[tile], "dx": down_d.at[tile, 0], "dy": down_d.at[tile, 1], "x": down_n.at[tile, 0], "y": down_n.at[tile, 1]}
        return (down_view(tile), name, phases_of(name), landing, one)

    def block_columns(block):
        return pl.ds(block * width, width)

    third = width // 3
    results = {"rdl": [gdown], "ro": [gout], "rS": [gsmall]}
    for t in range(n_z):
        units[f"ru{t}"] = row_unit(4 + t, f"ru{t}")
        units[f"rd{t}"] = down_unit(t, f"rd{t}")
        results[f"ru{t}"] = [gup.at[:, block_columns(t)]]
    for g in range(3):
        units[f"rh{g}"] = row_unit(g, f"rh{g}")
        results[f"rh{g}"] = [gqkv.at[:, pl.ds(j * width + g * third, third)] for j in range(3)]
    units["ro"] = row_unit(3, "ro")
    small_landing = {"core": sm_c, "dx": sm_d, "x": sm_n.at[0], "y": sm_n.at[1], "z": sm_z}
    units["rS"] = (small_view(gsmalls), "rS", phases_of("rS"), small_landing, one)
    units["rdl"] = (lambda at: downs.at[at], "rdl", phases_of("rdl"), {"z": down_z}, one)
    whole_results = {"rdl": [gdown_ref], "ro": [gout_ref], "rS": [gsmall_ref]}
    for t in range(n_z):
        whole_results[f"ru{t}"] = [gup_ref.at[:, block_columns(t)]]
    for g in range(3):
        whole_results[f"rh{g}"] = [gqkv_ref.at[:, pl.ds(j * width + g * third, third)] for j in range(3)]
    last_copies = []

    def point(name):
        for unit_name, stage in TABLE.get(name, ()):
            unit = units[unit_name]
            if unit_name[0] == "a":
                ag_stage(unit, stage)
            elif unit_name in results and stage == len(unit[2]):
                rs_end(unit, *results[unit_name])
                for src, dst in zip(results[unit_name], whole_results[unit_name]):
                    last_copies.append(pltpu.make_async_copy(src, dst, local.at[2 + len(last_copies)]))
                    last_copies[-1].start()
            else:
                rs_stage(unit, stage)

    def points_at(index, names):
        for k, name in enumerate(names):
            if TABLE.get(name):
                pl.when(index == k)(functools.partial(point, name))

    barrier = pltpu.get_barrier_semaphore()
    partners = [*along_z, to_x, to_y, to_c]
    for to in partners:
        pl.semaphore_signal(barrier, inc=1, device_id=to, device_id_type=MESH)
    shards = []
    for g in range(3):
        for j in range(3):
            shards.append((wqkv_ref.at[:, pl.ds(j * width + g * third, third)], slabs.at[g, z, x, core, y, :, pl.ds(j * third, third)]))
    shards.append((wout_ref, slabs.at[3, z, x, core, y]))
    for tile in range(n_z):
        shards.append((wup_ref.at[:, block_columns(tile)], slabs.at[4 + tile, z, x, core, y]))
    shards.append((wdown_ref, downs.at[z, x, core, y]))
    shard_copies = [pltpu.make_async_copy(src, dst, local.at[k]) for k, (src, dst) in enumerate(shards)]
    row_copies = [pltpu.make_async_copy(tok_ref, tok, local.at[len(shards)]), pltpu.make_async_copy(cot_ref, cot, local.at[len(shards) + 1])]
    do_all(shard_copies + row_copies, "start")
    smalls[z, x, core, y] = jnp.zeros((8, 128), F32)
    for k, vector in enumerate((v0, v1, v2, v3, v4, v5, v6, v7)):
        smalls[z, x, core, y, k, 0 : vector.shape[0]] = vector[...].astype(F32)
    do_all(shard_copies, "wait")
    pl.semaphore_wait(barrier, len(partners))
    point("mask")
    do_all(row_copies, "wait")

    ends = []
    for k in range(clip_ref.shape[1]):
        ends.append(clip_ref[0, k] + (ends[-1] if ends else 0))

    def segment_of(position):
        total = jnp.zeros(position.shape, jnp.int32)
        for end in ends:
            total = total + jnp.where(position >= end, 1, 0)
        return total

    across = segment_of(lax.broadcasted_iota(jnp.int32, (CHUNK, count), 1))

    def live_of(step):
        position = lax.broadcasted_iota(jnp.int32, (CHUNK, 1), 0) + step * CHUNK
        return jnp.where(position < ends[-1], 1.0, 0.0)

    ones = jnp.ones((8, count), BF16)

    def column_sums(values):
        return nn_dot(ones, values)

    def mask_step(i, carry):
        down = segment_of(lax.broadcasted_iota(jnp.int32, (CHUNK, count), 0) + i * CHUNK)
        bias[rows_of(i), :] = jnp.where(down == across, 0.0, -1e30)
        g2[rows_of(i), :] = (live_of(i) * cot[rows_of(i), :].astype(F32)).astype(BF16)
        return carry

    lax.fori_loop(0, chunks, mask_step, 0)
    sums[...] = jnp.zeros_like(sums)
    up_sums[...] = jnp.zeros_like(up_sums)
    sums[0, 7:8, :] = column_sums(g2[...])[0:1]

    point("vec")
    vec24[...] = spread(smalls[...], 24, width)
    for k in range(2):
        vec48[k] = spread(smalls[k * n_z // 2 : (k + 1) * n_z // 2], 48, width)
    for k in range(n_z):
        vec96[k] = spread(smalls[k], 96, width)
    for g in range(3):
        span = slice(g * third, (g + 1) * third)
        merged_bias[g, 0:1, :] = jnp.concatenate(
            [vec48[0, 2:3, span], jnp.zeros((1, width - 2 * third), F32), vec48[1, 2:3, span]], axis=1
        )

    def norm_one(i, carry):
        normed, _ = norm_parts(tok[rows_of(i), :].astype(F32))
        n1[rows_of(i), :] = (normed * vec24[0:1, :] + vec24[1:2, :]).astype(BF16)
        return carry

    lax.fori_loop(0, chunks, norm_one, 0)

    def turn(source, target):
        def step(i, carry):
            at = rows_of(i, 128)
            target[at, :] = source[:, at].T
            return carry

        lax.fori_loop(0, pairs, step, 0)

    point("turn")
    turn(n1, n1t)

    def assemble(block, target):
        def step(z_at, carry):
            for x_at in range(2):
                for c_at in range(2):
                    two = slabs[block, z_at, x_at, c_at].astype(F32)
                    size = 2 * two.shape[1]
                    first = pl.multiple_of(((z_at * 2 + x_at) * 2 + c_at) * size, 16)
                    target[pl.ds(first, size), :] = two.reshape(size, width).astype(BF16)
            return carry

        lax.fori_loop(0, n_z, step, 0)

    lane = lax.broadcasted_iota(jnp.int32, (count, 128), 1)

    def one_head(values, head):
        keep = lane < 64 if head == 0 else lane >= 64
        return jnp.where(keep, values, jnp.zeros_like(values))

    q_block = 512
    parts = count // q_block
    per_group = pairs // 3

    def places(p):
        first = lax.rem(p, per_group) * 128
        return lax.div(p, per_group), [pl.ds(pl.multiple_of(first + j * third, 128), 128) for j in range(3)]

    def attend(p, carry):
        group, (at_q, at_k, at_v) = places(p)
        points_at(p, [f"q{k // per_group}" if k % per_group == 0 else "" for k in range(pairs)])

        @pl.when(lax.rem(p, per_group) == 0)
        def _():
            assemble(group, weights.at[group])
            qkv[group] = (nn_dot(n1[...], weights[group]) + merged_bias[group, 0:1, :]).astype(BF16)

        points_at(p, [f"t{k}" for k in range(pairs)])
        keys = qkv[group, :, at_k]
        queries = qkv[group, :, at_q] * 0.125
        values_t = qkv[group, :, at_v].T
        for head in range(2):
            mine = one_head(queries, head)
            for part in range(parts):
                span = slice(part * q_block, (part + 1) * q_block)
                scores = nt_dot(keys, mine[span]) + bias[:, span]
                highest = jnp.max(scores, axis=0, keepdims=True)
                raised = jnp.exp(scores - highest)
                total = jnp.sum(raised, axis=0, keepdims=True)
                chances = (raised * (1.0 / total)).astype(BF16)
                lse[p, head : head + 1, span] = highest + jnp.log(total)
                result = nn_dot(values_t[64 * head : 64 * head + 64], chances)
                att_t[pl.ds(pl.multiple_of(p * 128 + 64 * head, 64), 64), span] = result.astype(BF16)
        return carry

    lax.fori_loop(0, pairs, attend, 0)
    point("tb")
    att = n1

    def turn_back(p, carry):
        at = rows_of(p, 128)
        att[:, at] = att_t[at, :].T
        return carry

    lax.fori_loop(0, pairs, turn_back, 0)
    point("out")
    assemble(3, weights.at[3])
    pre[...] = nn_dot(att[...], weights[3])

    def norm_two(i, carry):
        at = rows_of(i)
        branch = pre[at, :] + vec24[3:4, :]
        mid = tok[at, :].astype(F32) + live_of(i) * branch
        middle[at, :] = mid
        normed, _ = norm_parts(mid)
        n2[at, :] = (normed * vec24[4:5, :] + vec24[5:6, :]).astype(BF16)
        return carry

    point("n2a")
    lax.fori_loop(0, chunks // 2, norm_two, 0)
    point("n2b")
    lax.fori_loop(chunks // 2, chunks, norm_two, 0)
    point("n2t")
    turn(n2, n2t)
    acc_out[...] = jnp.zeros_like(acc_out)
    acc_grad[...] = jnp.zeros_like(acc_grad)

    def store_rows(block, lhs_t, rhs):
        size = slabs.shape[-2]
        for first in range(0, width, 192):
            total = nn_dot(lhs_t[first : first + 192, :], rhs)
            for k in range(192 // size // 2):
                at = first // size + 2 * k
                two = total[2 * k * size : 2 * (k + 1) * size].reshape(2, size, width).astype(BF16)
                slabs[block, at // 8, at // 4 % 2, at // 2 % 2] = two

    def feed(t, carry):
        def step_point(name):
            points_at(t, [f"{name}{k}" for k in range(n_z)])

        step_point("fa")
        assemble(4 + t, w_up)
        up_bias = vec96[t, 6:7, :]
        half = count // 2

        def into_hidden(rows):
            pre[rows] = nn_dot(n2[rows], w_up[...])

        def into_grads(rows):
            grad_act[rows] = nt_dot(g2[rows], downs[t].reshape(width, width))

        def gelu_rows(first):
            for at in range(first, first + half, 32):
                rows = slice(at, at + 32)
                active, slope = gelu_both(pre[rows] + up_bias)
                act[rows] = active.astype(BF16)
                grad_h[rows] = (grad_act[rows] * slope).astype(BF16)

        def out_of(rows):
            acc_out[rows] += nn_dot(act[rows], downs[t].reshape(width, width))
            acc_grad[rows] += nt_dot(grad_h[rows], w_up[...])

        upper, lower = slice(0, half), slice(half, count)
        step_point("fb")
        into_hidden(upper)
        step_point("fc")
        into_grads(upper)
        step_point("fd")
        into_hidden(lower)
        into_grads(lower)
        gelu_rows(0)
        step_point("fe")
        out_of(upper)
        gelu_rows(half)
        step_point("ff")
        out_of(lower)
        step_point("fg")
        up_sums[t, 6:7, :] = column_sums(grad_h[...])[0:1]
        step_point("fh")
        store_rows(4 + t, n2t, grad_h[...])
        step_point("fi")
        for j in range(pairs):
            span = slice(j * 128, (j + 1) * 128)
            piece = nn_dot(act[:, span].T, g2[...]).astype(BF16)
            size = downs.shape[-2]
            at = j * 128
            while at < (j + 1) * 128:
                owner, inside = at // size, at % size
                length = min(size - inside, (j + 1) * 128 - at)
                downs[t, owner // 4, owner // 2 % 2, owner % 2, inside : inside + length, :] = piece[at - j * 128 : at - j * 128 + length]
                at += length
        return carry

    lax.fori_loop(0, n_z, feed, 0)

    def norm_two_back(i, carry):
        gain_sum, bias_sum = carry
        at = rows_of(i)
        alive = live_of(i)
        mid = middle[at, :]
        block_out[at, :] = (mid + alive * (acc_out[at, :] + vec24[7:8, :])).astype(BF16)
        normed, scale = norm_parts(mid)
        e = acc_grad[at, :]
        scaled = e * vec24[4:5, :]
        inner_part = scaled - jnp.mean(scaled, axis=-1, keepdims=True) - normed * jnp.mean(scaled * normed, axis=-1, keepdims=True)
        grad_mid = cot[at, :].astype(F32) + inner_part * scale
        acc_grad[at, :] = grad_mid
        g2[at, :] = (alive * grad_mid).astype(BF16)
        return (gain_sum + fold_rows(e * normed), bias_sum + fold_rows(e))

    zero = jnp.zeros((8, width), F32)
    block_out = act
    point("ba")
    carry = lax.fori_loop(0, chunks // 2, norm_two_back, (zero, zero))
    point("bb")
    gain_sum, bias_sum = lax.fori_loop(chunks // 2, chunks, norm_two_back, carry)
    sums[0, 4:5, :] = jnp.sum(gain_sum, axis=0, keepdims=True)
    sums[0, 5:6, :] = jnp.sum(bias_sum, axis=0, keepdims=True)
    sums[0, 3:4, :] = column_sums(g2[...])[0:1]
    out_copy = pltpu.make_async_copy(block_out, out_ref, local.at[0])
    out_copy.start()

    point("og")
    store_rows(3, att_t, g2[...])
    point("ga")
    grad_att = n2
    grad_att[...] = nt_dot(g2[...], weights[3]).astype(BF16)

    def attend_back(p, carry):
        group, (at_q, at_k, at_v) = places(p)
        points_at(p, [f"a{k}" for k in range(pairs)])
        keys = qkv[group, :, at_k]
        values = qkv[group, :, at_v]
        queries = qkv[group, :, at_q] * 0.125
        grads = grad_att[:, rows_of(p, 128)]
        keys_t = keys.T
        grad_keys = jnp.zeros((count, 128), F32)
        grad_values = jnp.zeros((count, 128), F32)
        for head in range(2):
            my_queries, my_grads = one_head(queries, head), one_head(grads, head)
            for part in range(parts):
                span = slice(part * q_block, (part + 1) * q_block)
                scores = nt_dot(keys, my_queries[span]) + bias[:, span]
                chances = jnp.exp(scores - lse[p, head : head + 1, span])
                slopes = nt_dot(values, my_grads[span])
                level = jnp.sum(chances * slopes, axis=0, keepdims=True)
                grad_scores = (chances * (slopes - level)).astype(BF16)
                grad_values += nn_dot(chances.astype(BF16), my_grads[span])
                grad_keys += nn_dot(grad_scores, my_queries[span])
                dq_t[64 * head : 64 * head + 64, span] = nn_dot(keys_t[64 * head : 64 * head + 64], grad_scores) * 0.125
        qkv[group, :, at_q] = dq_t[...].T.astype(BF16)
        qkv[group, :, at_k] = grad_keys.astype(BF16)
        qkv[group, :, at_v] = grad_values.astype(BF16)
        points_at(p, [f"H{k // per_group}" if k % per_group == per_group - 1 else "" for k in range(pairs)])

        @pl.when(lax.rem(p, per_group) == per_group - 1)
        def _():
            store_rows(group, n1t, qkv[group])
            group_sums[group] = column_sums(qkv[group])

        return carry

    lax.fori_loop(0, pairs, attend_back, 0)

    point("g2")
    pre[...] = nt_dot(qkv[2], weights[2])
    point("g1")
    pre[...] += nt_dot(qkv[1], weights[1])
    point("g0")
    pre[...] += nt_dot(qkv[0], weights[0])

    def norm_one_back(i, carry):
        gain_sum, bias_sum = carry
        at = rows_of(i)
        normed, scale = norm_parts(tok[at, :].astype(F32))
        e = pre[at, :]
        scaled = e * vec24[0:1, :]
        inner_part = scaled - jnp.mean(scaled, axis=-1, keepdims=True) - normed * jnp.mean(scaled * normed, axis=-1, keepdims=True)
        acc_grad[at, :] = acc_grad[at, :] + inner_part * scale
        return (gain_sum + fold_rows(e * normed), bias_sum + fold_rows(e))

    point("na")
    carry = lax.fori_loop(0, chunks // 2, norm_one_back, (zero, zero))
    point("nb")
    gain_sum, bias_sum = lax.fori_loop(chunks // 2, chunks, norm_one_back, carry)
    tgrad_copy = pltpu.make_async_copy(acc_grad, tgrad_ref, local.at[1])
    tgrad_copy.start()
    sums[0, 0:1, :] = jnp.sum(gain_sum, axis=0, keepdims=True)
    sums[0, 1:2, :] = jnp.sum(bias_sum, axis=0, keepdims=True)
    for g in range(3):
        span = slice(g * third, (g + 1) * third)
        sums[1, 2:3, span] = group_sums[g, 0:1, :third]
        sums[2, 2:3, span] = group_sums[g, 0:1, 2 * third :]
    point("gb")
    gsmalls[...] = gather_back(sums[0], 24).reshape(gsmalls.shape)
    for k in range(2):
        part = gather_back(sums[1 + k], 48)
        span = slice(k * n_z // 2, (k + 1) * n_z // 2)
        gsmalls[span] = gsmalls[span] + part.reshape(n_z // 2, 2, 2, 2, 8, 128)
    for k in range(n_z):
        gsmalls[k] = gsmalls[k] + gather_back(up_sums[k], 96).reshape(2, 2, 2, 8, 128)

    point("end")
    for name, unit in units.items():
        if name[0] == "r":
            rs_sent(unit)
    out_copy.wait()
    tgrad_copy.wait()
    do_all(last_copies, "wait")


def by_kernel(
    n_z, tokens, cotangent, clip_lengths, ln1_gain, ln1_bias, qkv_weight, qv_bias, out_weight, out_bias,
    ln2_gain, ln2_bias, up_weight, up_bias, down_weight, down_bias,
):
    count, width = tokens.shape
    size, deep = qkv_weight.shape[0], down_weight.shape[0]
    blocks = 4 + n_z
    vectors = (ln1_gain, ln1_bias, qv_bias, out_bias, ln2_gain, ln2_bias, up_bias, down_bias)
    vmem, dma = pltpu.VMEM, pltpu.SemaphoreType.DMA
    held = [
        vmem((blocks, n_z, 2, 2, 2, size, width), BF16),
        vmem((n_z, 2, 2, 2, deep, width), BF16),
        vmem((n_z, 2, 2, 2, 8, 128), F32),
        vmem((n_z, 2, 2, 2, 8, 128), F32),
        vmem((4, width, width), BF16),
        vmem((width, width), BF16),
        vmem((blocks, n_z, 2, 2, size, width), BF16),
        vmem((blocks - len(LATE_SUMS), 2, n_z, size, width // 2), BF16),
        vmem((blocks - len(LATE_SUMS), 2, n_z, size, width), BF16),
        vmem((blocks - len(LATE_SUMS), n_z, size, width), BF16),
        vmem((max(len(LATE_SUMS), 1), 2, size, width // 2), BF16),
        vmem((max(len(LATE_SUMS), 1), 2, size, width), BF16),
        vmem((max(len(LATE_SUMS), 1), n_z, 2, 2, size, width), BF16),
        vmem((n_z, 2, 2, deep, width), BF16),
        vmem((n_z, 2, deep, width // 2), BF16),
        vmem((n_z, 2, deep, width), BF16),
        vmem((n_z, deep, width), BF16),
        vmem((n_z, 2, 2, 8, 128), F32),
        vmem((n_z, 8, 128), F32),
        vmem((2, n_z, 8, 128), F32),
        vmem((n_z - 1, 8, 128), F32),
        vmem((3, count, width), BF16),
        vmem((width, count), BF16),
        vmem((count, width), BF16),
        vmem((width, count), BF16),
        vmem((count, width), F32),
        vmem((count, width), BF16),
        vmem((width, count), BF16),
        vmem((count, width), BF16),
        vmem((count, width), F32),
        vmem((count, width), F32),
        vmem((count, width), BF16),
        vmem((count, width), BF16),
        vmem((count, width), F32),
        vmem((count, width), F32),
        vmem((count, width), BF16),
        vmem((count, width), BF16),
        vmem((count, count), F32),
        vmem((width // 128, 2, count), F32),
        vmem((128, count), F32),
        vmem((8, width), F32),
        vmem((2, 8, width), F32),
        vmem((n_z, 8, width), F32),
        vmem((3, 8, width), F32),
        vmem((3, 8, width), F32),
        vmem((3, 8, width), F32),
        vmem((n_z, 8, width), F32),
        vmem(qkv_weight.shape, F32),
        vmem(out_weight.shape, F32),
        vmem(up_weight.shape, F32),
        vmem(down_weight.shape, F32),
        vmem((8, 128), F32),
        dma((semaphore_slots()[2],)),
        dma((len(semaphore_slots()[0]),)),
        dma((len(semaphore_slots()[1]),)),
        dma((16 + n_z,)),
    ]
    anywhere, whole = pl.BlockSpec(memory_space=pl.ANY), pl.BlockSpec(memory_space=pltpu.VMEM)
    shape = jax.ShapeDtypeStruct
    out, grad, g_qkv, g_out, g_up, g_down, g_small = pl.pallas_call(
        layer_kernel,
        out_shape=(
            shape((count, width), BF16),
            shape((count, width), F32),
            shape(qkv_weight.shape, F32),
            shape(out_weight.shape, F32),
            shape(up_weight.shape, F32),
            shape(down_weight.shape, F32),
            shape((8, 128), F32),
        ),
        in_specs=[pl.BlockSpec(memory_space=pltpu.SMEM)] + [anywhere] * 2 + [whole] * 8 + [anywhere] * 4,
        out_specs=(anywhere,) * 7,
        scratch_shapes=held,
        compiler_params=pltpu.CompilerParams(collective_id=0, has_side_effects=True, vmem_limit_bytes=VMEM_BYTES),
    )(clip_lengths, tokens, cotangent, *vectors, qkv_weight, out_weight, up_weight, down_weight)
    large = (out, grad, g_qkv, g_out, g_up, g_down)
    done = pl.pallas_call(
        hand_over,
        out_shape=tuple(shape(a.shape, a.dtype) for a in large) + tuple(shape(v.shape, F32) for v in vectors),
        in_specs=[anywhere] * (1 + len(large)),
        out_specs=(anywhere,) * (len(large) + len(vectors)),
        scratch_shapes=[vmem(a.shape, a.dtype) for a in (g_small, *large)] + [vmem(v.shape, F32) for v in vectors] + [dma((2, 24))],
    )(g_small, *large)
    out, grad, g_qkv, g_out, g_up, g_down = done[:6]
    parts = done[6:]
    return (out, grad, parts[0], parts[1], g_qkv, parts[2], g_out, parts[3], parts[4], parts[5], g_up, parts[6], g_down, parts[7])


def hand_over(*refs):
    small_ref, sources, targets, vectors = refs[0], refs[1:7], refs[7:13], refs[13:21]
    small, held, cut, sems = refs[21], refs[22:28], refs[28:36], refs[36]
    small_copy = pltpu.make_async_copy(small_ref, small, sems.at[0, 23])
    small_copy.start()
    pieces = []
    for src, mid, dst in zip(sources, held, targets):
        rows = src.shape[0]
        parts = 4 if rows % 64 == 0 else 1
        for k in range(parts):
            pieces.append([ref.at[pl.ds(k * (rows // parts), rows // parts)] for ref in (src, mid, dst)])
    inward = [pltpu.make_async_copy(src, mid, sems.at[0, k]) for k, (src, mid, _) in enumerate(pieces)]
    outward = [pltpu.make_async_copy(mid, dst, sems.at[1, k]) for k, (_, mid, dst) in enumerate(pieces)]
    for copy in inward:
        copy.start()
    small_copy.wait()
    cuts = []
    for k, (part, vector) in enumerate(zip(cut, vectors)):
        part[...] = small[k, 0 : part.shape[0]]
        cuts.append(pltpu.make_async_copy(part, vector, sems.at[1, 15 + k]))
        cuts[-1].start()
    for arrived, onward in zip(inward, outward):
        arrived.wait()
        onward.start()
    for copy in outward + cuts:
        copy.wait()


KINDS = {
    "ab1": "boot",
    "ab2": "boot",
    "au0": "direct",
    "au1": "late",
    "au2": "late",
    "au3": "boot",
    "ro": "late",
    "ru0": "late",
    "ru2": "late",
}
LATE_SUMS = ("ro", "ru0", "ru2")
TABLE = {
    "mask": (("au0", 0), ("ab1", 0), ("au2", 0), ("ab2", 0),),
    "vec": (("ab0", 0), ("au3", 0), ("aS", 0), ("ab1", 1), ("au2", 1), ("ab3", 0), ("au0", 1), ("ab0", 1), ("ab2", 1), ("aS", 1), ("ab1", 2), ("adp", 0), ("au0", 2), ("au1", 0), ("aS", 2), ("ab1", 3), ("ab3", 1), ("ab0", 2), ("au0", 3), ("aS", 3), ("au1", 1), ("au0", 4), ("ab2", 2), ("aS", 4),),
    "turn": (("ab1", 4),),
    "q0": (("ab2", 3), ("adp", 1), ("au1", 2), ("ab0", 3), ("ab1", 5), ("ab3", 2), ("ab1", 6), ("ab2", 4), ("ab0", 4), ("adp", 2), ("ad0", 0), ("ab0", 5),),
    "t1": (("ab3", 3), ("au1", 3), ("au3", 1),),
    "q1": (("ad1", 0), ("ab2", 5),),
    "q2": (("ad0", 1), ("au2", 2), ("ab2", 6),),
    "t4": (("ab3", 4), ("au1", 4),),
    "t5": (("ad2", 0),),
    "tb": (("ab3", 5),),
    "n2a": (("au1", 5), ("ad1", 1),),
    "n2b": (("ad0", 2),),
    "fa0": (("au3", 2),),
    "fc0": (("au3", 3), ("ad0", 3),),
    "fe0": (("ad2", 1),),
    "ff0": (("au2", 3),),
    "fg0": (("ad1", 2), ("ad3", 0),),
    "fi0": (("ru0", 0),),
    "fa1": (("rd0", 0),),
    "fc1": (("ad1", 3),),
    "fe1": (("au3", 4),),
    "ff1": (("ru0", 1), ("ad2", 2),),
    "fg1": (("rd0", 1), ("au2", 4),),
    "fi1": (("ru1", 0),),
    "fa2": (("rd1", 0), ("ad2", 3), ("ad3", 1), ("au2", 5),),
    "fc2": (("au3", 5),),
    "fe2": (("ru1", 1), ("ru0", 2), ("rd0", 2),),
    "fg2": (("ad3", 2),),
    "fi2": (("ru2", 0), ("au3", 6),),
    "fa3": (("rd1", 1), ("rd2", 0),),
    "fc3": (("ad3", 3),),
    "fe3": (("ru1", 2), ("ru2", 1),),
    "fg3": (("rd0", 3),),
    "fi3": (("ru3", 0), ("rd2", 1),),
    "ba": (("rd3", 0),),
    "bb": (("rd1", 2),),
    "ga": (("ro", 0), ("ru2", 2),),
    "a1": (("ru3", 1), ("rd3", 1), ("ro", 1),),
    "H0": (("rd1", 3), ("rd2", 2),),
    "a2": (("ru1", 3), ("rh0", 0),),
    "a3": (("ro", 2), ("ru3", 2),),
    "H1": (("rd3", 2),),
    "a4": (("rh1", 0), ("rd2", 3),),
    "a5": (("rh1", 1), ("ru3", 3),),
    "H2": (("ru1", 4), ("rh0", 1), ("ru0", 3),),
    "g2": (("rh2", 0), ("ru3", 4), ("rd3", 3), ("rdl", 0), ("ru2", 3),),
    "g0": (("rh1", 2),),
    "nb": (("rh2", 1),),
    "end": (("ro", 3), ("rS", 0), ("ru1", 5), ("rdl", 1), ("ru3", 5), ("rh0", 2), ("rS", 1), ("ru0", 4), ("rh2", 2), ("rh1", 3), ("rh0", 3), ("ro", 4), ("rS", 2), ("rh1", 4), ("ru0", 5), ("ru2", 4), ("rh0", 4), ("rdl", 2), ("rh2", 3), ("ro", 5), ("rS", 3), ("ru2", 5), ("rh1", 5), ("rh2", 4), ("rh0", 5), ("rS", 4), ("rh2", 5),),
}

ROW_SUMS = ("rh0", "rh1", "rh2", "ro", "ru0", "ru1", "ru2", "ru3")
VMEM_BYTES = 63 * 1024 * 1024


def kernel_fits(n_wide, n_narrow, tokens, qkv_weight, up_weight, down_weight):
    width, hidden = qkv_weight.shape[0], up_weight.shape[1]
    n_z = n_wide // 4
    devices = n_wide * n_narrow
    return (
        n_narrow == 2
        and n_wide == 4 * n_z
        and n_z == 4
        and hidden == n_z * width
        and width % (8 * devices) == 0
        and hidden % (16 * devices) == 0
        and 2 * width // devices <= 128
        and hidden // devices <= 128
        and width // devices == 24
        and (tokens.shape[0] // devices) % (2 * CHUNK) == 0
    )


def solution(mesh):
    n_wide, n_narrow = mesh.shape["wide"], mesh.shape["narrow"]
    both = ("wide", "narrow")
    matrix, vector = P(both, None), P(both)
    in_specs = (
        matrix, matrix, matrix, vector, vector, matrix, vector, matrix, vector, vector, vector, matrix, vector, matrix, vector,
    )
    out_specs = (
        matrix, matrix, vector, vector, matrix, vector, matrix, vector, vector, vector, matrix, vector, matrix, vector,
    )

    def run(*arrays):
        fits = kernel_fits(n_wide, n_narrow, arrays[0], arrays[5], arrays[11], arrays[13])
        body = functools.partial(by_kernel, n_wide // 4) if fits else by_collectives
        return jax.shard_map(body, mesh=mesh, in_specs=in_specs, out_specs=out_specs, check_vma=False)(*arrays)

    return run
```

```python
import functools
import math

import jax
import jax.numpy as jnp
from jax import lax
from jax.experimental import pallas as pl
from jax.experimental.pallas import tpu as pltpu
from jax.sharding import PartitionSpec as P

H = 12
MASKED_SCORE = -1000000000.0
MESH = pl.DeviceIdType.MESH
F32 = jnp.float32
BF16 = jnp.bfloat16
ALL = slice(None)
CHUNK = 256
BOTH_AXES = ("wide", "narrow")
ACROSS = "across"
Z_FAR = "z far"
CORE = "core"
Z_LAST = "z last"
NEAR = "near"
RELAY = "relay"
WAIT_SEND = "wait_send"
WAIT_RECV = "wait_recv"
START = "start"
LATE = "late"
PLAIN = "plain"
Z_OUTER = "z outer"
Z_NEAR = "z near"
DIRECT = "direct"
Z_ALL = "zd"
LATE_DIRECT = "late direct"
REST = "rest"
PAIR = "pair"
OWN = "own"
BOOT = "boot"
Z_TWO = "z"


def layer_norm(inputs, ln_gain, ln_bias):
    row_mean = jnp.mean(inputs, axis=-1, keepdims=True)
    centred = inputs - row_mean
    spread = jnp.mean(centred * centred, axis=-1, keepdims=True)
    return centred * lax.rsqrt(spread + 1e-06) * ln_gain + ln_bias


def gelu_exact(inputs):
    return 0.5 * inputs * (1.0 + lax.erf(inputs * 0.7071067811865476))


def clip_index(lengths, row_count):
    clip_ends = jnp.cumsum(lengths)
    position = jnp.arange(row_count, dtype=jnp.int32)
    return jnp.sum((position[:, None] >= clip_ends[None, :]).astype(jnp.int32), axis=1)


def split_heads(matrix, head_count):
    row_count = matrix.shape[0]
    return matrix.reshape(row_count, head_count, -1).transpose(1, 0, 2)


def join_heads(stacked):
    head_count, row_count, head_size = stacked.shape
    return stacked.transpose(1, 0, 2).reshape(row_count, head_count * head_size)


def attend_forward(queries, key_rows, value_rows, segment, block_rows, score_scale):
    scores = (
        lax.dot_general(
            queries, key_rows, (((1,), (1,)), ((), ())), preferred_element_type=jnp.float32
        )
        * score_scale
    )
    allowed = segment[0:block_rows, None] == segment[None, :]
    scores = jnp.where(allowed, scores, MASKED_SCORE)
    highest = jnp.max(scores, axis=1, keepdims=True)
    raised = jnp.exp(scores - highest)
    denominator = jnp.sum(raised, axis=1, keepdims=True)
    softmax = (raised / denominator).astype(jnp.bfloat16)
    outputs = [jnp.dot(softmax, value_rows, preferred_element_type=jnp.float32)]
    totals = [highest + jnp.log(denominator)]
    return (jnp.concatenate(outputs, 0), jnp.concatenate(totals, 0))


def attend_backward(
    queries, key_rows, value_rows, segment, grad_out, lse_rows, block_rows, score_scale
):
    grad_keys = jnp.zeros(key_rows.shape, jnp.float32)
    grad_values = jnp.zeros(value_rows.shape, jnp.float32)
    g_rows = grad_out[0:block_rows]
    scores = (
        lax.dot_general(
            queries, key_rows, (((1,), (1,)), ((), ())), preferred_element_type=jnp.float32
        )
        * score_scale
    )
    allowed = segment[0:block_rows, None] == segment[None, :]
    softmax = jnp.where(allowed, jnp.exp(scores - lse_rows[0:block_rows]), 0.0)
    grad_values = grad_values + lax.dot_general(
        softmax.astype(jnp.bfloat16),
        g_rows,
        (((0,), (0,)), ((), ())),
        preferred_element_type=jnp.float32,
    )
    grad_probs = lax.dot_general(
        g_rows, value_rows, (((1,), (1,)), ((), ())), preferred_element_type=jnp.float32
    )
    grad_scores = (
        softmax * (grad_probs - jnp.sum(softmax * grad_probs, axis=1, keepdims=True))
    ).astype(jnp.bfloat16)
    grad_queries = [
        jnp.dot(grad_scores, key_rows, preferred_element_type=jnp.float32) * score_scale
    ]
    grad_keys = (
        grad_keys
        + lax.dot_general(
            grad_scores, queries, (((0,), (0,)), ((), ())), preferred_element_type=jnp.float32
        )
        * score_scale
    )
    return (jnp.concatenate(grad_queries, 0), grad_keys, grad_values)


def by_collectives(
    tokens,
    cotangent,
    clip_lengths,
    ln1_gain,
    ln1_bias,
    qkv_weight,
    qv_bias,
    out_weight,
    out_bias,
    ln2_gain,
    ln2_bias,
    up_weight,
    up_bias,
    down_weight,
    down_bias,
):
    gathered = (
        lax.all_gather(ln1_gain, BOTH_AXES, axis=0, tiled=True),
        lax.all_gather(ln1_bias, BOTH_AXES, axis=0, tiled=True),
        lax.all_gather(qkv_weight, BOTH_AXES, axis=0, tiled=True),
        lax.all_gather(qv_bias, BOTH_AXES, axis=0, tiled=True),
        lax.all_gather(out_weight, BOTH_AXES, axis=0, tiled=True),
        lax.all_gather(out_bias, BOTH_AXES, axis=0, tiled=True),
        lax.all_gather(ln2_gain, BOTH_AXES, axis=0, tiled=True),
        lax.all_gather(ln2_bias, BOTH_AXES, axis=0, tiled=True),
        lax.all_gather(up_weight, BOTH_AXES, axis=0, tiled=True),
        lax.all_gather(up_bias, BOTH_AXES, axis=0, tiled=True),
        lax.all_gather(down_weight, BOTH_AXES, axis=0, tiled=True),
        lax.all_gather(down_bias, BOTH_AXES, axis=0, tiled=True),
    )
    (
        gain_one,
        bias_one,
        merged_weight,
        merged_bias,
        proj_weight,
        proj_bias,
        gain_two,
        bias_two,
        w_up,
        b_up,
        w_down,
        b_down,
    ) = gathered
    inputs = tokens.astype(jnp.float32)
    row_count, model_width = inputs.shape
    head_size = model_width // H
    score_scale = 1.0 / math.sqrt(head_size)
    block_rows = min(512, row_count)
    clip_count = clip_lengths.shape[1]
    segment = clip_index(clip_lengths[0], row_count)
    live_rows = (segment < clip_count).astype(jnp.float32)[:, None]
    normed_one = layer_norm(
        inputs, gain_one.astype(jnp.float32), bias_one.astype(jnp.float32)
    ).astype(jnp.bfloat16)
    bias_float = merged_bias.astype(jnp.float32)
    full_bias = jnp.concatenate(
        [bias_float[:model_width], jnp.zeros((model_width,), jnp.float32), bias_float[model_width:]]
    )
    merged_rows = (
        jnp.dot(normed_one, merged_weight, preferred_element_type=jnp.float32) + full_bias
    ).astype(jnp.bfloat16)
    q_heads = split_heads(merged_rows[:, :model_width], H)
    k_heads = split_heads(merged_rows[:, model_width : 2 * model_width], H)
    v_heads = split_heads(merged_rows[:, 2 * model_width :], H)

    def head_forward(triple):
        return attend_forward(triple[0], triple[1], triple[2], segment, block_rows, score_scale)

    att_heads, lse_heads = lax.map(head_forward, (q_heads, k_heads, v_heads))
    attended = join_heads(att_heads).astype(jnp.bfloat16)
    branch_one = jnp.dot(
        attended, proj_weight, preferred_element_type=jnp.float32
    ) + proj_bias.astype(jnp.float32)
    middle = inputs + live_rows * branch_one
    normed_two = layer_norm(
        middle, gain_two.astype(jnp.float32), bias_two.astype(jnp.float32)
    ).astype(jnp.bfloat16)
    hidden_pre = jnp.dot(normed_two, w_up, preferred_element_type=jnp.float32) + b_up.astype(
        jnp.float32
    )
    activated, gelu_pull = jax.vjp(gelu_exact, hidden_pre)
    activated = activated.astype(jnp.bfloat16)
    branch_two = jnp.dot(activated, w_down, preferred_element_type=jnp.float32) + b_down.astype(
        jnp.float32
    )
    block_out = (middle + live_rows * branch_two).astype(jnp.bfloat16)
    back_gain_one, back_merged, back_proj, back_gain_two, back_up, back_down = (
        lax.all_gather(ln1_gain, BOTH_AXES, axis=0, tiled=True),
        lax.all_gather(qkv_weight, BOTH_AXES, axis=0, tiled=True),
        lax.all_gather(out_weight, BOTH_AXES, axis=0, tiled=True),
        lax.all_gather(ln2_gain, BOTH_AXES, axis=0, tiled=True),
        lax.all_gather(up_weight, BOTH_AXES, axis=0, tiled=True),
        lax.all_gather(down_weight, BOTH_AXES, axis=0, tiled=True),
    )
    upstream = cotangent.astype(jnp.float32)
    grad_two = (live_rows * upstream).astype(jnp.bfloat16)
    grad_b_down = jnp.sum(grad_two.astype(jnp.float32), axis=0)
    grad_w_down = jnp.einsum("tf,td->fd", activated, grad_two, preferred_element_type=jnp.float32)
    grad_act = jnp.einsum("td,fd->tf", grad_two, back_down, preferred_element_type=jnp.float32)
    grad_hidden = gelu_pull(grad_act)[0].astype(jnp.bfloat16)
    grad_b_up = jnp.sum(grad_hidden.astype(jnp.float32), axis=0)
    grad_w_up = jnp.einsum("td,tf->df", normed_two, grad_hidden, preferred_element_type=jnp.float32)
    grad_normed_two = jnp.einsum(
        "tf,df->td", grad_hidden, back_up, preferred_element_type=jnp.float32
    )
    _, norm_pull_two = jax.vjp(
        layer_norm, middle, back_gain_two.astype(jnp.float32), bias_two.astype(jnp.float32)
    )
    grad_middle_norm, grad_gain_two, grad_bias_two = norm_pull_two(grad_normed_two)
    grad_middle = upstream + grad_middle_norm
    grad_one = (live_rows * grad_middle).astype(jnp.bfloat16)
    grad_b_proj = jnp.sum(grad_one.astype(jnp.float32), axis=0)
    grad_w_proj = jnp.einsum("te,td->ed", attended, grad_one, preferred_element_type=jnp.float32)
    grad_att = jnp.einsum(
        "td,ed->te", grad_one, back_proj, preferred_element_type=jnp.float32
    ).astype(jnp.bfloat16)
    grad_att_heads = split_heads(grad_att, H)

    def head_backward(members):
        return attend_backward(
            members[0],
            members[1],
            members[2],
            segment,
            members[3],
            members[4],
            block_rows,
            score_scale,
        )

    grad_q, grad_k, grad_v = lax.map(
        head_backward, (q_heads, k_heads, v_heads, grad_att_heads, lse_heads)
    )
    grad_merged = jnp.concatenate(
        [join_heads(grad_q), join_heads(grad_k), join_heads(grad_v)], 1
    ).astype(jnp.bfloat16)
    column_sums = jnp.sum(grad_merged.astype(jnp.float32), axis=0)
    grad_merged_bias = jnp.concatenate([column_sums[:model_width], column_sums[2 * model_width :]])
    grad_w_merged = jnp.einsum(
        "te,tf->ef", normed_one, grad_merged, preferred_element_type=jnp.float32
    )
    grad_normed_one = jnp.einsum(
        "tf,ef->te", grad_merged, back_merged, preferred_element_type=jnp.float32
    )
    _, norm_pull_one = jax.vjp(
        layer_norm, inputs, back_gain_one.astype(jnp.float32), bias_one.astype(jnp.float32)
    )
    grad_input_norm, grad_gain_one, grad_bias_one = norm_pull_one(grad_normed_one)
    tokens_grad = grad_middle + grad_input_norm
    shares = (
        lax.psum_scatter(grad_gain_one, BOTH_AXES, scatter_dimension=0, tiled=True),
        lax.psum_scatter(grad_bias_one, BOTH_AXES, scatter_dimension=0, tiled=True),
        lax.psum_scatter(grad_w_merged, BOTH_AXES, scatter_dimension=0, tiled=True),
        lax.psum_scatter(grad_merged_bias, BOTH_AXES, scatter_dimension=0, tiled=True),
        lax.psum_scatter(grad_w_proj, BOTH_AXES, scatter_dimension=0, tiled=True),
        lax.psum_scatter(grad_b_proj, BOTH_AXES, scatter_dimension=0, tiled=True),
        lax.psum_scatter(grad_gain_two, BOTH_AXES, scatter_dimension=0, tiled=True),
        lax.psum_scatter(grad_bias_two, BOTH_AXES, scatter_dimension=0, tiled=True),
        lax.psum_scatter(grad_w_up, BOTH_AXES, scatter_dimension=0, tiled=True),
        lax.psum_scatter(grad_b_up, BOTH_AXES, scatter_dimension=0, tiled=True),
        lax.psum_scatter(grad_w_down, BOTH_AXES, scatter_dimension=0, tiled=True),
        lax.psum_scatter(grad_b_down, BOTH_AXES, scatter_dimension=0, tiled=True),
    )
    return (
        block_out,
        tokens_grad,
        shares[0],
        shares[1],
        shares[2],
        shares[3],
        shares[4],
        shares[5],
        shares[6],
        shares[7],
        shares[8],
        shares[9],
        shares[10],
        shares[11],
    )


def nt_dot(left, right):
    return lax.dot_general(left, right, (((1,), (1,)), ((), ())), preferred_element_type=F32)


def nn_dot(left, right):
    return jnp.dot(left, right, preferred_element_type=F32)


def rows_of(step, size=CHUNK):
    return pl.ds(pl.multiple_of(step * size, size), size)


def norm_parts(values):
    centred = values - jnp.mean(values, axis=-1, keepdims=True)
    scale = lax.rsqrt(jnp.mean(centred * centred, axis=-1, keepdims=True) + 1e-06)
    return centred * scale, scale


def fold_rows(values):
    return jnp.sum(values.reshape(-1, 8, values.shape[-1]), axis=0)


def gelu_both(u):
    tail = 0.5 * (1.0 + lax.erf(u * 0.7071067811865476))
    return u * tail, tail + u * jnp.exp(-0.5 * u * u) * 0.3989422804014327


def spread_maps(width, columns):
    column = lax.broadcasted_iota(jnp.int32, (1, columns), 1).astype(F32)
    group = jnp.floor((column + 0.5) * (1.0 / width))
    place = column - group * width
    lane = lax.broadcasted_iota(jnp.int32, (128, columns), 0).astype(F32)
    picks = jnp.where(lane == place, 1.0, 0.0).astype(BF16)
    owners = columns // width
    owner = lax.broadcasted_iota(jnp.int32, (owners, 8, columns), 0).astype(F32)
    mine = owner == group.reshape(1, 1, columns)
    return picks, mine


def spread(pieces, width, columns):
    picks, mine = spread_maps(width, columns)
    wide_rows = nn_dot(pieces.reshape(-1, 128).astype(BF16), picks)
    return jnp.sum(jnp.where(mine, wide_rows.reshape(-1, 8, columns), 0.0), axis=0)


def gather_back(vectors, width):
    columns = vectors.shape[-1]
    picks, mine = spread_maps(width, columns)
    rest = jnp.where(mine, vectors[None], 0.0).reshape(-1, columns)
    total = None
    for _ in range(3):
        part = rest.astype(BF16)
        rest = rest - part.astype(F32)
        term = nt_dot(part, picks)
        total = term if total is None else total + term
    return total.reshape(-1, 8, 128)


Z0, Z1, Z2, ZR, X0, Y0, X1, Y1, X2, Y2, DX, DY, C0 = range(13)
ORDERS = {
    PLAIN: (Z_TWO, RELAY, NEAR, ACROSS, CORE),
    DIRECT: (Z_ALL, NEAR, ACROSS, CORE),
    BOOT: (OWN, Z_ALL, PAIR, REST, ACROSS, CORE),
    LATE: (NEAR, ACROSS, Z_TWO, RELAY, CORE),
    LATE_DIRECT: (NEAR, ACROSS, Z_ALL, CORE),
}
BACK = {
    PLAIN: (CORE, ACROSS, NEAR, Z_TWO, Z_FAR),
    DIRECT: (CORE, ACROSS, NEAR, Z_ALL),
    LATE: (CORE, Z_TWO, Z_FAR, ACROSS, NEAR),
    LATE_DIRECT: (CORE, Z_ALL, ACROSS, NEAR),
}


def phases_of(name):
    kind = DIRECT if name[1:] == "S" else KINDS.get(name, PLAIN)
    if name[:2] == "ad":
        return ((Z_TWO, RELAY) if kind == PLAIN else (Z_ALL,)) if name == "adp" else (NEAR, ACROSS, CORE)
    if name[:2] == "rd":
        return ((Z_TWO, Z_FAR) if kind == PLAIN else (Z_ALL,)) if name == "rdl" else (CORE, ACROSS, NEAR)
    return (ORDERS if name[0] == "a" else BACK)[kind]


def semaphore_slots():
    used = {
        Z_TWO: (Z0, Z1, Z2), RELAY: (ZR,), Z_ALL: (Z0, Z1, Z2), OWN: (X1, Y1), PAIR: (X2, Y2), REST: (X0, Y0),
        NEAR: (X0, Y0), ACROSS: (DX, DY), CORE: (C0,), Z_FAR: (ZR, Z1),
    }
    gathers = list(dict(aS=0, ab0=0, ab1=0, ab2=0, ab3=0, adp=0, au0=0, ad0=0, au1=0, ad1=0, au2=0, ad2=0, au3=0, ad3=0))
    sums = list(dict(ru0=0, rd0=0, ru1=0, rd1=0, ru2=0, rd2=0, ru3=0, rd3=0, ro=0, rdl=0, rh0=0, rh1=0, rh2=0, rS=0))
    slots = []
    for names in (gathers, sums):
        places = {}
        for name in names:
            for sem in sorted({sem for phase in phases_of(name) for sem in used[phase]}):
                places[name, sem] = len(places)
        slots.append(places)
    return slots[0], slots[1], max(len(slots[0]), len(slots[1])), len(slots[0])


def layer_kernel(
    clip_ref, tok_ref, cot_ref, v0, v1, v2, v3, v4, v5, v6, v7, wqkv_ref, wout_ref, wup_ref, wdown_ref,
    out_ref, tgrad_ref, gqkv_ref, gout_ref, gup_ref, gdown_ref, gsmall_ref,
    slabs, downs, smalls, gsmalls, weights, w_up,
    row_c, row_d, row_n, row_z, late_d, late_n, late_z, down_c, down_d, down_n, down_z, sm_c, sm_d, sm_n, sm_z,
    qkv, n1t, n1, att_t, middle, n2, n2t, g2, acc_out, acc_grad, act, grad_h, pre, grad_act,
    tok, cot, bias, lse, dq_t, vec24, vec48, vec96, merged_bias, group_sums, sums, up_sums, gqkv, gout, gup, gdown, gsmall,
    sends, ag_recv, rs_recv, local,
):
    n_z, width = slabs.shape[1], slabs.shape[-1]
    count = tok.shape[0]
    pairs = width // 128
    chunks = count // CHUNK
    wide_at, y = lax.axis_index(BOTH_AXES[0]), lax.axis_index(BOTH_AXES[1])
    core = lax.rem(wide_at, 2)
    x = lax.rem(lax.div(wide_at, 2), 2)
    z = lax.div(wide_at, 4)

    def device(z_at, x_at, c_at, y_at):
        return ((z_at * 2 + x_at) * 2 + c_at, y_at)

    def row_view(block):
        def view(at):
            return slabs.at[(block, *at)]
        return view

    def down_view(tile):
        def view(at):
            return downs.at[(tile, *at[1:])]
        return view

    def small_view(ref):
        def view(at):
            return ref.at[at]
        return view

    def half_of(ref, side):
        if ref.shape[-1] < 2 * 128:
            return ref
        cut = ref.shape[-1] // 2
        return ref.at[(*([ALL] * (len(ref.shape) - 1)), pl.ds(side * cut, cut))]

    to_x, to_y, to_c = device(z, 1 - x, core, y), device(z, x, core, 1 - y), device(z, x, 1 - core, y)
    z_places = (z + 1 - 2 * lax.rem(z, 2), lax.rem(z + 2, n_z), n_z - 1 - z)
    along_z = [device(at, x, core, y) for at in z_places]
    other_pair = pl.ds(2 * (1 - lax.div(z, 2)), 2)
    inner = lax.rem(z + 1, n_z) >= 2

    ag_slots, rs_slots, _, _ = semaphore_slots()

    def remote(src, dst, sums, unit_name, sem, to, recv_sem=None):
        slots = rs_slots if sums else ag_slots
        recv = rs_recv if sums else ag_recv
        return pltpu.make_async_remote_copy(
            src_ref=src, dst_ref=dst, send_sem=sends.at[slots[unit_name, sem]],
            recv_sem=recv.at[slots[unit_name, sem if recv_sem is None else recv_sem]],
            device_id=to, device_id_type=MESH,
        )

    def do_all(copies, what):
        for copy in copies:
            getattr(copy, what)()

    one, plane = (x, core, y), (ALL, core, ALL)

    def ag_copies(unit, phase):
        view, row, phases, along = unit
        sems = False
        held = z if along is plane else ALL

        def both(at, sem):
            mine = view((at, x, core, y))
            return [remote(mine, mine, sems, row, sem, to_x), remote(mine, mine, sems, row, sem + 1, to_y)]

        def own_to(*which):
            own = view((z, *along))
            return [remote(own, own, sems, row, k, along_z[k]) for k in which]

        if phase == Z_TWO:
            return own_to(Z0, Z1)
        if phase == Z_ALL:
            return own_to(Z0, Z1, Z2)
        if phase in (Z_NEAR, Z_FAR, Z_LAST):
            return own_to((Z_NEAR, Z_FAR, Z_LAST).index(phase))
        if phase == RELAY:
            passed = view((z_places[1], *along))
            return [remote(passed, passed, sems, row, ZR, along_z[0], Z2)]
        if phase == OWN:
            return both(z, X1)
        if phase == PAIR:
            return both(z_places[0], X2)
        if phase == REST:
            return both(other_pair, X0)
        if phase == NEAR:
            return both(held, X0)
        if phase == ACROSS:
            from_x, from_y = view((held, 1 - x, core, y)), view((held, x, core, 1 - y))
            first = half_of(from_x, 0)
            copies = [remote(first, first, sems, row, DY, to_y)]
            if from_x.shape[-1] >= 2 * 128:
                second = half_of(from_y, 1)
                copies.append(remote(second, second, sems, row, DX, to_x))
            return copies
        whole_plane = view((ALL, ALL, core, ALL))
        return [remote(whole_plane, whole_plane, sems, row, C0, to_c)]

    def ag_wait(unit, *phases):
        for phase in phases:
            do_all(ag_copies(unit, phase), WAIT_RECV)

    def ag_stage(unit, stage):
        phases = unit[2]
        phase = phases[stage] if stage < len(phases) else None
        if phase == RELAY:
            @pl.when(inner)
            def _():
                ag_wait(unit, Z_FAR)
                do_all(ag_copies(unit, RELAY), START)
            return
        if phase == PAIR:
            ag_wait(unit, Z_NEAR)
        elif phase == REST:
            ag_wait(unit, Z_FAR, Z_LAST)
        elif phase == ACROSS and OWN in phases:
            ag_wait(unit, OWN, PAIR, REST)
        elif stage > 0 and phases[stage - 1] == RELAY:
            @pl.when(jnp.logical_not(inner))
            def _():
                ag_wait(unit, Z_FAR)
            ag_wait(unit, Z_NEAR, Z_LAST)
        elif stage > 0 and phases[stage - 1] != OWN:
            ag_wait(unit, phases[stage - 1])
        if phase:
            do_all(ag_copies(unit, phase), START)
            if phase == Z_TWO:
                @pl.when(inner)
                def _():
                    do_all(ag_copies(unit, Z_LAST), START)
        else:
            for sent in phases:
                if sent != RELAY:
                    do_all(ag_copies(unit, sent), WAIT_SEND)
            if RELAY in phases:
                @pl.when(inner)
                def _():
                    do_all(ag_copies(unit, Z_LAST) + ag_copies(unit, RELAY), WAIT_SEND)

    def gather_unit(name, view):
        kind = KINDS.get(name, PLAIN)
        return (view, name, phases_of(name), plane if kind[:4] == LATE else one)

    units = {"aS": gather_unit("aS", small_view(smalls)), "adp": gather_unit("adp", lambda at: downs.at[at])}
    for block in range(4):
        units[f"ab{block}"] = gather_unit(f"ab{block}", row_view(block))
    for tile in range(n_z):
        units[f"au{tile}"] = gather_unit(f"au{tile}", row_view(4 + tile))
        units[f"ad{tile}"] = gather_unit(f"ad{tile}", down_view(tile))

    def rs_copies(unit, phase):
        view, row, phases, landing, along = unit
        sems = True
        held = z if along is plane else ALL
        if phase == CORE:
            return [remote(view((ALL, ALL, 1 - core, ALL)), landing[CORE], sems, row, C0, to_c)]
        if phase == ACROSS:
            away = view((held, 1 - x, core, 1 - y))
            copies = [remote(half_of(away, 0), landing["dx"], sems, row, DX, to_x)]
            if away.shape[-1] >= 2 * 128:
                copies.append(remote(half_of(away, 1), landing["dy"], sems, row, DY, to_y))
            return copies
        if phase == NEAR:
            return [
                remote(view((held, 1 - x, core, y)), landing["x"], sems, row, X0, to_x),
                remote(view((held, x, core, 1 - y)), landing["y"], sems, row, Y0, to_y),
            ]
        if phase == Z_OUTER:
            return [remote(view((z_places[2], *along)), landing[Z_TWO].at[ZR], sems, row, ZR, along_z[0])]
        which = {Z_TWO: (Z0,), Z_FAR: (Z1,), Z_LAST: (Z2,), Z_ALL: (Z0, Z1, Z2)}[phase]
        return [remote(view((z_places[k], *along)), landing[Z_TWO].at[k], sems, row, k, along_z[k]) for k in which]

    def add_into(target, *sources):
        total = target[...].astype(F32)
        for source in sources:
            total = total + source[...].astype(F32)
        target[...] = total.astype(target.dtype)

    def add_all(target, *sources):
        free = len(target.shape) - 2
        if free == 0:
            add_into(target, *sources)
            return
        places = [()]
        for extent in target.shape[1:free]:
            places = [place + (k,) for place in places for k in range(extent)]

        def step(i, carry):
            for place in places:
                add_into(target.at[(i, *place)], *[source.at[(i, *place)] for source in sources])
            return carry

        lax.fori_loop(0, target.shape[0], step, 0)

    def rs_stage(unit, stage):
        view, _, phases, landing, along = unit
        held = z if along is plane else ALL
        before = phases[stage - 1] if stage > 0 else None
        phase = phases[stage] if stage < len(phases) else None
        if phase == Z_FAR:
            @pl.when(inner)
            def _():
                do_all(rs_copies(unit, Z_OUTER), WAIT_RECV)
                add_all(view((z_places[1], *along)), landing[Z_TWO].at[ZR])
        elif before == Z_FAR:
            rs_wait(unit, Z_TWO, Z_FAR)
            add_all(view((z, *along)), landing[Z_TWO].at[Z0], landing[Z_TWO].at[Z1])

            @pl.when(inner)
            def _():
                rs_wait(unit, Z_LAST)
                add_all(view((z, *along)), landing[Z_TWO].at[Z2])
        elif before:
            rs_wait(unit, before)
        if before == CORE:
            add_all(view((ALL, ALL, core, ALL)), landing[CORE])
        elif before == ACROSS:
            on_y = view((held, x, core, 1 - y))
            add_all(half_of(on_y, 0), landing["dx"])
            if on_y.shape[-1] >= 2 * 128:
                add_all(half_of(view((held, 1 - x, core, y)), 1), landing["dy"])
        elif before == NEAR:
            add_all(view((held, x, core, y)), landing["x"], landing["y"])
        elif before == Z_ALL:
            add_all(view((z, *along)), *[landing[Z_TWO].at[k] for k in (Z0, Z1, Z2)])
        if phase:
            do_all(rs_copies(unit, phase), START)
        if phase == Z_TWO:
            @pl.when(inner)
            def _():
                do_all(rs_copies(unit, Z_LAST), START)

            @pl.when(jnp.logical_not(inner))
            def _():
                do_all(rs_copies(unit, Z_OUTER), START)

    def rs_wait(unit, *phases):
        for phase in phases:
            do_all(rs_copies(unit, phase), WAIT_RECV)

    def rs_end(unit, *results):
        view, _, phases, landing, along = unit
        last = phases[-1]
        if last == NEAR:
            sources = [landing["x"], landing["y"]]
        else:
            sources = [landing[Z_TWO].at[k] for k in ((Z0, Z1) if last == Z_FAR else (Z0, Z1, Z2))]
        rs_wait(unit, *((Z_TWO, Z_FAR) if last == Z_FAR else (last,)))
        total = view((z, x, core, y))[...].astype(F32)
        for part in sources:
            total = total + part[...].astype(F32)
        size = total.shape[-1] // len(results)
        for k, result in enumerate(results):
            result[...] = total[:, k * size : (k + 1) * size]
        if last == Z_FAR:
            @pl.when(inner)
            def _():
                rs_wait(unit, Z_LAST)
                for k, result in enumerate(results):
                    result[...] += landing[Z_TWO][Z2, :, k * size : (k + 1) * size].astype(F32)

    def rs_sent(unit):
        for phase in unit[2]:
            do_all(rs_copies(unit, phase), WAIT_SEND)
        if Z_FAR in unit[2]:
            @pl.when(inner)
            def _():
                do_all(rs_copies(unit, Z_LAST), WAIT_SEND)

            @pl.when(jnp.logical_not(inner))
            def _():
                do_all(rs_copies(unit, Z_OUTER), WAIT_SEND)

    def row_unit(block, name):
        if name in LATE_SUMS:
            late = LATE_SUMS.index(name)
            landing = {CORE: row_c.at[block], "dx": late_d.at[late, 0], "dy": late_d.at[late, 1], "x": late_n.at[late, 0], "y": late_n.at[late, 1], Z_TWO: late_z.at[late]}
            return (row_view(block), name, phases_of(name), landing, plane)
        at = block - sum(earlier in LATE_SUMS for earlier in ROW_SUMS[:block])
        landing = {CORE: row_c.at[block], "dx": row_d.at[at, 0], "dy": row_d.at[at, 1], "x": row_n.at[at, 0], "y": row_n.at[at, 1], Z_TWO: row_z.at[at]}
        return (row_view(block), name, phases_of(name), landing, one)

    def down_unit(tile, name):
        landing = {CORE: down_c.at[tile], "dx": down_d.at[tile, 0], "dy": down_d.at[tile, 1], "x": down_n.at[tile, 0], "y": down_n.at[tile, 1]}
        return (down_view(tile), name, phases_of(name), landing, one)

    def block_columns(block):
        return pl.ds(block * width, width)

    third = width // 3
    results = {"rdl": [gdown], "ro": [gout], "rS": [gsmall]}
    for t in range(n_z):
        units[f"ru{t}"] = row_unit(4 + t, f"ru{t}")
        units[f"rd{t}"] = down_unit(t, f"rd{t}")
        results[f"ru{t}"] = [gup.at[:, block_columns(t)]]
    for g in range(3):
        units[f"rh{g}"] = row_unit(g, f"rh{g}")
        results[f"rh{g}"] = [gqkv.at[:, pl.ds(j * width + g * third, third)] for j in range(3)]
    units["ro"] = row_unit(3, "ro")
    small_landing = {CORE: sm_c, "dx": sm_d, "x": sm_n.at[0], "y": sm_n.at[1], Z_TWO: sm_z}
    units["rS"] = (small_view(gsmalls), "rS", phases_of("rS"), small_landing, one)
    units["rdl"] = (lambda at: downs.at[at], "rdl", phases_of("rdl"), {Z_TWO: down_z}, one)
    whole_results = {"rdl": [gdown_ref], "ro": [gout_ref], "rS": [gsmall_ref]}
    for t in range(n_z):
        whole_results[f"ru{t}"] = [gup_ref.at[:, block_columns(t)]]
    for g in range(3):
        whole_results[f"rh{g}"] = [gqkv_ref.at[:, pl.ds(j * width + g * third, third)] for j in range(3)]
    last_copies = []

    def point(name):
        for unit_name, stage in TABLE.get(name, ()):
            unit = units[unit_name]
            if unit_name[0] == "a":
                ag_stage(unit, stage)
            elif unit_name in results and stage == len(unit[2]):
                rs_end(unit, *results[unit_name])
                for src, dst in zip(results[unit_name], whole_results[unit_name]):
                    last_copies.append(pltpu.make_async_copy(src, dst, local.at[2 + len(last_copies)]))
                    last_copies[-1].start()
            else:
                rs_stage(unit, stage)

    def points_at(index, names):
        for k, name in enumerate(names):
            if TABLE.get(name):
                pl.when(index == k)(functools.partial(point, name))

    barrier = pltpu.get_barrier_semaphore()
    partners = [*along_z, to_x, to_y, to_c]
    for to in partners:
        pl.semaphore_signal(barrier, inc=1, device_id=to, device_id_type=MESH)
    shards = []
    for g in range(3):
        for j in range(3):
            shards.append((wqkv_ref.at[:, pl.ds(j * width + g * third, third)], slabs.at[g, z, x, core, y, :, pl.ds(j * third, third)]))
    shards.append((wout_ref, slabs.at[3, z, x, core, y]))
    for tile in range(n_z):
        shards.append((wup_ref.at[:, block_columns(tile)], slabs.at[4 + tile, z, x, core, y]))
    shards.append((wdown_ref, downs.at[z, x, core, y]))
    shard_copies = [pltpu.make_async_copy(src, dst, local.at[k]) for k, (src, dst) in enumerate(shards)]
    row_copies = [pltpu.make_async_copy(tok_ref, tok, local.at[len(shards)]), pltpu.make_async_copy(cot_ref, cot, local.at[len(shards) + 1])]
    do_all(shard_copies + row_copies, START)
    smalls[z, x, core, y] = jnp.zeros((8, 128), F32)
    for k, vector in enumerate((v0, v1, v2, v3, v4, v5, v6, v7)):
        smalls[z, x, core, y, k, 0 : vector.shape[0]] = vector[...].astype(F32)
    do_all(shard_copies, "wait")
    pl.semaphore_wait(barrier, len(partners))
    point("mask")
    do_all(row_copies, "wait")

    ends = []
    for k in range(clip_ref.shape[1]):
        ends.append(clip_ref[0, k] + (ends[-1] if ends else 0))

    def segment_of(position):
        total = jnp.zeros(position.shape, jnp.int32)
        for end in ends:
            total = total + jnp.where(position >= end, 1, 0)
        return total

    across = segment_of(lax.broadcasted_iota(jnp.int32, (CHUNK, count), 1))

    def live_of(step):
        position = lax.broadcasted_iota(jnp.int32, (CHUNK, 1), 0) + step * CHUNK
        return jnp.where(position < ends[-1], 1.0, 0.0)

    ones = jnp.ones((8, count), BF16)

    def column_sums(values):
        return nn_dot(ones, values)

    def mask_step(i, carry):
        down = segment_of(lax.broadcasted_iota(jnp.int32, (CHUNK, count), 0) + i * CHUNK)
        bias[rows_of(i), :] = jnp.where(down == across, 0.0, -1e30)
        g2[rows_of(i), :] = (live_of(i) * cot[rows_of(i), :].astype(F32)).astype(BF16)
        return carry

    lax.fori_loop(0, chunks, mask_step, 0)
    sums[...] = jnp.zeros_like(sums)
    up_sums[...] = jnp.zeros_like(up_sums)
    sums[0, 7:8, :] = column_sums(g2[...])[0:1]

    point("vec")
    vec24[...] = spread(smalls[...], 24, width)
    for k in range(2):
        vec48[k] = spread(smalls[k * n_z // 2 : (k + 1) * n_z // 2], 48, width)
    for k in range(n_z):
        vec96[k] = spread(smalls[k], 96, width)
    for g in range(3):
        span = slice(g * third, (g + 1) * third)
        merged_bias[g, 0:1, :] = jnp.concatenate(
            [vec48[0, 2:3, span], jnp.zeros((1, width - 2 * third), F32), vec48[1, 2:3, span]], axis=1
        )

    def norm_one(i, carry):
        normed, _ = norm_parts(tok[rows_of(i), :].astype(F32))
        n1[rows_of(i), :] = (normed * vec24[0:1, :] + vec24[1:2, :]).astype(BF16)
        return carry

    lax.fori_loop(0, chunks, norm_one, 0)

    def turn(source, target):
        def step(i, carry):
            at = rows_of(i, 128)
            target[at, :] = source[:, at].T
            return carry

        lax.fori_loop(0, pairs, step, 0)

    point("turn")
    turn(n1, n1t)

    def assemble(block, target):
        def step(z_at, carry):
            for x_at in range(2):
                for c_at in range(2):
                    two = slabs[block, z_at, x_at, c_at].astype(F32)
                    size = 2 * two.shape[1]
                    first = pl.multiple_of(((z_at * 2 + x_at) * 2 + c_at) * size, 16)
                    target[pl.ds(first, size), :] = two.reshape(size, width).astype(BF16)
            return carry

        lax.fori_loop(0, n_z, step, 0)

    lane = lax.broadcasted_iota(jnp.int32, (count, 128), 1)

    def one_head(values, head):
        keep = lane < 64 if head == 0 else lane >= 64
        return jnp.where(keep, values, jnp.zeros_like(values))

    q_block = 512
    parts = count // q_block
    per_group = pairs // 3

    def places(p):
        first = lax.rem(p, per_group) * 128
        return lax.div(p, per_group), [pl.ds(pl.multiple_of(first + j * third, 128), 128) for j in range(3)]

    def attend(p, carry):
        group, (at_q, at_k, at_v) = places(p)
        points_at(p, [f"q{k // per_group}" if k % per_group == 0 else "" for k in range(pairs)])

        @pl.when(lax.rem(p, per_group) == 0)
        def _():
            assemble(group, weights.at[group])
            qkv[group] = (nn_dot(n1[...], weights[group]) + merged_bias[group, 0:1, :]).astype(BF16)

        points_at(p, [f"t{k}" for k in range(pairs)])
        keys = qkv[group, :, at_k]
        queries = qkv[group, :, at_q] * 0.125
        values_t = qkv[group, :, at_v].T
        for head in range(2):
            mine = one_head(queries, head)
            for part in range(parts):
                span = slice(part * q_block, (part + 1) * q_block)
                scores = nt_dot(keys, mine[span]) + bias[:, span]
                highest = jnp.max(scores, axis=0, keepdims=True)
                raised = jnp.exp(scores - highest)
                total = jnp.sum(raised, axis=0, keepdims=True)
                chances = (raised * (1.0 / total)).astype(BF16)
                lse[p, head : head + 1, span] = highest + jnp.log(total)
                result = nn_dot(values_t[64 * head : 64 * head + 64], chances)
                att_t[pl.ds(pl.multiple_of(p * 128 + 64 * head, 64), 64), span] = result.astype(BF16)
        return carry

    lax.fori_loop(0, pairs, attend, 0)
    point("tb")
    att = n1

    def turn_back(p, carry):
        at = rows_of(p, 128)
        att[:, at] = att_t[at, :].T
        return carry

    lax.fori_loop(0, pairs, turn_back, 0)
    point("out")
    assemble(3, weights.at[3])
    pre[...] = nn_dot(att[...], weights[3])

    def norm_two(i, carry):
        at = rows_of(i)
        branch = pre[at, :] + vec24[3:4, :]
        mid = tok[at, :].astype(F32) + live_of(i) * branch
        middle[at, :] = mid
        normed, _ = norm_parts(mid)
        n2[at, :] = (normed * vec24[4:5, :] + vec24[5:6, :]).astype(BF16)
        return carry

    point("n2a")
    lax.fori_loop(0, chunks // 2, norm_two, 0)
    point("n2b")
    lax.fori_loop(chunks // 2, chunks, norm_two, 0)
    point("n2t")
    turn(n2, n2t)
    acc_out[...] = jnp.zeros_like(acc_out)
    acc_grad[...] = jnp.zeros_like(acc_grad)

    def store_rows(block, lhs_t, rhs):
        size = slabs.shape[-2]
        for first in range(0, width, 192):
            total = nn_dot(lhs_t[first : first + 192, :], rhs)
            for k in range(192 // size // 2):
                at = first // size + 2 * k
                two = total[2 * k * size : 2 * (k + 1) * size].reshape(2, size, width).astype(BF16)
                slabs[block, at // 8, at // 4 % 2, at // 2 % 2] = two

    def feed(t, carry):
        def step_point(name):
            points_at(t, [f"{name}{k}" for k in range(n_z)])

        step_point("fa")
        assemble(4 + t, w_up)
        up_bias = vec96[t, 6:7, :]
        half = count // 2

        def into_hidden(rows):
            pre[rows] = nn_dot(n2[rows], w_up[...])

        def into_grads(rows):
            grad_act[rows] = nt_dot(g2[rows], downs[t].reshape(width, width))

        def gelu_rows(first):
            for at in range(first, first + half, 32):
                rows = slice(at, at + 32)
                active, slope = gelu_both(pre[rows] + up_bias)
                act[rows] = active.astype(BF16)
                grad_h[rows] = (grad_act[rows] * slope).astype(BF16)

        def out_of(rows):
            acc_out[rows] += nn_dot(act[rows], downs[t].reshape(width, width))
            acc_grad[rows] += nt_dot(grad_h[rows], w_up[...])

        upper, lower = slice(0, half), slice(half, count)
        step_point("fb")
        into_hidden(upper)
        step_point("fc")
        into_grads(upper)
        step_point("fd")
        into_hidden(lower)
        into_grads(lower)
        gelu_rows(0)
        step_point("fe")
        out_of(upper)
        gelu_rows(half)
        step_point("ff")
        out_of(lower)
        step_point("fg")
        up_sums[t, 6:7, :] = column_sums(grad_h[...])[0:1]
        step_point("fh")
        store_rows(4 + t, n2t, grad_h[...])
        step_point("fi")
        for j in range(pairs):
            span = slice(j * 128, (j + 1) * 128)
            piece = nn_dot(act[:, span].T, g2[...]).astype(BF16)
            size = downs.shape[-2]
            at = j * 128
            while at < (j + 1) * 128:
                owner, inside = at // size, at % size
                length = min(size - inside, (j + 1) * 128 - at)
                downs[t, owner // 4, owner // 2 % 2, owner % 2, inside : inside + length, :] = piece[at - j * 128 : at - j * 128 + length]
                at += length
        return carry

    lax.fori_loop(0, n_z, feed, 0)

    def norm_two_back(i, carry):
        gain_sum, bias_sum = carry
        at = rows_of(i)
        alive = live_of(i)
        mid = middle[at, :]
        block_out[at, :] = (mid + alive * (acc_out[at, :] + vec24[7:8, :])).astype(BF16)
        normed, scale = norm_parts(mid)
        e = acc_grad[at, :]
        scaled = e * vec24[4:5, :]
        inner_part = scaled - jnp.mean(scaled, axis=-1, keepdims=True) - normed * jnp.mean(scaled * normed, axis=-1, keepdims=True)
        grad_mid = cot[at, :].astype(F32) + inner_part * scale
        acc_grad[at, :] = grad_mid
        g2[at, :] = (alive * grad_mid).astype(BF16)
        return (gain_sum + fold_rows(e * normed), bias_sum + fold_rows(e))

    zero = jnp.zeros((8, width), F32)
    block_out = act
    point("ba")
    carry = lax.fori_loop(0, chunks // 2, norm_two_back, (zero, zero))
    point("bb")
    gain_sum, bias_sum = lax.fori_loop(chunks // 2, chunks, norm_two_back, carry)
    sums[0, 4:5, :] = jnp.sum(gain_sum, axis=0, keepdims=True)
    sums[0, 5:6, :] = jnp.sum(bias_sum, axis=0, keepdims=True)
    sums[0, 3:4, :] = column_sums(g2[...])[0:1]
    out_copy = pltpu.make_async_copy(block_out, out_ref, local.at[0])
    out_copy.start()

    point("og")
    store_rows(3, att_t, g2[...])
    point("ga")
    grad_att = n2
    grad_att[...] = nt_dot(g2[...], weights[3]).astype(BF16)

    def attend_back(p, carry):
        group, (at_q, at_k, at_v) = places(p)
        points_at(p, [f"a{k}" for k in range(pairs)])
        keys = qkv[group, :, at_k]
        values = qkv[group, :, at_v]
        queries = qkv[group, :, at_q] * 0.125
        grads = grad_att[:, rows_of(p, 128)]
        keys_t = keys.T
        grad_keys = jnp.zeros((count, 128), F32)
        grad_values = jnp.zeros((count, 128), F32)
        for head in range(2):
            my_queries, my_grads = one_head(queries, head), one_head(grads, head)
            for part in range(parts):
                span = slice(part * q_block, (part + 1) * q_block)
                scores = nt_dot(keys, my_queries[span]) + bias[:, span]
                chances = jnp.exp(scores - lse[p, head : head + 1, span])
                slopes = nt_dot(values, my_grads[span])
                level = jnp.sum(chances * slopes, axis=0, keepdims=True)
                grad_scores = (chances * (slopes - level)).astype(BF16)
                grad_values += nn_dot(chances.astype(BF16), my_grads[span])
                grad_keys += nn_dot(grad_scores, my_queries[span])
                dq_t[64 * head : 64 * head + 64, span] = nn_dot(keys_t[64 * head : 64 * head + 64], grad_scores) * 0.125
        qkv[group, :, at_q] = dq_t[...].T.astype(BF16)
        qkv[group, :, at_k] = grad_keys.astype(BF16)
        qkv[group, :, at_v] = grad_values.astype(BF16)
        points_at(p, [f"H{k // per_group}" if k % per_group == per_group - 1 else "" for k in range(pairs)])

        @pl.when(lax.rem(p, per_group) == per_group - 1)
        def _():
            store_rows(group, n1t, qkv[group])
            group_sums[group] = column_sums(qkv[group])

        return carry

    lax.fori_loop(0, pairs, attend_back, 0)

    point("g2")
    pre[...] = nt_dot(qkv[2], weights[2])
    point("g1")
    pre[...] += nt_dot(qkv[1], weights[1])
    point("g0")
    pre[...] += nt_dot(qkv[0], weights[0])

    def norm_one_back(i, carry):
        gain_sum, bias_sum = carry
        at = rows_of(i)
        normed, scale = norm_parts(tok[at, :].astype(F32))
        e = pre[at, :]
        scaled = e * vec24[0:1, :]
        inner_part = scaled - jnp.mean(scaled, axis=-1, keepdims=True) - normed * jnp.mean(scaled * normed, axis=-1, keepdims=True)
        acc_grad[at, :] = acc_grad[at, :] + inner_part * scale
        return (gain_sum + fold_rows(e * normed), bias_sum + fold_rows(e))

    point("na")
    carry = lax.fori_loop(0, chunks // 2, norm_one_back, (zero, zero))
    point("nb")
    gain_sum, bias_sum = lax.fori_loop(chunks // 2, chunks, norm_one_back, carry)
    tgrad_copy = pltpu.make_async_copy(acc_grad, tgrad_ref, local.at[1])
    tgrad_copy.start()
    sums[0, 0:1, :] = jnp.sum(gain_sum, axis=0, keepdims=True)
    sums[0, 1:2, :] = jnp.sum(bias_sum, axis=0, keepdims=True)
    for g in range(3):
        span = slice(g * third, (g + 1) * third)
        sums[1, 2:3, span] = group_sums[g, 0:1, :third]
        sums[2, 2:3, span] = group_sums[g, 0:1, 2 * third :]
    point("gb")
    gsmalls[...] = gather_back(sums[0], 24).reshape(gsmalls.shape)
    for k in range(2):
        part = gather_back(sums[1 + k], 48)
        span = slice(k * n_z // 2, (k + 1) * n_z // 2)
        gsmalls[span] = gsmalls[span] + part.reshape(n_z // 2, 2, 2, 2, 8, 128)
    for k in range(n_z):
        gsmalls[k] = gsmalls[k] + gather_back(up_sums[k], 96).reshape(2, 2, 2, 8, 128)

    point("end")
    for name, unit in units.items():
        if name[0] == "r":
            rs_sent(unit)
    out_copy.wait()
    tgrad_copy.wait()
    do_all(last_copies, "wait")


def by_kernel(
    n_z, tokens, cotangent, clip_lengths, ln1_gain, ln1_bias, qkv_weight, qv_bias, out_weight, out_bias,
    ln2_gain, ln2_bias, up_weight, up_bias, down_weight, down_bias,
):
    count, width = tokens.shape
    size, deep = qkv_weight.shape[0], down_weight.shape[0]
    blocks = 4 + n_z
    vectors = (ln1_gain, ln1_bias, qv_bias, out_bias, ln2_gain, ln2_bias, up_bias, down_bias)
    vmem, dma = pltpu.VMEM, pltpu.SemaphoreType.DMA
    held = [
        vmem((blocks, n_z, 2, 2, 2, size, width), BF16),
        vmem((n_z, 2, 2, 2, deep, width), BF16),
        vmem((n_z, 2, 2, 2, 8, 128), F32),
        vmem((n_z, 2, 2, 2, 8, 128), F32),
        vmem((4, width, width), BF16),
        vmem((width, width), BF16),
        vmem((blocks, n_z, 2, 2, size, width), BF16),
        vmem((blocks - len(LATE_SUMS), 2, n_z, size, width // 2), BF16),
        vmem((blocks - len(LATE_SUMS), 2, n_z, size, width), BF16),
        vmem((blocks - len(LATE_SUMS), n_z, size, width), BF16),
        vmem((max(len(LATE_SUMS), 1), 2, size, width // 2), BF16),
        vmem((max(len(LATE_SUMS), 1), 2, size, width), BF16),
        vmem((max(len(LATE_SUMS), 1), n_z, 2, 2, size, width), BF16),
        vmem((n_z, 2, 2, deep, width), BF16),
        vmem((n_z, 2, deep, width // 2), BF16),
        vmem((n_z, 2, deep, width), BF16),
        vmem((n_z, deep, width), BF16),
        vmem((n_z, 2, 2, 8, 128), F32),
        vmem((n_z, 8, 128), F32),
        vmem((2, n_z, 8, 128), F32),
        vmem((n_z - 1, 8, 128), F32),
        vmem((3, count, width), BF16),
        vmem((width, count), BF16),
        vmem((count, width), BF16),
        vmem((width, count), BF16),
        vmem((count, width), F32),
        vmem((count, width), BF16),
        vmem((width, count), BF16),
        vmem((count, width), BF16),
        vmem((count, width), F32),
        vmem((count, width), F32),
        vmem((count, width), BF16),
        vmem((count, width), BF16),
        vmem((count, width), F32),
        vmem((count, width), F32),
        vmem((count, width), BF16),
        vmem((count, width), BF16),
        vmem((count, count), F32),
        vmem((width // 128, 2, count), F32),
        vmem((128, count), F32),
        vmem((8, width), F32),
        vmem((2, 8, width), F32),
        vmem((n_z, 8, width), F32),
        vmem((3, 8, width), F32),
        vmem((3, 8, width), F32),
        vmem((3, 8, width), F32),
        vmem((n_z, 8, width), F32),
        vmem(qkv_weight.shape, F32),
        vmem(out_weight.shape, F32),
        vmem(up_weight.shape, F32),
        vmem(down_weight.shape, F32),
        vmem((8, 128), F32),
        dma((semaphore_slots()[2],)),
        dma((len(semaphore_slots()[0]),)),
        dma((len(semaphore_slots()[1]),)),
        dma((16 + n_z,)),
    ]
    anywhere, whole = pl.BlockSpec(memory_space=pl.ANY), pl.BlockSpec(memory_space=pltpu.VMEM)
    shape = jax.ShapeDtypeStruct
    out, grad, g_qkv, g_out, g_up, g_down, g_small = pl.pallas_call(
        layer_kernel,
        out_shape=(
            shape((count, width), BF16),
            shape((count, width), F32),
            shape(qkv_weight.shape, F32),
            shape(out_weight.shape, F32),
            shape(up_weight.shape, F32),
            shape(down_weight.shape, F32),
            shape((8, 128), F32),
        ),
        in_specs=[pl.BlockSpec(memory_space=pltpu.SMEM)] + [anywhere] * 2 + [whole] * 8 + [anywhere] * 4,
        out_specs=(anywhere,) * 7,
        scratch_shapes=held,
        compiler_params=pltpu.CompilerParams(collective_id=0, has_side_effects=True, vmem_limit_bytes=VMEM_BYTES),
    )(clip_lengths, tokens, cotangent, *vectors, qkv_weight, out_weight, up_weight, down_weight)
    large = (out, grad, g_qkv, g_out, g_up, g_down)
    done = pl.pallas_call(
        hand_over,
        out_shape=tuple(shape(a.shape, a.dtype) for a in large) + tuple(shape(v.shape, F32) for v in vectors),
        in_specs=[anywhere] * (1 + len(large)),
        out_specs=(anywhere,) * (len(large) + len(vectors)),
        scratch_shapes=[vmem(a.shape, a.dtype) for a in (g_small, *large)] + [vmem(v.shape, F32) for v in vectors] + [dma((2, 24))],
    )(g_small, *large)
    out, grad, g_qkv, g_out, g_up, g_down = done[:6]
    parts = done[6:]
    return (out, grad, parts[0], parts[1], g_qkv, parts[2], g_out, parts[3], parts[4], parts[5], g_up, parts[6], g_down, parts[7])


def hand_over(*refs):
    small_ref, sources, targets, vectors = refs[0], refs[1:7], refs[7:13], refs[13:21]
    small, held, cut, sems = refs[21], refs[22:28], refs[28:36], refs[36]
    small_copy = pltpu.make_async_copy(small_ref, small, sems.at[0, 23])
    small_copy.start()
    pieces = []
    for src, mid, dst in zip(sources, held, targets):
        rows = src.shape[0]
        parts = 4 if rows % 64 == 0 else 1
        for k in range(parts):
            pieces.append([ref.at[pl.ds(k * (rows // parts), rows // parts)] for ref in (src, mid, dst)])
    inward = [pltpu.make_async_copy(src, mid, sems.at[0, k]) for k, (src, mid, _) in enumerate(pieces)]
    outward = [pltpu.make_async_copy(mid, dst, sems.at[1, k]) for k, (_, mid, dst) in enumerate(pieces)]
    for copy in inward:
        copy.start()
    small_copy.wait()
    cuts = []
    for k, (part, vector) in enumerate(zip(cut, vectors)):
        part[...] = small[k, 0 : part.shape[0]]
        cuts.append(pltpu.make_async_copy(part, vector, sems.at[1, 15 + k]))
        cuts[-1].start()
    for arrived, onward in zip(inward, outward):
        arrived.wait()
        onward.start()
    for copy in outward + cuts:
        copy.wait()


def step(**named):
    return next(iter(named.items()))


KINDS = dict(
    ab1=BOOT,
    ab2=BOOT,
    au0=DIRECT,
    au1=LATE,
    au2=LATE,
    au3=BOOT,
    ro=LATE,
    ru0=LATE,
    ru2=LATE,
)
LATE_SUMS = tuple(dict(ro=0, ru0=0, ru2=0))
TABLE = dict(
    mask=(step(au0=0), step(ab1=0), step(au2=0), step(ab2=0),),
    vec=(step(ab0=0), step(au3=0), step(aS=0), step(ab1=1), step(au2=1), step(ab3=0), step(au0=1), step(ab0=1), step(ab2=1), step(aS=1), step(ab1=2), step(adp=0), step(au0=2), step(au1=0), step(aS=2), step(ab1=3), step(ab3=1), step(ab0=2), step(au0=3), step(aS=3), step(au1=1), step(au0=4), step(ab2=2), step(aS=4),),
    turn=(step(ab1=4),),
    q0=(step(ab2=3), step(adp=1), step(au1=2), step(ab0=3), step(ab1=5), step(ab3=2), step(ab1=6), step(ab2=4), step(ab0=4), step(adp=2), step(ad0=0), step(ab0=5),),
    t1=(step(ab3=3), step(au1=3), step(au3=1),),
    q1=(step(ad1=0), step(ab2=5),),
    q2=(step(ad0=1), step(au2=2), step(ab2=6),),
    t4=(step(ab3=4), step(au1=4),),
    t5=(step(ad2=0),),
    tb=(step(ab3=5),),
    n2a=(step(au1=5), step(ad1=1),),
    n2b=(step(ad0=2),),
    fa0=(step(au3=2),),
    fc0=(step(au3=3), step(ad0=3),),
    fe0=(step(ad2=1),),
    ff0=(step(au2=3),),
    fg0=(step(ad1=2), step(ad3=0),),
    fi0=(step(ru0=0),),
    fa1=(step(rd0=0),),
    fc1=(step(ad1=3),),
    fe1=(step(au3=4),),
    ff1=(step(ru0=1), step(ad2=2),),
    fg1=(step(rd0=1), step(au2=4),),
    fi1=(step(ru1=0),),
    fa2=(step(rd1=0), step(ad2=3), step(ad3=1), step(au2=5),),
    fc2=(step(au3=5),),
    fe2=(step(ru1=1), step(ru0=2), step(rd0=2),),
    fg2=(step(ad3=2),),
    fi2=(step(ru2=0), step(au3=6),),
    fa3=(step(rd1=1), step(rd2=0),),
    fc3=(step(ad3=3),),
    fe3=(step(ru1=2), step(ru2=1),),
    fg3=(step(rd0=3),),
    fi3=(step(ru3=0), step(rd2=1),),
    ba=(step(rd3=0),),
    bb=(step(rd1=2),),
    ga=(step(ro=0), step(ru2=2),),
    a1=(step(ru3=1), step(rd3=1), step(ro=1),),
    H0=(step(rd1=3), step(rd2=2),),
    a2=(step(ru1=3), step(rh0=0),),
    a3=(step(ro=2), step(ru3=2),),
    H1=(step(rd3=2),),
    a4=(step(rh1=0), step(rd2=3),),
    a5=(step(rh1=1), step(ru3=3),),
    H2=(step(ru1=4), step(rh0=1), step(ru0=3),),
    g2=(step(rh2=0), step(ru3=4), step(rd3=3), step(rdl=0), step(ru2=3),),
    g0=(step(rh1=2),),
    nb=(step(rh2=1),),
    end=(step(ro=3), step(rS=0), step(ru1=5), step(rdl=1), step(ru3=5), step(rh0=2), step(rS=1), step(ru0=4), step(rh2=2), step(rh1=3), step(rh0=3), step(ro=4), step(rS=2), step(rh1=4), step(ru0=5), step(ru2=4), step(rh0=4), step(rdl=2), step(rh2=3), step(ro=5), step(rS=3), step(ru2=5), step(rh1=5), step(rh2=4), step(rh0=5), step(rS=4), step(rh2=5),),
)

ROW_SUMS = tuple(dict(rh0=0, rh1=0, rh2=0, ro=0, ru0=0, ru1=0, ru2=0, ru3=0))
VMEM_BYTES = 63 * 1024 * 1024


def kernel_fits(n_wide, n_narrow, tokens, qkv_weight, up_weight, down_weight):
    width, hidden = qkv_weight.shape[0], up_weight.shape[1]
    n_z = n_wide // 4
    devices = n_wide * n_narrow
    return (
        n_narrow == 2
        and n_wide == 4 * n_z
        and n_z == 4
        and hidden == n_z * width
        and width % (8 * devices) == 0
        and hidden % (16 * devices) == 0
        and 2 * width // devices <= 128
        and hidden // devices <= 128
        and width // devices == 24
        and (tokens.shape[0] // devices) % (2 * CHUNK) == 0
    )


def solution(mesh):
    n_wide, n_narrow = [mesh.shape[axis] for axis in BOTH_AXES]
    matrix, vector = P(BOTH_AXES, None), P(BOTH_AXES)
    in_specs = (
        matrix, matrix, matrix, vector, vector, matrix, vector, matrix, vector, vector, vector, matrix, vector, matrix, vector,
    )
    out_specs = (
        matrix, matrix, vector, vector, matrix, vector, matrix, vector, vector, vector, matrix, vector, matrix, vector,
    )

    def run(*arrays):
        fits = kernel_fits(n_wide, n_narrow, arrays[0], arrays[5], arrays[11], arrays[13])
        body = functools.partial(by_kernel, n_wide // 4) if fits else by_collectives
        return jax.shard_map(body, mesh=mesh, in_specs=in_specs, out_specs=out_specs, check_vma=False)(*arrays)

    return run
```

```python
import functools
import math

import jax
import jax.numpy as jnp
from jax import lax
from jax.experimental import pallas as pl
from jax.experimental.pallas import tpu as pltpu
from jax.sharding import PartitionSpec as P

H = 12
MASKED_SCORE = -1000000000.0
MESH = pl.DeviceIdType.MESH
F32 = jnp.float32
BF16 = jnp.bfloat16
ALL = slice(None)
CHUNK = 256
LAST_POINT = "end"
BOTH_AXES = ("wide", "narrow")
ACROSS = "across"
Z_FAR = "z far"
CORE = "core"
Z_LAST = "z last"
NEAR = "near"
RELAY = "relay"
WAIT_SEND = "wait_send"
WAIT_RECV = "wait_recv"
START = "start"
LATE = "late"
PLAIN = "plain"
Z_OUTER = "z outer"
Z_NEAR = "z near"
DIRECT = "direct"
Z_ALL = "zd"
LATE_DIRECT = "late direct"
REST = "rest"
PAIR = "pair"
OWN = "own"
BOOT = "boot"
Z_TWO = "z"


def layer_norm(inputs, ln_gain, ln_bias):
    row_mean = jnp.mean(inputs, axis=-1, keepdims=True)
    centred = inputs - row_mean
    spread = jnp.mean(centred * centred, axis=-1, keepdims=True)
    return centred * lax.rsqrt(spread + 1e-06) * ln_gain + ln_bias


def gelu_exact(inputs):
    return 0.5 * inputs * (1.0 + lax.erf(inputs * 0.7071067811865476))


def clip_index(lengths, row_count):
    clip_ends = jnp.cumsum(lengths)
    position = jnp.arange(row_count, dtype=jnp.int32)
    return jnp.sum((position[:, None] >= clip_ends[None, :]).astype(jnp.int32), axis=1)


def split_heads(matrix, head_count):
    row_count = matrix.shape[0]
    return matrix.reshape(row_count, head_count, -1).transpose(1, 0, 2)


def join_heads(stacked):
    head_count, row_count, head_size = stacked.shape
    return stacked.transpose(1, 0, 2).reshape(row_count, head_count * head_size)


def attend_forward(queries, key_rows, value_rows, segment, block_rows, score_scale):
    scores = (
        lax.dot_general(
            queries, key_rows, (((1,), (1,)), ((), ())), preferred_element_type=jnp.float32
        )
        * score_scale
    )
    allowed = segment[0:block_rows, None] == segment[None, :]
    scores = jnp.where(allowed, scores, MASKED_SCORE)
    highest = jnp.max(scores, axis=1, keepdims=True)
    raised = jnp.exp(scores - highest)
    denominator = jnp.sum(raised, axis=1, keepdims=True)
    softmax = (raised / denominator).astype(jnp.bfloat16)
    outputs = [jnp.dot(softmax, value_rows, preferred_element_type=jnp.float32)]
    totals = [highest + jnp.log(denominator)]
    return (jnp.concatenate(outputs, 0), jnp.concatenate(totals, 0))


def attend_backward(
    queries, key_rows, value_rows, segment, grad_out, lse_rows, block_rows, score_scale
):
    grad_keys = jnp.zeros(key_rows.shape, jnp.float32)
    grad_values = jnp.zeros(value_rows.shape, jnp.float32)
    g_rows = grad_out[0:block_rows]
    scores = (
        lax.dot_general(
            queries, key_rows, (((1,), (1,)), ((), ())), preferred_element_type=jnp.float32
        )
        * score_scale
    )
    allowed = segment[0:block_rows, None] == segment[None, :]
    softmax = jnp.where(allowed, jnp.exp(scores - lse_rows[0:block_rows]), 0.0)
    grad_values = grad_values + lax.dot_general(
        softmax.astype(jnp.bfloat16),
        g_rows,
        (((0,), (0,)), ((), ())),
        preferred_element_type=jnp.float32,
    )
    grad_probs = lax.dot_general(
        g_rows, value_rows, (((1,), (1,)), ((), ())), preferred_element_type=jnp.float32
    )
    grad_scores = (
        softmax * (grad_probs - jnp.sum(softmax * grad_probs, axis=1, keepdims=True))
    ).astype(jnp.bfloat16)
    grad_queries = [
        jnp.dot(grad_scores, key_rows, preferred_element_type=jnp.float32) * score_scale
    ]
    grad_keys = (
        grad_keys
        + lax.dot_general(
            grad_scores, queries, (((0,), (0,)), ((), ())), preferred_element_type=jnp.float32
        )
        * score_scale
    )
    return (jnp.concatenate(grad_queries, 0), grad_keys, grad_values)


def by_collectives(
    tokens,
    cotangent,
    clip_lengths,
    ln1_gain,
    ln1_bias,
    qkv_weight,
    qv_bias,
    out_weight,
    out_bias,
    ln2_gain,
    ln2_bias,
    up_weight,
    up_bias,
    down_weight,
    down_bias,
):
    gathered = (
        lax.all_gather(ln1_gain, BOTH_AXES, axis=0, tiled=True),
        lax.all_gather(ln1_bias, BOTH_AXES, axis=0, tiled=True),
        lax.all_gather(qkv_weight, BOTH_AXES, axis=0, tiled=True),
        lax.all_gather(qv_bias, BOTH_AXES, axis=0, tiled=True),
        lax.all_gather(out_weight, BOTH_AXES, axis=0, tiled=True),
        lax.all_gather(out_bias, BOTH_AXES, axis=0, tiled=True),
        lax.all_gather(ln2_gain, BOTH_AXES, axis=0, tiled=True),
        lax.all_gather(ln2_bias, BOTH_AXES, axis=0, tiled=True),
        lax.all_gather(up_weight, BOTH_AXES, axis=0, tiled=True),
        lax.all_gather(up_bias, BOTH_AXES, axis=0, tiled=True),
        lax.all_gather(down_weight, BOTH_AXES, axis=0, tiled=True),
        lax.all_gather(down_bias, BOTH_AXES, axis=0, tiled=True),
    )
    (
        gain_one,
        bias_one,
        merged_weight,
        merged_bias,
        proj_weight,
        proj_bias,
        gain_two,
        bias_two,
        w_up,
        b_up,
        w_down,
        b_down,
    ) = gathered
    inputs = tokens.astype(jnp.float32)
    row_count, model_width = inputs.shape
    head_size = model_width // H
    score_scale = 1.0 / math.sqrt(head_size)
    block_rows = min(512, row_count)
    clip_count = clip_lengths.shape[1]
    segment = clip_index(clip_lengths[0], row_count)
    live_rows = (segment < clip_count).astype(jnp.float32)[:, None]
    normed_one = layer_norm(
        inputs, gain_one.astype(jnp.float32), bias_one.astype(jnp.float32)
    ).astype(jnp.bfloat16)
    bias_float = merged_bias.astype(jnp.float32)
    full_bias = jnp.concatenate(
        [bias_float[:model_width], jnp.zeros((model_width,), jnp.float32), bias_float[model_width:]]
    )
    merged_rows = (
        jnp.dot(normed_one, merged_weight, preferred_element_type=jnp.float32) + full_bias
    ).astype(jnp.bfloat16)
    q_heads = split_heads(merged_rows[:, :model_width], H)
    k_heads = split_heads(merged_rows[:, model_width : 2 * model_width], H)
    v_heads = split_heads(merged_rows[:, 2 * model_width :], H)

    def head_forward(triple):
        return attend_forward(triple[0], triple[1], triple[2], segment, block_rows, score_scale)

    att_heads, lse_heads = lax.map(head_forward, (q_heads, k_heads, v_heads))
    attended = join_heads(att_heads).astype(jnp.bfloat16)
    branch_one = jnp.dot(
        attended, proj_weight, preferred_element_type=jnp.float32
    ) + proj_bias.astype(jnp.float32)
    middle = inputs + live_rows * branch_one
    normed_two = layer_norm(
        middle, gain_two.astype(jnp.float32), bias_two.astype(jnp.float32)
    ).astype(jnp.bfloat16)
    hidden_pre = jnp.dot(normed_two, w_up, preferred_element_type=jnp.float32) + b_up.astype(
        jnp.float32
    )
    activated, gelu_pull = jax.vjp(gelu_exact, hidden_pre)
    activated = activated.astype(jnp.bfloat16)
    branch_two = jnp.dot(activated, w_down, preferred_element_type=jnp.float32) + b_down.astype(
        jnp.float32
    )
    block_out = (middle + live_rows * branch_two).astype(jnp.bfloat16)
    back_gain_one, back_merged, back_proj, back_gain_two, back_up, back_down = (
        lax.all_gather(ln1_gain, BOTH_AXES, axis=0, tiled=True),
        lax.all_gather(qkv_weight, BOTH_AXES, axis=0, tiled=True),
        lax.all_gather(out_weight, BOTH_AXES, axis=0, tiled=True),
        lax.all_gather(ln2_gain, BOTH_AXES, axis=0, tiled=True),
        lax.all_gather(up_weight, BOTH_AXES, axis=0, tiled=True),
        lax.all_gather(down_weight, BOTH_AXES, axis=0, tiled=True),
    )
    upstream = cotangent.astype(jnp.float32)
    grad_two = (live_rows * upstream).astype(jnp.bfloat16)
    grad_b_down = jnp.sum(grad_two.astype(jnp.float32), axis=0)
    grad_w_down = jnp.einsum("tf,td->fd", activated, grad_two, preferred_element_type=jnp.float32)
    grad_act = jnp.einsum("td,fd->tf", grad_two, back_down, preferred_element_type=jnp.float32)
    grad_hidden = gelu_pull(grad_act)[0].astype(jnp.bfloat16)
    grad_b_up = jnp.sum(grad_hidden.astype(jnp.float32), axis=0)
    grad_w_up = jnp.einsum("td,tf->df", normed_two, grad_hidden, preferred_element_type=jnp.float32)
    grad_normed_two = jnp.einsum(
        "tf,df->td", grad_hidden, back_up, preferred_element_type=jnp.float32
    )
    _, norm_pull_two = jax.vjp(
        layer_norm, middle, back_gain_two.astype(jnp.float32), bias_two.astype(jnp.float32)
    )
    grad_middle_norm, grad_gain_two, grad_bias_two = norm_pull_two(grad_normed_two)
    grad_middle = upstream + grad_middle_norm
    grad_one = (live_rows * grad_middle).astype(jnp.bfloat16)
    grad_b_proj = jnp.sum(grad_one.astype(jnp.float32), axis=0)
    grad_w_proj = jnp.einsum("te,td->ed", attended, grad_one, preferred_element_type=jnp.float32)
    grad_att = jnp.einsum(
        "td,ed->te", grad_one, back_proj, preferred_element_type=jnp.float32
    ).astype(jnp.bfloat16)
    grad_att_heads = split_heads(grad_att, H)

    def head_backward(members):
        return attend_backward(
            members[0],
            members[1],
            members[2],
            segment,
            members[3],
            members[4],
            block_rows,
            score_scale,
        )

    grad_q, grad_k, grad_v = lax.map(
        head_backward, (q_heads, k_heads, v_heads, grad_att_heads, lse_heads)
    )
    grad_merged = jnp.concatenate(
        [join_heads(grad_q), join_heads(grad_k), join_heads(grad_v)], 1
    ).astype(jnp.bfloat16)
    column_sums = jnp.sum(grad_merged.astype(jnp.float32), axis=0)
    grad_merged_bias = jnp.concatenate([column_sums[:model_width], column_sums[2 * model_width :]])
    grad_w_merged = jnp.einsum(
        "te,tf->ef", normed_one, grad_merged, preferred_element_type=jnp.float32
    )
    grad_normed_one = jnp.einsum(
        "tf,ef->te", grad_merged, back_merged, preferred_element_type=jnp.float32
    )
    _, norm_pull_one = jax.vjp(
        layer_norm, inputs, back_gain_one.astype(jnp.float32), bias_one.astype(jnp.float32)
    )
    grad_input_norm, grad_gain_one, grad_bias_one = norm_pull_one(grad_normed_one)
    tokens_grad = grad_middle + grad_input_norm
    shares = (
        lax.psum_scatter(grad_gain_one, BOTH_AXES, scatter_dimension=0, tiled=True),
        lax.psum_scatter(grad_bias_one, BOTH_AXES, scatter_dimension=0, tiled=True),
        lax.psum_scatter(grad_w_merged, BOTH_AXES, scatter_dimension=0, tiled=True),
        lax.psum_scatter(grad_merged_bias, BOTH_AXES, scatter_dimension=0, tiled=True),
        lax.psum_scatter(grad_w_proj, BOTH_AXES, scatter_dimension=0, tiled=True),
        lax.psum_scatter(grad_b_proj, BOTH_AXES, scatter_dimension=0, tiled=True),
        lax.psum_scatter(grad_gain_two, BOTH_AXES, scatter_dimension=0, tiled=True),
        lax.psum_scatter(grad_bias_two, BOTH_AXES, scatter_dimension=0, tiled=True),
        lax.psum_scatter(grad_w_up, BOTH_AXES, scatter_dimension=0, tiled=True),
        lax.psum_scatter(grad_b_up, BOTH_AXES, scatter_dimension=0, tiled=True),
        lax.psum_scatter(grad_w_down, BOTH_AXES, scatter_dimension=0, tiled=True),
        lax.psum_scatter(grad_b_down, BOTH_AXES, scatter_dimension=0, tiled=True),
    )
    return (
        block_out,
        tokens_grad,
        shares[0],
        shares[1],
        shares[2],
        shares[3],
        shares[4],
        shares[5],
        shares[6],
        shares[7],
        shares[8],
        shares[9],
        shares[10],
        shares[11],
    )


def nt_dot(left, right):
    return lax.dot_general(left, right, (((1,), (1,)), ((), ())), preferred_element_type=F32)


def nn_dot(left, right):
    return jnp.dot(left, right, preferred_element_type=F32)


def rows_of(step, size=CHUNK):
    return pl.ds(pl.multiple_of(step * size, size), size)


def norm_parts(values):
    centred = values - jnp.mean(values, axis=-1, keepdims=True)
    scale = lax.rsqrt(jnp.mean(centred * centred, axis=-1, keepdims=True) + 1e-06)
    return centred * scale, scale


def fold_rows(values):
    return jnp.sum(values.reshape(-1, 8, values.shape[-1]), axis=0)


def gelu_both(u):
    tail = 0.5 * (1.0 + lax.erf(u * 0.7071067811865476))
    return u * tail, tail + u * jnp.exp(-0.5 * u * u) * 0.3989422804014327


def spread_maps(width, columns):
    column = lax.broadcasted_iota(jnp.int32, (1, columns), 1).astype(F32)
    group = jnp.floor((column + 0.5) * (1.0 / width))
    place = column - group * width
    lane = lax.broadcasted_iota(jnp.int32, (128, columns), 0).astype(F32)
    picks = jnp.where(lane == place, 1.0, 0.0).astype(BF16)
    owners = columns // width
    owner = lax.broadcasted_iota(jnp.int32, (owners, 8, columns), 0).astype(F32)
    mine = owner == group.reshape(1, 1, columns)
    return picks, mine


def spread(pieces, width, columns):
    picks, mine = spread_maps(width, columns)
    wide_rows = nn_dot(pieces.reshape(-1, 128).astype(BF16), picks)
    return jnp.sum(jnp.where(mine, wide_rows.reshape(-1, 8, columns), 0.0), axis=0)


def gather_back(vectors, width):
    columns = vectors.shape[-1]
    picks, mine = spread_maps(width, columns)
    rest = jnp.where(mine, vectors[None], 0.0).reshape(-1, columns)
    total = None
    for _ in range(3):
        part = rest.astype(BF16)
        rest = rest - part.astype(F32)
        term = nt_dot(part, picks)
        total = term if total is None else total + term
    return total.reshape(-1, 8, 128)


Z0, Z1, Z2, ZR, X0, Y0, X1, Y1, X2, Y2, DX, DY, C0 = range(13)
ORDERS = {
    PLAIN: (Z_TWO, RELAY, NEAR, ACROSS, CORE),
    DIRECT: (Z_ALL, NEAR, ACROSS, CORE),
    BOOT: (OWN, Z_ALL, PAIR, REST, ACROSS, CORE),
    LATE: (NEAR, ACROSS, Z_TWO, RELAY, CORE),
    LATE_DIRECT: (NEAR, ACROSS, Z_ALL, CORE),
}
BACK = {
    PLAIN: (CORE, ACROSS, NEAR, Z_TWO, Z_FAR),
    DIRECT: (CORE, ACROSS, NEAR, Z_ALL),
    LATE: (CORE, Z_TWO, Z_FAR, ACROSS, NEAR),
    LATE_DIRECT: (CORE, Z_ALL, ACROSS, NEAR),
}


def phases_of(name):
    kind = DIRECT if name[1:] == "S" else KINDS.get(name, PLAIN)
    if name[:2] == "ad":
        return ((Z_TWO, RELAY) if kind == PLAIN else (Z_ALL,)) if name == "adp" else (NEAR, ACROSS, CORE)
    if name[:2] == "rd":
        return ((Z_TWO, Z_FAR) if kind == PLAIN else (Z_ALL,)) if name == "rdl" else (CORE, ACROSS, NEAR)
    return (ORDERS if name[0] == "a" else BACK)[kind]


def semaphore_slots():
    used = {
        Z_TWO: (Z0, Z1, Z2), RELAY: (ZR,), Z_ALL: (Z0, Z1, Z2), OWN: (X1, Y1), PAIR: (X2, Y2), REST: (X0, Y0),
        NEAR: (X0, Y0), ACROSS: (DX, DY), CORE: (C0,), Z_FAR: (ZR, Z1),
    }
    gathers = list(dict(aS=0, ab0=0, ab1=0, ab2=0, ab3=0, adp=0, au0=0, ad0=0, au1=0, ad1=0, au2=0, ad2=0, au3=0, ad3=0))
    sums = list(dict(ru0=0, rd0=0, ru1=0, rd1=0, ru2=0, rd2=0, ru3=0, rd3=0, ro=0, rdl=0, rh0=0, rh1=0, rh2=0, rS=0))
    slots = []
    for names in (gathers, sums):
        places = {}
        for name in names:
            for sem in sorted({sem for phase in phases_of(name) for sem in used[phase]}):
                places[name, sem] = len(places)
        slots.append(places)
    return slots[0], slots[1], max(len(slots[0]), len(slots[1])), len(slots[0])


def layer_kernel(
    clip_ref, tok_ref, cot_ref, v0, v1, v2, v3, v4, v5, v6, v7, wqkv_ref, wout_ref, wup_ref, wdown_ref,
    out_ref, tgrad_ref, gqkv_ref, gout_ref, gup_ref, gdown_ref, gsmall_ref,
    slabs, downs, smalls, gsmalls, weights, w_up,
    row_c, row_d, row_n, row_z, late_d, late_n, late_z, down_c, down_d, down_n, down_z, sm_c, sm_d, sm_n, sm_z,
    qkv, n1t, n1, att_t, middle, n2, n2t, g2, acc_out, acc_grad, act, grad_h, pre, grad_act,
    tok, cot, bias, lse, dq_t, vec24, vec48, vec96, merged_bias, group_sums, sums, up_sums, gqkv, gout, gup, gdown, gsmall,
    sends, ag_recv, rs_recv, local,
):
    n_z, width = slabs.shape[1], slabs.shape[-1]
    count = tok.shape[0]
    pairs = width // 128
    chunks = count // CHUNK
    wide_at, y = lax.axis_index(BOTH_AXES[0]), lax.axis_index(BOTH_AXES[1])
    core = lax.rem(wide_at, 2)
    x = lax.rem(lax.div(wide_at, 2), 2)
    z = lax.div(wide_at, 4)

    def device(z_at, x_at, c_at, y_at):
        return ((z_at * 2 + x_at) * 2 + c_at, y_at)

    def row_view(block):
        def view(at):
            return slabs.at[(block, *at)]
        return view

    def down_view(tile):
        def view(at):
            return downs.at[(tile, *at[1:])]
        return view

    def small_view(ref):
        def view(at):
            return ref.at[at]
        return view

    def half_of(ref, side):
        if ref.shape[-1] < 2 * 128:
            return ref
        cut = ref.shape[-1] // 2
        return ref.at[(*([ALL] * (len(ref.shape) - 1)), pl.ds(side * cut, cut))]

    to_x, to_y, to_c = device(z, 1 - x, core, y), device(z, x, core, 1 - y), device(z, x, 1 - core, y)
    z_places = (z + 1 - 2 * lax.rem(z, 2), lax.rem(z + 2, n_z), n_z - 1 - z)
    along_z = [device(at, x, core, y) for at in z_places]
    other_pair = pl.ds(2 * (1 - lax.div(z, 2)), 2)
    inner = lax.rem(z + 1, n_z) >= 2

    ag_slots, rs_slots, _, _ = semaphore_slots()

    def remote(src, dst, sums, unit_name, sem, to, recv_sem=None):
        slots = rs_slots if sums else ag_slots
        recv = rs_recv if sums else ag_recv
        return pltpu.make_async_remote_copy(
            src_ref=src, dst_ref=dst, send_sem=sends.at[slots[unit_name, sem]],
            recv_sem=recv.at[slots[unit_name, sem if recv_sem is None else recv_sem]],
            device_id=to, device_id_type=MESH,
        )

    def do_all(copies, what):
        for copy in copies:
            getattr(copy, what)()

    one, plane = (x, core, y), (ALL, core, ALL)

    def ag_copies(unit, phase):
        view, row, phases, along = unit
        sems = False
        held = z if along is plane else ALL

        def both(at, sem):
            mine = view((at, x, core, y))
            return [remote(mine, mine, sems, row, sem, to_x), remote(mine, mine, sems, row, sem + 1, to_y)]

        def own_to(*which):
            own = view((z, *along))
            return [remote(own, own, sems, row, k, along_z[k]) for k in which]

        if phase == Z_TWO:
            return own_to(Z0, Z1)
        if phase == Z_ALL:
            return own_to(Z0, Z1, Z2)
        if phase in (Z_NEAR, Z_FAR, Z_LAST):
            return own_to((Z_NEAR, Z_FAR, Z_LAST).index(phase))
        if phase == RELAY:
            passed = view((z_places[1], *along))
            return [remote(passed, passed, sems, row, ZR, along_z[0], Z2)]
        if phase == OWN:
            return both(z, X1)
        if phase == PAIR:
            return both(z_places[0], X2)
        if phase == REST:
            return both(other_pair, X0)
        if phase == NEAR:
            return both(held, X0)
        if phase == ACROSS:
            from_x, from_y = view((held, 1 - x, core, y)), view((held, x, core, 1 - y))
            first = half_of(from_x, 0)
            copies = [remote(first, first, sems, row, DY, to_y)]
            if from_x.shape[-1] >= 2 * 128:
                second = half_of(from_y, 1)
                copies.append(remote(second, second, sems, row, DX, to_x))
            return copies
        whole_plane = view((ALL, ALL, core, ALL))
        return [remote(whole_plane, whole_plane, sems, row, C0, to_c)]

    def ag_wait(unit, *phases):
        for phase in phases:
            do_all(ag_copies(unit, phase), WAIT_RECV)

    def ag_stage(unit, stage):
        phases = unit[2]
        phase = phases[stage] if stage < len(phases) else None
        if phase == RELAY:
            @pl.when(inner)
            def _():
                ag_wait(unit, Z_FAR)
                do_all(ag_copies(unit, RELAY), START)
            return
        if phase == PAIR:
            ag_wait(unit, Z_NEAR)
        elif phase == REST:
            ag_wait(unit, Z_FAR, Z_LAST)
        elif phase == ACROSS and OWN in phases:
            ag_wait(unit, OWN, PAIR, REST)
        elif stage > 0 and phases[stage - 1] == RELAY:
            @pl.when(jnp.logical_not(inner))
            def _():
                ag_wait(unit, Z_FAR)
            ag_wait(unit, Z_NEAR, Z_LAST)
        elif stage > 0 and phases[stage - 1] != OWN:
            ag_wait(unit, phases[stage - 1])
        if phase:
            do_all(ag_copies(unit, phase), START)
            if phase == Z_TWO:
                @pl.when(inner)
                def _():
                    do_all(ag_copies(unit, Z_LAST), START)
        else:
            for sent in phases:
                if sent != RELAY:
                    do_all(ag_copies(unit, sent), WAIT_SEND)
            if RELAY in phases:
                @pl.when(inner)
                def _():
                    do_all(ag_copies(unit, Z_LAST) + ag_copies(unit, RELAY), WAIT_SEND)

    def gather_unit(name, view):
        kind = KINDS.get(name, PLAIN)
        return (view, name, phases_of(name), plane if kind[:4] == LATE else one)

    units = {"aS": gather_unit("aS", small_view(smalls)), "adp": gather_unit("adp", lambda at: downs.at[at])}
    for block in range(4):
        units[f"ab{block}"] = gather_unit(f"ab{block}", row_view(block))
    for tile in range(n_z):
        units[f"au{tile}"] = gather_unit(f"au{tile}", row_view(4 + tile))
        units[f"ad{tile}"] = gather_unit(f"ad{tile}", down_view(tile))

    def rs_copies(unit, phase):
        view, row, phases, landing, along = unit
        sems = True
        held = z if along is plane else ALL
        if phase == CORE:
            return [remote(view((ALL, ALL, 1 - core, ALL)), landing[CORE], sems, row, C0, to_c)]
        if phase == ACROSS:
            away = view((held, 1 - x, core, 1 - y))
            copies = [remote(half_of(away, 0), landing["dx"], sems, row, DX, to_x)]
            if away.shape[-1] >= 2 * 128:
                copies.append(remote(half_of(away, 1), landing["dy"], sems, row, DY, to_y))
            return copies
        if phase == NEAR:
            return [
                remote(view((held, 1 - x, core, y)), landing["x"], sems, row, X0, to_x),
                remote(view((held, x, core, 1 - y)), landing["y"], sems, row, Y0, to_y),
            ]
        if phase == Z_OUTER:
            return [remote(view((z_places[2], *along)), landing[Z_TWO].at[ZR], sems, row, ZR, along_z[0])]
        which = {Z_TWO: (Z0,), Z_FAR: (Z1,), Z_LAST: (Z2,), Z_ALL: (Z0, Z1, Z2)}[phase]
        return [remote(view((z_places[k], *along)), landing[Z_TWO].at[k], sems, row, k, along_z[k]) for k in which]

    def add_into(target, *sources):
        total = target[...].astype(F32)
        for source in sources:
            total = total + source[...].astype(F32)
        target[...] = total.astype(target.dtype)

    def add_all(target, *sources):
        free = len(target.shape) - 2
        if free == 0:
            add_into(target, *sources)
            return
        places = [()]
        for extent in target.shape[1:free]:
            places = [place + (k,) for place in places for k in range(extent)]

        def step(i, carry):
            for place in places:
                add_into(target.at[(i, *place)], *[source.at[(i, *place)] for source in sources])
            return carry

        lax.fori_loop(0, target.shape[0], step, 0)

    def rs_stage(unit, stage):
        view, _, phases, landing, along = unit
        held = z if along is plane else ALL
        before = phases[stage - 1] if stage > 0 else None
        phase = phases[stage] if stage < len(phases) else None
        if phase == Z_FAR:
            @pl.when(inner)
            def _():
                do_all(rs_copies(unit, Z_OUTER), WAIT_RECV)
                add_all(view((z_places[1], *along)), landing[Z_TWO].at[ZR])
        elif before == Z_FAR:
            rs_wait(unit, Z_TWO, Z_FAR)
            add_all(view((z, *along)), landing[Z_TWO].at[Z0], landing[Z_TWO].at[Z1])

            @pl.when(inner)
            def _():
                rs_wait(unit, Z_LAST)
                add_all(view((z, *along)), landing[Z_TWO].at[Z2])
        elif before:
            rs_wait(unit, before)
        if before == CORE:
            add_all(view((ALL, ALL, core, ALL)), landing[CORE])
        elif before == ACROSS:
            on_y = view((held, x, core, 1 - y))
            add_all(half_of(on_y, 0), landing["dx"])
            if on_y.shape[-1] >= 2 * 128:
                add_all(half_of(view((held, 1 - x, core, y)), 1), landing["dy"])
        elif before == NEAR:
            add_all(view((held, x, core, y)), landing["x"], landing["y"])
        elif before == Z_ALL:
            add_all(view((z, *along)), *[landing[Z_TWO].at[k] for k in (Z0, Z1, Z2)])
        if phase:
            do_all(rs_copies(unit, phase), START)
        if phase == Z_TWO:
            @pl.when(inner)
            def _():
                do_all(rs_copies(unit, Z_LAST), START)

            @pl.when(jnp.logical_not(inner))
            def _():
                do_all(rs_copies(unit, Z_OUTER), START)

    def rs_wait(unit, *phases):
        for phase in phases:
            do_all(rs_copies(unit, phase), WAIT_RECV)

    def rs_end(unit, *results):
        view, _, phases, landing, along = unit
        last = phases[-1]
        if last == NEAR:
            sources = [landing["x"], landing["y"]]
        else:
            sources = [landing[Z_TWO].at[k] for k in ((Z0, Z1) if last == Z_FAR else (Z0, Z1, Z2))]
        rs_wait(unit, *((Z_TWO, Z_FAR) if last == Z_FAR else (last,)))
        total = view((z, x, core, y))[...].astype(F32)
        for part in sources:
            total = total + part[...].astype(F32)
        size = total.shape[-1] // len(results)
        for k, result in enumerate(results):
            result[...] = total[:, k * size : (k + 1) * size]
        if last == Z_FAR:
            @pl.when(inner)
            def _():
                rs_wait(unit, Z_LAST)
                for k, result in enumerate(results):
                    result[...] += landing[Z_TWO][Z2, :, k * size : (k + 1) * size].astype(F32)

    def rs_sent(unit):
        for phase in unit[2]:
            do_all(rs_copies(unit, phase), WAIT_SEND)
        if Z_FAR in unit[2]:
            @pl.when(inner)
            def _():
                do_all(rs_copies(unit, Z_LAST), WAIT_SEND)

            @pl.when(jnp.logical_not(inner))
            def _():
                do_all(rs_copies(unit, Z_OUTER), WAIT_SEND)

    def row_unit(block, name):
        if name in LATE_SUMS:
            late = LATE_SUMS.index(name)
            landing = {CORE: row_c.at[block], "dx": late_d.at[late, 0], "dy": late_d.at[late, 1], "x": late_n.at[late, 0], "y": late_n.at[late, 1], Z_TWO: late_z.at[late]}
            return (row_view(block), name, phases_of(name), landing, plane)
        at = block - sum(earlier in LATE_SUMS for earlier in ROW_SUMS[:block])
        landing = {CORE: row_c.at[block], "dx": row_d.at[at, 0], "dy": row_d.at[at, 1], "x": row_n.at[at, 0], "y": row_n.at[at, 1], Z_TWO: row_z.at[at]}
        return (row_view(block), name, phases_of(name), landing, one)

    def down_unit(tile, name):
        landing = {CORE: down_c.at[tile], "dx": down_d.at[tile, 0], "dy": down_d.at[tile, 1], "x": down_n.at[tile, 0], "y": down_n.at[tile, 1]}
        return (down_view(tile), name, phases_of(name), landing, one)

    def block_columns(block):
        return pl.ds(block * width, width)

    third = width // 3
    results = {"rdl": [gdown], "ro": [gout], "rS": [gsmall]}
    for t in range(n_z):
        units[f"ru{t}"] = row_unit(4 + t, f"ru{t}")
        units[f"rd{t}"] = down_unit(t, f"rd{t}")
        results[f"ru{t}"] = [gup.at[:, block_columns(t)]]
    for g in range(3):
        units[f"rh{g}"] = row_unit(g, f"rh{g}")
        results[f"rh{g}"] = [gqkv.at[:, pl.ds(j * width + g * third, third)] for j in range(3)]
    units["ro"] = row_unit(3, "ro")
    small_landing = {CORE: sm_c, "dx": sm_d, "x": sm_n.at[0], "y": sm_n.at[1], Z_TWO: sm_z}
    units["rS"] = (small_view(gsmalls), "rS", phases_of("rS"), small_landing, one)
    units["rdl"] = (lambda at: downs.at[at], "rdl", phases_of("rdl"), {Z_TWO: down_z}, one)
    whole_results = {"rdl": [gdown_ref], "ro": [gout_ref], "rS": [gsmall_ref]}
    for t in range(n_z):
        whole_results[f"ru{t}"] = [gup_ref.at[:, block_columns(t)]]
    for g in range(3):
        whole_results[f"rh{g}"] = [gqkv_ref.at[:, pl.ds(j * width + g * third, third)] for j in range(3)]
    last_copies = []

    def set_of_sums():
        return [unit_name for unit_name in units if unit_name[0] == "r"]

    def point(name):
        listed = TABLE.get(name, ())
        for place, (unit_name, stage) in enumerate(listed):
            if name == LAST_POINT and place == len(listed) - 2:
                for other in set_of_sums():
                    if other not in (unit_name, listed[-1][0]):
                        rs_sent(units[other])
            unit = units[unit_name]
            if unit_name[0] == "a":
                ag_stage(unit, stage)
            elif unit_name in results and stage == len(unit[2]):
                rs_end(unit, *results[unit_name])
                for src, dst in zip(results[unit_name], whole_results[unit_name]):
                    last_copies.append(pltpu.make_async_copy(src, dst, local.at[2 + len(last_copies)]))
                    last_copies[-1].start()
            else:
                rs_stage(unit, stage)

    def points_at(index, names):
        for k, name in enumerate(names):
            if TABLE.get(name):
                pl.when(index == k)(functools.partial(point, name))

    barrier = pltpu.get_barrier_semaphore()
    partners = [*along_z, to_x, to_y, to_c]
    for to in partners:
        pl.semaphore_signal(barrier, inc=1, device_id=to, device_id_type=MESH)
    shards = []
    for g in range(3):
        for j in range(3):
            shards.append((wqkv_ref.at[:, pl.ds(j * width + g * third, third)], slabs.at[g, z, x, core, y, :, pl.ds(j * third, third)]))
    shards.append((wout_ref, slabs.at[3, z, x, core, y]))
    for tile in range(n_z):
        shards.append((wup_ref.at[:, block_columns(tile)], slabs.at[4 + tile, z, x, core, y]))
    shards.append((wdown_ref, downs.at[z, x, core, y]))
    shard_copies = [pltpu.make_async_copy(src, dst, local.at[k]) for k, (src, dst) in enumerate(shards)]
    row_copies = [pltpu.make_async_copy(tok_ref, tok, local.at[len(shards)]), pltpu.make_async_copy(cot_ref, cot, local.at[len(shards) + 1])]
    do_all(shard_copies + row_copies, START)
    smalls[z, x, core, y] = jnp.zeros((8, 128), F32)
    for k, vector in enumerate((v0, v1, v2, v3, v4, v5, v6, v7)):
        smalls[z, x, core, y, k, 0 : vector.shape[0]] = vector[...].astype(F32)
    do_all(shard_copies, "wait")
    pl.semaphore_wait(barrier, len(partners))
    point("mask")
    do_all(row_copies, "wait")

    ends = []
    for k in range(clip_ref.shape[1]):
        ends.append(clip_ref[0, k] + (ends[-1] if ends else 0))

    def segment_of(position):
        total = jnp.zeros(position.shape, jnp.int32)
        for end in ends:
            total = total + jnp.where(position >= end, 1, 0)
        return total

    across = segment_of(lax.broadcasted_iota(jnp.int32, (CHUNK, count), 1))

    def live_of(step):
        position = lax.broadcasted_iota(jnp.int32, (CHUNK, 1), 0) + step * CHUNK
        return jnp.where(position < ends[-1], 1.0, 0.0)

    ones = jnp.ones((8, count), BF16)

    def column_sums(values):
        return nn_dot(ones, values)

    def mask_step(i, carry):
        down = segment_of(lax.broadcasted_iota(jnp.int32, (CHUNK, count), 0) + i * CHUNK)
        bias[rows_of(i), :] = jnp.where(down == across, 0.0, -1e30)
        g2[rows_of(i), :] = (live_of(i) * cot[rows_of(i), :].astype(F32)).astype(BF16)
        return carry

    lax.fori_loop(0, chunks, mask_step, 0)
    sums[...] = jnp.zeros_like(sums)
    up_sums[...] = jnp.zeros_like(up_sums)
    sums[0, 7:8, :] = column_sums(g2[...])[0:1]

    point("vec")
    vec24[...] = spread(smalls[...], 24, width)
    for k in range(2):
        vec48[k] = spread(smalls[k * n_z // 2 : (k + 1) * n_z // 2], 48, width)
    for k in range(n_z):
        vec96[k] = spread(smalls[k], 96, width)
    for g in range(3):
        span = slice(g * third, (g + 1) * third)
        merged_bias[g, 0:1, :] = jnp.concatenate(
            [vec48[0, 2:3, span], jnp.zeros((1, width - 2 * third), F32), vec48[1, 2:3, span]], axis=1
        )

    def norm_one(i, carry):
        normed, _ = norm_parts(tok[rows_of(i), :].astype(F32))
        n1[rows_of(i), :] = (normed * vec24[0:1, :] + vec24[1:2, :]).astype(BF16)
        return carry

    lax.fori_loop(0, chunks, norm_one, 0)

    def turn(source, target):
        def step(i, carry):
            at = rows_of(i, 128)
            target[at, :] = source[:, at].T
            return carry

        lax.fori_loop(0, pairs, step, 0)

    point("turn")
    turn(n1, n1t)

    def assemble(block, target):
        def step(z_at, carry):
            for x_at in range(2):
                for c_at in range(2):
                    two = slabs[block, z_at, x_at, c_at].astype(F32)
                    size = 2 * two.shape[1]
                    first = pl.multiple_of(((z_at * 2 + x_at) * 2 + c_at) * size, 16)
                    target[pl.ds(first, size), :] = two.reshape(size, width).astype(BF16)
            return carry

        lax.fori_loop(0, n_z, step, 0)

    lane = lax.broadcasted_iota(jnp.int32, (count, 128), 1)

    def one_head(values, head):
        keep = lane < 64 if head == 0 else lane >= 64
        return jnp.where(keep, values, jnp.zeros_like(values))

    q_block = 512
    parts = count // q_block
    per_group = pairs // 3

    def places(p):
        first = lax.rem(p, per_group) * 128
        return lax.div(p, per_group), [pl.ds(pl.multiple_of(first + j * third, 128), 128) for j in range(3)]

    def attend(p, carry):
        group, (at_q, at_k, at_v) = places(p)
        points_at(p, [f"q{k // per_group}" if k % per_group == 0 else "" for k in range(pairs)])

        @pl.when(lax.rem(p, per_group) == 0)
        def _():
            assemble(group, weights.at[group])
            qkv[group] = (nn_dot(n1[...], weights[group]) + merged_bias[group, 0:1, :]).astype(BF16)

        points_at(p, [f"t{k}" for k in range(pairs)])
        keys = qkv[group, :, at_k]
        queries = qkv[group, :, at_q] * 0.125
        values_t = qkv[group, :, at_v].T
        for head in range(2):
            mine = one_head(queries, head)
            for part in range(parts):
                span = slice(part * q_block, (part + 1) * q_block)
                scores = nt_dot(keys, mine[span]) + bias[:, span]
                highest = jnp.max(scores, axis=0, keepdims=True)
                raised = jnp.exp(scores - highest)
                total = jnp.sum(raised, axis=0, keepdims=True)
                chances = (raised * (1.0 / total)).astype(BF16)
                lse[p, head : head + 1, span] = highest + jnp.log(total)
                result = nn_dot(values_t[64 * head : 64 * head + 64], chances)
                att_t[pl.ds(pl.multiple_of(p * 128 + 64 * head, 64), 64), span] = result.astype(BF16)
        return carry

    lax.fori_loop(0, pairs, attend, 0)
    point("tb")
    att = n1

    def turn_back(p, carry):
        at = rows_of(p, 128)
        att[:, at] = att_t[at, :].T
        return carry

    lax.fori_loop(0, pairs, turn_back, 0)
    point("out")
    assemble(3, weights.at[3])
    pre[...] = nn_dot(att[...], weights[3])

    def norm_two(i, carry):
        at = rows_of(i)
        branch = pre[at, :] + vec24[3:4, :]
        mid = tok[at, :].astype(F32) + live_of(i) * branch
        middle[at, :] = mid
        normed, _ = norm_parts(mid)
        n2[at, :] = (normed * vec24[4:5, :] + vec24[5:6, :]).astype(BF16)
        return carry

    point("n2a")
    lax.fori_loop(0, chunks // 2, norm_two, 0)
    point("n2b")
    lax.fori_loop(chunks // 2, chunks, norm_two, 0)
    point("n2t")
    turn(n2, n2t)
    acc_out[...] = jnp.zeros_like(acc_out)
    acc_grad[...] = jnp.zeros_like(acc_grad)

    def store_rows(block, lhs_t, rhs):
        size = slabs.shape[-2]
        for first in range(0, width, 192):
            total = nn_dot(lhs_t[first : first + 192, :], rhs)
            for k in range(192 // size // 2):
                at = first // size + 2 * k
                two = total[2 * k * size : 2 * (k + 1) * size].reshape(2, size, width).astype(BF16)
                slabs[block, at // 8, at // 4 % 2, at // 2 % 2] = two

    def feed(t, carry):
        def step_point(name):
            points_at(t, [f"{name}{k}" for k in range(n_z)])

        step_point("fa")
        assemble(4 + t, w_up)
        up_bias = vec96[t, 6:7, :]
        half = count // 2

        def into_hidden(rows):
            pre[rows] = nn_dot(n2[rows], w_up[...])

        def into_grads(rows):
            grad_act[rows] = nt_dot(g2[rows], downs[t].reshape(width, width))

        def gelu_rows(first):
            for at in range(first, first + half, 32):
                rows = slice(at, at + 32)
                active, slope = gelu_both(pre[rows] + up_bias)
                act[rows] = active.astype(BF16)
                grad_h[rows] = (grad_act[rows] * slope).astype(BF16)

        def out_of(rows):
            acc_out[rows] += nn_dot(act[rows], downs[t].reshape(width, width))
            acc_grad[rows] += nt_dot(grad_h[rows], w_up[...])

        upper, lower = slice(0, half), slice(half, count)
        step_point("fb")
        into_hidden(upper)
        step_point("fc")
        into_grads(upper)
        step_point("fd")
        into_hidden(lower)
        into_grads(lower)
        gelu_rows(0)
        step_point("fe")
        out_of(upper)
        gelu_rows(half)
        step_point("ff")
        out_of(lower)
        step_point("fg")
        up_sums[t, 6:7, :] = column_sums(grad_h[...])[0:1]
        step_point("fh")
        store_rows(4 + t, n2t, grad_h[...])
        step_point("fi")
        for j in range(pairs):
            span = slice(j * 128, (j + 1) * 128)
            piece = nn_dot(act[:, span].T, g2[...]).astype(BF16)
            size = downs.shape[-2]
            at = j * 128
            while at < (j + 1) * 128:
                owner, inside = at // size, at % size
                length = min(size - inside, (j + 1) * 128 - at)
                downs[t, owner // 4, owner // 2 % 2, owner % 2, inside : inside + length, :] = piece[at - j * 128 : at - j * 128 + length]
                at += length
        return carry

    lax.fori_loop(0, n_z, feed, 0)

    def norm_two_back(i, carry):
        gain_sum, bias_sum = carry
        at = rows_of(i)
        alive = live_of(i)
        mid = middle[at, :]
        block_out[at, :] = (mid + alive * (acc_out[at, :] + vec24[7:8, :])).astype(BF16)
        normed, scale = norm_parts(mid)
        e = acc_grad[at, :]
        scaled = e * vec24[4:5, :]
        inner_part = scaled - jnp.mean(scaled, axis=-1, keepdims=True) - normed * jnp.mean(scaled * normed, axis=-1, keepdims=True)
        grad_mid = cot[at, :].astype(F32) + inner_part * scale
        acc_grad[at, :] = grad_mid
        g2[at, :] = (alive * grad_mid).astype(BF16)
        return (gain_sum + fold_rows(e * normed), bias_sum + fold_rows(e))

    zero = jnp.zeros((8, width), F32)
    block_out = act
    point("ba")
    carry = lax.fori_loop(0, chunks // 2, norm_two_back, (zero, zero))
    point("bb")
    gain_sum, bias_sum = lax.fori_loop(chunks // 2, chunks, norm_two_back, carry)
    sums[0, 4:5, :] = jnp.sum(gain_sum, axis=0, keepdims=True)
    sums[0, 5:6, :] = jnp.sum(bias_sum, axis=0, keepdims=True)
    sums[0, 3:4, :] = column_sums(g2[...])[0:1]
    out_copy = pltpu.make_async_copy(block_out, out_ref, local.at[0])
    out_copy.start()

    point("og")
    store_rows(3, att_t, g2[...])
    point("ga")
    grad_att = n2
    grad_att[...] = nt_dot(g2[...], weights[3]).astype(BF16)

    def attend_back(p, carry):
        group, (at_q, at_k, at_v) = places(p)
        points_at(p, [f"a{k}" for k in range(pairs)])
        keys = qkv[group, :, at_k]
        values = qkv[group, :, at_v]
        queries = qkv[group, :, at_q] * 0.125
        grads = grad_att[:, rows_of(p, 128)]
        keys_t = keys.T
        grad_keys = jnp.zeros((count, 128), F32)
        grad_values = jnp.zeros((count, 128), F32)
        for head in range(2):
            my_queries, my_grads = one_head(queries, head), one_head(grads, head)
            for part in range(parts):
                span = slice(part * q_block, (part + 1) * q_block)
                scores = nt_dot(keys, my_queries[span]) + bias[:, span]
                chances = jnp.exp(scores - lse[p, head : head + 1, span])
                slopes = nt_dot(values, my_grads[span])
                level = jnp.sum(chances * slopes, axis=0, keepdims=True)
                grad_scores = (chances * (slopes - level)).astype(BF16)
                grad_values += nn_dot(chances.astype(BF16), my_grads[span])
                grad_keys += nn_dot(grad_scores, my_queries[span])
                dq_t[64 * head : 64 * head + 64, span] = nn_dot(keys_t[64 * head : 64 * head + 64], grad_scores) * 0.125
        qkv[group, :, at_q] = dq_t[...].T.astype(BF16)
        qkv[group, :, at_k] = grad_keys.astype(BF16)
        qkv[group, :, at_v] = grad_values.astype(BF16)
        points_at(p, [f"H{k // per_group}" if k % per_group == per_group - 1 else "" for k in range(pairs)])

        @pl.when(lax.rem(p, per_group) == per_group - 1)
        def _():
            store_rows(group, n1t, qkv[group])
            group_sums[group] = column_sums(qkv[group])

        return carry

    lax.fori_loop(0, pairs, attend_back, 0)

    point("g2")
    pre[...] = nt_dot(qkv[2], weights[2])
    point("g1")
    pre[...] += nt_dot(qkv[1], weights[1])
    point("g0")
    pre[...] += nt_dot(qkv[0], weights[0])

    def norm_one_back(i, carry):
        gain_sum, bias_sum = carry
        at = rows_of(i)
        normed, scale = norm_parts(tok[at, :].astype(F32))
        e = pre[at, :]
        scaled = e * vec24[0:1, :]
        inner_part = scaled - jnp.mean(scaled, axis=-1, keepdims=True) - normed * jnp.mean(scaled * normed, axis=-1, keepdims=True)
        acc_grad[at, :] = acc_grad[at, :] + inner_part * scale
        return (gain_sum + fold_rows(e * normed), bias_sum + fold_rows(e))

    point("na")
    carry = lax.fori_loop(0, chunks // 2, norm_one_back, (zero, zero))
    point("nb")
    gain_sum, bias_sum = lax.fori_loop(chunks // 2, chunks, norm_one_back, carry)
    tgrad_copy = pltpu.make_async_copy(acc_grad, tgrad_ref, local.at[1])
    tgrad_copy.start()
    sums[0, 0:1, :] = jnp.sum(gain_sum, axis=0, keepdims=True)
    sums[0, 1:2, :] = jnp.sum(bias_sum, axis=0, keepdims=True)
    for g in range(3):
        span = slice(g * third, (g + 1) * third)
        sums[1, 2:3, span] = group_sums[g, 0:1, :third]
        sums[2, 2:3, span] = group_sums[g, 0:1, 2 * third :]
    point("gb")
    gsmalls[...] = gather_back(sums[0], 24).reshape(gsmalls.shape)
    for k in range(2):
        part = gather_back(sums[1 + k], 48)
        span = slice(k * n_z // 2, (k + 1) * n_z // 2)
        gsmalls[span] = gsmalls[span] + part.reshape(n_z // 2, 2, 2, 2, 8, 128)
    for k in range(n_z):
        gsmalls[k] = gsmalls[k] + gather_back(up_sums[k], 96).reshape(2, 2, 2, 8, 128)

    point(LAST_POINT)
    for unit_name in dict(TABLE[LAST_POINT][-2:]):
        rs_sent(units[unit_name])
    out_copy.wait()
    tgrad_copy.wait()
    do_all(last_copies, "wait")


def by_kernel(
    n_z, tokens, cotangent, clip_lengths, ln1_gain, ln1_bias, qkv_weight, qv_bias, out_weight, out_bias,
    ln2_gain, ln2_bias, up_weight, up_bias, down_weight, down_bias,
):
    count, width = tokens.shape
    size, deep = qkv_weight.shape[0], down_weight.shape[0]
    blocks = 4 + n_z
    vectors = (ln1_gain, ln1_bias, qv_bias, out_bias, ln2_gain, ln2_bias, up_bias, down_bias)
    vmem, dma = pltpu.VMEM, pltpu.SemaphoreType.DMA
    held = [
        vmem((blocks, n_z, 2, 2, 2, size, width), BF16),
        vmem((n_z, 2, 2, 2, deep, width), BF16),
        vmem((n_z, 2, 2, 2, 8, 128), F32),
        vmem((n_z, 2, 2, 2, 8, 128), F32),
        vmem((4, width, width), BF16),
        vmem((width, width), BF16),
        vmem((blocks, n_z, 2, 2, size, width), BF16),
        vmem((blocks - len(LATE_SUMS), 2, n_z, size, width // 2), BF16),
        vmem((blocks - len(LATE_SUMS), 2, n_z, size, width), BF16),
        vmem((blocks - len(LATE_SUMS), n_z, size, width), BF16),
        vmem((max(len(LATE_SUMS), 1), 2, size, width // 2), BF16),
        vmem((max(len(LATE_SUMS), 1), 2, size, width), BF16),
        vmem((max(len(LATE_SUMS), 1), n_z, 2, 2, size, width), BF16),
        vmem((n_z, 2, 2, deep, width), BF16),
        vmem((n_z, 2, deep, width // 2), BF16),
        vmem((n_z, 2, deep, width), BF16),
        vmem((n_z, deep, width), BF16),
        vmem((n_z, 2, 2, 8, 128), F32),
        vmem((n_z, 8, 128), F32),
        vmem((2, n_z, 8, 128), F32),
        vmem((n_z - 1, 8, 128), F32),
        vmem((3, count, width), BF16),
        vmem((width, count), BF16),
        vmem((count, width), BF16),
        vmem((width, count), BF16),
        vmem((count, width), F32),
        vmem((count, width), BF16),
        vmem((width, count), BF16),
        vmem((count, width), BF16),
        vmem((count, width), F32),
        vmem((count, width), F32),
        vmem((count, width), BF16),
        vmem((count, width), BF16),
        vmem((count, width), F32),
        vmem((count, width), F32),
        vmem((count, width), BF16),
        vmem((count, width), BF16),
        vmem((count, count), F32),
        vmem((width // 128, 2, count), F32),
        vmem((128, count), F32),
        vmem((8, width), F32),
        vmem((2, 8, width), F32),
        vmem((n_z, 8, width), F32),
        vmem((3, 8, width), F32),
        vmem((3, 8, width), F32),
        vmem((3, 8, width), F32),
        vmem((n_z, 8, width), F32),
        vmem(qkv_weight.shape, F32),
        vmem(out_weight.shape, F32),
        vmem(up_weight.shape, F32),
        vmem(down_weight.shape, F32),
        vmem((8, 128), F32),
        dma((semaphore_slots()[2],)),
        dma((len(semaphore_slots()[0]),)),
        dma((len(semaphore_slots()[1]),)),
        dma((16 + n_z,)),
    ]
    anywhere, whole = pl.BlockSpec(memory_space=pl.ANY), pl.BlockSpec(memory_space=pltpu.VMEM)
    shape = jax.ShapeDtypeStruct
    out, grad, g_qkv, g_out, g_up, g_down, g_small = pl.pallas_call(
        layer_kernel,
        out_shape=(
            shape((count, width), BF16),
            shape((count, width), F32),
            shape(qkv_weight.shape, F32),
            shape(out_weight.shape, F32),
            shape(up_weight.shape, F32),
            shape(down_weight.shape, F32),
            shape((8, 128), F32),
        ),
        in_specs=[pl.BlockSpec(memory_space=pltpu.SMEM)] + [anywhere] * 2 + [whole] * 8 + [anywhere] * 4,
        out_specs=(anywhere,) * 7,
        scratch_shapes=held,
        compiler_params=pltpu.CompilerParams(collective_id=0, has_side_effects=True, vmem_limit_bytes=VMEM_BYTES),
    )(clip_lengths, tokens, cotangent, *vectors, qkv_weight, out_weight, up_weight, down_weight)
    large = (out, grad, g_qkv, g_out, g_up, g_down)
    done = pl.pallas_call(
        hand_over,
        out_shape=tuple(shape(a.shape, a.dtype) for a in large) + tuple(shape(v.shape, F32) for v in vectors),
        in_specs=[anywhere] * (1 + len(large)),
        out_specs=(anywhere,) * (len(large) + len(vectors)),
        scratch_shapes=[vmem(a.shape, a.dtype) for a in (g_small, *large)] + [vmem(v.shape, F32) for v in vectors] + [dma((2, 24))],
    )(g_small, *large)
    out, grad, g_qkv, g_out, g_up, g_down = done[:6]
    parts = done[6:]
    return (out, grad, parts[0], parts[1], g_qkv, parts[2], g_out, parts[3], parts[4], parts[5], g_up, parts[6], g_down, parts[7])


def hand_over(*refs):
    small_ref, sources, targets, vectors = refs[0], refs[1:7], refs[7:13], refs[13:21]
    small, held, cut, sems = refs[21], refs[22:28], refs[28:36], refs[36]
    small_copy = pltpu.make_async_copy(small_ref, small, sems.at[0, 23])
    small_copy.start()
    pieces = []
    for src, mid, dst in zip(sources, held, targets):
        rows = src.shape[0]
        parts = 4 if rows % 64 == 0 else 1
        for k in range(parts):
            pieces.append([ref.at[pl.ds(k * (rows // parts), rows // parts)] for ref in (src, mid, dst)])
    inward = [pltpu.make_async_copy(src, mid, sems.at[0, k]) for k, (src, mid, _) in enumerate(pieces)]
    outward = [pltpu.make_async_copy(mid, dst, sems.at[1, k]) for k, (_, mid, dst) in enumerate(pieces)]
    for copy in inward:
        copy.start()
    small_copy.wait()
    cuts = []
    for k, (part, vector) in enumerate(zip(cut, vectors)):
        part[...] = small[k, 0 : part.shape[0]]
        cuts.append(pltpu.make_async_copy(part, vector, sems.at[1, 15 + k]))
        cuts[-1].start()
    for arrived, onward in zip(inward, outward):
        arrived.wait()
        onward.start()
    for copy in outward + cuts:
        copy.wait()


def step(**named):
    return next(iter(named.items()))


KINDS = dict(
    ab1=BOOT,
    ab2=BOOT,
    au0=DIRECT,
    au1=LATE,
    au2=LATE,
    au3=BOOT,
    ro=LATE,
    ru0=LATE,
    ru2=LATE,
)
LATE_SUMS = tuple(dict(ro=0, ru0=0, ru2=0))
TABLE = dict(
    mask=(step(au0=0), step(ab1=0), step(au2=0), step(ab2=0),),
    vec=(step(ab0=0), step(au3=0), step(aS=0), step(ab1=1), step(au2=1), step(ab3=0), step(au0=1), step(ab0=1), step(ab2=1), step(aS=1), step(ab1=2), step(adp=0), step(au0=2), step(au1=0), step(aS=2), step(ab1=3), step(ab3=1), step(ab0=2), step(au0=3), step(aS=3), step(au1=1), step(au0=4), step(ab2=2), step(aS=4),),
    turn=(step(ab1=4),),
    q0=(step(ab2=3), step(adp=1), step(au1=2), step(ab0=3), step(ab1=5), step(ab3=2), step(ab1=6), step(ab2=4), step(ab0=4), step(adp=2), step(ad0=0), step(ab0=5),),
    t1=(step(ab3=3), step(au1=3), step(au3=1),),
    q1=(step(ad1=0), step(ab2=5),),
    q2=(step(ad0=1), step(au2=2), step(ab2=6),),
    t4=(step(ab3=4), step(au1=4),),
    t5=(step(ad2=0),),
    tb=(step(ab3=5),),
    n2a=(step(au1=5), step(ad1=1),),
    n2b=(step(ad0=2),),
    fa0=(step(au3=2),),
    fc0=(step(au3=3), step(ad0=3),),
    fe0=(step(ad2=1),),
    ff0=(step(au2=3),),
    fg0=(step(ad1=2), step(ad3=0),),
    fi0=(step(ru0=0),),
    fa1=(step(rd0=0),),
    fc1=(step(ad1=3),),
    fe1=(step(au3=4),),
    ff1=(step(ru0=1), step(ad2=2),),
    fg1=(step(rd0=1), step(au2=4),),
    fi1=(step(ru1=0),),
    fa2=(step(rd1=0), step(ad2=3), step(ad3=1), step(au2=5),),
    fc2=(step(au3=5),),
    fe2=(step(ru1=1), step(ru0=2), step(rd0=2),),
    fg2=(step(ad3=2),),
    fi2=(step(ru2=0), step(au3=6),),
    fa3=(step(rd1=1), step(rd2=0),),
    fc3=(step(ad3=3),),
    fe3=(step(ru1=2), step(ru2=1),),
    fg3=(step(rd0=3),),
    fi3=(step(ru3=0), step(rd2=1),),
    ba=(step(rd3=0),),
    bb=(step(rd1=2),),
    ga=(step(ro=0), step(ru2=2),),
    a1=(step(ru3=1), step(rd3=1), step(ro=1),),
    H0=(step(rd1=3), step(rd2=2),),
    a2=(step(ru1=3), step(rh0=0),),
    a3=(step(ro=2), step(ru3=2),),
    H1=(step(rd3=2),),
    a4=(step(rh1=0), step(rd2=3),),
    a5=(step(rh1=1), step(ru3=3),),
    H2=(step(ru1=4), step(rh0=1), step(ru0=3),),
    g2=(step(rh2=0), step(ru3=4), step(rd3=3), step(rdl=0), step(ru2=3),),
    g0=(step(rh1=2),),
    nb=(step(rh2=1),),
    end=(step(ro=3), step(rS=0), step(ru1=5), step(rdl=1), step(ru3=5), step(rh0=2), step(rS=1), step(ru0=4), step(rh2=2), step(rh1=3), step(rh0=3), step(ro=4), step(rS=2), step(rh1=4), step(ru0=5), step(ru2=4), step(rh0=4), step(rdl=2), step(rh2=3), step(ro=5), step(rS=3), step(ru2=5), step(rh1=5), step(rh2=4), step(rh0=5), step(rS=4), step(rh2=5),),
)

ROW_SUMS = tuple(dict(rh0=0, rh1=0, rh2=0, ro=0, ru0=0, ru1=0, ru2=0, ru3=0))
VMEM_BYTES = 63 * 1024 * 1024


def kernel_fits(n_wide, n_narrow, tokens, qkv_weight, up_weight, down_weight):
    width, hidden = qkv_weight.shape[0], up_weight.shape[1]
    n_z = n_wide // 4
    devices = n_wide * n_narrow
    return (
        n_narrow == 2
        and n_wide == 4 * n_z
        and n_z == 4
        and hidden == n_z * width
        and width % (8 * devices) == 0
        and hidden % (16 * devices) == 0
        and 2 * width // devices <= 128
        and hidden // devices <= 128
        and width // devices == 24
        and (tokens.shape[0] // devices) % (2 * CHUNK) == 0
    )


def solution(mesh):
    n_wide, n_narrow = [mesh.shape[axis] for axis in BOTH_AXES]
    matrix, vector = P(BOTH_AXES, None), P(BOTH_AXES)
    in_specs = (
        matrix, matrix, matrix, vector, vector, matrix, vector, matrix, vector, vector, vector, matrix, vector, matrix, vector,
    )
    out_specs = (
        matrix, matrix, vector, vector, matrix, vector, matrix, vector, vector, vector, matrix, vector, matrix, vector,
    )

    def run(*arrays):
        fits = kernel_fits(n_wide, n_narrow, arrays[0], arrays[5], arrays[11], arrays[13])
        body = functools.partial(by_kernel, n_wide // 4) if fits else by_collectives
        return jax.shard_map(body, mesh=mesh, in_specs=in_specs, out_specs=out_specs, check_vma=False)(*arrays)

    return run
```
